32 devices in a mesh: gx: 8 (over y, x, core), gy: 4 (over z).
Axes of the slice: x: 2, y: 2, z: 4, core: 2. Of those that a mesh axis runs over, the one named last changes fastest.
Arguments:
- thermal_anomaly: float32 [32, 12, 38400], P(('gx', 'gy')), may hold values from -4 to 4
- zonal_flow_ratio: float32 [32, 12, 38400], P(('gx', 'gy')), may hold values from -0.9 to 0.9
- meridional_flow_ratio: float32 [32, 12, 38400], P(('gx', 'gy')), may hold values from -0.9 to 0.9
- diffusion_rates: float32 [32, 11, 38400], P(('gx', 'gy')), may hold values from 0.05 to 5
- ocean_bottom_scaled: float32 [32, 38400], P(('gx', 'gy')), may hold values from 0.5 to 2
- ocean_indicator: int32 [32, 38400], P(('gx', 'gy')), may hold values 0 or 1
- operator_diagonal: float32 [32, 38400], P(('gx', 'gy')), may hold values from 0.05 to 0.5
- elevation_source: float32 [32, 38400], P(('gx', 'gy')), may hold values from -32 to 32
- block_positions: int32 [32], replicated, may hold values from 0 to 31, as said below
Outputs:
- new_temp: float32 [32, 12, 38400], P(('gx', 'gy'))
- surface_height: float32 [32, 38400], P(('gx', 'gy'))
The draws below stay inside these ranges and needn't reach their ends.
Inputs may be any that keep to these rules, and one draw needn't show every extreme that they name: `block_positions`: A permutation of 0 to 31. Tiles held by consecutive devices (the last and the first counted as consecutive) share an edge of the tile grid, which is periodic along x, except for two such pairs, 16 apart.
All inputs are finite; a program needn't handle non-finite values. No bound on the sum of `ocean_indicator` on one device may be relied on, other than what follows from the above.
Results may differ from the reference program's by a relative error of at most 0.0001.
Values sent between devices are 32-bit elements; how exact they have to be, the bound alone decides.
No kernel may reach another device: no remote copies, remote signals or barrier semaphores. Data moves between devices by JAX's collectives and lax.ppermute only.
A program may use at most 128 MiB of HBM per device.

```python
import math
from functools import partial
import jax
import jax.numpy as jnp
from jax import lax

DEPTH_LAYERS = 12
ITERS = 4
BLOCK_SPAN_EAST = 240
BLOCK_SPAN_NORTH = 160
TILES_X = 8
TILES_Y = 4
BLOCK_TOTAL = 32


def hilbert_cells(side, curve_index):
    coord_x = jnp.zeros_like(curve_index)
    coord_y = jnp.zeros_like(curve_index)
    remain = curve_index
    scale_now = 1
    while scale_now < side:
        turn_x = remain // 2 % 2
        turn_y = (remain + turn_x) % 2
        flipped = jnp.logical_and(turn_y == 0, turn_x == 1)
        first_x = jnp.where(flipped, scale_now - 1 - coord_x, coord_x)
        first_y = jnp.where(flipped, scale_now - 1 - coord_y, coord_y)
        swapped = turn_y == 0
        coord_x = jnp.where(swapped, first_y, first_x) + scale_now * turn_x
        coord_y = jnp.where(swapped, first_x, first_y) + scale_now * turn_y
        remain = remain // 4
        scale_now = scale_now * 2
    return (coord_x, coord_y)


def draw_block_positions(key, part):
    key = jax.random.fold_in(key, 5)
    key_shift, key_fx, key_fy = jax.random.split(key, 3)
    side = TILES_Y
    half_count = side * side
    offset = jax.random.randint(key_shift, (), 0, BLOCK_TOTAL)
    flip_x = jax.random.randint(key_fx, (), 0, 2)
    flip_y = jax.random.randint(key_fy, (), 0, 2)
    curve = (jnp.arange(BLOCK_TOTAL, dtype=jnp.int32) + offset) % BLOCK_TOTAL
    square = curve // half_count
    local = curve % half_count
    local = jnp.where(square == 1, half_count - 1 - local, local)
    coord_x, coord_y = hilbert_cells(side, local)
    coord_x = coord_x + side * square
    coord_x = jnp.where(flip_x == 1, TILES_X - 1 - coord_x, coord_x)
    coord_y = jnp.where(flip_y == 1, TILES_Y - 1 - coord_y, coord_y)
    return (coord_y * TILES_X + coord_x).astype(jnp.int32)


def draw_elevation_source(key, part):
    key = jax.random.fold_in(key, 11)
    key_base, key_row, key_col = jax.random.split(key, 3)
    ramp = 1.0 + 2.0 * jnp.arange(BLOCK_TOTAL, dtype=jnp.float32) / max(BLOCK_TOTAL - 1, 1)
    row_scale = jnp.exp(jax.random.uniform(key_row, (BLOCK_TOTAL, BLOCK_SPAN_NORTH, 1), jnp.float32, 0.0, 1.15))
    col_scale = jnp.exp(jax.random.uniform(key_col, (BLOCK_TOTAL, 1, BLOCK_SPAN_EAST), jnp.float32, 0.0, 1.15))
    values = jnp.clip(jax.random.normal(key_base, (BLOCK_TOTAL, BLOCK_SPAN_NORTH, BLOCK_SPAN_EAST), jnp.float32), -4.0, 4.0)
    result = 0.25 * values * row_scale * col_scale * ramp[:, None, None]
    return result.reshape(BLOCK_TOTAL, BLOCK_SPAN_NORTH * BLOCK_SPAN_EAST).astype(jnp.float32)


def plant(array, own_key, low, high):
    spot = [jax.random.randint(jax.random.fold_in(own_key, axis), (), 0, length) for axis, length in enumerate(array.shape)]
    longest = array.shape.index(max(array.shape))
    beside = spot[:longest] + [(spot[longest] + 1) % array.shape[longest]] + spot[longest + 1:]
    return array.at[tuple(spot)].set(low).at[tuple(beside)].set(high)


def block_scale(key, dims, cuts, low, high):
    gain = 1.0
    for dim, parts in cuts:
        heights = jax.random.uniform(jax.random.fold_in(jax.random.fold_in(key, 6), dim), (parts,), jnp.float32, low / len(cuts), high / len(cuts))
        gain = gain * jnp.repeat(jnp.exp(heights), dims[dim] // parts).reshape((-1,) + (1,) * (len(dims) - 1 - dim))
    return gain


def noise(rng, extent, spread, limit, cuts=(), kind=jnp.bfloat16):
    drawn = spread * jax.random.normal(rng, extent, jnp.float32)
    if cuts:
        drawn = drawn * block_scale(rng, extent, cuts, -0.22, 0.18)
    return jnp.clip(drawn, -limit, limit).astype(kind)


def setup_inputs(seed: int = 0) -> dict:
    key_list = jax.random.split(jax.random.key(seed), 10)
    thermal_anomaly = noise(key_list[0], (BLOCK_TOTAL, DEPTH_LAYERS, BLOCK_SPAN_NORTH * BLOCK_SPAN_EAST), 1.0, 4.0, ((0, 32),), jnp.float32)
    zonal_flow_ratio = noise(key_list[1], (BLOCK_TOTAL, DEPTH_LAYERS, BLOCK_SPAN_NORTH * BLOCK_SPAN_EAST), 0.3, 0.9, ((0, 32),), jnp.float32)
    meridional_flow_ratio = noise(key_list[2], (BLOCK_TOTAL, DEPTH_LAYERS, BLOCK_SPAN_NORTH * BLOCK_SPAN_EAST), 0.3, 0.9, ((0, 32),), jnp.float32)
    diffusion_rates = jnp.clip(jnp.exp(math.log(5.0) - 4.6051702 * jax.random.uniform(key_list[3], (BLOCK_TOTAL, DEPTH_LAYERS - 1, BLOCK_SPAN_NORTH * BLOCK_SPAN_EAST), jnp.float32) ** block_scale(key_list[3], (BLOCK_TOTAL, DEPTH_LAYERS - 1, BLOCK_SPAN_NORTH * BLOCK_SPAN_EAST), ((0, 32),), -0.2, 0.2)), 0.05, 5.0)
    ocean_bottom_scaled = jnp.clip(0.5 + 1.5 * jax.random.uniform(key_list[4], (BLOCK_TOTAL, BLOCK_SPAN_NORTH * BLOCK_SPAN_EAST), jnp.float32) ** block_scale(key_list[4], (BLOCK_TOTAL, BLOCK_SPAN_NORTH * BLOCK_SPAN_EAST), ((0, 32),), -0.2, 0.2), 0.5, 2.0)
    ocean_indicator = plant((jax.random.randint(key_list[5], (BLOCK_TOTAL, BLOCK_SPAN_NORTH * BLOCK_SPAN_EAST), 0, 4) < 3).astype(jnp.int32), jax.random.fold_in(key_list[5], 1), 0, 1)
    operator_diagonal = jnp.clip(jnp.exp(math.log(0.5) - 2.3025851 * jax.random.uniform(key_list[6], (BLOCK_TOTAL, BLOCK_SPAN_NORTH * BLOCK_SPAN_EAST), jnp.float32) ** block_scale(key_list[6], (BLOCK_TOTAL, BLOCK_SPAN_NORTH * BLOCK_SPAN_EAST), ((0, 32),), -0.2, 0.2)), 0.05, 0.5)
    elevation_source = draw_elevation_source(jax.random.fold_in(key_list[9], 71), 0)
    block_positions = draw_block_positions(jax.random.fold_in(key_list[9], 71), 0)
    return dict(thermal_anomaly=thermal_anomaly, zonal_flow_ratio=zonal_flow_ratio, meridional_flow_ratio=meridional_flow_ratio, diffusion_rates=diffusion_rates, ocean_bottom_scaled=ocean_bottom_scaled, ocean_indicator=ocean_indicator, operator_diagonal=operator_diagonal, elevation_source=elevation_source, block_positions=block_positions)


ADVECT = 0.25
DIFFUSE = 0.12
STERIC = 0.5


def blocks_onto_domain(tiled, block_positions):
    leading = tiled.shape[1:-1]
    count_lead = len(leading)
    placed = jnp.zeros_like(tiled).at[block_positions].set(tiled)
    placed = placed.reshape((TILES_Y, TILES_X) + leading + (BLOCK_SPAN_NORTH, BLOCK_SPAN_EAST))
    axis_order = tuple(range(2, 2 + count_lead)) + (0, 2 + count_lead, 1, 3 + count_lead)
    return placed.transpose(axis_order).reshape(leading + (TILES_Y * BLOCK_SPAN_NORTH, TILES_X * BLOCK_SPAN_EAST))


def to_tiles(grid_field, block_positions):
    leading = grid_field.shape[:-2]
    count_lead = len(leading)
    blocks = grid_field.reshape(leading + (TILES_Y, BLOCK_SPAN_NORTH, TILES_X, BLOCK_SPAN_EAST))
    axis_order = (count_lead, count_lead + 2) + tuple(range(count_lead)) + (count_lead + 1, count_lead + 3)
    blocks = blocks.transpose(axis_order).reshape((BLOCK_TOTAL,) + leading + (BLOCK_SPAN_NORTH * BLOCK_SPAN_EAST,))
    return blocks[block_positions]


def east_of(source):
    return jnp.roll(source, -1, axis=-1)


def west_of(source):
    return jnp.roll(source, 1, axis=-1)


def north_of(source):
    empty_row = jnp.zeros_like(source[..., :1, :])
    return jnp.concatenate([source[..., 1:, :], empty_row], axis=-2)


def south_of(source):
    empty_row = jnp.zeros_like(source[..., :1, :])
    return jnp.concatenate([empty_row, source[..., :-1, :]], axis=-2)


def horizontal(level_data, wet_cells):
    scalar_quantity, zonal_vel, merid_vel = level_data
    flux_x = zonal_vel * scalar_quantity
    flux_y = merid_vel * scalar_quantity
    east_term = -ADVECT * flux_x + DIFFUSE * scalar_quantity
    west_term = ADVECT * flux_x + DIFFUSE * scalar_quantity
    north_term = -ADVECT * flux_y + DIFFUSE * scalar_quantity
    south_term = ADVECT * flux_y + DIFFUSE * scalar_quantity
    tendency = east_of(east_term) + west_of(west_term) + north_of(north_term) + south_of(south_term) - 4.0 * DIFFUSE * scalar_quantity
    return scalar_quantity + wet_cells * tendency


def vertical_solve(stepped, mixing_rates):
    count_levels = stepped.shape[0]
    gain_list = []
    partial_sol = []
    for level_at in range(count_levels):
        pivot_val = jnp.ones_like(stepped[0])
        source = stepped[level_at]
        if level_at > 0:
            upper_rate = mixing_rates[level_at - 1]
            pivot_val = pivot_val + upper_rate - upper_rate * gain_list[-1]
            source = source + upper_rate * partial_sol[-1]
        if level_at < count_levels - 1:
            pivot_val = pivot_val + mixing_rates[level_at]
            gain_list.append(mixing_rates[level_at] / pivot_val)
        else:
            gain_list.append(jnp.zeros_like(pivot_val))
        partial_sol.append(source / pivot_val)
    result = [partial_sol[-1]]
    for level_at in range(count_levels - 2, -1, -1):
        result.insert(0, partial_sol[level_at] + gain_list[level_at] * result[0])
    return jnp.stack(result)


def reference(thermal_anomaly, zonal_flow_ratio, meridional_flow_ratio, diffusion_rates, ocean_bottom_scaled, ocean_indicator, operator_diagonal, elevation_source, block_positions):
    scalar_quantity = blocks_onto_domain(thermal_anomaly, block_positions)
    zonal_vel = blocks_onto_domain(zonal_flow_ratio, block_positions)
    merid_vel = blocks_onto_domain(meridional_flow_ratio, block_positions)
    wet_cells = blocks_onto_domain(ocean_indicator.astype(jnp.float32), block_positions)
    stepped = lax.map(partial(horizontal, wet_cells=wet_cells), (scalar_quantity, zonal_vel, merid_vel))
    new_tracer = vertical_solve(stepped, blocks_onto_domain(diffusion_rates, block_positions))
    masked_depth = blocks_onto_domain(ocean_bottom_scaled, block_positions) * wet_cells
    weight_east = masked_depth * east_of(masked_depth)
    weight_west = masked_depth * west_of(masked_depth)
    weight_north = masked_depth * north_of(masked_depth)
    weight_south = masked_depth * south_of(masked_depth)
    centre = blocks_onto_domain(operator_diagonal, block_positions) + weight_east + weight_west + weight_north + weight_south

    def operate(vector):
        beside_sum = weight_east * east_of(vector) + weight_west * west_of(vector) + weight_north * north_of(vector) + weight_south * south_of(vector)
        return centre * vector - beside_sum

    forcing = blocks_onto_domain(elevation_source, block_positions) + STERIC * wet_cells * (jnp.sum(new_tracer, axis=0) / DEPTH_LAYERS)
    solution = jnp.zeros_like(forcing)
    residual = forcing
    direction = forcing
    norm_now = jnp.sum(residual * residual)
    for iteration in range(ITERS):
        image_vec = operate(direction)
        step_size = norm_now / jnp.sum(direction * image_vec)
        solution = solution + step_size * direction
        residual = residual - step_size * image_vec
        norm_next = jnp.sum(residual * residual)
        direction = residual + (norm_next / norm_now) * direction
        norm_now = norm_next
    return to_tiles(new_tracer, block_positions), to_tiles(solution, block_positions)
```

```python
import jax
import jax.numpy as jnp
from jax import lax
from jax.sharding import PartitionSpec as P

ITERS = 4
SPAN_X = 240
SPAN_Y = 160
RIM = 4
ADVECT = 0.25
DIFFUSE = 0.12
STERIC = 0.5
LOW_RATE = 0.05
ROOTS = (0.02, 0.35, 0.1, 0.2)
BOTH = ("gx", "gy")
SIDES = ((-1, 0), (1, 0), (0, -1), (0, 1), (-1, -1), (1, -1), (-1, 1), (1, 1))


def neighbour_table(block_positions, tiles_x, tiles_y):
    count = block_positions.shape[0]
    ids = jnp.arange(count, dtype=jnp.int32)
    column = block_positions % tiles_x
    row = block_positions // tiles_x
    table = []
    for dx, dy in SIDES:
        target_row = row + dy
        target = target_row * tiles_x + (column + dx + tiles_x) % tiles_x
        match = target[:, None] == block_positions[None, :]
        found = jnp.sum(jnp.where(match, ids[None, :], 0), axis=1)
        inside = jnp.logical_and(target_row >= 0, target_row < tiles_y)
        table.append(jnp.where(inside, found, -1))
    return jnp.stack(table)


def shift(field, dx, dy):
    rows, columns = field.shape[-2:]
    if dx == 1:
        return jnp.concatenate([field[..., 1:], jnp.zeros_like(field[..., :1])], axis=-1)
    if dx == -1:
        return jnp.concatenate([jnp.zeros_like(field[..., :1]), field[..., :-1]], axis=-1)
    if dy == 1:
        return jnp.concatenate([field[..., 1:, :], jnp.zeros_like(field[..., :1, :])], axis=-2)
    return jnp.concatenate([jnp.zeros_like(field[..., :1, :]), field[..., :-1, :]], axis=-2)


def vertical_solve(stepped, mixing_rates):
    count_levels = stepped.shape[0]
    gain_list = []
    partial_sol = []
    for level_at in range(count_levels):
        pivot_val = jnp.ones_like(stepped[0])
        source = stepped[level_at]
        if level_at > 0:
            upper_rate = mixing_rates[level_at - 1]
            pivot_val = pivot_val + upper_rate - upper_rate * gain_list[-1]
            source = source + upper_rate * partial_sol[-1]
        if level_at < count_levels - 1:
            pivot_val = pivot_val + mixing_rates[level_at]
            gain_list.append(mixing_rates[level_at] / pivot_val)
        partial_sol.append(source / pivot_val)
    result = [partial_sol[-1]]
    for level_at in range(count_levels - 2, -1, -1):
        result.insert(0, partial_sol[level_at] + gain_list[level_at] * result[0])
    return jnp.stack(result)


def pick(stacked, index):
    return lax.dynamic_index_in_dim(stacked, index, 0, keepdims=False)


def tree_sum(value, nx, ny):
    for axis, size in (("gy", ny), ("gx", nx)):
        step = 1
        while step < size:
            value = value + lax.ppermute(value, axis, [(i, i ^ step) for i in range(size)])
            step *= 2
    return value


def on_device(
    thermal_anomaly,
    zonal_flow_ratio,
    meridional_flow_ratio,
    diffusion_rates,
    ocean_bottom_scaled,
    ocean_indicator,
    operator_diagonal,
    elevation_source,
    block_positions,
):
    levels = thermal_anomaly.shape[1]
    nx = lax.axis_size("gx")
    ny = lax.axis_size("gy")
    my_x = lax.axis_index("gx")
    my_y = lax.axis_index("gy")
    me = my_x * ny + my_y
    table = neighbour_table(block_positions, nx, ny)
    mine = lax.dynamic_index_in_dim(table, me, 1, keepdims=False)

    def plane(array):
        return array[0].reshape(array.shape[1:-1] + (SPAN_Y, SPAN_X))

    temp = plane(thermal_anomaly)
    flux_x = ADVECT * plane(zonal_flow_ratio) * temp
    flux_y = ADVECT * plane(meridional_flow_ratio) * temp
    spread = DIFFUSE * temp
    wet = plane(ocean_indicator).astype(jnp.float32)
    depth = plane(ocean_bottom_scaled) * wet
    diag = plane(operator_diagonal)

    sum_temp = jnp.sum(temp, axis=0)
    sum_x = jnp.sum(flux_x, axis=0)
    sum_y = jnp.sum(flux_y, axis=0)
    weight = STERIC / levels
    part = plane(elevation_source) + weight * wet * (
        sum_temp
        + wet
        * (
            shift(DIFFUSE * sum_temp - sum_x, 1, 0)
            + shift(DIFFUSE * sum_temp + sum_x, -1, 0)
            + shift(DIFFUSE * sum_temp - sum_y, 0, 1)
            + shift(DIFFUSE * sum_temp + sum_y, 0, -1)
            - 4.0 * DIFFUSE * sum_temp
        )
    )
    east_first = DIFFUSE * sum_temp[:, 0] - sum_x[:, 0]
    west_last = DIFFUSE * sum_temp[:, -1] + sum_x[:, -1]
    north_first = DIFFUSE * sum_temp[0] - sum_y[0]
    south_last = DIFFUSE * sum_temp[-1] + sum_y[-1]
    bound = jnp.max(diag) + 0.0

    fields = jnp.stack([part, depth, diag])
    ends_x = jnp.stack([north_first, south_last])
    give_w = jnp.concatenate([fields[:, :, :RIM].transpose(0, 2, 1).reshape(-1), east_first, ends_x[:, :RIM].reshape(-1)])
    give_e = jnp.concatenate([fields[:, :, -RIM:].transpose(0, 2, 1).reshape(-1), west_last, ends_x[:, -RIM:].reshape(-1)])
    ends_y = jnp.stack([east_first, west_last])
    give_s = jnp.concatenate([fields[:, :RIM].reshape(-1), north_first, ends_y[:, :RIM].reshape(-1)])
    give_n = jnp.concatenate([fields[:, -RIM:].reshape(-1), south_last, ends_y[:, -RIM:].reshape(-1)])
    size_x = give_w.shape[0]
    size_y = give_s.shape[0]
    def corner(rows, columns, row_term, column_term):
        return jnp.concatenate([fields[:, rows, columns].reshape(-1), row_term[columns], column_term[rows]])

    first, last = slice(0, RIM), slice(-RIM, None)
    give_sw = corner(first, first, north_first, east_first)
    give_se = corner(first, last, north_first, west_last)
    give_nw = corner(last, first, south_last, east_first)
    give_ne = corner(last, last, south_last, west_last)
    gives = (give_e, give_w, give_n, give_s, give_ne, give_nw, give_se, give_sw)
    cuts = []
    at = 0
    for give in gives:
        cuts.append((at, at + give.shape[0]))
        at += give.shape[0]
    block = jnp.concatenate(gives)
    held = [block] + [
        lax.ppermute(block, "gy", [(i, (i + s) % ny) for i in range(ny)]) for s in range(1, ny)
    ]
    held = jnp.stack(held)
    slots = []
    for target in range(nx):
        wanted = table[:, target * ny + my_y]
        order = (my_y - wanted % ny + ny) % ny
        slots.append(jnp.concatenate([pick(held[:, a:b], order[c]) for c, (a, b) in enumerate(cuts)]))
    came = lax.all_to_all(jnp.stack(slots), "gx", 0, 0, tiled=True)
    parts = []
    for c, (a, b) in enumerate(cuts):
        value = pick(came[:, a:b], jnp.maximum(mine[c], 0) // ny)
        parts.append(jnp.where(mine[c] >= 0, value, 0.0))

    edge_w = -flux_x[:, :, 0] + spread[:, :, 0]
    edge_e = flux_x[:, :, -1] + spread[:, :, -1]
    edge_s = -flux_y[:, 0] + spread[:, 0]
    edge_n = flux_y[:, -1] + spread[:, -1]
    slot_size = levels * max(SPAN_X, SPAN_Y)
    outs = jnp.zeros((nx * ny, slot_size), jnp.float32)
    for c, value in enumerate((edge_w, edge_e, edge_s, edge_n)):
        flat = value.reshape(1, -1)
        flat = jnp.pad(flat, ((0, 0), (0, slot_size - flat.shape[1])))
        outs = jnp.where((jnp.arange(nx * ny) == mine[c])[:, None], flat, outs)
    edges = lax.all_to_all(outs, BOTH, 0, 0, tiled=True)
    halos = []
    for c, extent in enumerate((SPAN_Y, SPAN_Y, SPAN_X, SPAN_X)):
        value = pick(edges, jnp.maximum(mine[c], 0))[: levels * extent].reshape(levels, extent)
        halos.append(jnp.where(mine[c] >= 0, value, 0.0))

    def strip_x(c):
        body = parts[c]
        f = body[: 3 * RIM * SPAN_Y].reshape(3, RIM, SPAN_Y).transpose(0, 2, 1)
        edge = body[3 * RIM * SPAN_Y : 3 * RIM * SPAN_Y + SPAN_Y]
        return f, edge, body[-2 * RIM :].reshape(2, RIM)

    def strip_y(c):
        body = parts[c]
        f = body[: 3 * RIM * SPAN_X].reshape(3, RIM, SPAN_X)
        edge = body[3 * RIM * SPAN_X : 3 * RIM * SPAN_X + SPAN_X]
        return f, edge, body[-2 * RIM :].reshape(2, RIM)

    def corner_in(c):
        body = parts[c]
        f = body[: 3 * RIM * RIM].reshape(3, RIM, RIM)
        return f, body[-2 * RIM : -RIM], body[-RIM:]

    fw, west_in, ends_w = strip_x(0)
    fe, east_in, ends_e = strip_x(1)
    fs, south_in, ends_s = strip_y(2)
    fn, north_in, ends_n = strip_y(3)
    sw, sw_row, sw_col = corner_in(4)
    se, se_row, se_col = corner_in(5)
    nw, nw_row, nw_col = corner_in(6)
    ne, ne_row, ne_col = corner_in(7)
    cat = jnp.concatenate
    ext = cat(
        [
            cat([sw, fs, se], axis=2),
            cat([fw, fields, fe], axis=2),
            cat([nw, fn, ne], axis=2),
        ],
        axis=1,
    )
    part_x, depth_x, diag_x = ext[0], ext[1], ext[2]
    wet_x = (depth_x > 0).astype(jnp.float32)
    seam = jnp.zeros_like(part_x)
    col_m1 = cat([se_col * 0 + ends_s[0], east_first, ends_n[0]])
    seam = seam.at[:, RIM - 1].add(col_m1)
    seam = seam.at[:, RIM].add(cat([sw_col, west_in, nw_col]))
    seam = seam.at[:, RIM + SPAN_X - 1].add(cat([se_col, east_in, ne_col]))
    seam = seam.at[:, RIM + SPAN_X].add(cat([ends_s[1], west_last, ends_n[1]]))
    seam = seam.at[RIM - 1].add(cat([ends_w[0], north_first, ends_e[0]]))
    seam = seam.at[RIM].add(cat([sw_row, south_in, se_row]))
    seam = seam.at[RIM + SPAN_Y - 1].add(cat([nw_row, north_in, ne_row]))
    seam = seam.at[RIM + SPAN_Y].add(cat([ends_w[1], south_last, ends_e[1]]))
    forcing = part_x + weight * wet_x * seam

    w_east = depth_x * shift(depth_x, 1, 0)
    w_north = depth_x * shift(depth_x, 0, 1)

    def operate(v):
        flow_x = w_east * (v - shift(v, 1, 0))
        flow_y = w_north * (v - shift(v, 0, 1))
        return diag_x * v + flow_x - shift(flow_x, -1, 0) + flow_y - shift(flow_y, 0, -1)

    rows_sum = diag_x + 2.0 * (w_east + shift(w_east, -1, 0) + w_north + shift(w_north, 0, -1))
    inner = (slice(RIM, RIM + SPAN_Y), slice(RIM, RIM + SPAN_X))
    top = lax.pmax(jnp.max(rows_sum[inner]), BOTH)
    scale = 4.0 / top
    vectors = [forcing]
    for k in range(4):
        vectors.append(scale * operate(vectors[k]) - (4.0 * ROOTS[k]) * vectors[k])
    own = jnp.stack([v[inner] for v in vectors]).reshape(5, -1)
    gram = jnp.stack([jnp.sum(own[i] * own[j]) for i in range(5) for j in range(i, 5)])
    gram = tree_sum(gram, nx, ny)
    entry = {}
    at = 0
    for i in range(5):
        for j in range(i, 5):
            entry[i, j] = entry[j, i] = gram[at]
            at += 1

    def apply_op(c):
        out = [0.0] * 5
        for k in range(4):
            out[k] = out[k] + ROOTS[k] * top * c[k]
            out[k + 1] = out[k + 1] + top * 0.25 * c[k]
        return out

    def dot(a, b):
        return sum(a[i] * sum(entry[i, j] * b[j] for j in range(5)) for i in range(5))

    one = jnp.ones_like(top)
    zero = jnp.zeros_like(top)
    tiny = 1e-30
    x = [zero] * 5
    r = [one] + [zero] * 4
    p = list(r)
    rr = entry[0, 0]
    for _ in range(ITERS):
        q = apply_op(p)
        step = jnp.clip(rr / jnp.maximum(dot(p, q), tiny), 1.0 / top, 1.0 / LOW_RATE)
        x = [a + step * b for a, b in zip(x, p)]
        r = [a - step * b for a, b in zip(r, q)]
        fresh = jnp.maximum(dot(r, r), 0.0)
        beta = fresh / jnp.maximum(rr, tiny)
        p = [a + beta * b for a, b in zip(r, p)]
        rr = fresh
    surface = sum(x[k] * own[k] for k in range(4))

    cat_e = cat([(spread - flux_x)[..., 1:], halos[1][..., None]], axis=-1)
    cat_w = cat([halos[0][..., None], (spread + flux_x)[..., :-1]], axis=-1)
    cat_n = cat([(spread - flux_y)[..., 1:, :], halos[3][..., None, :]], axis=-2)
    cat_s = cat([halos[2][..., None, :], (spread + flux_y)[..., :-1, :]], axis=-2)
    stepped = temp + wet * (cat_e + cat_w + cat_n + cat_s - 4.0 * spread)
    new_temp = vertical_solve(stepped, plane(diffusion_rates))
    return new_temp.reshape(1, levels, -1), surface.reshape(1, -1)


def solution(mesh):
    deep = P(BOTH, None, None)
    flat = P(BOTH, None)
    return jax.shard_map(
        on_device,
        mesh=mesh,
        in_specs=(deep, deep, deep, deep, flat, flat, flat, flat, P()),
        out_specs=(deep, flat),
        check_vma=False,
    )
```

```python
import functools

import jax
import jax.numpy as jnp
from jax import lax
from jax.experimental import pallas as pl
from jax.experimental.pallas import tpu as pltpu
from jax.sharding import PartitionSpec as P

ITERS = 4
SPAN_X = 240
SPAN_Y = 160
RIM = 4
ADVECT = 0.25
DIFFUSE = 0.12
STERIC = 0.5
LOW_RATE = 0.05
HIGH_RATE = 32.5
ROOTS = (0.02, 0.35, 0.1, 0.2)
STRETCH = 4.0
TINY = 1e-30
BOTH = ("gx", "gy")
SIDES = ((-1, 0), (1, 0), (0, -1), (0, 1), (-1, -1), (1, -1), (-1, 1), (1, 1))

LANES = 128
GROUP = 8
GROUPS = SPAN_Y // GROUP
PLANES = GROUP * SPAN_X // LANES
ROWS = GROUPS * PLANES
SLABS = GROUPS + 4
WIDE = SLABS * PLANES
START = [SPAN_X * j // LANES for j in range(GROUP)]
OFF = [SPAN_X * j % LANES for j in range(GROUP)]
LAST = [(SPAN_X * j + SPAN_X - 1) // LANES for j in range(GROUP)]
END = [(SPAN_X * j + SPAN_X - 1) % LANES for j in range(GROUP)]
FIRST_OF = [[OFF[j] for j in range(GROUP) if START[j] == a] for a in range(PLANES)]
LAST_OF = [[END[j] for j in range(GROUP) if LAST[j] == a] for a in range(PLANES)]
SLOT = 24
BUDGET = 56 * 1024 * 1024


def turn(value, shift, axis=1):
    shift = shift % value.shape[axis]
    return value if shift == 0 else pltpu.roll(value, shift, axis)


def lane_of(shape):
    return lax.broadcasted_iota(jnp.int32, shape, len(shape) - 1)


def row_of(shape):
    return lax.broadcasted_iota(jnp.int32, shape, 0)


def comb(a, count=GROUPS):
    return pl.ds(a, count, stride=PLANES)


def drop(value, lanes, lane):
    for at in lanes:
        value = jnp.where(lane == at, 0.0, value)
    return value


def store_terms(a, temp, flow_x, flow_y, te, tw, tn, ts):
    spread = DIFFUSE * temp
    te[a] = spread - flow_x
    tw[a] = spread + flow_x
    tn[a, 8 : 8 + GROUPS] = spread - flow_y
    ts[a, 8 : 8 + GROUPS] = spread + flow_y


def clear_terms(tn, ts):
    none = jnp.zeros((PLANES, 1, LANES), jnp.float32)
    for ref in (tn, ts):
        ref[:, 7:8] = none
        ref[:, 8 + GROUPS : 9 + GROUPS] = none


def inner_sum(a, te, tw, tn, ts):
    lane = lane_of((GROUPS, LANES))
    here = te[a]
    east = here if a == PLANES - 1 else jnp.where(lane == 0, te[a + 1], here)
    east = drop(turn(east, -1), LAST_OF[a], lane)
    here = tw[a]
    west = here if a == 0 else jnp.where(lane == LANES - 1, tw[a - 1], here)
    west = drop(turn(west, 1), FIRST_OF[a], lane)

    def plane(ref, at):
        down = 8 + (at >= PLANES) - (at < 0)
        return ref[at % PLANES, down : down + GROUPS]

    north = turn(jnp.where(lane >= LANES - 16, plane(tn, a + 1), plane(tn, a + 2)), 16)
    south = turn(jnp.where(lane < 16, plane(ts, a - 1), plane(ts, a - 2)), -16)
    return east + west + north + south


def choose(planes, lane, get):
    value = get(planes[0])
    for j in range(1, GROUP):
        low = (OFF[j] - (32 if planes is LAST else 0)) % LANES
        value = jnp.where(jnp.logical_and(lane >= low, lane < low + 16), get(planes[j]), value)
    return value


def forcing_kernel(
    levels, per, tiles_x, tiles_y,
    pos, temp, zonal, merid, depth, ocean, diag, source,
    part, own, slots, table,
    st, sx, sy, pt, te, tw, tn, ts, holder,
):
    step = pl.program_id(0)
    count = pos.shape[0]
    depth, ocean, diag, source = (ref.reshape(ROWS, LANES) for ref in (depth, ocean, diag, source))
    flats = [[ref.at[k].reshape(ROWS, LANES) for k in range(per)] for ref in (temp, zonal, merid)]

    def add(low, size, fresh):
        rows = pl.ds(low, size)
        total = [None] * 3
        for t, u, v in zip(*flats):
            t = t[rows, :]
            new = (t, t * u[rows, :], t * v[rows, :])
            total = [b if a is None else a + b for a, b in zip(total, new)]
        for ref, value in zip((st, sx, sy), total):
            ref[rows, :] = value if fresh else ref[rows, :] + value

    def run(fresh):
        def some(m, carry):
            add(pl.multiple_of(m * 8, 8), 8, fresh)
            return carry

        lax.fori_loop(0, ROWS // 8, some, 0, unroll=4)
        if ROWS % 8:
            add(ROWS - ROWS % 8, ROWS % 8, fresh)

    pl.when(step == 0)(lambda: run(True))
    pl.when(step > 0)(lambda: run(False))

    @pl.when(step == pl.num_programs(0) - 1)
    def _():
        lane = lane_of((GROUPS, LANES))

        def wet_of(rows):
            return ocean[rows, :].astype(jnp.float32)

        def masked(rows):
            return depth[rows, :] * wet_of(rows)

        def number(d, carry):
            holder[pos[d]] = d
            return carry

        lax.fori_loop(0, count, number, 0)
        me = lax.axis_index("gx") * tiles_y + lax.axis_index("gy")
        here = pos[me]
        row = here // tiles_x
        column = here % tiles_x
        sides = []
        for c, (dx, dy) in enumerate(SIDES):
            there = row + dy
            inside = jnp.logical_and(there >= 0, there < tiles_y)
            target = jnp.where(inside, there, 0) * tiles_x + (column + dx + tiles_x) % tiles_x
            device = jnp.where(inside, holder[target], -1)
            table[c] = device
            sides.append(device)

        clear_terms(tn, ts)
        for a in range(PLANES):
            total = st[comb(a), :]
            pt[a] = total
            store_terms(a, total, ADVECT * sx[comb(a), :], ADVECT * sy[comb(a), :], te, tw, tn, ts)
        for a in range(PLANES):
            total = pt[a]
            wet = wet_of(comb(a))
            change = inner_sum(a, te, tw, tn, ts) - 4.0 * DIFFUSE * total
            part[comb(a), :] = source[comb(a), :] + (STERIC / levels) * wet * (total + wet * change)

        q = lane % 16

        def mix(values):
            value = values[4]
            for at, low in ((3, 12), (2, 11), (1, 8), (0, 4)):
                value = jnp.where(q < low, values[at], value)
            return value

        def flat(ref):
            return lambda a: ref[comb(a), :]

        def ends(planes, low):
            value = tn[planes[0], 8 : 8 + GROUPS]
            last = jnp.logical_and(lane >= low, lane < low + 16)
            return jnp.where(last, ts[planes[7], 8 : 8 + GROUPS], value)

        pack_w = mix([
            choose(START, lane, flat(part)),
            turn(choose(START, lane, lambda a: masked(comb(a))), 4),
            turn(choose(START, lane, flat(diag)), 8),
            turn(choose(START, lane, lambda a: te[a]), 11),
            turn(ends(START, OFF[7]), 12),
        ])
        pack_e = mix([
            turn(choose(LAST, lane, flat(part)), 20),
            turn(choose(LAST, lane, lambda a: masked(comb(a))), 24),
            turn(choose(LAST, lane, flat(diag)), 27),
            turn(choose(LAST, lane, lambda a: tw[a]), 28),
            turn(ends(LAST, LANES - 16), 32),
        ])
        own[0:GROUPS] = pack_w
        own[SLABS : SLABS + GROUPS] = pack_e
        one = lane_of((1, LANES))
        north_l = tn[0, 8:9]
        north_r = tn[1, 8:9]
        south_13 = ts[PLANES - 2, 7 + GROUPS : 8 + GROUPS]
        south_14 = ts[PLANES - 1, 7 + GROUPS : 8 + GROUPS]
        south_l = turn(jnp.where(one >= 16, south_13, south_14), -16)
        south_r = turn(south_14, -16)
        own[48:49] = north_l
        own[49:50] = north_r
        own[50:51] = south_l
        own[51:52] = south_r
        deep = jnp.max(masked(slice(0, ROWS)), axis=(0, 1), keepdims=True)
        top = jnp.max(diag[...], axis=(0, 1), keepdims=True) + 8.0 * deep * deep
        top = jnp.broadcast_to(top, (1, LANES))

        def mark(d, carry):
            slots[d, SLOT - 1 : SLOT] = top
            return carry

        lax.fori_loop(0, count, mark, 0)
        eight = lane_of((8, LANES))
        eighth = row_of((8, LANES))
        for c, first, rows_l, rows_r in ((2, True, north_l, north_r), (3, False, south_l, south_r)):
            base = 0 if first else ROWS - 8
            spare = jnp.logical_and(eighth == 7, eight >= 64) if first else jnp.logical_and(eighth == 0, eight < 64)
            g = 0 if first else GROUPS - 1
            blocks = []
            block = slice(base, base + 8)
            for value, at in ((part[block, :], g), (masked(block), SLABS + g)):
                extra = jnp.broadcast_to(turn(own[at : at + 1], -16), (8, LANES))
                blocks.append(jnp.where(spare, extra, value))
            low = 0 if first else ROWS - 6
            diag_rows = diag[low : low + 6, :]
            last_row = jnp.where(one == LANES - 1, top, rows_r)

            @pl.when(sides[c] >= 0)
            def _(c=c, blocks=blocks, diag_rows=diag_rows, rows_l=rows_l, last_row=last_row):
                at = sides[c]
                slots[at, 0:8] = blocks[0]
                slots[at, 8:16] = blocks[1]
                slots[at, 16:22] = diag_rows
                slots[at, 22:23] = rows_l
                slots[at, 23:24] = last_row

        slots[sides[0], 0:GROUPS] = pack_w
        slots[sides[1], 0:GROUPS] = pack_e
        for c, at in ((4, 0), (5, SLABS), (6, GROUPS - 1), (7, SLABS + GROUPS - 1)):
            @pl.when(sides[c] >= 0)
            def _(c=c, at=at):
                slots[sides[c], 0:1] = own[at : at + 1]


def whole(*shape):
    return pl.BlockSpec(shape, lambda *_: (0,) * len(shape))


SMEM = pl.BlockSpec(memory_space=pltpu.SMEM)


def solve_kernel(
    levels,
    table, came, own, part, depth, ocean, diag,
    vectors, gram, size,
    fb, fd, fg, pw, pe, ow, oe, ed, eg, we, wn, last, rows,
):
    depth, ocean, diag = (ref.reshape(ROWS, LANES) for ref in (depth, ocean, diag))
    lane = lane_of((SLABS, LANES))
    slab = row_of((SLABS, LANES))
    one = lane_of((1, LANES))
    src = [table[c] for c in range(8)]

    def fetch(c, low, high):
        value = came[jnp.maximum(src[c], 0), low:high]
        return jnp.where(src[c] >= 0, value, 0.0)

    none = jnp.zeros((WIDE - ROWS + 4, LANES), jnp.float32)
    for ref in (fb, fd, fg):
        ref[ROWS - 4 : WIDE] = none
    fb[0:ROWS] = part[...]
    fd[0:ROWS] = depth[...] * ocean[...].astype(jnp.float32)
    fg[0:ROWS] = diag[...]
    for ref, low, high in ((fb, 0, 8), (fd, 8, 16), (fg, 16, 22)):
        ref[ROWS : ROWS + high - low] = fetch(3, low, high)
        ref[WIDE - high + low : WIDE] = fetch(2, low, high)
    empty = jnp.zeros((SLABS, LANES), jnp.float32)
    for ref, side, north, south in ((pw, 0, 6, 4), (pe, 1, 7, 5)):
        ref[...] = empty
        ref[0:GROUPS] = fetch(side, 0, GROUPS)
        ref[GROUPS : GROUPS + 1] = fetch(north, 0, 1)
        ref[SLABS - 1 : SLABS] = fetch(south, 0, 1)
    for ref, at, north, south in ((ow, 0, 7, 0), (oe, SLABS, 15, 8)):
        ref[...] = empty
        ref[0:GROUPS] = own[at : at + GROUPS]
        ref[GROUPS : GROUPS + 1] = turn(fetch(3, north, north + 1), 16)
        ref[SLABS - 1 : SLABS] = turn(fetch(2, south, south + 1), 16)

    def spread(ref, j):
        a = START[j]
        first, second = ref[comb(a, SLABS), :], ref[comb(a + 1, SLABS), :]
        third = ref[comb(a + 2, SLABS), :] if a + 2 < PLANES else second
        left = turn(jnp.where(lane >= OFF[j], first, second), -OFF[j])
        right = turn(jnp.where(lane >= OFF[j], second, third), -OFF[j])
        return left, right

    def seam_row(left, right, slab_at, lanes_at):
        east = turn(pe[slab_at : slab_at + 1], 112 - lanes_at)
        west = turn(pw[slab_at : slab_at + 1], 124 - lanes_at)
        right = jnp.where(one < 112, right, jnp.where(one < 116, east, jnp.where(one >= 124, west, 0.0)))
        return jnp.broadcast_to(left, (SLABS, LANES)), jnp.broadcast_to(right, (SLABS, LANES))

    seams = {
        0: ((0, seam_row(fetch(2, 22, 23), fetch(2, 23, 24), SLABS - 1, 28)),
            (GROUPS, seam_row(own[50:51], own[51:52], GROUPS - 1, 28))),
        GROUP - 1: ((GROUPS - 1, seam_row(fetch(3, 22, 23), fetch(3, 23, 24), GROUPS, 12)),
                    (SLABS - 1, seam_row(own[48:49], own[49:50], 0, 12))),
    }
    weight = STERIC / levels
    for j in range(GROUP):
        o = OFF[j]

        def rim(right, q, width):
            east = turn(pe[...], 112 - o - q)
            west = turn(pw[...], 128 - width - o - q)
            value = jnp.where(lane < 112 + width, east, jnp.where(lane >= 128 - width, west, 0.0))
            return jnp.where(lane < 112, right, value)

        left, right = spread(fd, j)
        right = rim(right, 4, 4)
        wet_l = jnp.where(left > 0, weight, 0.0)
        wet_r = jnp.where(right > 0, weight, 0.0)
        ed[j, :, 0:LANES] = left
        ed[j, :, LANES:] = right
        left, right = spread(fg, j)
        eg[j, :, 0:LANES] = left
        eg[j, :, LANES:] = rim(right, 8, 3)
        left, right = spread(fb, j)
        right = rim(right, 0, 4)
        seam_l = jnp.where(lane == 0, turn(pw[...], -o - 11), 0.0)
        seam_r = jnp.where(lane == 127, turn(ow[...], 127 - o - 11), 0.0)
        seam_r = jnp.where(lane == 111, turn(pe[...], 111 - o - 11), seam_r)
        seam_r = jnp.where(lane == 112, turn(oe[...], 112 - o - 11), seam_r)
        for at, (row_l, row_r) in seams.get(j, ()):
            seam_l = seam_l + jnp.where(slab == at, row_l, 0.0)
            seam_r = seam_r + jnp.where(slab == at, row_r, 0.0)
        vectors[0, j, :, 0:LANES] = left + wet_l * seam_l
        vectors[0, j, :, LANES:] = right + wet_r * seam_r

    for j in range(GROUP):
        d = ed[j]
        we[j] = d * turn(d, -1)
        above = ed[j + 1] if j < GROUP - 1 else turn(ed[0], -1, 0)
        wn[j] = d * above

    top = jnp.max(came[:, SLOT - 1, :], axis=0, keepdims=True)
    top = jnp.max(jnp.where(one == LANES - 1, top, 0.0), axis=1, keepdims=True)
    size[...] = jnp.broadcast_to(top, size.shape)
    scale = STRETCH / top

    big = (SLABS, 2 * LANES)
    mine = jnp.logical_and(row_of(big) < GROUPS, lane_of(big) < SPAN_X)
    pair = 0
    names = {}
    for k in range(5):
        sums = [None] * (k + 1)
        new = last if k == 4 else vectors.at[k]
        if k:
            v = vectors.at[k - 1]
            flow_below = wn[GROUP - 1] * (v[GROUP - 1] - turn(v[0], -1, 0))
            flow_below = turn(flow_below, 1, 0)
        for j in range(GROUP):
            if k:
                here = v[j]
                above = v[j + 1] if j < GROUP - 1 else turn(v[0], -1, 0)
                flow_x = we[j] * (here - turn(here, -1))
                flow_y = wn[j] * (here - above)
                image = eg[j] * here + (flow_x - turn(flow_x, 1)) + (flow_y - flow_below)
                fresh = scale * image - (STRETCH * ROOTS[k - 1]) * here
                flow_below = flow_y
                new[j] = fresh
            else:
                fresh = new[j]
            held = jnp.where(mine, fresh, 0.0)
            for i in range(k + 1):
                other = vectors[i, j] if i < k else held
                value = held * other
                sums[i] = value if sums[i] is None else sums[i] + value
        for i in range(k + 1):
            rows[pair : pair + 1] = jnp.sum(sums[i][:, 0:LANES] + sums[i][:, LANES:], axis=0, keepdims=True)
            names[i, k] = pair
            pair += 1
    rows[pair : pair + 1] = jnp.zeros((1, LANES), jnp.float32)
    total = jnp.sum(rows[...], axis=1, keepdims=True)
    spot = row_of((16, LANES)) == lane_of((16, LANES))
    line = jnp.sum(jnp.where(spot, total, 0.0), axis=0, keepdims=True)
    gram[...] = jnp.broadcast_to(line[None], gram.shape)


def combine_kernel(came, size, vectors, out, left, right):
    row = jnp.sum(came[:, 0, :], axis=0, keepdims=True)
    one = lane_of((1, LANES))
    entry = {}
    pair = 0
    for k in range(5):
        for i in range(k + 1):
            value = jnp.sum(jnp.where(one == pair, row, 0.0), axis=1, keepdims=True)
            entry[i, k] = entry[k, i] = value
            pair += 1
    top = size[0:1, 0:1]

    def image(c):
        out = [None] * 5
        for k in range(4):
            if c[k] is None:
                continue
            low = ROOTS[k] * c[k]
            out[k] = low if out[k] is None else out[k] + low
            out[k + 1] = (1.0 / STRETCH) * c[k]
        return out

    def dot(a, b):
        total = None
        for i in range(5):
            if a[i] is None:
                continue
            inner = None
            for j in range(5):
                if b[j] is not None:
                    value = entry[i, j] * b[j]
                    inner = value if inner is None else inner + value
            total = a[i] * inner if total is None else total + a[i] * inner
        return total

    def axpy(a, s, b):
        return [
            x if y is None else (s * y if x is None else x + s * y) for x, y in zip(a, b)
        ]

    r = [jnp.ones((1, 1), jnp.float32)] + [None] * 4
    p = list(r)
    x = [None] * 5
    rr = entry[0, 0]
    for n in range(ITERS):
        q = image(p)
        step = rr / jnp.maximum(dot(p, q), TINY)
        step = jnp.clip(step, top * (1.0 / HIGH_RATE), top * (1.0 / LOW_RATE))
        x = axpy(x, step, p)
        if n < ITERS - 1:
            r = axpy(r, -step, q)
            fresh = jnp.maximum(dot(r, r), 0.0)
            p = axpy(r, fresh / jnp.maximum(rr, TINY), p)
            rr = fresh
    flat = out.reshape(ROWS, LANES)
    factors = [c / top for c in x[:4]]
    for j in range(GROUP):
        value = None
        for k in range(4):
            term = factors[k] * vectors[k, j]
            value = term if value is None else value + term
        left[j] = turn(value[:, 0:LANES], OFF[j])
        right[j] = turn(value[:, LANES:], OFF[j])
    lane = lane_of((SLABS, LANES))
    for a in range(PLANES):
        value = None
        for j in range(GROUP):
            for half, ref in ((0, left), (1, right)):
                low = max(SPAN_X * j + LANES * half - LANES * a, 0)
                high = min(SPAN_X * j + (LANES if half == 0 else SPAN_X) - LANES * a, LANES)
                if low >= high:
                    continue
                value = ref[j] if value is None else jnp.where(lane >= low, ref[j], value)
        flat[comb(a), :] = value[0:GROUPS]


def spread_kernel(
    levels, per, table, temp, zonal, merid, ocean,
    partial, slots, te, tw, tn, ts, strips, packs,
):
    step = pl.program_id(0)
    lane = lane_of((GROUPS, LANES))
    q = lane % 16
    one = lane_of((1, LANES))
    ocean = ocean.reshape(ROWS, LANES)

    @pl.when(step == 0)
    def _():
        clear_terms(tn, ts)
        packs[...] = jnp.zeros_like(packs)

    for n in range(per):
        k = step * per + n
        t, u, v = (ref.at[n].reshape(ROWS, LANES) for ref in (temp, zonal, merid))
        for a in range(PLANES):
            own = t[comb(a), :]
            quarter = ADVECT * own
            store_terms(a, own, u[comb(a), :] * quarter, v[comb(a), :] * quarter, te, tw, tn, ts)
        for a in range(PLANES):
            own = t[comb(a), :]
            change = inner_sum(a, te, tw, tn, ts) - 4.0 * DIFFUSE * own
            partial[n, a, 0:GROUPS] = own + ocean[comb(a), :].astype(jnp.float32) * change
        west = choose(START, lane, lambda a: te[a])
        east = choose(LAST, lane, lambda a: tw[a])
        packs[0] = jnp.where(q == k, pltpu.roll(west, k, 1), packs[0])
        packs[1] = jnp.where(q == k, pltpu.roll(east, k + 17, 1), packs[1])
        south_13 = ts[PLANES - 2, 7 + GROUPS : 8 + GROUPS]
        south_14 = ts[PLANES - 1, 7 + GROUPS : 8 + GROUPS]
        strips[0, pl.ds(k, 1)] = tn[0, 8:9]
        strips[0, pl.ds(k + levels, 1)] = tn[1, 8:9]
        strips[1, pl.ds(k, 1)] = turn(jnp.where(one >= 16, south_13, south_14), -16)
        strips[1, pl.ds(k + levels, 1)] = turn(south_14, -16)

    @pl.when(step == pl.num_programs(0) - 1)
    def _():
        slots[table[0], 0:GROUPS] = packs[0]
        slots[table[1], 0:GROUPS] = packs[1]
        for c in (2, 3):
            @pl.when(table[c] >= 0)
            def _(c=c):
                slots[table[c], 0 : 2 * levels] = strips[c - 2]


def column_kernel(levels, table, came, partial, ocean, rates, out, stepped):
    lane = lane_of((GROUPS, LANES))
    slab = row_of((GROUPS, LANES))
    ocean = ocean.reshape(ROWS, LANES)
    rates = rates.reshape((levels - 1) * ROWS, LANES)

    def fetch(c, rows):
        value = came[jnp.maximum(table[c], 0), rows]
        return jnp.where(table[c] >= 0, value, 0.0)

    def level(k, carry):
        west = pltpu.roll(fetch(0, slice(0, GROUPS)), LANES - k, 1)
        east = pltpu.roll(fetch(1, slice(0, GROUPS)), 2 * LANES - 17 - k, 1)
        north_l = pltpu.roll(fetch(3, pl.ds(k, 1)), 16, 1)
        north_r = pltpu.roll(fetch(3, pl.ds(k + levels, 1)), 16, 1)
        south_l = fetch(2, pl.ds(k, 1))
        south_r = fetch(2, pl.ds(k + levels, 1))
        for a in range(PLANES):
            value = partial[k, a, 0:GROUPS]
            rim = None
            lanes = [(at, west) for at in FIRST_OF[a]] + [(at, east) for at in LAST_OF[a]]
            for at, source in lanes:
                rim = jnp.where(lane == at, source, 0.0 if rim is None else rim)
            if a == 0:
                rim = rim + jnp.where(slab == 0, south_l, 0.0)
            if a == 1:
                rim = rim + jnp.where(jnp.logical_and(slab == 0, lane < 112), south_r, 0.0)
            if a == PLANES - 2:
                rim = rim + jnp.where(jnp.logical_and(slab == GROUPS - 1, lane >= 16), north_l, 0.0)
            if a == PLANES - 1:
                rim = rim + jnp.where(slab == GROUPS - 1, jnp.where(lane < 16, north_l, north_r), 0.0)
            if rim is not None:
                value = value + ocean[comb(a), :].astype(jnp.float32) * rim
            stepped[k, a, 0:GROUPS] = value
        return carry

    lax.fori_loop(0, levels, level, 0)

    def block(a, carry):
        for low in range(0, GROUPS, 8):
            size = min(8, GROUPS - low)

            def rows(k):
                return pl.ds(k * ROWS + low * PLANES + a, size, stride=PLANES)

            gains = []
            sums = []
            for k in range(levels):
                value = stepped[k, a, low : low + size]
                pivot = 1.0
                if k > 0:
                    pivot = pivot + upper - upper * gains[-1]
                    value = value + upper * sums[-1]
                if k < levels - 1:
                    lower = rates[rows(k), :]
                    inverse = 1.0 / (pivot + lower)
                    gains.append(lower * inverse)
                    upper = lower
                else:
                    inverse = 1.0 / pivot
                sums.append(value * inverse)
            result = sums[-1]
            out[rows(levels - 1), :] = result
            for k in range(levels - 2, -1, -1):
                result = sums[k] + gains[k] * result
                out[rows(k), :] = result
        return carry

    lax.fori_loop(0, PLANES, block, 0)


def on_device(
    thermal_anomaly,
    zonal_flow_ratio,
    meridional_flow_ratio,
    diffusion_rates,
    ocean_bottom_scaled,
    ocean_indicator,
    operator_diagonal,
    elevation_source,
    block_positions,
):
    levels, cells = thermal_anomaly.shape[1:]
    nx = lax.axis_size("gx")
    ny = lax.axis_size("gy")
    count = block_positions.shape[0]
    planes = (ocean_bottom_scaled, ocean_indicator, operator_diagonal, elevation_source)
    depth, ocean, diag, source = planes
    f32 = jnp.float32
    steps = next(n for n in (4, 3, 2, 1) if levels % n == 0)
    per = levels // steps
    params = pltpu.CompilerParams(vmem_limit_bytes=BUDGET)
    temp, zonal, merid, rates = (
        array.reshape(array.shape[1], 1, cells)
        for array in (thermal_anomaly, zonal_flow_ratio, meridional_flow_ratio, diffusion_rates)
    )
    some = pl.BlockSpec((per, 1, cells), lambda i: (i, 0, 0))
    flat = whole(1, cells)

    def vmem(*shape):
        return pltpu.VMEM(shape, f32)

    def out(*shape):
        return jax.ShapeDtypeStruct(shape, f32)

    plane = vmem(PLANES, GROUPS, LANES)
    tall = vmem(PLANES, 40, LANES)
    part, own, slots, table = pl.pallas_call(
        functools.partial(forcing_kernel, levels, per, nx, ny),
        grid=(steps,),
        in_specs=[SMEM, some, some, some, flat, flat, flat, flat],
        out_specs=[whole(ROWS, LANES), whole(56, LANES), whole(count, SLOT, LANES), SMEM],
        out_shape=[
            out(ROWS, LANES), out(56, LANES), out(count, SLOT, LANES),
            jax.ShapeDtypeStruct((8,), jnp.int32),
        ],
        scratch_shapes=[vmem(ROWS, LANES)] * 3 + [plane] * 3 + [tall] * 2 + [pltpu.SMEM((count,), jnp.int32)],
        compiler_params=params,
        name="forcing",
    )(block_positions, temp, zonal, merid, depth, ocean, diag, source)
    came = lax.all_to_all(slots, BOTH, 0, 0, tiled=True)

    partial, edges = pl.pallas_call(
        functools.partial(spread_kernel, levels, per),
        grid=(steps,),
        in_specs=[SMEM, some, some, some, flat],
        out_specs=[
            pl.BlockSpec((per, PLANES, SLABS, LANES), lambda i: (i, 0, 0, 0)),
            whole(count, 2 * levels, LANES),
        ],
        out_shape=[out(levels, PLANES, SLABS, LANES), out(count, 2 * levels, LANES)],
        scratch_shapes=[plane] * 2 + [tall] * 2 + [vmem(2, 2 * levels, LANES), vmem(2, GROUPS, LANES)],
        compiler_params=params,
        name="spread",
    )(table, temp, zonal, merid, ocean)
    edges_in = lax.all_to_all(edges, BOTH, 0, 0, tiled=True)

    extended = vmem(GROUP, SLABS, 2 * LANES)
    vectors, gram, size = pl.pallas_call(
        functools.partial(solve_kernel, levels),
        grid=(1,),
        in_specs=[SMEM, whole(count, SLOT, LANES), whole(56, LANES), whole(ROWS, LANES), flat, flat, flat],
        out_specs=[whole(4, GROUP, SLABS, 2 * LANES), whole(count, 1, LANES), whole(8, LANES)],
        out_shape=[out(4, GROUP, SLABS, 2 * LANES), out(count, 1, LANES), out(8, LANES)],
        scratch_shapes=[vmem(WIDE, LANES)] * 3 + [vmem(SLABS, LANES)] * 4 + [extended] * 5 + [vmem(16, LANES)],
        compiler_params=params,
        name="vectors",
    )(table, came, own, part, depth, ocean, diag)
    grams = lax.all_to_all(gram, BOTH, 0, 0, tiled=True)

    new_temp = pl.pallas_call(
        functools.partial(column_kernel, levels),
        grid=(1,),
        in_specs=[
            SMEM, whole(count, 2 * levels, LANES), whole(levels, PLANES, SLABS, LANES), flat,
            whole(levels - 1, 1, cells),
        ],
        out_specs=whole(levels * ROWS, LANES),
        out_shape=out(levels * ROWS, LANES),
        scratch_shapes=[vmem(levels, PLANES, SLABS, LANES)],
        compiler_params=params,
        name="columns",
    )(table, edges_in, partial, ocean, rates)

    surface = pl.pallas_call(
        combine_kernel,
        grid=(1,),
        in_specs=[whole(count, 1, LANES), whole(8, LANES), whole(4, GROUP, SLABS, 2 * LANES)],
        out_specs=flat,
        out_shape=out(1, cells),
        scratch_shapes=[vmem(GROUP, SLABS, LANES)] * 2,
        compiler_params=params,
        name="combine",
    )(grams, size, vectors)
    return new_temp.reshape(1, levels, cells), surface


def solution(mesh):
    deep = P(BOTH, None, None)
    flat = P(BOTH, None)
    return jax.shard_map(
        on_device,
        mesh=mesh,
        in_specs=(deep, deep, deep, deep, flat, flat, flat, flat, P()),
        out_specs=(deep, flat),
        check_vma=False,
    )
```

```python
import functools

import jax
import jax.numpy as jnp
from jax import lax
from jax.experimental import pallas as pl
from jax.experimental.pallas import tpu as pltpu
from jax.sharding import PartitionSpec as P

ITERS = 4
SPAN_X = 240
SPAN_Y = 160
RIM = 4
ADVECT = 0.25
DIFFUSE = 0.12
STERIC = 0.5
LOW_RATE = 0.05
HIGH_RATE = 32.5
ROOTS = (0.02, 0.35, 0.1, 0.2)
STRETCH = 4.0
TINY = 1e-30
BOTH = ("gx", "gy")
SIDES = ((-1, 0), (1, 0), (0, -1), (0, 1), (-1, -1), (1, -1), (-1, 1), (1, 1))

LANES = 128
GROUP = 8
GROUPS = SPAN_Y // GROUP
PLANES = GROUP * SPAN_X // LANES
ROWS = GROUPS * PLANES
SLABS = GROUPS + 4
WIDE = SLABS * PLANES
START = [SPAN_X * j // LANES for j in range(GROUP)]
OFF = [SPAN_X * j % LANES for j in range(GROUP)]
LAST = [(SPAN_X * j + SPAN_X - 1) // LANES for j in range(GROUP)]
END = [(SPAN_X * j + SPAN_X - 1) % LANES for j in range(GROUP)]
FIRST_OF = [[OFF[j] for j in range(GROUP) if START[j] == a] for a in range(PLANES)]
LAST_OF = [[END[j] for j in range(GROUP) if LAST[j] == a] for a in range(PLANES)]
RIM_ROWS = 24
SLOT = RIM_ROWS + 4
HAND = 5
EDGE = 56
BUDGET = 24 * 1024 * 1024


def turn(value, shift, axis=1):
    shift = shift % value.shape[axis]
    return value if shift == 0 else pltpu.roll(value, shift, axis)


def lane_of(shape):
    return lax.broadcasted_iota(jnp.int32, shape, len(shape) - 1)


def row_of(shape):
    return lax.broadcasted_iota(jnp.int32, shape, 0)


def comb(a, count=GROUPS):
    return pl.ds(a, count, stride=PLANES)


def drop(value, lanes, lane):
    for at in lanes:
        value = jnp.where(lane == at, 0.0, value)
    return value


def store_terms(a, temp, flow_x, flow_y, te, tw, tn, ts):
    spread = DIFFUSE * temp
    te[a] = spread - flow_x
    tw[a] = spread + flow_x
    tn[a, 8 : 8 + GROUPS] = spread - flow_y
    ts[a, 8 : 8 + GROUPS] = spread + flow_y


def clear_terms(tn, ts):
    none = jnp.zeros((PLANES, 1, LANES), jnp.float32)
    for ref in (tn, ts):
        ref[:, 7:8] = none
        ref[:, 8 + GROUPS : 9 + GROUPS] = none


def inner_sum(a, te, tw, tn, ts):
    lane = lane_of((GROUPS, LANES))
    here = te[a]
    east = here if a == PLANES - 1 else jnp.where(lane == 0, te[a + 1], here)
    east = drop(turn(east, -1), LAST_OF[a], lane)
    here = tw[a]
    west = here if a == 0 else jnp.where(lane == LANES - 1, tw[a - 1], here)
    west = drop(turn(west, 1), FIRST_OF[a], lane)

    def plane(ref, at):
        down = 8 + (at >= PLANES) - (at < 0)
        return ref[at % PLANES, down : down + GROUPS]

    north = turn(jnp.where(lane >= LANES - 16, plane(tn, a + 1), plane(tn, a + 2)), 16)
    south = turn(jnp.where(lane < 16, plane(ts, a - 1), plane(ts, a - 2)), -16)
    return east + west + north + south


def choose(planes, lane, get):
    value = get(planes[0])
    for j in range(1, GROUP):
        low = (OFF[j] - (32 if planes is LAST else 0)) % LANES
        value = jnp.where(jnp.logical_and(lane >= low, lane < low + 16), get(planes[j]), value)
    return value


def forcing_kernel(
    levels, per, tiles_x, tiles_y,
    pos, temp, zonal, merid, depth, ocean, diag, source,
    part, own, out, table,
    st, sx, sy, pt, te, tw, tn, ts, edges, holder,
):
    step = pl.program_id(0)
    count = pos.shape[0]
    depth, ocean, diag, source = (ref.reshape(ROWS, LANES) for ref in (depth, ocean, diag, source))
    slots = out.reshape(count * SLOT, LANES)
    lane = lane_of((GROUPS, LANES))
    one = lane_of((1, LANES))
    q = lane % 16
    flats = [[ref.at[k].reshape(ROWS, LANES) for k in range(per)] for ref in (temp, zonal, merid)]

    def add(low, size, fresh):
        rows = pl.ds(low, size)
        total = [None] * 3
        for t, u, v in zip(*flats):
            t = t[rows, :]
            new = (t, t * u[rows, :], t * v[rows, :])
            total = [b if a is None else a + b for a, b in zip(total, new)]
        for ref, value in zip((st, sx, sy), total):
            ref[rows, :] = value if fresh else ref[rows, :] + value

    def run(fresh):
        def some(m, carry):
            add(pl.multiple_of(m * 8, 8), 8, fresh)
            return carry

        lax.fori_loop(0, ROWS // 8, some, 0, unroll=4)
        if ROWS % 8:
            add(ROWS - ROWS % 8, ROWS % 8, fresh)

    @pl.when(step == 0)
    def _():
        edges[...] = jnp.zeros_like(edges)
        run(True)

    pl.when(step > 0)(lambda: run(False))

    for n in range(per):
        k = step * per + n
        t, u, v = (flat[n] for flat in flats)

        def term(planes, sign):
            own = choose(planes, lane, lambda a: t[comb(a), :])
            flow = choose(planes, lane, lambda a: u[comb(a), :])
            return DIFFUSE * own + sign * ADVECT * (flow * own)

        edges[0, 0:GROUPS] = jnp.where(q == k, pltpu.roll(term(START, -1.0), k, 1), edges[0, 0:GROUPS])
        edges[1, 0:GROUPS] = jnp.where(q == k, pltpu.roll(term(LAST, 1.0), k + 17, 1), edges[1, 0:GROUPS])
        rows = t[0:2, :]
        rows = DIFFUSE * rows - ADVECT * (v[0:2, :] * rows)
        edges[2, pl.ds(k, 1)] = rows[0:1]
        edges[2, pl.ds(k + levels, 1)] = rows[1:2]
        rows = t[ROWS - 2 : ROWS, :]
        rows = DIFFUSE * rows + ADVECT * (v[ROWS - 2 : ROWS, :] * rows)
        edges[3, pl.ds(k, 1)] = turn(jnp.where(one >= 16, rows[0:1], rows[1:2]), -16)
        edges[3, pl.ds(k + levels, 1)] = turn(rows[1:2], -16)

    @pl.when(step == pl.num_programs(0) - 1)
    def _():
        for c in range(4):
            slots[pl.ds(RIM_ROWS + c, 2 * levels, stride=SLOT), :] = edges[c]

        def wet_of(rows):
            return ocean[rows, :].astype(jnp.float32)

        def masked(rows):
            return depth[rows, :] * wet_of(rows)

        def number(d, carry):
            holder[pos[d]] = d
            return carry

        lax.fori_loop(0, count, number, 0)
        me = lax.axis_index("gx") * tiles_y + lax.axis_index("gy")
        here = pos[me]
        row = here // tiles_x
        column = here % tiles_x
        sides = []
        for c, (dx, dy) in enumerate(SIDES):
            there = row + dy
            inside = jnp.logical_and(there >= 0, there < tiles_y)
            target = jnp.where(inside, there, 0) * tiles_x + (column + dx + tiles_x) % tiles_x
            device = jnp.where(inside, holder[target], -1)
            table[c] = device
            sides.append(device)

        clear_terms(tn, ts)
        for a in range(PLANES):
            total = st[comb(a), :]
            pt[a] = total
            store_terms(a, total, ADVECT * sx[comb(a), :], ADVECT * sy[comb(a), :], te, tw, tn, ts)
        for a in range(PLANES):
            total = pt[a]
            wet = wet_of(comb(a))
            change = inner_sum(a, te, tw, tn, ts) - 4.0 * DIFFUSE * total
            part[comb(a), :] = source[comb(a), :] + (STERIC / levels) * wet * (total + wet * change)

        def mix(values):
            value = values[4]
            for at, low in ((3, 12), (2, 11), (1, 8), (0, 4)):
                value = jnp.where(q < low, values[at], value)
            return value

        def flat(ref):
            return lambda a: ref[comb(a), :]

        def ends(planes, low):
            value = tn[planes[0], 8 : 8 + GROUPS]
            last = jnp.logical_and(lane >= low, lane < low + 16)
            return jnp.where(last, ts[planes[7], 8 : 8 + GROUPS], value)

        pack_w = mix([
            choose(START, lane, flat(part)),
            turn(choose(START, lane, lambda a: masked(comb(a))), 4),
            turn(choose(START, lane, flat(diag)), 8),
            turn(choose(START, lane, lambda a: te[a]), 11),
            turn(ends(START, OFF[7]), 12),
        ])
        pack_e = mix([
            turn(choose(LAST, lane, flat(part)), 20),
            turn(choose(LAST, lane, lambda a: masked(comb(a))), 24),
            turn(choose(LAST, lane, flat(diag)), 27),
            turn(choose(LAST, lane, lambda a: tw[a]), 28),
            turn(ends(LAST, LANES - 16), 32),
        ])
        own[0:GROUPS] = pack_w
        own[SLABS : SLABS + GROUPS] = pack_e
        north_l = tn[0, 8:9]
        north_r = tn[1, 8:9]
        south_13 = ts[PLANES - 2, 7 + GROUPS : 8 + GROUPS]
        south_14 = ts[PLANES - 1, 7 + GROUPS : 8 + GROUPS]
        south_l = turn(jnp.where(one >= 16, south_13, south_14), -16)
        south_r = turn(south_14, -16)
        own[48:49] = north_l
        own[49:50] = north_r
        own[50:51] = south_l
        own[51:52] = south_r
        deep = jnp.max(masked(slice(0, ROWS)), axis=(0, 1), keepdims=True)
        top = jnp.max(diag[...], axis=(0, 1), keepdims=True) + 8.0 * deep * deep
        top = jnp.broadcast_to(top, (1, LANES))

        slots[pl.ds(RIM_ROWS - 1, count, stride=SLOT), :] = jnp.broadcast_to(top, (count, LANES))
        eight = lane_of((8, LANES))
        eighth = row_of((8, LANES))
        for c, first, rows_l, rows_r in ((2, True, north_l, north_r), (3, False, south_l, south_r)):
            base = 0 if first else ROWS - 8
            spare = jnp.logical_and(eighth == 7, eight >= 64) if first else jnp.logical_and(eighth == 0, eight < 64)
            g = 0 if first else GROUPS - 1
            blocks = []
            block = slice(base, base + 8)
            for value, at in ((part[block, :], g), (masked(block), SLABS + g)):
                extra = jnp.broadcast_to(turn(own[at : at + 1], -16), (8, LANES))
                blocks.append(jnp.where(spare, extra, value))
            low = 0 if first else ROWS - 6
            diag_rows = diag[low : low + 6, :]
            last_row = jnp.where(one == LANES - 1, top, rows_r)

            @pl.when(sides[c] >= 0)
            def _(c=c, blocks=blocks, diag_rows=diag_rows, rows_l=rows_l, last_row=last_row):
                at = sides[c] * SLOT
                slots[pl.ds(at, 8), :] = blocks[0]
                slots[pl.ds(at + 8, 8), :] = blocks[1]
                slots[pl.ds(at + 16, 6), :] = diag_rows
                slots[pl.ds(at + 22, 1), :] = rows_l
                slots[pl.ds(at + 23, 1), :] = last_row

        slots[pl.ds(sides[0] * SLOT, GROUPS), :] = pack_w
        slots[pl.ds(sides[1] * SLOT, GROUPS), :] = pack_e
        for c, at in ((4, 0), (5, SLABS), (6, GROUPS - 1), (7, SLABS + GROUPS - 1)):
            @pl.when(sides[c] >= 0)
            def _(c=c, at=at):
                slots[pl.ds(sides[c] * SLOT, 1), :] = own[at : at + 1]


def whole(*shape):
    return pl.BlockSpec(shape, lambda *_: (0,) * len(shape))


SMEM = pl.BlockSpec(memory_space=pltpu.SMEM)


def solve_kernel(
    levels,
    table, around, rims, own, part, depth, ocean, diag,
    vectors, out, size,
    fb, fd, fg, pw, pe, ow, oe, ed, eg, we, wn, last, rows,
):
    depth, ocean, diag = (ref.reshape(ROWS, LANES) for ref in (depth, ocean, diag))
    count = rims.shape[0]
    came = rims.reshape(count * SLOT, LANES)
    hand = out.reshape(count * HAND, LANES)
    lane = lane_of((SLABS, LANES))
    slab = row_of((SLABS, LANES))
    one = lane_of((1, LANES))
    src = [table[c] for c in range(8)]

    def fetch(c, low, high):
        value = came[pl.ds(jnp.maximum(src[c], 0) * SLOT + low, high - low), :]
        return jnp.where(src[c] >= 0, value, 0.0)

    def relay(d, carry):
        for c in range(4):
            row = jnp.maximum(around[c * count + d], 0) * SLOT + RIM_ROWS + (c ^ 1)
            hand[pl.ds(d * HAND + 1 + c, 1), :] = came[pl.ds(row, 1), :]
        return carry

    lax.fori_loop(0, count, relay, 0)

    none = jnp.zeros((WIDE - ROWS + 4, LANES), jnp.float32)
    for ref in (fb, fd, fg):
        ref[ROWS - 4 : WIDE] = none
    fb[0:ROWS] = part[...]
    fd[0:ROWS] = depth[...] * ocean[...].astype(jnp.float32)
    fg[0:ROWS] = diag[...]
    for ref, low, high in ((fb, 0, 8), (fd, 8, 16), (fg, 16, 22)):
        ref[ROWS : ROWS + high - low] = fetch(3, low, high)
        ref[WIDE - high + low : WIDE] = fetch(2, low, high)
    empty = jnp.zeros((SLABS, LANES), jnp.float32)
    for ref, side, north, south in ((pw, 0, 6, 4), (pe, 1, 7, 5)):
        ref[...] = empty
        ref[0:GROUPS] = fetch(side, 0, GROUPS)
        ref[GROUPS : GROUPS + 1] = fetch(north, 0, 1)
        ref[SLABS - 1 : SLABS] = fetch(south, 0, 1)
    for ref, at, north, south in ((ow, 0, 7, 0), (oe, SLABS, 15, 8)):
        ref[...] = empty
        ref[0:GROUPS] = own[at : at + GROUPS]
        ref[GROUPS : GROUPS + 1] = turn(fetch(3, north, north + 1), 16)
        ref[SLABS - 1 : SLABS] = turn(fetch(2, south, south + 1), 16)

    def spread(ref, j):
        a = START[j]
        first, second = ref[comb(a, SLABS), :], ref[comb(a + 1, SLABS), :]
        third = ref[comb(a + 2, SLABS), :] if a + 2 < PLANES else second
        left = turn(jnp.where(lane >= OFF[j], first, second), -OFF[j])
        right = turn(jnp.where(lane >= OFF[j], second, third), -OFF[j])
        return left, right

    def seam_row(left, right, slab_at, lanes_at):
        east = turn(pe[slab_at : slab_at + 1], 112 - lanes_at)
        west = turn(pw[slab_at : slab_at + 1], 124 - lanes_at)
        right = jnp.where(one < 112, right, jnp.where(one < 116, east, jnp.where(one >= 124, west, 0.0)))
        return jnp.broadcast_to(left, (SLABS, LANES)), jnp.broadcast_to(right, (SLABS, LANES))

    seams = {
        0: ((0, seam_row(fetch(2, 22, 23), fetch(2, 23, 24), SLABS - 1, 28)),
            (GROUPS, seam_row(own[50:51], own[51:52], GROUPS - 1, 28))),
        GROUP - 1: ((GROUPS - 1, seam_row(fetch(3, 22, 23), fetch(3, 23, 24), GROUPS, 12)),
                    (SLABS - 1, seam_row(own[48:49], own[49:50], 0, 12))),
    }
    weight = STERIC / levels
    for j in range(GROUP):
        o = OFF[j]

        def rim(right, q, width):
            east = turn(pe[...], 112 - o - q)
            west = turn(pw[...], 128 - width - o - q)
            value = jnp.where(lane < 112 + width, east, jnp.where(lane >= 128 - width, west, 0.0))
            return jnp.where(lane < 112, right, value)

        left, right = spread(fd, j)
        right = rim(right, 4, 4)
        wet_l = jnp.where(left > 0, weight, 0.0)
        wet_r = jnp.where(right > 0, weight, 0.0)
        ed[j, :, 0:LANES] = left
        ed[j, :, LANES:] = right
        left, right = spread(fg, j)
        eg[j, :, 0:LANES] = left
        eg[j, :, LANES:] = rim(right, 8, 3)
        left, right = spread(fb, j)
        right = rim(right, 0, 4)
        seam_l = jnp.where(lane == 0, turn(pw[...], -o - 11), 0.0)
        seam_r = jnp.where(lane == 127, turn(ow[...], 127 - o - 11), 0.0)
        seam_r = jnp.where(lane == 111, turn(pe[...], 111 - o - 11), seam_r)
        seam_r = jnp.where(lane == 112, turn(oe[...], 112 - o - 11), seam_r)
        for at, (row_l, row_r) in seams.get(j, ()):
            seam_l = seam_l + jnp.where(slab == at, row_l, 0.0)
            seam_r = seam_r + jnp.where(slab == at, row_r, 0.0)
        vectors[0, j, :, 0:LANES] = left + wet_l * seam_l
        vectors[0, j, :, LANES:] = right + wet_r * seam_r

    for j in range(GROUP):
        d = ed[j]
        we[j] = d * turn(d, -1)
        above = ed[j + 1] if j < GROUP - 1 else turn(ed[0], -1, 0)
        wn[j] = d * above

    top = jnp.max(came[pl.ds(RIM_ROWS - 1, count, stride=SLOT), :], axis=0, keepdims=True)
    top = jnp.max(jnp.where(one == LANES - 1, top, 0.0), axis=1, keepdims=True)
    size[...] = jnp.broadcast_to(top, size.shape)
    scale = STRETCH / top

    big = (SLABS, 2 * LANES)
    mine = jnp.logical_and(row_of(big) < GROUPS, lane_of(big) < SPAN_X)
    pair = 0
    names = {}
    for k in range(5):
        sums = [None] * (k + 1)
        new = last if k == 4 else vectors.at[k]
        if k:
            v = vectors.at[k - 1]
            flow_below = wn[GROUP - 1] * (v[GROUP - 1] - turn(v[0], -1, 0))
            flow_below = turn(flow_below, 1, 0)
        for j in range(GROUP):
            if k:
                here = v[j]
                above = v[j + 1] if j < GROUP - 1 else turn(v[0], -1, 0)
                flow_x = we[j] * (here - turn(here, -1))
                flow_y = wn[j] * (here - above)
                image = eg[j] * here + (flow_x - turn(flow_x, 1)) + (flow_y - flow_below)
                fresh = scale * image - (STRETCH * ROOTS[k - 1]) * here
                flow_below = flow_y
                new[j] = fresh
            else:
                fresh = new[j]
            held = jnp.where(mine, fresh, 0.0)
            for i in range(k + 1):
                other = vectors[i, j] if i < k else held
                value = held * other
                sums[i] = value if sums[i] is None else sums[i] + value
        for i in range(k + 1):
            rows[pair : pair + 1] = jnp.sum(sums[i][:, 0:LANES] + sums[i][:, LANES:], axis=0, keepdims=True)
            names[i, k] = pair
            pair += 1
    rows[pair : pair + 1] = jnp.zeros((1, LANES), jnp.float32)
    total = jnp.sum(rows[...], axis=1, keepdims=True)
    spot = row_of((16, LANES)) == lane_of((16, LANES))
    line = jnp.sum(jnp.where(spot, total, 0.0), axis=0, keepdims=True)
    hand[pl.ds(0, count, stride=HAND), :] = jnp.broadcast_to(line, (count, LANES))


def finish_kernel(
    levels, table, hands, size, vectors, inner, edges, tracer, surface, left, right, message,
):
    count = hands.shape[0]
    came = hands.reshape(count * HAND, LANES)
    row = jnp.sum(came[pl.ds(0, count, stride=HAND), :], axis=0, keepdims=True)
    one = lane_of((1, LANES))
    entry = {}
    pair = 0
    for k in range(5):
        for i in range(k + 1):
            value = jnp.sum(jnp.where(one == pair, row, 0.0), axis=1, keepdims=True)
            entry[i, k] = entry[k, i] = value
            pair += 1
    top = size[0:1, 0:1]

    def image(c):
        out = [None] * 5
        for k in range(4):
            if c[k] is None:
                continue
            low = ROOTS[k] * c[k]
            out[k] = low if out[k] is None else out[k] + low
            out[k + 1] = (1.0 / STRETCH) * c[k]
        return out

    def dot(a, b):
        total = None
        for i in range(5):
            if a[i] is None:
                continue
            inner = None
            for j in range(5):
                if b[j] is not None:
                    value = entry[i, j] * b[j]
                    inner = value if inner is None else inner + value
            total = a[i] * inner if total is None else total + a[i] * inner
        return total

    def axpy(a, s, b):
        return [
            x if y is None else (s * y if x is None else x + s * y) for x, y in zip(a, b)
        ]

    r = [jnp.ones((1, 1), jnp.float32)] + [None] * 4
    p = list(r)
    x = [None] * 5
    rr = entry[0, 0]
    for n in range(ITERS):
        q = image(p)
        step = rr / jnp.maximum(dot(p, q), TINY)
        step = jnp.clip(step, top * (1.0 / HIGH_RATE), top * (1.0 / LOW_RATE))
        x = axpy(x, step, p)
        if n < ITERS - 1:
            r = axpy(r, -step, q)
            fresh = jnp.maximum(dot(r, r), 0.0)
            p = axpy(r, fresh / jnp.maximum(rr, TINY), p)
            rr = fresh
    flat = surface.reshape(ROWS, LANES)
    factors = [c / top for c in x[:4]]
    for j in range(GROUP):
        value = None
        for k in range(4):
            term = factors[k] * vectors[k, j]
            value = term if value is None else value + term
        left[j] = turn(value[:, 0:LANES], OFF[j])
        right[j] = turn(value[:, LANES:], OFF[j])
    lane = lane_of((SLABS, LANES))
    for a in range(PLANES):
        value = None
        for j in range(GROUP):
            for half, ref in ((0, left), (1, right)):
                low = max(SPAN_X * j + LANES * half - LANES * a, 0)
                high = min(SPAN_X * j + (LANES if half == 0 else SPAN_X) - LANES * a, LANES)
                if low >= high:
                    continue
                value = ref[j] if value is None else jnp.where(lane >= low, ref[j], value)
        flat[comb(a), :] = value[0:GROUPS]

    for c in range(4):
        value = came[pl.ds(1 + c, 2 * levels, stride=HAND), :]
        message[c] = jnp.where(table[c] >= 0, value, 0.0)
    sums = []
    for k in range(levels):
        value = edges[2 * levels - 1] * jnp.concatenate([
            turn(message[0], -k), turn(message[1], -k),
            message[2, k : k + 1], message[2, k + levels : k + levels + 1],
            message[3, k : k + 1], message[3, k + levels : k + levels + 1],
            jnp.zeros((4, LANES), jnp.float32),
        ], axis=0)
        if k:
            value = value + edges[2 * levels + k - 1] * sums[-1]
        sums.append(value * edges[levels - 1 + k])
    for k in range(levels - 2, -1, -1):
        sums[k] = sums[k] + edges[k] * sums[k + 1]
    tracer[...] = inner[...]
    lane = lane_of((GROUPS, LANES))
    slab = row_of((GROUPS, LANES))
    for k in range(levels):
        west = sums[k][0:GROUPS]
        east = turn(sums[k][SLABS : SLABS + GROUPS], -17)
        south_l, south_r = sums[k][48:49], sums[k][49:50]
        north_l, north_r = turn(sums[k][50:51], 16), turn(sums[k][51:52], 16)
        for a in range(PLANES):
            rim = None
            for at, source in [(at, west) for at in FIRST_OF[a]] + [(at, east) for at in LAST_OF[a]]:
                rim = jnp.where(lane == at, source, 0.0 if rim is None else rim)
            if rim is None:
                continue
            if a == 0:
                rim = rim + jnp.where(slab == 0, south_l, 0.0)
            if a == 1:
                rim = rim + jnp.where(jnp.logical_and(slab == 0, lane < 112), south_r, 0.0)
            if a == PLANES - 2:
                rim = rim + jnp.where(jnp.logical_and(slab == GROUPS - 1, lane >= 16), north_l, 0.0)
            if a == PLANES - 1:
                rim = rim + jnp.where(slab == GROUPS - 1, jnp.where(lane < 16, north_l, north_r), 0.0)
            rows = comb(k * ROWS + a)
            tracer[rows, :] = tracer[rows, :] + rim


def tracer_kernel(
    levels, per, tiles_x, tiles_y, pos, temp, zonal, merid, rates, ocean,
    out, edges, around, te, tw, tn, ts, stepped, border, holder,
):
    step = pl.program_id(0)
    count = pos.shape[0]
    lane = lane_of((GROUPS, LANES))
    one = lane_of((1, LANES))
    ocean = ocean.reshape(ROWS, LANES)
    rates = rates.reshape((levels - 1) * ROWS, LANES)

    @pl.when(step == 0)
    def _():
        clear_terms(tn, ts)

        def number(d, carry):
            holder[pos[d]] = d
            return carry

        lax.fori_loop(0, count, number, 0)

        def look(d, carry):
            row = pos[d] // tiles_x
            column = pos[d] % tiles_x
            for c, (dx, dy) in enumerate(SIDES[:4]):
                there = row + dy
                inside = jnp.logical_and(there >= 0, there < tiles_y)
                target = jnp.where(inside, there, 0) * tiles_x + (column + dx + tiles_x) % tiles_x
                around[c * count + d] = jnp.where(inside, holder[target], -1)
            return carry

        lax.fori_loop(0, count, look, 0)

    for n in range(per):
        t, u, v = (ref.at[n].reshape(ROWS, LANES) for ref in (temp, zonal, merid))
        for a in range(PLANES):
            own = t[comb(a), :]
            quarter = ADVECT * own
            store_terms(a, own, u[comb(a), :] * quarter, v[comb(a), :] * quarter, te, tw, tn, ts)
        for a in range(PLANES):
            own = t[comb(a), :]
            change = inner_sum(a, te, tw, tn, ts) - 4.0 * DIFFUSE * own
            stepped[step * per + n, a] = own + ocean[comb(a), :].astype(jnp.float32) * change

    @pl.when(step == pl.num_programs(0) - 1)
    def _():
        def block(a, carry):
            for low in range(0, GROUPS, 8):
                size = min(8, GROUPS - low)

                def rows(k):
                    return pl.ds(k * ROWS + low * PLANES + a, size, stride=PLANES)

                gains = []
                sums = []
                for k in range(levels):
                    value = stepped[k, a, low : low + size]
                    pivot = 1.0
                    if k > 0:
                        pivot = pivot + upper - upper * gains[-1]
                        value = value + upper * sums[-1]
                    if k < levels - 1:
                        lower = rates[rows(k), :]
                        inverse = 1.0 / (pivot + lower)
                        gains.append(lower * inverse)
                        upper = lower
                    else:
                        inverse = 1.0 / pivot
                    sums.append(value * inverse)
                result = sums[-1]
                out[rows(levels - 1), :] = result
                for k in range(levels - 2, -1, -1):
                    result = sums[k] + gains[k] * result
                    out[rows(k), :] = result
            return carry

        lax.fori_loop(0, PLANES, block, 0)

        def edge(ref, base, at):
            def get(a):
                return ref[comb(base + a), :].astype(jnp.float32)

            border[0:GROUPS] = choose(START, lane, get)
            border[SLABS : SLABS + GROUPS] = turn(choose(LAST, lane, get), 17)
            border[48:50] = ref[base : base + 2, :].astype(jnp.float32)
            rows = ref[base + ROWS - 2 : base + ROWS, :].astype(jnp.float32)
            border[50:51] = turn(jnp.where(one >= 16, rows[0:1], rows[1:2]), -16)
            border[51:52] = turn(rows[1:2], -16)
            edges[at] = border[...]

        border[...] = jnp.zeros_like(border)
        edge(ocean, 0, 2 * levels - 1)
        gain = None
        for k in range(levels):
            pivot = 1.0
            if k > 0:
                upper = edges[2 * levels + k - 1]
                pivot = pivot + upper - upper * gain
            if k < levels - 1:
                edge(rates, k * ROWS, 2 * levels + k)
                lower = edges[2 * levels + k]
                inverse = 1.0 / (pivot + lower)
                gain = lower * inverse
                edges[k] = gain
            else:
                inverse = 1.0 / pivot
            edges[levels - 1 + k] = inverse


def on_device(
    thermal_anomaly,
    zonal_flow_ratio,
    meridional_flow_ratio,
    diffusion_rates,
    ocean_bottom_scaled,
    ocean_indicator,
    operator_diagonal,
    elevation_source,
    block_positions,
):
    levels, cells = thermal_anomaly.shape[1:]
    nx = lax.axis_size("gx")
    ny = lax.axis_size("gy")
    count = block_positions.shape[0]
    planes = (ocean_bottom_scaled, ocean_indicator, operator_diagonal, elevation_source)
    depth, ocean, diag, source = planes
    f32 = jnp.float32
    steps = next(n for n in (4, 3, 2, 1) if levels % n == 0)
    per = levels // steps
    params = pltpu.CompilerParams(vmem_limit_bytes=BUDGET)
    temp, zonal, merid, rates = (
        array.reshape(array.shape[1], 1, cells)
        for array in (thermal_anomaly, zonal_flow_ratio, meridional_flow_ratio, diffusion_rates)
    )
    some = pl.BlockSpec((per, 1, cells), lambda i: (i, 0, 0))
    flat = whole(1, cells)

    def vmem(*shape):
        return pltpu.VMEM(shape, f32)

    def out(*shape):
        return jax.ShapeDtypeStruct(shape, f32)

    plane = vmem(PLANES, GROUPS, LANES)
    tall = vmem(PLANES, 40, LANES)
    here = pl.BlockSpec(memory_space=pltpu.VMEM)
    numbers = pltpu.SMEM((count,), jnp.int32)
    part, own, slots, table = pl.pallas_call(
        functools.partial(forcing_kernel, levels, per, nx, ny),
        grid=(steps,),
        in_specs=[SMEM, some, some, some, flat, flat, flat, flat],
        out_specs=[whole(ROWS, LANES), whole(56, LANES), whole(count, 1, SLOT * LANES), SMEM],
        out_shape=[
            out(ROWS, LANES), out(56, LANES), out(count, 1, SLOT * LANES),
            jax.ShapeDtypeStruct((8,), jnp.int32),
        ],
        scratch_shapes=[vmem(ROWS, LANES)] * 3 + [plane] * 3 + [tall] * 2
        + [vmem(4, 2 * levels, LANES), numbers],
        compiler_params=params,
        name="forcing",
    )(block_positions, temp, zonal, merid, depth, ocean, diag, source)
    rims = lax.all_to_all(slots, BOTH, 0, 0, tiled=True)

    inner, edges, around = pl.pallas_call(
        functools.partial(tracer_kernel, levels, per, nx, ny),
        grid=(steps,),
        in_specs=[SMEM, some, some, some, whole(levels - 1, 1, cells), flat],
        out_specs=[whole(levels * ROWS, LANES), whole(3 * levels - 1, EDGE, LANES), SMEM],
        out_shape=[
            out(levels * ROWS, LANES), out(3 * levels - 1, EDGE, LANES),
            jax.ShapeDtypeStruct((4 * count,), jnp.int32),
        ],
        scratch_shapes=[plane] * 2 + [tall] * 2
        + [vmem(levels, PLANES, GROUPS, LANES), vmem(EDGE, LANES), numbers],
        compiler_params=params,
        name="tracer",
    )(block_positions, temp, zonal, merid, rates, ocean)

    extended = vmem(GROUP, SLABS, 2 * LANES)
    vectors, hand, size = pl.pallas_call(
        functools.partial(solve_kernel, levels),
        in_specs=[SMEM, SMEM] + [here] * 6,
        out_specs=[here] * 3,
        out_shape=[out(4, GROUP, SLABS, 2 * LANES), out(count, 1, HAND * LANES), out(8, LANES)],
        scratch_shapes=[vmem(WIDE, LANES)] * 3 + [vmem(SLABS, LANES)] * 4 + [extended] * 5 + [vmem(16, LANES)],
        compiler_params=params,
        name="vectors",
    )(table, around, rims, own, part, depth, ocean, diag)
    hands = lax.all_to_all(hand, BOTH, 0, 0, tiled=True)

    new_temp, surface = pl.pallas_call(
        functools.partial(finish_kernel, levels),
        in_specs=[SMEM] + [here] * 5,
        out_specs=[here] * 2,
        out_shape=[out(levels * ROWS, LANES), out(1, cells)],
        scratch_shapes=[vmem(GROUP, SLABS, LANES)] * 2 + [vmem(4, 2 * levels, LANES)],
        compiler_params=params,
        name="finish",
    )(table, hands, size, vectors, inner, edges)
    return new_temp.reshape(1, levels, cells), surface


def solution(mesh):
    deep = P(BOTH, None, None)
    flat = P(BOTH, None)
    return jax.shard_map(
        on_device,
        mesh=mesh,
        in_specs=(deep, deep, deep, deep, flat, flat, flat, flat, P()),
        out_specs=(deep, flat),
        check_vma=False,
    )
```

```python
import functools

import jax
import jax.numpy as jnp
from jax import lax
from jax.experimental import pallas as pl
from jax.experimental.pallas import tpu as pltpu
from jax.sharding import PartitionSpec as P

ITERS = 4
SPAN_X = 240
SPAN_Y = 160
RIM = 4
ADVECT = 0.25
DIFFUSE = 0.12
STERIC = 0.5
LOW_RATE = 0.05
HIGH_RATE = 32.5
ROOTS = (0.02, 0.35, 0.1, 0.2)
STRETCH = 4.0
TINY = 1e-30
BOTH = ("gx", "gy")
SIDES = ((-1, 0), (1, 0), (0, -1), (0, 1), (-1, -1), (1, -1), (-1, 1), (1, 1))

LANES = 128
GROUP = 8
GROUPS = SPAN_Y // GROUP
PLANES = GROUP * SPAN_X // LANES
ROWS = GROUPS * PLANES
SLABS = GROUPS + 4
WIDE = SLABS * PLANES
START = [SPAN_X * j // LANES for j in range(GROUP)]
OFF = [SPAN_X * j % LANES for j in range(GROUP)]
LAST = [(SPAN_X * j + SPAN_X - 1) // LANES for j in range(GROUP)]
END = [(SPAN_X * j + SPAN_X - 1) % LANES for j in range(GROUP)]
FIRST_OF = [[OFF[j] for j in range(GROUP) if START[j] == a] for a in range(PLANES)]
LAST_OF = [[END[j] for j in range(GROUP) if LAST[j] == a] for a in range(PLANES)]
RIM_ROWS = 24
SLOT = RIM_ROWS + 4
HAND = 5
EDGE = 56
BUDGET = 56 * 1024 * 1024


def turn(value, shift, axis=1):
    shift = shift % value.shape[axis]
    return value if shift == 0 else pltpu.roll(value, shift, axis)


def lane_of(shape):
    return lax.broadcasted_iota(jnp.int32, shape, len(shape) - 1)


def row_of(shape):
    return lax.broadcasted_iota(jnp.int32, shape, 0)


def comb(a, count=GROUPS):
    return pl.ds(a, count, stride=PLANES)


def drop(value, lanes, lane):
    for at in lanes:
        value = jnp.where(lane == at, 0.0, value)
    return value


def store_terms(a, temp, flow_x, flow_y, te, tw, tn, ts):
    spread = DIFFUSE * temp
    te[a] = spread - flow_x
    tw[a] = spread + flow_x
    tn[a, 8 : 8 + GROUPS] = spread - flow_y
    ts[a, 8 : 8 + GROUPS] = spread + flow_y


def clear_terms(tn, ts):
    none = jnp.zeros((PLANES, 1, LANES), jnp.float32)
    for ref in (tn, ts):
        ref[:, 7:8] = none
        ref[:, 8 + GROUPS : 9 + GROUPS] = none


def inner_sum(a, te, tw, tn, ts):
    lane = lane_of((GROUPS, LANES))
    here = te[a]
    east = here if a == PLANES - 1 else jnp.where(lane == 0, te[a + 1], here)
    east = drop(turn(east, -1), LAST_OF[a], lane)
    here = tw[a]
    west = here if a == 0 else jnp.where(lane == LANES - 1, tw[a - 1], here)
    west = drop(turn(west, 1), FIRST_OF[a], lane)

    def plane(ref, at):
        down = 8 + (at >= PLANES) - (at < 0)
        return ref[at % PLANES, down : down + GROUPS]

    north = turn(jnp.where(lane >= LANES - 16, plane(tn, a + 1), plane(tn, a + 2)), 16)
    south = turn(jnp.where(lane < 16, plane(ts, a - 1), plane(ts, a - 2)), -16)
    return east + west + north + south


def choose(planes, lane, get):
    value = get(planes[0])
    for j in range(1, GROUP):
        low = (OFF[j] - (32 if planes is LAST else 0)) % LANES
        value = jnp.where(jnp.logical_and(lane >= low, lane < low + 16), get(planes[j]), value)
    return value


def forcing_kernel(
    levels, per, tiles_x, tiles_y,
    pos, temp, zonal, merid, depth, ocean, diag, source,
    part, own, out, table,
    st, sx, sy, pt, te, tw, tn, ts, edges, holder,
):
    step = pl.program_id(0)
    count = pos.shape[0]
    depth, ocean, diag, source = (ref.reshape(ROWS, LANES) for ref in (depth, ocean, diag, source))
    slots = out.reshape(count * SLOT, LANES)
    lane = lane_of((GROUPS, LANES))
    one = lane_of((1, LANES))
    q = lane % 16
    flats = [[ref.at[k].reshape(ROWS, LANES) for k in range(per)] for ref in (temp, zonal, merid)]

    def add(low, size, fresh):
        rows = pl.ds(low, size)
        total = [None] * 3
        for t, u, v in zip(*flats):
            t = t[rows, :]
            new = (t, t * u[rows, :], t * v[rows, :])
            total = [b if a is None else a + b for a, b in zip(total, new)]
        for ref, value in zip((st, sx, sy), total):
            ref[rows, :] = value if fresh else ref[rows, :] + value

    def run(fresh):
        def some(m, carry):
            add(pl.multiple_of(m * 8, 8), 8, fresh)
            return carry

        lax.fori_loop(0, ROWS // 8, some, 0, unroll=4)
        if ROWS % 8:
            add(ROWS - ROWS % 8, ROWS % 8, fresh)

    @pl.when(step == 0)
    def _():
        edges[...] = jnp.zeros_like(edges)
        run(True)

    pl.when(step > 0)(lambda: run(False))

    for n in range(per):
        k = step * per + n
        t, u, v = (flat[n] for flat in flats)

        def term(planes, sign):
            own = choose(planes, lane, lambda a: t[comb(a), :])
            flow = choose(planes, lane, lambda a: u[comb(a), :])
            return DIFFUSE * own + sign * ADVECT * (flow * own)

        edges[0, 0:GROUPS] = jnp.where(q == k, pltpu.roll(term(START, -1.0), k, 1), edges[0, 0:GROUPS])
        edges[1, 0:GROUPS] = jnp.where(q == k, pltpu.roll(term(LAST, 1.0), k + 17, 1), edges[1, 0:GROUPS])
        rows = t[0:2, :]
        rows = DIFFUSE * rows - ADVECT * (v[0:2, :] * rows)
        edges[2, pl.ds(k, 1)] = rows[0:1]
        edges[2, pl.ds(k + levels, 1)] = rows[1:2]
        rows = t[ROWS - 2 : ROWS, :]
        rows = DIFFUSE * rows + ADVECT * (v[ROWS - 2 : ROWS, :] * rows)
        edges[3, pl.ds(k, 1)] = turn(jnp.where(one >= 16, rows[0:1], rows[1:2]), -16)
        edges[3, pl.ds(k + levels, 1)] = turn(rows[1:2], -16)

    @pl.when(step == pl.num_programs(0) - 1)
    def _():
        for c in range(4):
            slots[pl.ds(RIM_ROWS + c, 2 * levels, stride=SLOT), :] = edges[c]

        def wet_of(rows):
            return ocean[rows, :].astype(jnp.float32)

        def masked(rows):
            return depth[rows, :] * wet_of(rows)

        def number(d, carry):
            holder[pos[d]] = d
            return carry

        lax.fori_loop(0, count, number, 0)
        me = lax.axis_index("gx") * tiles_y + lax.axis_index("gy")
        here = pos[me]
        row = here // tiles_x
        column = here % tiles_x
        sides = []
        for c, (dx, dy) in enumerate(SIDES):
            there = row + dy
            inside = jnp.logical_and(there >= 0, there < tiles_y)
            target = jnp.where(inside, there, 0) * tiles_x + (column + dx + tiles_x) % tiles_x
            device = jnp.where(inside, holder[target], -1)
            table[c] = device
            sides.append(device)

        clear_terms(tn, ts)
        for a in range(PLANES):
            total = st[comb(a), :]
            pt[a] = total
            store_terms(a, total, ADVECT * sx[comb(a), :], ADVECT * sy[comb(a), :], te, tw, tn, ts)
        for a in range(PLANES):
            total = pt[a]
            wet = wet_of(comb(a))
            change = inner_sum(a, te, tw, tn, ts) - 4.0 * DIFFUSE * total
            part[comb(a), :] = source[comb(a), :] + (STERIC / levels) * wet * (total + wet * change)

        def mix(values):
            value = values[4]
            for at, low in ((3, 12), (2, 11), (1, 8), (0, 4)):
                value = jnp.where(q < low, values[at], value)
            return value

        def flat(ref):
            return lambda a: ref[comb(a), :]

        def ends(planes, low):
            value = tn[planes[0], 8 : 8 + GROUPS]
            last = jnp.logical_and(lane >= low, lane < low + 16)
            return jnp.where(last, ts[planes[7], 8 : 8 + GROUPS], value)

        pack_w = mix([
            choose(START, lane, flat(part)),
            turn(choose(START, lane, lambda a: masked(comb(a))), 4),
            turn(choose(START, lane, flat(diag)), 8),
            turn(choose(START, lane, lambda a: te[a]), 11),
            turn(ends(START, OFF[7]), 12),
        ])
        pack_e = mix([
            turn(choose(LAST, lane, flat(part)), 20),
            turn(choose(LAST, lane, lambda a: masked(comb(a))), 24),
            turn(choose(LAST, lane, flat(diag)), 27),
            turn(choose(LAST, lane, lambda a: tw[a]), 28),
            turn(ends(LAST, LANES - 16), 32),
        ])
        own[0:GROUPS] = pack_w
        own[SLABS : SLABS + GROUPS] = pack_e
        north_l = tn[0, 8:9]
        north_r = tn[1, 8:9]
        south_13 = ts[PLANES - 2, 7 + GROUPS : 8 + GROUPS]
        south_14 = ts[PLANES - 1, 7 + GROUPS : 8 + GROUPS]
        south_l = turn(jnp.where(one >= 16, south_13, south_14), -16)
        south_r = turn(south_14, -16)
        own[48:49] = north_l
        own[49:50] = north_r
        own[50:51] = south_l
        own[51:52] = south_r
        deep = jnp.max(masked(slice(0, ROWS)), axis=(0, 1), keepdims=True)
        top = jnp.max(diag[...], axis=(0, 1), keepdims=True) + 8.0 * deep * deep
        top = jnp.broadcast_to(top, (1, LANES))

        slots[pl.ds(RIM_ROWS - 1, count, stride=SLOT), :] = jnp.broadcast_to(top, (count, LANES))
        eight = lane_of((8, LANES))
        eighth = row_of((8, LANES))
        for c, first, rows_l, rows_r in ((2, True, north_l, north_r), (3, False, south_l, south_r)):
            base = 0 if first else ROWS - 8
            spare = jnp.logical_and(eighth == 7, eight >= 64) if first else jnp.logical_and(eighth == 0, eight < 64)
            g = 0 if first else GROUPS - 1
            blocks = []
            block = slice(base, base + 8)
            for value, at in ((part[block, :], g), (masked(block), SLABS + g)):
                extra = jnp.broadcast_to(turn(own[at : at + 1], -16), (8, LANES))
                blocks.append(jnp.where(spare, extra, value))
            low = 0 if first else ROWS - 6
            diag_rows = diag[low : low + 6, :]
            last_row = jnp.where(one == LANES - 1, top, rows_r)

            @pl.when(sides[c] >= 0)
            def _(c=c, blocks=blocks, diag_rows=diag_rows, rows_l=rows_l, last_row=last_row):
                at = sides[c] * SLOT
                slots[pl.ds(at, 8), :] = blocks[0]
                slots[pl.ds(at + 8, 8), :] = blocks[1]
                slots[pl.ds(at + 16, 6), :] = diag_rows
                slots[pl.ds(at + 22, 1), :] = rows_l
                slots[pl.ds(at + 23, 1), :] = last_row

        slots[pl.ds(sides[0] * SLOT, GROUPS), :] = pack_w
        slots[pl.ds(sides[1] * SLOT, GROUPS), :] = pack_e
        for c, at in ((4, 0), (5, SLABS), (6, GROUPS - 1), (7, SLABS + GROUPS - 1)):
            @pl.when(sides[c] >= 0)
            def _(c=c, at=at):
                slots[pl.ds(sides[c] * SLOT, 1), :] = own[at : at + 1]


def whole(*shape):
    return pl.BlockSpec(shape, lambda *_: (0,) * len(shape))


SMEM = pl.BlockSpec(memory_space=pltpu.SMEM)


def solve_kernel(
    levels,
    table, around, rims, own, part, depth, ocean, diag,
    vectors, out, size,
    fb, fd, fg, pw, pe, ow, oe, ed, eg, we, wn, last, rows,
):
    depth, ocean, diag = (ref.reshape(ROWS, LANES) for ref in (depth, ocean, diag))
    count = rims.shape[0]
    came = rims.reshape(count * SLOT, LANES)
    hand = out.reshape(count * HAND, LANES)
    lane = lane_of((SLABS, LANES))
    slab = row_of((SLABS, LANES))
    one = lane_of((1, LANES))
    src = [table[c] for c in range(8)]

    def fetch(c, low, high):
        value = came[pl.ds(jnp.maximum(src[c], 0) * SLOT + low, high - low), :]
        return jnp.where(src[c] >= 0, value, 0.0)

    def relay(d, carry):
        for c in range(4):
            row = jnp.maximum(around[c * count + d], 0) * SLOT + RIM_ROWS + (c ^ 1)
            hand[pl.ds(d * HAND + 1 + c, 1), :] = came[pl.ds(row, 1), :]
        return carry

    lax.fori_loop(0, count, relay, 0)

    none = jnp.zeros((WIDE - ROWS + 4, LANES), jnp.float32)
    for ref in (fb, fd, fg):
        ref[ROWS - 4 : WIDE] = none
    fb[0:ROWS] = part[...]
    fd[0:ROWS] = depth[...] * ocean[...].astype(jnp.float32)
    fg[0:ROWS] = diag[...]
    for ref, low, high in ((fb, 0, 8), (fd, 8, 16), (fg, 16, 22)):
        ref[ROWS : ROWS + high - low] = fetch(3, low, high)
        ref[WIDE - high + low : WIDE] = fetch(2, low, high)
    empty = jnp.zeros((SLABS, LANES), jnp.float32)
    for ref, side, north, south in ((pw, 0, 6, 4), (pe, 1, 7, 5)):
        ref[...] = empty
        ref[0:GROUPS] = fetch(side, 0, GROUPS)
        ref[GROUPS : GROUPS + 1] = fetch(north, 0, 1)
        ref[SLABS - 1 : SLABS] = fetch(south, 0, 1)
    for ref, at, north, south in ((ow, 0, 7, 0), (oe, SLABS, 15, 8)):
        ref[...] = empty
        ref[0:GROUPS] = own[at : at + GROUPS]
        ref[GROUPS : GROUPS + 1] = turn(fetch(3, north, north + 1), 16)
        ref[SLABS - 1 : SLABS] = turn(fetch(2, south, south + 1), 16)

    def spread(ref, j):
        a = START[j]
        first, second = ref[comb(a, SLABS), :], ref[comb(a + 1, SLABS), :]
        third = ref[comb(a + 2, SLABS), :] if a + 2 < PLANES else second
        left = turn(jnp.where(lane >= OFF[j], first, second), -OFF[j])
        right = turn(jnp.where(lane >= OFF[j], second, third), -OFF[j])
        return left, right

    def seam_row(left, right, slab_at, lanes_at):
        east = turn(pe[slab_at : slab_at + 1], 112 - lanes_at)
        west = turn(pw[slab_at : slab_at + 1], 124 - lanes_at)
        right = jnp.where(one < 112, right, jnp.where(one < 116, east, jnp.where(one >= 124, west, 0.0)))
        return jnp.broadcast_to(left, (SLABS, LANES)), jnp.broadcast_to(right, (SLABS, LANES))

    seams = {
        0: ((0, seam_row(fetch(2, 22, 23), fetch(2, 23, 24), SLABS - 1, 28)),
            (GROUPS, seam_row(own[50:51], own[51:52], GROUPS - 1, 28))),
        GROUP - 1: ((GROUPS - 1, seam_row(fetch(3, 22, 23), fetch(3, 23, 24), GROUPS, 12)),
                    (SLABS - 1, seam_row(own[48:49], own[49:50], 0, 12))),
    }
    weight = STERIC / levels
    for j in range(GROUP):
        o = OFF[j]

        def rim(right, q, width):
            east = turn(pe[...], 112 - o - q)
            west = turn(pw[...], 128 - width - o - q)
            value = jnp.where(lane < 112 + width, east, jnp.where(lane >= 128 - width, west, 0.0))
            return jnp.where(lane < 112, right, value)

        left, right = spread(fd, j)
        right = rim(right, 4, 4)
        wet_l = jnp.where(left > 0, weight, 0.0)
        wet_r = jnp.where(right > 0, weight, 0.0)
        ed[j, :, 0:LANES] = left
        ed[j, :, LANES:] = right
        left, right = spread(fg, j)
        eg[j, :, 0:LANES] = left
        eg[j, :, LANES:] = rim(right, 8, 3)
        left, right = spread(fb, j)
        right = rim(right, 0, 4)
        seam_l = jnp.where(lane == 0, turn(pw[...], -o - 11), 0.0)
        seam_r = jnp.where(lane == 127, turn(ow[...], 127 - o - 11), 0.0)
        seam_r = jnp.where(lane == 111, turn(pe[...], 111 - o - 11), seam_r)
        seam_r = jnp.where(lane == 112, turn(oe[...], 112 - o - 11), seam_r)
        for at, (row_l, row_r) in seams.get(j, ()):
            seam_l = seam_l + jnp.where(slab == at, row_l, 0.0)
            seam_r = seam_r + jnp.where(slab == at, row_r, 0.0)
        vectors[0, j, :, 0:LANES] = left + wet_l * seam_l
        vectors[0, j, :, LANES:] = right + wet_r * seam_r

    for j in range(GROUP):
        d = ed[j]
        we[j] = d * turn(d, -1)
        above = ed[j + 1] if j < GROUP - 1 else turn(ed[0], -1, 0)
        wn[j] = d * above

    top = jnp.max(came[pl.ds(RIM_ROWS - 1, count, stride=SLOT), :], axis=0, keepdims=True)
    top = jnp.max(jnp.where(one == LANES - 1, top, 0.0), axis=1, keepdims=True)
    size[...] = jnp.broadcast_to(top, size.shape)
    scale = STRETCH / top

    big = (SLABS, 2 * LANES)
    mine = jnp.logical_and(row_of(big) < GROUPS, lane_of(big) < SPAN_X)
    pair = 0
    names = {}
    for k in range(5):
        sums = [None] * (k + 1)
        new = last if k == 4 else vectors.at[k]
        if k:
            v = vectors.at[k - 1]
            flow_below = wn[GROUP - 1] * (v[GROUP - 1] - turn(v[0], -1, 0))
            flow_below = turn(flow_below, 1, 0)
        for j in range(GROUP):
            if k:
                here = v[j]
                above = v[j + 1] if j < GROUP - 1 else turn(v[0], -1, 0)
                flow_x = we[j] * (here - turn(here, -1))
                flow_y = wn[j] * (here - above)
                image = eg[j] * here + (flow_x - turn(flow_x, 1)) + (flow_y - flow_below)
                fresh = scale * image - (STRETCH * ROOTS[k - 1]) * here
                flow_below = flow_y
                new[j] = fresh
            else:
                fresh = new[j]
            held = jnp.where(mine, fresh, 0.0)
            for i in range(k + 1):
                other = vectors[i, j] if i < k else held
                value = held * other
                sums[i] = value if sums[i] is None else sums[i] + value
        for i in range(k + 1):
            rows[pair : pair + 1] = jnp.sum(sums[i][:, 0:LANES] + sums[i][:, LANES:], axis=0, keepdims=True)
            names[i, k] = pair
            pair += 1
    rows[pair : pair + 1] = jnp.zeros((1, LANES), jnp.float32)
    total = jnp.sum(rows[...], axis=1, keepdims=True)
    spot = row_of((16, LANES)) == lane_of((16, LANES))
    line = jnp.sum(jnp.where(spot, total, 0.0), axis=0, keepdims=True)
    hand[pl.ds(0, count, stride=HAND), :] = jnp.broadcast_to(line, (count, LANES))


def finish_kernel(
    levels, table, hands, size, vectors, inner, edges, tracer, surface, left, right, message,
):
    count = hands.shape[0]
    came = hands.reshape(count * HAND, LANES)
    row = jnp.sum(came[pl.ds(0, count, stride=HAND), :], axis=0, keepdims=True)
    one = lane_of((1, LANES))
    entry = {}
    pair = 0
    for k in range(5):
        for i in range(k + 1):
            value = jnp.sum(jnp.where(one == pair, row, 0.0), axis=1, keepdims=True)
            entry[i, k] = entry[k, i] = value
            pair += 1
    top = size[0:1, 0:1]

    def image(c):
        out = [None] * 5
        for k in range(4):
            if c[k] is None:
                continue
            low = ROOTS[k] * c[k]
            out[k] = low if out[k] is None else out[k] + low
            out[k + 1] = (1.0 / STRETCH) * c[k]
        return out

    def dot(a, b):
        total = None
        for i in range(5):
            if a[i] is None:
                continue
            inner = None
            for j in range(5):
                if b[j] is not None:
                    value = entry[i, j] * b[j]
                    inner = value if inner is None else inner + value
            total = a[i] * inner if total is None else total + a[i] * inner
        return total

    def axpy(a, s, b):
        return [
            x if y is None else (s * y if x is None else x + s * y) for x, y in zip(a, b)
        ]

    r = [jnp.ones((1, 1), jnp.float32)] + [None] * 4
    p = list(r)
    x = [None] * 5
    rr = entry[0, 0]
    for n in range(ITERS):
        q = image(p)
        step = rr / jnp.maximum(dot(p, q), TINY)
        step = jnp.clip(step, top * (1.0 / HIGH_RATE), top * (1.0 / LOW_RATE))
        x = axpy(x, step, p)
        if n < ITERS - 1:
            r = axpy(r, -step, q)
            fresh = jnp.maximum(dot(r, r), 0.0)
            p = axpy(r, fresh / jnp.maximum(rr, TINY), p)
            rr = fresh
    flat = surface.reshape(ROWS, LANES)
    factors = [c / top for c in x[:4]]
    for j in range(GROUP):
        value = None
        for k in range(4):
            term = factors[k] * vectors[k, j]
            value = term if value is None else value + term
        left[j] = turn(value[:, 0:LANES], OFF[j])
        right[j] = turn(value[:, LANES:], OFF[j])
    lane = lane_of((SLABS, LANES))
    for a in range(PLANES):
        value = None
        for j in range(GROUP):
            for half, ref in ((0, left), (1, right)):
                low = max(SPAN_X * j + LANES * half - LANES * a, 0)
                high = min(SPAN_X * j + (LANES if half == 0 else SPAN_X) - LANES * a, LANES)
                if low >= high:
                    continue
                value = ref[j] if value is None else jnp.where(lane >= low, ref[j], value)
        flat[comb(a), :] = value[0:GROUPS]

    for c in range(4):
        value = came[pl.ds(1 + c, 2 * levels, stride=HAND), :]
        message[c] = jnp.where(table[c] >= 0, value, 0.0)
    sums = []
    for k in range(levels):
        value = edges[2 * levels - 1] * jnp.concatenate([
            turn(message[0], -k), turn(message[1], -k),
            message[2, k : k + 1], message[2, k + levels : k + levels + 1],
            message[3, k : k + 1], message[3, k + levels : k + levels + 1],
            jnp.zeros((4, LANES), jnp.float32),
        ], axis=0)
        if k:
            value = value + edges[2 * levels + k - 1] * sums[-1]
        sums.append(value * edges[levels - 1 + k])
    for k in range(levels - 2, -1, -1):
        sums[k] = sums[k] + edges[k] * sums[k + 1]
    tracer[...] = inner[...]
    lane = lane_of((GROUPS, LANES))
    slab = row_of((GROUPS, LANES))
    for k in range(levels):
        west = sums[k][0:GROUPS]
        east = turn(sums[k][SLABS : SLABS + GROUPS], -17)
        south_l, south_r = sums[k][48:49], sums[k][49:50]
        north_l, north_r = turn(sums[k][50:51], 16), turn(sums[k][51:52], 16)
        for a in range(PLANES):
            rim = None
            for at, source in [(at, west) for at in FIRST_OF[a]] + [(at, east) for at in LAST_OF[a]]:
                rim = jnp.where(lane == at, source, 0.0 if rim is None else rim)
            if rim is None:
                continue
            if a == 0:
                rim = rim + jnp.where(slab == 0, south_l, 0.0)
            if a == 1:
                rim = rim + jnp.where(jnp.logical_and(slab == 0, lane < 112), south_r, 0.0)
            if a == PLANES - 2:
                rim = rim + jnp.where(jnp.logical_and(slab == GROUPS - 1, lane >= 16), north_l, 0.0)
            if a == PLANES - 1:
                rim = rim + jnp.where(slab == GROUPS - 1, jnp.where(lane < 16, north_l, north_r), 0.0)
            rows = comb(k * ROWS + a)
            tracer[rows, :] = tracer[rows, :] + rim


def tracer_kernel(
    levels, per, tiles_x, tiles_y, pos, temp, zonal, merid, rates, ocean,
    out, edges, around, te, tw, tn, ts, stepped, border, holder,
):
    step = pl.program_id(0)
    count = pos.shape[0]
    lane = lane_of((GROUPS, LANES))
    one = lane_of((1, LANES))
    ocean = ocean.reshape(ROWS, LANES)
    rates = rates.reshape((levels - 1) * ROWS, LANES)

    @pl.when(step == 0)
    def _():
        clear_terms(tn, ts)

        def number(d, carry):
            holder[pos[d]] = d
            return carry

        lax.fori_loop(0, count, number, 0)

        def look(d, carry):
            row = pos[d] // tiles_x
            column = pos[d] % tiles_x
            for c, (dx, dy) in enumerate(SIDES[:4]):
                there = row + dy
                inside = jnp.logical_and(there >= 0, there < tiles_y)
                target = jnp.where(inside, there, 0) * tiles_x + (column + dx + tiles_x) % tiles_x
                around[c * count + d] = jnp.where(inside, holder[target], -1)
            return carry

        lax.fori_loop(0, count, look, 0)

    for n in range(per):
        t, u, v = (ref.at[n].reshape(ROWS, LANES) for ref in (temp, zonal, merid))
        for a in range(PLANES):
            own = t[comb(a), :]
            quarter = ADVECT * own
            store_terms(a, own, u[comb(a), :] * quarter, v[comb(a), :] * quarter, te, tw, tn, ts)
        for a in range(PLANES):
            own = t[comb(a), :]
            change = inner_sum(a, te, tw, tn, ts) - 4.0 * DIFFUSE * own
            stepped[step * per + n, a] = own + ocean[comb(a), :].astype(jnp.float32) * change

    @pl.when(step == pl.num_programs(0) - 1)
    def _():
        def block(a, carry):
            for low in range(0, GROUPS, 8):
                size = min(8, GROUPS - low)

                def rows(k):
                    return pl.ds(k * ROWS + low * PLANES + a, size, stride=PLANES)

                gains = []
                sums = []
                for k in range(levels):
                    value = stepped[k, a, low : low + size]
                    pivot = 1.0
                    if k > 0:
                        pivot = pivot + upper - upper * gains[-1]
                        value = value + upper * sums[-1]
                    if k < levels - 1:
                        lower = rates[rows(k), :]
                        inverse = 1.0 / (pivot + lower)
                        gains.append(lower * inverse)
                        upper = lower
                    else:
                        inverse = 1.0 / pivot
                    sums.append(value * inverse)
                result = sums[-1]
                out[rows(levels - 1), :] = result
                for k in range(levels - 2, -1, -1):
                    result = sums[k] + gains[k] * result
                    out[rows(k), :] = result
            return carry

        lax.fori_loop(0, PLANES, block, 0)

        def edge(ref, base, at):
            def get(a):
                return ref[comb(base + a), :].astype(jnp.float32)

            border[0:GROUPS] = choose(START, lane, get)
            border[SLABS : SLABS + GROUPS] = turn(choose(LAST, lane, get), 17)
            border[48:50] = ref[base : base + 2, :].astype(jnp.float32)
            rows = ref[base + ROWS - 2 : base + ROWS, :].astype(jnp.float32)
            border[50:51] = turn(jnp.where(one >= 16, rows[0:1], rows[1:2]), -16)
            border[51:52] = turn(rows[1:2], -16)
            edges[at] = border[...]

        border[...] = jnp.zeros_like(border)
        edge(ocean, 0, 2 * levels - 1)
        gain = None
        for k in range(levels):
            pivot = 1.0
            if k > 0:
                upper = edges[2 * levels + k - 1]
                pivot = pivot + upper - upper * gain
            if k < levels - 1:
                edge(rates, k * ROWS, 2 * levels + k)
                lower = edges[2 * levels + k]
                inverse = 1.0 / (pivot + lower)
                gain = lower * inverse
                edges[k] = gain
            else:
                inverse = 1.0 / pivot
            edges[levels - 1 + k] = inverse


def on_device(
    thermal_anomaly,
    zonal_flow_ratio,
    meridional_flow_ratio,
    diffusion_rates,
    ocean_bottom_scaled,
    ocean_indicator,
    operator_diagonal,
    elevation_source,
    block_positions,
):
    levels, cells = thermal_anomaly.shape[1:]
    nx = lax.axis_size("gx")
    ny = lax.axis_size("gy")
    count = block_positions.shape[0]
    planes = (ocean_bottom_scaled, ocean_indicator, operator_diagonal, elevation_source)
    depth, ocean, diag, source = planes
    f32 = jnp.float32
    steps = next(n for n in (4, 3, 2, 1) if levels % n == 0)
    per = levels // steps
    params = pltpu.CompilerParams(vmem_limit_bytes=BUDGET)
    temp, zonal, merid, rates = (
        array.reshape(array.shape[1], 1, cells)
        for array in (thermal_anomaly, zonal_flow_ratio, meridional_flow_ratio, diffusion_rates)
    )
    some = pl.BlockSpec((per, 1, cells), lambda i: (i, 0, 0))
    flat = whole(1, cells)

    def vmem(*shape):
        return pltpu.VMEM(shape, f32)

    def out(*shape):
        return jax.ShapeDtypeStruct(shape, f32)

    plane = vmem(PLANES, GROUPS, LANES)
    tall = vmem(PLANES, 40, LANES)
    numbers = pltpu.SMEM((count,), jnp.int32)
    part, own, slots, table = pl.pallas_call(
        functools.partial(forcing_kernel, levels, per, nx, ny),
        grid=(steps,),
        in_specs=[SMEM, some, some, some, flat, flat, flat, flat],
        out_specs=[whole(ROWS, LANES), whole(56, LANES), whole(count, 1, SLOT * LANES), SMEM],
        out_shape=[
            out(ROWS, LANES), out(56, LANES), out(count, 1, SLOT * LANES),
            jax.ShapeDtypeStruct((8,), jnp.int32),
        ],
        scratch_shapes=[vmem(ROWS, LANES)] * 3 + [plane] * 3 + [tall] * 2
        + [vmem(4, 2 * levels, LANES), numbers],
        compiler_params=params,
        name="forcing",
    )(block_positions, temp, zonal, merid, depth, ocean, diag, source)
    rims = lax.all_to_all(slots, BOTH, 0, 0, tiled=True)

    inner, edges, around = pl.pallas_call(
        functools.partial(tracer_kernel, levels, per, nx, ny),
        grid=(steps,),
        in_specs=[SMEM, some, some, some, whole(levels - 1, 1, cells), flat],
        out_specs=[whole(levels * ROWS, LANES), whole(3 * levels - 1, EDGE, LANES), SMEM],
        out_shape=[
            out(levels * ROWS, LANES), out(3 * levels - 1, EDGE, LANES),
            jax.ShapeDtypeStruct((4 * count,), jnp.int32),
        ],
        scratch_shapes=[plane] * 2 + [tall] * 2
        + [vmem(levels, PLANES, GROUPS, LANES), vmem(EDGE, LANES), numbers],
        compiler_params=params,
        name="tracer",
    )(block_positions, temp, zonal, merid, rates, ocean)

    extended = vmem(GROUP, SLABS, 2 * LANES)
    vectors, hand, size = pl.pallas_call(
        functools.partial(solve_kernel, levels),
        grid=(1,),
        in_specs=[
            SMEM, SMEM, whole(count, 1, SLOT * LANES), whole(56, LANES), whole(ROWS, LANES), flat, flat, flat,
        ],
        out_specs=[whole(4, GROUP, SLABS, 2 * LANES), whole(count, 1, HAND * LANES), whole(8, LANES)],
        out_shape=[out(4, GROUP, SLABS, 2 * LANES), out(count, 1, HAND * LANES), out(8, LANES)],
        scratch_shapes=[vmem(WIDE, LANES)] * 3 + [vmem(SLABS, LANES)] * 4 + [extended] * 5 + [vmem(16, LANES)],
        compiler_params=params,
        name="vectors",
    )(table, around, rims, own, part, depth, ocean, diag)
    hands = lax.all_to_all(hand, BOTH, 0, 0, tiled=True)

    new_temp, surface = pl.pallas_call(
        functools.partial(finish_kernel, levels),
        grid=(1,),
        in_specs=[
            SMEM, whole(count, 1, HAND * LANES), whole(8, LANES), whole(4, GROUP, SLABS, 2 * LANES),
            whole(levels * ROWS, LANES), whole(3 * levels - 1, EDGE, LANES),
        ],
        out_specs=[whole(levels * ROWS, LANES), flat],
        out_shape=[out(levels * ROWS, LANES), out(1, cells)],
        scratch_shapes=[vmem(GROUP, SLABS, LANES)] * 2 + [vmem(4, 2 * levels, LANES)],
        compiler_params=params,
        name="finish",
    )(table, hands, size, vectors, inner, edges)
    return new_temp.reshape(1, levels, cells), surface


def solution(mesh):
    deep = P(BOTH, None, None)
    flat = P(BOTH, None)
    return jax.shard_map(
        on_device,
        mesh=mesh,
        in_specs=(deep, deep, deep, deep, flat, flat, flat, flat, P()),
        out_specs=(deep, flat),
        check_vma=False,
    )
```

```python
import functools

import jax
import jax.numpy as jnp
from jax import lax
from jax.experimental import pallas as pl
from jax.experimental.pallas import tpu as pltpu
from jax.sharding import PartitionSpec as P

ITERS = 4
SPAN_X = 240
SPAN_Y = 160
RIM = 4
ADVECT = 0.25
DIFFUSE = 0.12
STERIC = 0.5
LOW_RATE = 0.05
HIGH_RATE = 32.5
ROOTS = (0.02, 0.35, 0.1, 0.2)
STRETCH = 4.0
TINY = 1e-30
BOTH = ("gx", "gy")
SIDES = ((-1, 0), (1, 0), (0, -1), (0, 1), (-1, -1), (1, -1), (-1, 1), (1, 1))

LANES = 128
GROUP = 8
GROUPS = SPAN_Y // GROUP
PLANES = GROUP * SPAN_X // LANES
ROWS = GROUPS * PLANES
SLABS = GROUPS + 4
WIDE = SLABS * PLANES
START = [SPAN_X * j // LANES for j in range(GROUP)]
OFF = [SPAN_X * j % LANES for j in range(GROUP)]
LAST = [(SPAN_X * j + SPAN_X - 1) // LANES for j in range(GROUP)]
END = [(SPAN_X * j + SPAN_X - 1) % LANES for j in range(GROUP)]
FIRST_OF = [[OFF[j] for j in range(GROUP) if START[j] == a] for a in range(PLANES)]
LAST_OF = [[END[j] for j in range(GROUP) if LAST[j] == a] for a in range(PLANES)]
RIM_ROWS = 24
SLOT = RIM_ROWS + 4
HAND = 5
EDGE = 56
BUDGET = 56 * 1024 * 1024


def turn(value, shift, axis=1):
    shift = shift % value.shape[axis]
    return value if shift == 0 else pltpu.roll(value, shift, axis)


def fetching(pairs, sems):
    copies = [pltpu.make_async_copy(a, b, sems.at[n]) for n, (a, b) in enumerate(pairs)]
    for copy in copies:
        copy.start()
    return copies


def lane_of(shape):
    return lax.broadcasted_iota(jnp.int32, shape, len(shape) - 1)


def row_of(shape):
    return lax.broadcasted_iota(jnp.int32, shape, 0)


def comb(a, count=GROUPS):
    return pl.ds(a, count, stride=PLANES)


def drop(value, lanes, lane):
    for at in lanes:
        value = jnp.where(lane == at, 0.0, value)
    return value


def store_terms(a, temp, flow_x, flow_y, te, tw, tn, ts):
    spread = DIFFUSE * temp
    te[a] = spread - flow_x
    tw[a] = spread + flow_x
    tn[a, 8 : 8 + GROUPS] = spread - flow_y
    ts[a, 8 : 8 + GROUPS] = spread + flow_y


def clear_terms(tn, ts):
    none = jnp.zeros((PLANES, 1, LANES), jnp.float32)
    for ref in (tn, ts):
        ref[:, 7:8] = none
        ref[:, 8 + GROUPS : 9 + GROUPS] = none


def inner_sum(a, te, tw, tn, ts):
    lane = lane_of((GROUPS, LANES))
    here = te[a]
    east = here if a == PLANES - 1 else jnp.where(lane == 0, te[a + 1], here)
    east = drop(turn(east, -1), LAST_OF[a], lane)
    here = tw[a]
    west = here if a == 0 else jnp.where(lane == LANES - 1, tw[a - 1], here)
    west = drop(turn(west, 1), FIRST_OF[a], lane)

    def plane(ref, at):
        down = 8 + (at >= PLANES) - (at < 0)
        return ref[at % PLANES, down : down + GROUPS]

    north = turn(jnp.where(lane >= LANES - 16, plane(tn, a + 1), plane(tn, a + 2)), 16)
    south = turn(jnp.where(lane < 16, plane(ts, a - 1), plane(ts, a - 2)), -16)
    return east + west + north + south


def choose(planes, lane, get):
    value = get(planes[0])
    for j in range(1, GROUP):
        low = (OFF[j] - (32 if planes is LAST else 0)) % LANES
        value = jnp.where(jnp.logical_and(lane >= low, lane < low + 16), get(planes[j]), value)
    return value


def forcing_kernel(
    levels, per, tiles_x, tiles_y,
    pos, temp_in, zonal_in, merid_in, depth_in, ocean_in, diag_in, source_in,
    part_out, own_out, slots_out, table,
    temp, zonal, merid, depth, ocean, diag, source, part, own, out,
    st, sx, sy, pt, te, tw, tn, ts, edges, holder, sems, out_sems,
):
    count = pos.shape[0]
    steps = levels // per
    pairs = []
    for step in range(steps):
        chunk = pl.ds(step * per, per)
        pairs += [
            (a.at[chunk], b.at[chunk]) for a, b in ((temp_in, temp), (zonal_in, zonal), (merid_in, merid))
        ]
    pairs += [(source_in, source), (ocean_in, ocean), (depth_in, depth), (diag_in, diag)]
    copies = fetching(pairs, sems)
    results = []

    def send(value, target):
        copy = pltpu.make_async_copy(value, target, out_sems.at[len(results)])
        copy.start()
        results.append(copy)

    depth, ocean, diag, source = (ref.reshape(ROWS, LANES) for ref in (depth, ocean, diag, source))
    slots = out.reshape(count * SLOT, LANES)
    lane = lane_of((GROUPS, LANES))
    one = lane_of((1, LANES))
    q = lane % 16
    edges[...] = jnp.zeros_like(edges)

    def number(d, carry):
        holder[pos[d]] = d
        return carry

    lax.fori_loop(0, count, number, 0)
    me = lax.axis_index("gx") * tiles_y + lax.axis_index("gy")
    here = pos[me]
    row = here // tiles_x
    column = here % tiles_x
    sides = []
    for c, (dx, dy) in enumerate(SIDES):
        there = row + dy
        inside = jnp.logical_and(there >= 0, there < tiles_y)
        target = jnp.where(inside, there, 0) * tiles_x + (column + dx + tiles_x) % tiles_x
        device = jnp.where(inside, holder[target], -1)
        table[c] = device
        sides.append(device)
    clear_terms(tn, ts)

    def add(flats, low, size, fresh):
        rows = pl.ds(low, size)
        total = [None] * 3
        for t, u, v in zip(*flats):
            t = t[rows, :]
            new = (t, t * u[rows, :], t * v[rows, :])
            total = [b if a is None else a + b for a, b in zip(total, new)]
        for ref, value in zip((st, sx, sy), total):
            ref[rows, :] = value if fresh else ref[rows, :] + value

    for step in range(steps):
        for copy in copies[3 * step : 3 * step + 3]:
            copy.wait()
        flats = [
            [ref.at[step * per + n].reshape(ROWS, LANES) for n in range(per)] for ref in (temp, zonal, merid)
        ]

        def some(m, carry):
            add(flats, pl.multiple_of(m * 8, 8), 8, step == 0)
            return carry

        lax.fori_loop(0, ROWS // 8, some, 0, unroll=4)
        if ROWS % 8:
            add(flats, ROWS - ROWS % 8, ROWS % 8, step == 0)

        for n in range(per):
            k = step * per + n
            t, u, v = (flat[n] for flat in flats)

            def term(planes, sign):
                own = choose(planes, lane, lambda a: t[comb(a), :])
                flow = choose(planes, lane, lambda a: u[comb(a), :])
                return DIFFUSE * own + sign * ADVECT * (flow * own)

            edges[0, 0:GROUPS] = jnp.where(q == k, turn(term(START, -1.0), k), edges[0, 0:GROUPS])
            edges[1, 0:GROUPS] = jnp.where(q == k, turn(term(LAST, 1.0), k + 17), edges[1, 0:GROUPS])
            rows = t[0:2, :]
            rows = DIFFUSE * rows - ADVECT * (v[0:2, :] * rows)
            edges[2, k : k + 1] = rows[0:1]
            edges[2, k + levels : k + levels + 1] = rows[1:2]
            rows = t[ROWS - 2 : ROWS, :]
            rows = DIFFUSE * rows + ADVECT * (v[ROWS - 2 : ROWS, :] * rows)
            edges[3, k : k + 1] = turn(jnp.where(one >= 16, rows[0:1], rows[1:2]), -16)
            edges[3, k + levels : k + levels + 1] = turn(rows[1:2], -16)

    for c in range(4):
        slots[pl.ds(RIM_ROWS + c, 2 * levels, stride=SLOT), :] = edges[c]

    for copy in copies[3 * steps :]:
        copy.wait()

    def wet_of(rows):
        return ocean[rows, :].astype(jnp.float32)

    def masked(rows):
        return depth[rows, :] * wet_of(rows)

    for a in range(PLANES):
        total = st[comb(a), :]
        pt[a] = total
        store_terms(a, total, ADVECT * sx[comb(a), :], ADVECT * sy[comb(a), :], te, tw, tn, ts)
    for a in range(PLANES):
        total = pt[a]
        wet = wet_of(comb(a))
        change = inner_sum(a, te, tw, tn, ts) - 4.0 * DIFFUSE * total
        part[comb(a), :] = source[comb(a), :] + (STERIC / levels) * wet * (total + wet * change)
    send(part, part_out)

    def mix(values):
        value = values[4]
        for at, low in ((3, 12), (2, 11), (1, 8), (0, 4)):
            value = jnp.where(q < low, values[at], value)
        return value

    def flat(ref):
        return lambda a: ref[comb(a), :]

    def ends(planes, low):
        value = tn[planes[0], 8 : 8 + GROUPS]
        last = jnp.logical_and(lane >= low, lane < low + 16)
        return jnp.where(last, ts[planes[7], 8 : 8 + GROUPS], value)

    pack_w = mix([
        choose(START, lane, flat(part)),
        turn(choose(START, lane, lambda a: masked(comb(a))), 4),
        turn(choose(START, lane, flat(diag)), 8),
        turn(choose(START, lane, lambda a: te[a]), 11),
        turn(ends(START, OFF[7]), 12),
    ])
    pack_e = mix([
        turn(choose(LAST, lane, flat(part)), 20),
        turn(choose(LAST, lane, lambda a: masked(comb(a))), 24),
        turn(choose(LAST, lane, flat(diag)), 27),
        turn(choose(LAST, lane, lambda a: tw[a]), 28),
        turn(ends(LAST, LANES - 16), 32),
    ])
    own[0:GROUPS] = pack_w
    own[SLABS : SLABS + GROUPS] = pack_e
    north_l = tn[0, 8:9]
    north_r = tn[1, 8:9]
    south_13 = ts[PLANES - 2, 7 + GROUPS : 8 + GROUPS]
    south_14 = ts[PLANES - 1, 7 + GROUPS : 8 + GROUPS]
    south_l = turn(jnp.where(one >= 16, south_13, south_14), -16)
    south_r = turn(south_14, -16)
    own[48:49] = north_l
    own[49:50] = north_r
    own[50:51] = south_l
    own[51:52] = south_r
    send(own, own_out)
    deep = jnp.max(masked(slice(0, ROWS)), axis=(0, 1), keepdims=True)
    top = jnp.max(diag[...], axis=(0, 1), keepdims=True) + 8.0 * deep * deep
    top = jnp.broadcast_to(top, (1, LANES))

    slots[pl.ds(RIM_ROWS - 1, count, stride=SLOT), :] = jnp.broadcast_to(top, (count, LANES))
    eight = lane_of((8, LANES))
    eighth = row_of((8, LANES))
    for c, first, rows_l, rows_r in ((2, True, north_l, north_r), (3, False, south_l, south_r)):
        base = 0 if first else ROWS - 8
        spare = jnp.logical_and(eighth == 7, eight >= 64) if first else jnp.logical_and(eighth == 0, eight < 64)
        g = 0 if first else GROUPS - 1
        blocks = []
        block = slice(base, base + 8)
        for value, at in ((part[block, :], g), (masked(block), SLABS + g)):
            extra = jnp.broadcast_to(turn(own[at : at + 1], -16), (8, LANES))
            blocks.append(jnp.where(spare, extra, value))
        low = 0 if first else ROWS - 6
        diag_rows = diag[low : low + 6, :]
        last_row = jnp.where(one == LANES - 1, top, rows_r)

        @pl.when(sides[c] >= 0)
        def _(c=c, blocks=blocks, diag_rows=diag_rows, rows_l=rows_l, last_row=last_row):
            at = sides[c] * SLOT
            slots[pl.ds(at, 8), :] = blocks[0]
            slots[pl.ds(at + 8, 8), :] = blocks[1]
            slots[pl.ds(at + 16, 6), :] = diag_rows
            slots[pl.ds(at + 22, 1), :] = rows_l
            slots[pl.ds(at + 23, 1), :] = last_row

    slots[pl.ds(sides[0] * SLOT, GROUPS), :] = pack_w
    slots[pl.ds(sides[1] * SLOT, GROUPS), :] = pack_e
    for c, at in ((4, 0), (5, SLABS), (6, GROUPS - 1), (7, SLABS + GROUPS - 1)):
        @pl.when(sides[c] >= 0)
        def _(c=c, at=at):
            slots[pl.ds(sides[c] * SLOT, 1), :] = own[at : at + 1]
    send(out, slots_out)
    for copy in results:
        copy.wait()


SMEM = pl.BlockSpec(memory_space=pltpu.SMEM)


def solve_kernel(
    levels,
    table, around, rims, own_in, part_in, depth_in, ocean_in, diag_in,
    vectors_out, hand_out,
    own, part, depth, ocean, diag, vectors, out, sems, out_sems,
    fb, fd, fg, pw, pe, ow, oe, ed, eg, we, wn, last, rows,
):
    copies = fetching(
        [(own_in, own), (part_in, part), (depth_in, depth), (ocean_in, ocean), (diag_in, diag)], sems
    )
    depth, ocean, diag = (ref.reshape(ROWS, LANES) for ref in (depth, ocean, diag))
    count = rims.shape[0]
    came = rims.reshape(count * SLOT, LANES)
    hand = out.reshape(count * HAND, LANES)
    lane = lane_of((SLABS, LANES))
    slab = row_of((SLABS, LANES))
    one = lane_of((1, LANES))
    src = [table[c] for c in range(8)]

    def fetch(c, low, high):
        value = came[pl.ds(jnp.maximum(src[c], 0) * SLOT + low, high - low), :]
        return jnp.where(src[c] >= 0, value, 0.0)

    def relay(d, carry):
        for c in range(4):
            row = jnp.maximum(around[c * count + d], 0) * SLOT + RIM_ROWS + (c ^ 1)
            hand[pl.ds(d * HAND + 1 + c, 1), :] = came[pl.ds(row, 1), :]
        return carry

    lax.fori_loop(0, count, relay, 0)

    for copy in copies:
        copy.wait()
    none = jnp.zeros((WIDE - ROWS + 4, LANES), jnp.float32)
    for ref in (fb, fd, fg):
        ref[ROWS - 4 : WIDE] = none
    fb[0:ROWS] = part[...]
    fd[0:ROWS] = depth[...] * ocean[...].astype(jnp.float32)
    fg[0:ROWS] = diag[...]
    for ref, low, high in ((fb, 0, 8), (fd, 8, 16), (fg, 16, 22)):
        ref[ROWS : ROWS + high - low] = fetch(3, low, high)
        ref[WIDE - high + low : WIDE] = fetch(2, low, high)
    empty = jnp.zeros((SLABS, LANES), jnp.float32)
    for ref, side, north, south in ((pw, 0, 6, 4), (pe, 1, 7, 5)):
        ref[...] = empty
        ref[0:GROUPS] = fetch(side, 0, GROUPS)
        ref[GROUPS : GROUPS + 1] = fetch(north, 0, 1)
        ref[SLABS - 1 : SLABS] = fetch(south, 0, 1)
    for ref, at, north, south in ((ow, 0, 7, 0), (oe, SLABS, 15, 8)):
        ref[...] = empty
        ref[0:GROUPS] = own[at : at + GROUPS]
        ref[GROUPS : GROUPS + 1] = turn(fetch(3, north, north + 1), 16)
        ref[SLABS - 1 : SLABS] = turn(fetch(2, south, south + 1), 16)

    def spread(ref, j):
        a = START[j]
        first, second = ref[comb(a, SLABS), :], ref[comb(a + 1, SLABS), :]
        third = ref[comb(a + 2, SLABS), :] if a + 2 < PLANES else second
        left = turn(jnp.where(lane >= OFF[j], first, second), -OFF[j])
        right = turn(jnp.where(lane >= OFF[j], second, third), -OFF[j])
        return left, right

    def seam_row(left, right, slab_at, lanes_at):
        east = turn(pe[slab_at : slab_at + 1], 112 - lanes_at)
        west = turn(pw[slab_at : slab_at + 1], 124 - lanes_at)
        right = jnp.where(one < 112, right, jnp.where(one < 116, east, jnp.where(one >= 124, west, 0.0)))
        return jnp.broadcast_to(left, (SLABS, LANES)), jnp.broadcast_to(right, (SLABS, LANES))

    seams = {
        0: ((0, seam_row(fetch(2, 22, 23), fetch(2, 23, 24), SLABS - 1, 28)),
            (GROUPS, seam_row(own[50:51], own[51:52], GROUPS - 1, 28))),
        GROUP - 1: ((GROUPS - 1, seam_row(fetch(3, 22, 23), fetch(3, 23, 24), GROUPS, 12)),
                    (SLABS - 1, seam_row(own[48:49], own[49:50], 0, 12))),
    }
    weight = STERIC / levels
    for j in range(GROUP):
        o = OFF[j]

        def rim(right, q, width):
            east = turn(pe[...], 112 - o - q)
            west = turn(pw[...], 128 - width - o - q)
            value = jnp.where(lane < 112 + width, east, jnp.where(lane >= 128 - width, west, 0.0))
            return jnp.where(lane < 112, right, value)

        left, right = spread(fd, j)
        right = rim(right, 4, 4)
        wet_l = jnp.where(left > 0, weight, 0.0)
        wet_r = jnp.where(right > 0, weight, 0.0)
        ed[j, :, 0:LANES] = left
        ed[j, :, LANES:] = right
        left, right = spread(fg, j)
        eg[j, :, 0:LANES] = left
        eg[j, :, LANES:] = rim(right, 8, 3)
        left, right = spread(fb, j)
        right = rim(right, 0, 4)
        seam_l = jnp.where(lane == 0, turn(pw[...], -o - 11), 0.0)
        seam_r = jnp.where(lane == 127, turn(ow[...], 127 - o - 11), 0.0)
        seam_r = jnp.where(lane == 111, turn(pe[...], 111 - o - 11), seam_r)
        seam_r = jnp.where(lane == 112, turn(oe[...], 112 - o - 11), seam_r)
        for at, (row_l, row_r) in seams.get(j, ()):
            seam_l = seam_l + jnp.where(slab == at, row_l, 0.0)
            seam_r = seam_r + jnp.where(slab == at, row_r, 0.0)
        vectors[0, j, :, 0:LANES] = left + wet_l * seam_l
        vectors[0, j, :, LANES:] = right + wet_r * seam_r

    for j in range(GROUP):
        d = ed[j]
        we[j] = d * turn(d, -1)
        above = ed[j + 1] if j < GROUP - 1 else turn(ed[0], -1, 0)
        wn[j] = d * above

    top = jnp.max(came[pl.ds(RIM_ROWS - 1, count, stride=SLOT), :], axis=0, keepdims=True)
    top = jnp.max(jnp.where(one == LANES - 1, top, 0.0), axis=1, keepdims=True)
    scale = STRETCH / top

    big = (SLABS, 2 * LANES)
    mine = jnp.logical_and(row_of(big) < GROUPS, lane_of(big) < SPAN_X)
    pair = 0
    results = []
    for k in range(5):
        sums = [None] * (k + 1)
        new = last if k == 4 else vectors.at[k]
        if k:
            v = vectors.at[k - 1]
            flow_below = wn[GROUP - 1] * (v[GROUP - 1] - turn(v[0], -1, 0))
            flow_below = turn(flow_below, 1, 0)
        for j in range(GROUP):
            if k:
                here = v[j]
                above = v[j + 1] if j < GROUP - 1 else turn(v[0], -1, 0)
                flow_x = we[j] * (here - turn(here, -1))
                flow_y = wn[j] * (here - above)
                image = eg[j] * here + (flow_x - turn(flow_x, 1)) + (flow_y - flow_below)
                fresh = scale * image - (STRETCH * ROOTS[k - 1]) * here
                flow_below = flow_y
                new[j] = fresh
            else:
                fresh = new[j]
            held = jnp.where(mine, fresh, 0.0)
            for i in range(k + 1):
                other = vectors[i, j] if i < k else held
                value = held * other
                sums[i] = value if sums[i] is None else sums[i] + value
        if k < 4:
            results.append(pltpu.make_async_copy(vectors.at[k], vectors_out.at[k], out_sems.at[k]))
            results[-1].start()
        for i in range(k + 1):
            rows[pair : pair + 1] = jnp.sum(sums[i][:, 0:LANES] + sums[i][:, LANES:], axis=0, keepdims=True)
            pair += 1
    rows[pair : pair + 1] = jnp.where(one == 0, top, 0.0)
    total = jnp.sum(rows[...], axis=1, keepdims=True)
    spot = row_of((16, LANES)) == lane_of((16, LANES))
    line = jnp.sum(jnp.where(spot, total, 0.0), axis=0, keepdims=True)
    hand[pl.ds(0, count, stride=HAND), :] = jnp.broadcast_to(line, (count, LANES))
    results.append(pltpu.make_async_copy(out, hand_out, out_sems.at[4]))
    results[-1].start()
    for copy in results:
        copy.wait()


def finish_kernel(
    levels, per, table, hands, vectors_in, inner_in, edges_in, tracer_out, surface_out,
    vectors, tracer, edges, surface, left, right, message, sems, out_sems,
):
    count = hands.shape[0]
    steps = levels // per
    chunks = [pl.ds(step * per, per) for step in range(steps)]
    copies = fetching(
        [(vectors_in, vectors), (edges_in, edges)] + [(inner_in.at[c], tracer.at[c]) for c in chunks], sems
    )
    cells = tracer.reshape(levels * ROWS, LANES)
    came = hands.reshape(count * HAND, LANES)
    row = jnp.sum(came[pl.ds(0, count, stride=HAND), :], axis=0, keepdims=True)
    one = lane_of((1, LANES))
    entry = {}
    pair = 0
    for k in range(5):
        for i in range(k + 1):
            value = jnp.sum(jnp.where(one == pair, row, 0.0), axis=1, keepdims=True)
            entry[i, k] = entry[k, i] = value
            pair += 1
    top = jnp.sum(jnp.where(one == pair, row, 0.0), axis=1, keepdims=True) * (1.0 / count)

    def image(c):
        out = [None] * 5
        for k in range(4):
            if c[k] is None:
                continue
            low = ROOTS[k] * c[k]
            out[k] = low if out[k] is None else out[k] + low
            out[k + 1] = (1.0 / STRETCH) * c[k]
        return out

    def dot(a, b):
        total = None
        for i in range(5):
            if a[i] is None:
                continue
            inner = None
            for j in range(5):
                if b[j] is not None:
                    value = entry[i, j] * b[j]
                    inner = value if inner is None else inner + value
            total = a[i] * inner if total is None else total + a[i] * inner
        return total

    def axpy(a, s, b):
        return [
            x if y is None else (s * y if x is None else x + s * y) for x, y in zip(a, b)
        ]

    r = [jnp.ones((1, 1), jnp.float32)] + [None] * 4
    p = list(r)
    x = [None] * 5
    rr = entry[0, 0]
    for n in range(ITERS):
        q = image(p)
        step = rr / jnp.maximum(dot(p, q), TINY)
        step = jnp.clip(step, top * (1.0 / HIGH_RATE), top * (1.0 / LOW_RATE))
        x = axpy(x, step, p)
        if n < ITERS - 1:
            r = axpy(r, -step, q)
            fresh = jnp.maximum(dot(r, r), 0.0)
            p = axpy(r, fresh / jnp.maximum(rr, TINY), p)
            rr = fresh
    flat = surface.reshape(ROWS, LANES)
    factors = [c / top for c in x[:4]]
    copies[0].wait()
    for j in range(GROUP):
        value = None
        for k in range(4):
            term = factors[k] * vectors[k, j]
            value = term if value is None else value + term
        left[j] = turn(value[:, 0:LANES], OFF[j])
        right[j] = turn(value[:, LANES:], OFF[j])
    lane = lane_of((SLABS, LANES))
    for a in range(PLANES):
        value = None
        for j in range(GROUP):
            for half, ref in ((0, left), (1, right)):
                low = max(SPAN_X * j + LANES * half - LANES * a, 0)
                high = min(SPAN_X * j + (LANES if half == 0 else SPAN_X) - LANES * a, LANES)
                if low >= high:
                    continue
                value = ref[j] if value is None else jnp.where(lane >= low, ref[j], value)
        flat[comb(a), :] = value[0:GROUPS]
    results = [pltpu.make_async_copy(surface, surface_out, out_sems.at[0])]
    results[0].start()
    copies[1].wait()

    for c in range(4):
        value = came[pl.ds(1 + c, 2 * levels, stride=HAND), :]
        message[c] = jnp.where(table[c] >= 0, value, 0.0)
    sums = []
    for k in range(levels):
        value = edges[2 * levels - 1] * jnp.concatenate([
            turn(message[0], -k), turn(message[1], -k),
            message[2, k : k + 1], message[2, k + levels : k + levels + 1],
            message[3, k : k + 1], message[3, k + levels : k + levels + 1],
            jnp.zeros((4, LANES), jnp.float32),
        ], axis=0)
        if k:
            value = value + edges[2 * levels + k - 1] * sums[-1]
        sums.append(value * edges[levels - 1 + k])
    for k in range(levels - 2, -1, -1):
        sums[k] = sums[k] + edges[k] * sums[k + 1]
    lane = lane_of((GROUPS, LANES))
    slab = row_of((GROUPS, LANES))
    for k in range(levels):
        if k % per == 0:
            copies[2 + k // per].wait()
        west = sums[k][0:GROUPS]
        east = turn(sums[k][SLABS : SLABS + GROUPS], -17)
        south_l, south_r = sums[k][48:49], sums[k][49:50]
        north_l, north_r = turn(sums[k][50:51], 16), turn(sums[k][51:52], 16)
        for a in range(PLANES):
            rim = None
            for at, source in [(at, west) for at in FIRST_OF[a]] + [(at, east) for at in LAST_OF[a]]:
                rim = jnp.where(lane == at, source, 0.0 if rim is None else rim)
            if rim is None:
                continue
            if a == 0:
                rim = rim + jnp.where(slab == 0, south_l, 0.0)
            if a == 1:
                rim = rim + jnp.where(jnp.logical_and(slab == 0, lane < 112), south_r, 0.0)
            if a == PLANES - 2:
                rim = rim + jnp.where(jnp.logical_and(slab == GROUPS - 1, lane >= 16), north_l, 0.0)
            if a == PLANES - 1:
                rim = rim + jnp.where(slab == GROUPS - 1, jnp.where(lane < 16, north_l, north_r), 0.0)
            rows = comb(k * ROWS + a)
            cells[rows, :] = cells[rows, :] + rim
        if k % per == per - 1:
            step = k // per
            copy = pltpu.make_async_copy(
                tracer.at[chunks[step]], tracer_out.at[chunks[step]], out_sems.at[1 + step]
            )
            copy.start()
            results.append(copy)
    for copy in results:
        copy.wait()


def tracer_kernel(
    levels, per, tiles_x, tiles_y, pos, temp_in, zonal_in, merid_in, rates_in, ocean_in,
    inner_out, edges_out, around,
    temp, zonal, merid, rates, ocean, inner, edges,
    te, tw, tn, ts, stepped, border, holder, sems, out_sems,
):
    count = pos.shape[0]
    steps = levels // per
    pairs = [(ocean_in, ocean)]
    for step in range(steps):
        chunk = pl.ds(step * per, per)
        pairs += [
            (a.at[chunk], b.at[chunk]) for a, b in ((temp_in, temp), (zonal_in, zonal), (merid_in, merid))
        ]
    copies = fetching(pairs + [(rates_in, rates)], sems)
    out = inner.reshape(levels * ROWS, LANES)
    lane = lane_of((GROUPS, LANES))
    one = lane_of((1, LANES))
    ocean = ocean.reshape(ROWS, LANES)
    rates = rates.reshape((levels - 1) * ROWS, LANES)

    clear_terms(tn, ts)

    def number(d, carry):
        holder[pos[d]] = d
        return carry

    lax.fori_loop(0, count, number, 0)

    def look(d, carry):
        row = pos[d] // tiles_x
        column = pos[d] % tiles_x
        for c, (dx, dy) in enumerate(SIDES[:4]):
            there = row + dy
            inside = jnp.logical_and(there >= 0, there < tiles_y)
            target = jnp.where(inside, there, 0) * tiles_x + (column + dx + tiles_x) % tiles_x
            around[c * count + d] = jnp.where(inside, holder[target], -1)
        return carry

    lax.fori_loop(0, count, look, 0)
    copies[0].wait()
    for step in range(steps):
        for copy in copies[1 + 3 * step : 4 + 3 * step]:
            copy.wait()

        def level(k, carry):
            t, u, v = (ref.at[k].reshape(ROWS, LANES) for ref in (temp, zonal, merid))
            for a in range(PLANES):
                own = t[comb(a), :]
                quarter = ADVECT * own
                store_terms(a, own, u[comb(a), :] * quarter, v[comb(a), :] * quarter, te, tw, tn, ts)
            for a in range(PLANES):
                own = t[comb(a), :]
                change = inner_sum(a, te, tw, tn, ts) - 4.0 * DIFFUSE * own
                stepped[k, a] = own + ocean[comb(a), :].astype(jnp.float32) * change
            return carry

        lax.fori_loop(step * per, step * per + per, level, 0)
    copies[-1].wait()

    def block(a, carry):
        for low in range(0, GROUPS, 8):
            size = min(8, GROUPS - low)

            def rows(k):
                return pl.ds(k * ROWS + low * PLANES + a, size, stride=PLANES)

            gains = []
            sums = []
            for k in range(levels):
                value = stepped[k, a, low : low + size]
                pivot = 1.0
                if k > 0:
                    pivot = pivot + upper - upper * gains[-1]
                    value = value + upper * sums[-1]
                if k < levels - 1:
                    lower = rates[rows(k), :]
                    inverse = 1.0 / (pivot + lower)
                    gains.append(lower * inverse)
                    upper = lower
                else:
                    inverse = 1.0 / pivot
                sums.append(value * inverse)
            result = sums[-1]
            out[rows(levels - 1), :] = result
            for k in range(levels - 2, -1, -1):
                result = sums[k] + gains[k] * result
                out[rows(k), :] = result
        return carry

    lax.fori_loop(0, PLANES, block, 0)

    def edge(ref, base, at):
        def get(a):
            return ref[comb(base + a), :].astype(jnp.float32)

        border[0:GROUPS] = choose(START, lane, get)
        border[SLABS : SLABS + GROUPS] = turn(choose(LAST, lane, get), 17)
        border[48:50] = ref[base : base + 2, :].astype(jnp.float32)
        rows = ref[base + ROWS - 2 : base + ROWS, :].astype(jnp.float32)
        border[50:51] = turn(jnp.where(one >= 16, rows[0:1], rows[1:2]), -16)
        border[51:52] = turn(rows[1:2], -16)
        edges[at] = border[...]

    border[...] = jnp.zeros_like(border)
    edge(ocean, 0, 2 * levels - 1)
    gain = None
    for k in range(levels):
        pivot = 1.0
        if k > 0:
            upper = edges[2 * levels + k - 1]
            pivot = pivot + upper - upper * gain
        if k < levels - 1:
            edge(rates, k * ROWS, 2 * levels + k)
            lower = edges[2 * levels + k]
            inverse = 1.0 / (pivot + lower)
            gain = lower * inverse
            edges[k] = gain
        else:
            inverse = 1.0 / pivot
        edges[levels - 1 + k] = inverse
        if k == 0:
            results = fetching([(inner, inner_out)], out_sems)
    results.append(pltpu.make_async_copy(edges, edges_out, out_sems.at[1]))
    results[-1].start()
    for copy in results:
        copy.wait()


def on_device(
    thermal_anomaly,
    zonal_flow_ratio,
    meridional_flow_ratio,
    diffusion_rates,
    ocean_bottom_scaled,
    ocean_indicator,
    operator_diagonal,
    elevation_source,
    block_positions,
):
    levels, cells = thermal_anomaly.shape[1:]
    nx = lax.axis_size("gx")
    ny = lax.axis_size("gy")
    count = block_positions.shape[0]
    planes = (ocean_bottom_scaled, ocean_indicator, operator_diagonal, elevation_source)
    depth, ocean, diag, source = planes
    f32 = jnp.float32
    steps = next(n for n in (4, 3, 2, 1) if levels % n == 0)
    per = levels // steps
    params = pltpu.CompilerParams(vmem_limit_bytes=BUDGET)
    temp, zonal, merid, rates = (
        array.reshape(array.shape[1], 1, cells)
        for array in (thermal_anomaly, zonal_flow_ratio, meridional_flow_ratio, diffusion_rates)
    )
    anywhere = pl.BlockSpec(memory_space=pl.ANY)
    here = pl.BlockSpec(memory_space=pltpu.VMEM)

    def vmem(*shape, kind=f32):
        return pltpu.VMEM(shape, kind)

    def out(*shape, kind=f32):
        return jax.ShapeDtypeStruct(shape, kind)

    def sems(number):
        return pltpu.SemaphoreType.DMA((number,))

    deep = vmem(levels, 1, cells)
    flat = vmem(1, cells)
    flat_int = vmem(1, cells, kind=jnp.int32)
    plane = vmem(PLANES, GROUPS, LANES)
    tall = vmem(PLANES, 40, LANES)
    numbers = pltpu.SMEM((count,), jnp.int32)
    part, own, slots, table = pl.pallas_call(
        functools.partial(forcing_kernel, levels, per, nx, ny),
        in_specs=[SMEM] + [anywhere] * 7,
        out_specs=[anywhere] * 3 + [SMEM],
        out_shape=[
            out(ROWS, LANES), out(56, LANES), out(count, 1, SLOT * LANES), out(8, kind=jnp.int32),
        ],
        scratch_shapes=[deep] * 3 + [flat, flat_int, flat, flat]
        + [vmem(ROWS, LANES), vmem(56, LANES), vmem(count, 1, SLOT * LANES)]
        + [vmem(ROWS, LANES)] * 3 + [plane] * 3 + [tall] * 2
        + [vmem(4, 2 * levels, LANES), numbers, sems(3 * steps + 4), sems(3)],
        compiler_params=params,
        name="forcing",
    )(block_positions, temp, zonal, merid, depth, ocean, diag, source)
    rims = lax.all_to_all(slots, BOTH, 0, 0, tiled=True)

    inner, edges, around = pl.pallas_call(
        functools.partial(tracer_kernel, levels, per, nx, ny),
        in_specs=[SMEM] + [anywhere] * 5,
        out_specs=[anywhere] * 2 + [SMEM],
        out_shape=[
            out(levels, 1, cells), out(3 * levels - 1, EDGE, LANES), out(4 * count, kind=jnp.int32),
        ],
        scratch_shapes=[deep] * 3 + [vmem(levels - 1, 1, cells), flat_int, deep]
        + [vmem(3 * levels - 1, EDGE, LANES)]
        + [plane] * 2 + [tall] * 2
        + [vmem(levels, PLANES, GROUPS, LANES), vmem(EDGE, LANES), numbers, sems(3 * steps + 2), sems(2)],
        compiler_params=params,
        name="tracer",
    )(block_positions, temp, zonal, merid, rates, ocean)

    extended = vmem(GROUP, SLABS, 2 * LANES)
    vectors, hand = pl.pallas_call(
        functools.partial(solve_kernel, levels),
        in_specs=[SMEM, SMEM, here] + [anywhere] * 5,
        out_specs=[anywhere] * 2,
        out_shape=[out(4, GROUP, SLABS, 2 * LANES), out(count, 1, HAND * LANES)],
        scratch_shapes=[vmem(56, LANES), vmem(ROWS, LANES), flat, flat_int, flat]
        + [vmem(4, GROUP, SLABS, 2 * LANES), vmem(count, 1, HAND * LANES), sems(5), sems(5)]
        + [vmem(WIDE, LANES)] * 3 + [vmem(SLABS, LANES)] * 4 + [extended] * 5 + [vmem(16, LANES)],
        compiler_params=params,
        name="vectors",
    )(table, around, rims, own, part, depth, ocean, diag)
    hands = lax.all_to_all(hand, BOTH, 0, 0, tiled=True)

    new_temp, surface = pl.pallas_call(
        functools.partial(finish_kernel, levels, per),
        in_specs=[SMEM, here] + [anywhere] * 3,
        out_specs=[anywhere] * 2,
        out_shape=[out(levels, 1, cells), out(1, cells)],
        scratch_shapes=[
            vmem(4, GROUP, SLABS, 2 * LANES), deep, vmem(3 * levels - 1, EDGE, LANES), flat,
            vmem(GROUP, SLABS, LANES), vmem(GROUP, SLABS, LANES), vmem(4, 2 * levels, LANES),
            sems(2 + steps), sems(1 + steps),
        ],
        compiler_params=params,
        name="finish",
    )(table, hands, vectors, inner, edges)
    return new_temp.reshape(1, levels, cells), surface


def solution(mesh):
    deep = P(BOTH, None, None)
    flat = P(BOTH, None)
    return jax.shard_map(
        on_device,
        mesh=mesh,
        in_specs=(deep, deep, deep, deep, flat, flat, flat, flat, P()),
        out_specs=(deep, flat),
        check_vma=False,
    )
```

```python
import functools

import jax
import jax.numpy as jnp
from jax import lax
from jax.experimental import pallas as pl
from jax.experimental.pallas import tpu as pltpu
from jax.sharding import PartitionSpec as P

ITERS = 4
SPAN_X = 240
SPAN_Y = 160
RIM = 4
ADVECT = 0.25
DIFFUSE = 0.12
STERIC = 0.5
LOW_RATE = 0.05
HIGH_RATE = 32.5
ROOTS = (0.02, 0.35, 0.1, 0.2)
STRETCH = 4.0
TINY = 1e-30
BOTH = ("gx", "gy")
SIDES = ((-1, 0), (1, 0), (0, -1), (0, 1), (-1, -1), (1, -1), (-1, 1), (1, 1))

LANES = 128
GROUP = 8
GROUPS = SPAN_Y // GROUP
PLANES = GROUP * SPAN_X // LANES
ROWS = GROUPS * PLANES
SLABS = GROUPS + 4
WIDE = SLABS * PLANES
START = [SPAN_X * j // LANES for j in range(GROUP)]
OFF = [SPAN_X * j % LANES for j in range(GROUP)]
LAST = [(SPAN_X * j + SPAN_X - 1) // LANES for j in range(GROUP)]
END = [(SPAN_X * j + SPAN_X - 1) % LANES for j in range(GROUP)]
FIRST_OF = [[OFF[j] for j in range(GROUP) if START[j] == a] for a in range(PLANES)]
LAST_OF = [[END[j] for j in range(GROUP) if LAST[j] == a] for a in range(PLANES)]
RIM_ROWS = 24
SLOT = RIM_ROWS + 4
HAND = 5
EDGE = 56
BUDGET = 56 * 1024 * 1024


def turn(value, shift, axis=1):
    shift = shift % value.shape[axis]
    return value if shift == 0 else pltpu.roll(value, shift, axis)


def fetching(pairs, sems):
    copies = [pltpu.make_async_copy(a, b, sems.at[n]) for n, (a, b) in enumerate(pairs)]
    for copy in copies:
        copy.start()
    return copies


class Level:
    def __init__(self, ref, base):
        self.ref, self.base = ref, base

    def plane(self, a):
        return self.ref[comb(self.base + a), :]

    def rows(self, low, size):
        return self.ref[pl.ds(self.base + low, size), :]


def lane_of(shape):
    return lax.broadcasted_iota(jnp.int32, shape, len(shape) - 1)


def row_of(shape):
    return lax.broadcasted_iota(jnp.int32, shape, 0)


def comb(a, count=GROUPS):
    return pl.ds(a, count, stride=PLANES)


def drop(value, lanes, lane):
    for at in lanes:
        value = jnp.where(lane == at, 0.0, value)
    return value


def store_terms(a, temp, flow_x, flow_y, te, tw, tn, ts):
    spread = DIFFUSE * temp
    te[a] = spread - flow_x
    tw[a] = spread + flow_x
    tn[a, 8 : 8 + GROUPS] = spread - flow_y
    ts[a, 8 : 8 + GROUPS] = spread + flow_y


def clear_terms(tn, ts):
    none = jnp.zeros((PLANES, 1, LANES), jnp.float32)
    for ref in (tn, ts):
        ref[:, 7:8] = none
        ref[:, 8 + GROUPS : 9 + GROUPS] = none


def inner_sum(a, te, tw, tn, ts):
    lane = lane_of((GROUPS, LANES))
    here = te[a]
    east = here if a == PLANES - 1 else jnp.where(lane == 0, te[a + 1], here)
    east = drop(turn(east, -1), LAST_OF[a], lane)
    here = tw[a]
    west = here if a == 0 else jnp.where(lane == LANES - 1, tw[a - 1], here)
    west = drop(turn(west, 1), FIRST_OF[a], lane)

    def plane(ref, at):
        down = 8 + (at >= PLANES) - (at < 0)
        return ref[at % PLANES, down : down + GROUPS]

    north = turn(jnp.where(lane >= LANES - 16, plane(tn, a + 1), plane(tn, a + 2)), 16)
    south = turn(jnp.where(lane < 16, plane(ts, a - 1), plane(ts, a - 2)), -16)
    return east + west + north + south


def choose(planes, lane, get):
    value = get(planes[0])
    for j in range(1, GROUP):
        low = (OFF[j] - (32 if planes is LAST else 0)) % LANES
        value = jnp.where(jnp.logical_and(lane >= low, lane < low + 16), get(planes[j]), value)
    return value


def forcing_kernel(
    levels, per, tiles_x, tiles_y,
    pos, temp_in, zonal_in, merid_in, depth_in, ocean_in, diag_in, source_in,
    part_out, own_out, slots_out, table,
    temp, zonal, merid, depth, ocean, diag, source, part, own, slots,
    st, sx, sy, pt, te, tw, tn, ts, edges, holder, sems, out_sems,
):
    count = pos.shape[0]
    steps = levels // per
    pairs = []
    for step in range(steps):
        chunk = pl.ds(step * per * ROWS, per * ROWS)
        pairs += [
            (a.at[chunk], b.at[chunk]) for a, b in ((temp_in, temp), (zonal_in, zonal), (merid_in, merid))
        ]
    pairs += [
        (a.reshape(ROWS, LANES), b)
        for a, b in ((source_in, source), (ocean_in, ocean), (depth_in, depth), (diag_in, diag))
    ]
    copies = fetching(pairs, sems)
    results = []

    def send(value, target):
        copy = pltpu.make_async_copy(value, target, out_sems.at[len(results)])
        copy.start()
        results.append(copy)

    lane = lane_of((GROUPS, LANES))
    one = lane_of((1, LANES))
    q = lane % 16
    edges[...] = jnp.zeros_like(edges)

    def number(d, carry):
        holder[pos[d]] = d
        return carry

    lax.fori_loop(0, count, number, 0)
    me = lax.axis_index("gx") * tiles_y + lax.axis_index("gy")
    here = pos[me]
    row = here // tiles_x
    column = here % tiles_x
    sides = []
    for c, (dx, dy) in enumerate(SIDES):
        there = row + dy
        inside = jnp.logical_and(there >= 0, there < tiles_y)
        target = jnp.where(inside, there, 0) * tiles_x + (column + dx + tiles_x) % tiles_x
        device = jnp.where(inside, holder[target], -1)
        table[c] = device
        sides.append(device)
    clear_terms(tn, ts)

    def add(flats, low, size, fresh):
        rows = pl.ds(low, size)
        total = [None] * 3
        for t, u, v in zip(*flats):
            t = t.rows(low, size)
            new = (t, t * u.rows(low, size), t * v.rows(low, size))
            total = [b if a is None else a + b for a, b in zip(total, new)]
        for ref, value in zip((st, sx, sy), total):
            ref[rows, :] = value if fresh else ref[rows, :] + value

    for step in range(steps):
        for copy in copies[3 * step : 3 * step + 3]:
            copy.wait()
        flats = [
            [Level(ref, (step * per + n) * ROWS) for n in range(per)] for ref in (temp, zonal, merid)
        ]

        def some(m, carry):
            add(flats, pl.multiple_of(m * 8, 8), 8, step == 0)
            return carry

        lax.fori_loop(0, ROWS // 8, some, 0, unroll=4)
        if ROWS % 8:
            add(flats, ROWS - ROWS % 8, ROWS % 8, step == 0)

        for n in range(per):
            k = step * per + n
            t, u, v = (flat[n] for flat in flats)

            def term(planes, sign):
                own = choose(planes, lane, t.plane)
                flow = choose(planes, lane, u.plane)
                return DIFFUSE * own + sign * ADVECT * (flow * own)

            edges[0, 0:GROUPS] = jnp.where(q == k, turn(term(START, -1.0), k), edges[0, 0:GROUPS])
            edges[1, 0:GROUPS] = jnp.where(q == k, turn(term(LAST, 1.0), k + 17), edges[1, 0:GROUPS])
            rows = t.rows(0, 2)
            rows = DIFFUSE * rows - ADVECT * (v.rows(0, 2) * rows)
            edges[2, k : k + 1] = rows[0:1]
            edges[2, k + levels : k + levels + 1] = rows[1:2]
            rows = t.rows(ROWS - 2, 2)
            rows = DIFFUSE * rows + ADVECT * (v.rows(ROWS - 2, 2) * rows)
            edges[3, k : k + 1] = turn(jnp.where(one >= 16, rows[0:1], rows[1:2]), -16)
            edges[3, k + levels : k + levels + 1] = turn(rows[1:2], -16)

    for c in range(4):
        slots[pl.ds(RIM_ROWS + c, 2 * levels, stride=SLOT), :] = edges[c]

    for copy in copies[3 * steps :]:
        copy.wait()

    def wet_of(rows):
        return ocean[rows, :].astype(jnp.float32)

    def masked(rows):
        return depth[rows, :] * wet_of(rows)

    for a in range(PLANES):
        total = st[comb(a), :]
        pt[a] = total
        store_terms(a, total, ADVECT * sx[comb(a), :], ADVECT * sy[comb(a), :], te, tw, tn, ts)
    for a in range(PLANES):
        total = pt[a]
        wet = wet_of(comb(a))
        change = inner_sum(a, te, tw, tn, ts) - 4.0 * DIFFUSE * total
        part[comb(a), :] = source[comb(a), :] + (STERIC / levels) * wet * (total + wet * change)
    send(part, part_out)

    def mix(values):
        value = values[4]
        for at, low in ((3, 12), (2, 11), (1, 8), (0, 4)):
            value = jnp.where(q < low, values[at], value)
        return value

    def flat(ref):
        return lambda a: ref[comb(a), :]

    def ends(planes, low):
        value = tn[planes[0], 8 : 8 + GROUPS]
        last = jnp.logical_and(lane >= low, lane < low + 16)
        return jnp.where(last, ts[planes[7], 8 : 8 + GROUPS], value)

    pack_w = mix([
        choose(START, lane, flat(part)),
        turn(choose(START, lane, lambda a: masked(comb(a))), 4),
        turn(choose(START, lane, flat(diag)), 8),
        turn(choose(START, lane, lambda a: te[a]), 11),
        turn(ends(START, OFF[7]), 12),
    ])
    pack_e = mix([
        turn(choose(LAST, lane, flat(part)), 20),
        turn(choose(LAST, lane, lambda a: masked(comb(a))), 24),
        turn(choose(LAST, lane, flat(diag)), 27),
        turn(choose(LAST, lane, lambda a: tw[a]), 28),
        turn(ends(LAST, LANES - 16), 32),
    ])
    own[0:GROUPS] = pack_w
    own[SLABS : SLABS + GROUPS] = pack_e
    north_l = tn[0, 8:9]
    north_r = tn[1, 8:9]
    south_13 = ts[PLANES - 2, 7 + GROUPS : 8 + GROUPS]
    south_14 = ts[PLANES - 1, 7 + GROUPS : 8 + GROUPS]
    south_l = turn(jnp.where(one >= 16, south_13, south_14), -16)
    south_r = turn(south_14, -16)
    own[48:49] = north_l
    own[49:50] = north_r
    own[50:51] = south_l
    own[51:52] = south_r
    send(own, own_out)
    deep = jnp.max(masked(slice(0, ROWS)), axis=(0, 1), keepdims=True)
    top = jnp.max(diag[...], axis=(0, 1), keepdims=True) + 8.0 * deep * deep
    top = jnp.broadcast_to(top, (1, LANES))

    slots[pl.ds(RIM_ROWS - 1, count, stride=SLOT), :] = jnp.broadcast_to(top, (count, LANES))
    eight = lane_of((8, LANES))
    eighth = row_of((8, LANES))
    for c, first, rows_l, rows_r in ((2, True, north_l, north_r), (3, False, south_l, south_r)):
        base = 0 if first else ROWS - 8
        spare = jnp.logical_and(eighth == 7, eight >= 64) if first else jnp.logical_and(eighth == 0, eight < 64)
        g = 0 if first else GROUPS - 1
        blocks = []
        block = slice(base, base + 8)
        for value, at in ((part[block, :], g), (masked(block), SLABS + g)):
            extra = jnp.broadcast_to(turn(own[at : at + 1], -16), (8, LANES))
            blocks.append(jnp.where(spare, extra, value))
        low = 0 if first else ROWS - 6
        diag_rows = diag[low : low + 6, :]
        last_row = jnp.where(one == LANES - 1, top, rows_r)

        @pl.when(sides[c] >= 0)
        def _(c=c, blocks=blocks, diag_rows=diag_rows, rows_l=rows_l, last_row=last_row):
            at = sides[c] * SLOT
            slots[pl.ds(at, 8), :] = blocks[0]
            slots[pl.ds(at + 8, 8), :] = blocks[1]
            slots[pl.ds(at + 16, 6), :] = diag_rows
            slots[pl.ds(at + 22, 1), :] = rows_l
            slots[pl.ds(at + 23, 1), :] = last_row

    slots[pl.ds(sides[0] * SLOT, GROUPS), :] = pack_w
    slots[pl.ds(sides[1] * SLOT, GROUPS), :] = pack_e
    for c, at in ((4, 0), (5, SLABS), (6, GROUPS - 1), (7, SLABS + GROUPS - 1)):
        @pl.when(sides[c] >= 0)
        def _(c=c, at=at):
            slots[pl.ds(sides[c] * SLOT, 1), :] = own[at : at + 1]
    send(slots, slots_out.reshape(count * SLOT, LANES))
    for copy in results:
        copy.wait()


SMEM = pl.BlockSpec(memory_space=pltpu.SMEM)


def solve_kernel(
    levels,
    table, around, rims, own_in, part_in, depth_in, ocean_in, diag_in,
    vectors, hand_out,
    came, own, part, depth, ocean, diag, hand, sems, out_sems,
    fb, fd, fg, pw, pe, ow, oe, ed, eg, we, wn, last, rows,
):
    count = rims.shape[0]
    copies = fetching(
        [
            (rims.reshape(count * SLOT, LANES), came), (own_in, own), (part_in, part),
            (depth_in.reshape(ROWS, LANES), depth), (ocean_in.reshape(ROWS, LANES), ocean),
            (diag_in.reshape(ROWS, LANES), diag),
        ],
        sems,
    )
    lane = lane_of((SLABS, LANES))
    slab = row_of((SLABS, LANES))
    one = lane_of((1, LANES))
    src = [table[c] for c in range(8)]

    def fetch(c, low, high):
        value = came[pl.ds(jnp.maximum(src[c], 0) * SLOT + low, high - low), :]
        return jnp.where(src[c] >= 0, value, 0.0)

    copies[0].wait()

    def relay(d, carry):
        for c in range(4):
            row = jnp.maximum(around[c * count + d], 0) * SLOT + RIM_ROWS + (c ^ 1)
            hand[pl.ds(d * HAND + 1 + c, 1), :] = came[pl.ds(row, 1), :]
        return carry

    lax.fori_loop(0, count, relay, 0)

    for copy in copies[1:]:
        copy.wait()
    none = jnp.zeros((WIDE - ROWS + 4, LANES), jnp.float32)
    for ref in (fb, fd, fg):
        ref[ROWS - 4 : WIDE] = none
    fb[0:ROWS] = part[...]
    fd[0:ROWS] = depth[...] * ocean[...].astype(jnp.float32)
    fg[0:ROWS] = diag[...]
    for ref, low, high in ((fb, 0, 8), (fd, 8, 16), (fg, 16, 22)):
        ref[ROWS : ROWS + high - low] = fetch(3, low, high)
        ref[WIDE - high + low : WIDE] = fetch(2, low, high)
    empty = jnp.zeros((SLABS, LANES), jnp.float32)
    for ref, side, north, south in ((pw, 0, 6, 4), (pe, 1, 7, 5)):
        ref[...] = empty
        ref[0:GROUPS] = fetch(side, 0, GROUPS)
        ref[GROUPS : GROUPS + 1] = fetch(north, 0, 1)
        ref[SLABS - 1 : SLABS] = fetch(south, 0, 1)
    for ref, at, north, south in ((ow, 0, 7, 0), (oe, SLABS, 15, 8)):
        ref[...] = empty
        ref[0:GROUPS] = own[at : at + GROUPS]
        ref[GROUPS : GROUPS + 1] = turn(fetch(3, north, north + 1), 16)
        ref[SLABS - 1 : SLABS] = turn(fetch(2, south, south + 1), 16)

    def spread(ref, j):
        a = START[j]
        first, second = ref[comb(a, SLABS), :], ref[comb(a + 1, SLABS), :]
        third = ref[comb(a + 2, SLABS), :] if a + 2 < PLANES else second
        left = turn(jnp.where(lane >= OFF[j], first, second), -OFF[j])
        right = turn(jnp.where(lane >= OFF[j], second, third), -OFF[j])
        return left, right

    def seam_row(left, right, slab_at, lanes_at):
        east = turn(pe[slab_at : slab_at + 1], 112 - lanes_at)
        west = turn(pw[slab_at : slab_at + 1], 124 - lanes_at)
        right = jnp.where(one < 112, right, jnp.where(one < 116, east, jnp.where(one >= 124, west, 0.0)))
        return jnp.broadcast_to(left, (SLABS, LANES)), jnp.broadcast_to(right, (SLABS, LANES))

    seams = {
        0: ((0, seam_row(fetch(2, 22, 23), fetch(2, 23, 24), SLABS - 1, 28)),
            (GROUPS, seam_row(own[50:51], own[51:52], GROUPS - 1, 28))),
        GROUP - 1: ((GROUPS - 1, seam_row(fetch(3, 22, 23), fetch(3, 23, 24), GROUPS, 12)),
                    (SLABS - 1, seam_row(own[48:49], own[49:50], 0, 12))),
    }
    weight = STERIC / levels
    for j in range(GROUP):
        o = OFF[j]

        def rim(right, q, width):
            east = turn(pe[...], 112 - o - q)
            west = turn(pw[...], 128 - width - o - q)
            value = jnp.where(lane < 112 + width, east, jnp.where(lane >= 128 - width, west, 0.0))
            return jnp.where(lane < 112, right, value)

        left, right = spread(fd, j)
        right = rim(right, 4, 4)
        wet_l = jnp.where(left > 0, weight, 0.0)
        wet_r = jnp.where(right > 0, weight, 0.0)
        ed[j, :, 0:LANES] = left
        ed[j, :, LANES:] = right
        left, right = spread(fg, j)
        eg[j, :, 0:LANES] = left
        eg[j, :, LANES:] = rim(right, 8, 3)
        left, right = spread(fb, j)
        right = rim(right, 0, 4)
        seam_l = jnp.where(lane == 0, turn(pw[...], -o - 11), 0.0)
        seam_r = jnp.where(lane == 127, turn(ow[...], 127 - o - 11), 0.0)
        seam_r = jnp.where(lane == 111, turn(pe[...], 111 - o - 11), seam_r)
        seam_r = jnp.where(lane == 112, turn(oe[...], 112 - o - 11), seam_r)
        for at, (row_l, row_r) in seams.get(j, ()):
            seam_l = seam_l + jnp.where(slab == at, row_l, 0.0)
            seam_r = seam_r + jnp.where(slab == at, row_r, 0.0)
        vectors[0, j, :, 0:LANES] = left + wet_l * seam_l
        vectors[0, j, :, LANES:] = right + wet_r * seam_r

    for j in range(GROUP):
        d = ed[j]
        we[j] = d * turn(d, -1)
        above = ed[j + 1] if j < GROUP - 1 else turn(ed[0], -1, 0)
        wn[j] = d * above

    top = jnp.max(came[pl.ds(RIM_ROWS - 1, count, stride=SLOT), :], axis=0, keepdims=True)
    top = jnp.max(jnp.where(one == LANES - 1, top, 0.0), axis=1, keepdims=True)
    scale = STRETCH / top

    big = (SLABS, 2 * LANES)
    mine = jnp.logical_and(row_of(big) < GROUPS, lane_of(big) < SPAN_X)
    pair = 0
    for k in range(5):
        sums = [None] * (k + 1)
        new = last if k == 4 else vectors.at[k]
        if k:
            v = vectors.at[k - 1]
            flow_below = wn[GROUP - 1] * (v[GROUP - 1] - turn(v[0], -1, 0))
            flow_below = turn(flow_below, 1, 0)
        for j in range(GROUP):
            if k:
                here = v[j]
                above = v[j + 1] if j < GROUP - 1 else turn(v[0], -1, 0)
                flow_x = we[j] * (here - turn(here, -1))
                flow_y = wn[j] * (here - above)
                image = eg[j] * here + (flow_x - turn(flow_x, 1)) + (flow_y - flow_below)
                fresh = scale * image - (STRETCH * ROOTS[k - 1]) * here
                flow_below = flow_y
                new[j] = fresh
            else:
                fresh = new[j]
            held = jnp.where(mine, fresh, 0.0)
            for i in range(k + 1):
                other = vectors[i, j] if i < k else held
                value = held * other
                sums[i] = value if sums[i] is None else sums[i] + value
        for i in range(k + 1):
            rows[pair : pair + 1] = jnp.sum(sums[i][:, 0:LANES] + sums[i][:, LANES:], axis=0, keepdims=True)
            pair += 1
    rows[pair : pair + 1] = jnp.where(one == 0, top, 0.0)
    total = jnp.sum(rows[...], axis=1, keepdims=True)
    spot = row_of((16, LANES)) == lane_of((16, LANES))
    line = jnp.sum(jnp.where(spot, total, 0.0), axis=0, keepdims=True)
    hand[pl.ds(0, count, stride=HAND), :] = jnp.broadcast_to(line, (count, LANES))
    for copy in fetching([(hand, hand_out.reshape(count * HAND, LANES))], out_sems):
        copy.wait()


def finish_kernel(
    levels, per, table, hands, vectors, inner_in, edges_in, tracer_out, surface_out,
    came, cells, edges, flat, left, right, message, sems, out_sems,
):
    count = hands.shape[0]
    steps = levels // per
    chunks = [pl.ds(step * per * ROWS, per * ROWS) for step in range(steps)]
    copies = fetching(
        [(hands.reshape(count * HAND, LANES), came), (edges_in, edges)]
        + [(inner_in.at[c], cells.at[c]) for c in chunks],
        sems,
    )
    copies[0].wait()
    row = jnp.sum(came[pl.ds(0, count, stride=HAND), :], axis=0, keepdims=True)
    one = lane_of((1, LANES))
    entry = {}
    pair = 0
    for k in range(5):
        for i in range(k + 1):
            value = jnp.sum(jnp.where(one == pair, row, 0.0), axis=1, keepdims=True)
            entry[i, k] = entry[k, i] = value
            pair += 1
    top = jnp.sum(jnp.where(one == pair, row, 0.0), axis=1, keepdims=True) * (1.0 / count)

    def image(c):
        out = [None] * 5
        for k in range(4):
            if c[k] is None:
                continue
            low = ROOTS[k] * c[k]
            out[k] = low if out[k] is None else out[k] + low
            out[k + 1] = (1.0 / STRETCH) * c[k]
        return out

    def dot(a, b):
        total = None
        for i in range(5):
            if a[i] is None:
                continue
            inner = None
            for j in range(5):
                if b[j] is not None:
                    value = entry[i, j] * b[j]
                    inner = value if inner is None else inner + value
            total = a[i] * inner if total is None else total + a[i] * inner
        return total

    def axpy(a, s, b):
        return [
            x if y is None else (s * y if x is None else x + s * y) for x, y in zip(a, b)
        ]

    r = [jnp.ones((1, 1), jnp.float32)] + [None] * 4
    p = list(r)
    x = [None] * 5
    rr = entry[0, 0]
    for n in range(ITERS):
        q = image(p)
        step = rr / jnp.maximum(dot(p, q), TINY)
        step = jnp.clip(step, top * (1.0 / HIGH_RATE), top * (1.0 / LOW_RATE))
        x = axpy(x, step, p)
        if n < ITERS - 1:
            r = axpy(r, -step, q)
            fresh = jnp.maximum(dot(r, r), 0.0)
            p = axpy(r, fresh / jnp.maximum(rr, TINY), p)
            rr = fresh
    factors = [c / top for c in x[:4]]
    for j in range(GROUP):
        value = None
        for k in range(4):
            term = factors[k] * vectors[k, j]
            value = term if value is None else value + term
        left[j] = turn(value[:, 0:LANES], OFF[j])
        right[j] = turn(value[:, LANES:], OFF[j])
    lane = lane_of((SLABS, LANES))
    for a in range(PLANES):
        value = None
        for j in range(GROUP):
            for half, ref in ((0, left), (1, right)):
                low = max(SPAN_X * j + LANES * half - LANES * a, 0)
                high = min(SPAN_X * j + (LANES if half == 0 else SPAN_X) - LANES * a, LANES)
                if low >= high:
                    continue
                value = ref[j] if value is None else jnp.where(lane >= low, ref[j], value)
        flat[comb(a), :] = value[0:GROUPS]
    results = [pltpu.make_async_copy(flat, surface_out.reshape(ROWS, LANES), out_sems.at[0])]
    results[0].start()
    copies[1].wait()

    for c in range(4):
        value = came[pl.ds(1 + c, 2 * levels, stride=HAND), :]
        message[c] = jnp.where(table[c] >= 0, value, 0.0)
    sums = []
    for k in range(levels):
        value = edges[2 * levels - 1] * jnp.concatenate([
            turn(message[0], -k), turn(message[1], -k),
            message[2, k : k + 1], message[2, k + levels : k + levels + 1],
            message[3, k : k + 1], message[3, k + levels : k + levels + 1],
            jnp.zeros((4, LANES), jnp.float32),
        ], axis=0)
        if k:
            value = value + edges[2 * levels + k - 1] * sums[-1]
        sums.append(value * edges[levels - 1 + k])
    for k in range(levels - 2, -1, -1):
        sums[k] = sums[k] + edges[k] * sums[k + 1]
    lane = lane_of((GROUPS, LANES))
    slab = row_of((GROUPS, LANES))
    for k in range(levels):
        if k % per == 0:
            copies[2 + k // per].wait()
        west = sums[k][0:GROUPS]
        east = turn(sums[k][SLABS : SLABS + GROUPS], -17)
        south_l, south_r = sums[k][48:49], sums[k][49:50]
        north_l, north_r = turn(sums[k][50:51], 16), turn(sums[k][51:52], 16)
        for a in range(PLANES):
            rim = None
            for at, source in [(at, west) for at in FIRST_OF[a]] + [(at, east) for at in LAST_OF[a]]:
                rim = jnp.where(lane == at, source, 0.0 if rim is None else rim)
            if rim is None:
                continue
            if a == 0:
                rim = rim + jnp.where(slab == 0, south_l, 0.0)
            if a == 1:
                rim = rim + jnp.where(jnp.logical_and(slab == 0, lane < 112), south_r, 0.0)
            if a == PLANES - 2:
                rim = rim + jnp.where(jnp.logical_and(slab == GROUPS - 1, lane >= 16), north_l, 0.0)
            if a == PLANES - 1:
                rim = rim + jnp.where(slab == GROUPS - 1, jnp.where(lane < 16, north_l, north_r), 0.0)
            rows = comb(k * ROWS + a)
            cells[rows, :] = cells[rows, :] + rim
        if k % per == per - 1:
            step = k // per
            copy = pltpu.make_async_copy(
                cells.at[chunks[step]], tracer_out.at[chunks[step]], out_sems.at[1 + step]
            )
            copy.start()
            results.append(copy)
    for copy in results:
        copy.wait()


def tracer_kernel(
    levels, per, tiles_x, tiles_y, pos, temp_in, zonal_in, merid_in, rates_in, ocean_in,
    inner_out, edges_out, around,
    temp, zonal, merid, rates, ocean, out, edges,
    te, tw, tn, ts, stepped, border, holder, sems, out_sems,
):
    count = pos.shape[0]
    steps = levels // per
    pairs = [(ocean_in.reshape(ROWS, LANES), ocean)]
    for step in range(steps):
        chunk = pl.ds(step * per * ROWS, per * ROWS)
        pairs += [
            (a.at[chunk], b.at[chunk]) for a, b in ((temp_in, temp), (zonal_in, zonal), (merid_in, merid))
        ]
    copies = fetching(pairs + [(rates_in.reshape((levels - 1) * ROWS, LANES), rates)], sems)
    lane = lane_of((GROUPS, LANES))
    one = lane_of((1, LANES))
    clear_terms(tn, ts)

    def number(d, carry):
        holder[pos[d]] = d
        return carry

    lax.fori_loop(0, count, number, 0)

    def look(d, carry):
        row = pos[d] // tiles_x
        column = pos[d] % tiles_x
        for c, (dx, dy) in enumerate(SIDES[:4]):
            there = row + dy
            inside = jnp.logical_and(there >= 0, there < tiles_y)
            target = jnp.where(inside, there, 0) * tiles_x + (column + dx + tiles_x) % tiles_x
            around[c * count + d] = jnp.where(inside, holder[target], -1)
        return carry

    lax.fori_loop(0, count, look, 0)
    copies[0].wait()
    for step in range(steps):
        for copy in copies[1 + 3 * step : 4 + 3 * step]:
            copy.wait()

        def level(k, carry):
            t, u, v = (Level(ref, k * ROWS) for ref in (temp, zonal, merid))
            for a in range(PLANES):
                own = t.plane(a)
                quarter = ADVECT * own
                store_terms(a, own, u.plane(a) * quarter, v.plane(a) * quarter, te, tw, tn, ts)
            for a in range(PLANES):
                own = t.plane(a)
                change = inner_sum(a, te, tw, tn, ts) - 4.0 * DIFFUSE * own
                stepped[k, a] = own + ocean[comb(a), :].astype(jnp.float32) * change
            return carry

        lax.fori_loop(step * per, step * per + per, level, 0)
    copies[-1].wait()

    def block(a, carry):
        for low in range(0, GROUPS, 8):
            size = min(8, GROUPS - low)

            def rows(k):
                return pl.ds(k * ROWS + low * PLANES + a, size, stride=PLANES)

            gains = []
            sums = []
            for k in range(levels):
                value = stepped[k, a, low : low + size]
                pivot = 1.0
                if k > 0:
                    pivot = pivot + upper - upper * gains[-1]
                    value = value + upper * sums[-1]
                if k < levels - 1:
                    lower = rates[rows(k), :]
                    inverse = 1.0 / (pivot + lower)
                    gains.append(lower * inverse)
                    upper = lower
                else:
                    inverse = 1.0 / pivot
                sums.append(value * inverse)
            result = sums[-1]
            out[rows(levels - 1), :] = result
            for k in range(levels - 2, -1, -1):
                result = sums[k] + gains[k] * result
                out[rows(k), :] = result
        return carry

    lax.fori_loop(0, PLANES, block, 0)

    def edge(ref, base, at):
        def get(a):
            return ref[comb(base + a), :].astype(jnp.float32)

        border[0:GROUPS] = choose(START, lane, get)
        border[SLABS : SLABS + GROUPS] = turn(choose(LAST, lane, get), 17)
        border[48:50] = ref[base : base + 2, :].astype(jnp.float32)
        rows = ref[base + ROWS - 2 : base + ROWS, :].astype(jnp.float32)
        border[50:51] = turn(jnp.where(one >= 16, rows[0:1], rows[1:2]), -16)
        border[51:52] = turn(rows[1:2], -16)
        edges[at] = border[...]

    border[...] = jnp.zeros_like(border)
    edge(ocean, 0, 2 * levels - 1)
    gain = None
    for k in range(levels):
        pivot = 1.0
        if k > 0:
            upper = edges[2 * levels + k - 1]
            pivot = pivot + upper - upper * gain
        if k < levels - 1:
            edge(rates, k * ROWS, 2 * levels + k)
            lower = edges[2 * levels + k]
            inverse = 1.0 / (pivot + lower)
            gain = lower * inverse
            edges[k] = gain
        else:
            inverse = 1.0 / pivot
        edges[levels - 1 + k] = inverse
        if k == 0:
            results = fetching([(out, inner_out)], out_sems)
    results.append(pltpu.make_async_copy(edges, edges_out, out_sems.at[1]))
    results[-1].start()
    for copy in results:
        copy.wait()


def on_device(
    thermal_anomaly,
    zonal_flow_ratio,
    meridional_flow_ratio,
    diffusion_rates,
    ocean_bottom_scaled,
    ocean_indicator,
    operator_diagonal,
    elevation_source,
    block_positions,
):
    levels, cells = thermal_anomaly.shape[1:]
    nx = lax.axis_size("gx")
    ny = lax.axis_size("gy")
    count = block_positions.shape[0]
    planes = (ocean_bottom_scaled, ocean_indicator, operator_diagonal, elevation_source)
    depth, ocean, diag, source = planes
    f32 = jnp.float32
    per = next(n for n in (4, 2, 6, levels) if levels % n == 0 and n * ROWS % 8 == 0)
    steps = levels // per
    large = pltpu.CompilerParams(vmem_limit_bytes=BUDGET)
    small = pltpu.CompilerParams(vmem_limit_bytes=BUDGET // 3)
    temp, zonal, merid = (
        array.reshape(levels * ROWS, LANES)
        for array in (thermal_anomaly, zonal_flow_ratio, meridional_flow_ratio)
    )
    rates = diffusion_rates.reshape(levels - 1, 1, cells)
    hbm = pl.BlockSpec(memory_space=pltpu.HBM)
    anywhere = pl.BlockSpec(memory_space=pl.ANY)
    here = pl.BlockSpec(memory_space=pltpu.VMEM)

    def vmem(*shape, kind=f32):
        return pltpu.VMEM(shape, kind)

    def out(*shape, kind=f32):
        return jax.ShapeDtypeStruct(shape, kind)

    def sems(number):
        return pltpu.SemaphoreType.DMA((number,))

    deep = vmem(levels * ROWS, LANES)
    flat = vmem(ROWS, LANES)
    flat_int = vmem(ROWS, LANES, kind=jnp.int32)
    plane = vmem(PLANES, GROUPS, LANES)
    tall = vmem(PLANES, 40, LANES)
    numbers = pltpu.SMEM((count,), jnp.int32)
    part, own, slots, table = pl.pallas_call(
        functools.partial(forcing_kernel, levels, per, nx, ny),
        in_specs=[SMEM] + [hbm] * 7,
        out_specs=[hbm] * 3 + [SMEM],
        out_shape=[
            out(ROWS, LANES), out(56, LANES), out(count, 1, SLOT * LANES), out(8, kind=jnp.int32),
        ],
        scratch_shapes=[deep] * 3 + [flat, flat_int, flat, flat]
        + [flat, vmem(56, LANES), vmem(count * SLOT, LANES)]
        + [flat] * 3 + [plane] * 3 + [tall] * 2
        + [vmem(4, 2 * levels, LANES), numbers, sems(3 * steps + 4), sems(3)],
        compiler_params=large,
        name="forcing",
    )(block_positions, temp, zonal, merid, depth, ocean, diag, source)
    rims = lax.all_to_all(slots, BOTH, 0, 0, tiled=True)

    inner, edges, around = pl.pallas_call(
        functools.partial(tracer_kernel, levels, per, nx, ny),
        in_specs=[SMEM] + [hbm] * 5,
        out_specs=[hbm] * 2 + [SMEM],
        out_shape=[
            out(levels * ROWS, LANES), out(3 * levels - 1, EDGE, LANES), out(4 * count, kind=jnp.int32),
        ],
        scratch_shapes=[deep] * 3 + [vmem((levels - 1) * ROWS, LANES), flat_int, deep]
        + [vmem(3 * levels - 1, EDGE, LANES)]
        + [plane] * 2 + [tall] * 2
        + [vmem(levels, PLANES, GROUPS, LANES), vmem(EDGE, LANES), numbers, sems(3 * steps + 2), sems(2)],
        compiler_params=large,
        name="tracer",
    )(block_positions, temp, zonal, merid, rates, ocean)

    extended = vmem(GROUP, SLABS, 2 * LANES)
    vectors, hand = pl.pallas_call(
        functools.partial(solve_kernel, levels),
        in_specs=[SMEM, SMEM, anywhere] + [hbm] * 5,
        out_specs=[here, hbm],
        out_shape=[out(4, GROUP, SLABS, 2 * LANES), out(count, 1, HAND * LANES)],
        scratch_shapes=[vmem(count * SLOT, LANES), vmem(56, LANES), flat, flat, flat_int, flat]
        + [vmem(count * HAND, LANES), sems(6), sems(1)]
        + [vmem(WIDE, LANES)] * 3 + [vmem(SLABS, LANES)] * 4 + [extended] * 5 + [vmem(16, LANES)],
        compiler_params=small,
        name="vectors",
    )(table, around, rims, own, part, depth, ocean, diag)
    hands = lax.all_to_all(hand, BOTH, 0, 0, tiled=True)

    new_temp, surface = pl.pallas_call(
        functools.partial(finish_kernel, levels, per),
        in_specs=[SMEM, anywhere, here] + [hbm] * 2,
        out_specs=[hbm] * 2,
        out_shape=[out(levels * ROWS, LANES), out(1, cells)],
        scratch_shapes=[
            vmem(count * HAND, LANES), deep, vmem(3 * levels - 1, EDGE, LANES), flat,
            vmem(GROUP, SLABS, LANES), vmem(GROUP, SLABS, LANES), vmem(4, 2 * levels, LANES),
            sems(2 + steps), sems(1 + steps),
        ],
        compiler_params=small,
        name="finish",
    )(table, hands, vectors, inner, edges)
    return new_temp.reshape(1, levels, cells), surface


def solution(mesh):
    deep = P(BOTH, None, None)
    flat = P(BOTH, None)
    return jax.shard_map(
        on_device,
        mesh=mesh,
        in_specs=(deep, deep, deep, deep, flat, flat, flat, flat, P()),
        out_specs=(deep, flat),
        check_vma=False,
    )
```

```python
import functools

import jax
import jax.numpy as jnp
from jax import lax
from jax.experimental import pallas as pl
from jax.experimental.pallas import tpu as pltpu
from jax.sharding import PartitionSpec as P

ITERS = 4
SPAN_X = 240
SPAN_Y = 160
RIM = 4
ADVECT = 0.25
DIFFUSE = 0.12
STERIC = 0.5
LOW_RATE = 0.05
HIGH_RATE = 32.5
ROOTS = (0.02, 0.35, 0.1, 0.2)
STRETCH = 4.0
TINY = 1e-30
BOTH = ("gx", "gy")
SIDES = ((-1, 0), (1, 0), (0, -1), (0, 1), (-1, -1), (1, -1), (-1, 1), (1, 1))

LANES = 128
GROUP = 8
GROUPS = SPAN_Y // GROUP
PLANES = GROUP * SPAN_X // LANES
ROWS = GROUPS * PLANES
SLABS = GROUPS + 4
WIDE = SLABS * PLANES
START = [SPAN_X * j // LANES for j in range(GROUP)]
OFF = [SPAN_X * j % LANES for j in range(GROUP)]
LAST = [(SPAN_X * j + SPAN_X - 1) // LANES for j in range(GROUP)]
END = [(SPAN_X * j + SPAN_X - 1) % LANES for j in range(GROUP)]
FIRST_OF = [[OFF[j] for j in range(GROUP) if START[j] == a] for a in range(PLANES)]
LAST_OF = [[END[j] for j in range(GROUP) if LAST[j] == a] for a in range(PLANES)]
RIM_ROWS = 24
EDGE = 56
BUDGET = 56 * 1024 * 1024


def turn(value, shift, axis=1):
    shift = shift % value.shape[axis]
    return value if shift == 0 else pltpu.roll(value, shift, axis)


def fetching(pairs, sems):
    copies = [pltpu.make_async_copy(a, b, sems.at[n]) for n, (a, b) in enumerate(pairs)]
    for copy in copies:
        copy.start()
    return copies


def pieces_of(levels, count):
    rows = 2 * levels
    number = -(-4 * rows // count)
    runs = [[] for _ in range(4)]
    for c in range(4):
        for j in range(number):
            low, high = max(c * rows, j * count), min((c + 1) * rows, (j + 1) * count)
            if low < high:
                runs[c].append((j, low - j * count, low - c * rows, high - low))
    return number, runs


class Level:
    def __init__(self, ref, base):
        self.ref, self.base = ref, base

    def plane(self, a):
        return self.ref[comb(self.base + a), :]

    def rows(self, low, size):
        return self.ref[pl.ds(self.base + low, size), :]


def lane_of(shape):
    return lax.broadcasted_iota(jnp.int32, shape, len(shape) - 1)


def row_of(shape):
    return lax.broadcasted_iota(jnp.int32, shape, 0)


def comb(a, count=GROUPS):
    return pl.ds(a, count, stride=PLANES)


def drop(value, lanes, lane):
    for at in lanes:
        value = jnp.where(lane == at, 0.0, value)
    return value


def store_terms(a, temp, flow_x, flow_y, te, tw, tn, ts):
    spread = DIFFUSE * temp
    te[a] = spread - flow_x
    tw[a] = spread + flow_x
    tn[a, 8 : 8 + GROUPS] = spread - flow_y
    ts[a, 8 : 8 + GROUPS] = spread + flow_y


def clear_terms(tn, ts):
    none = jnp.zeros((PLANES, 1, LANES), jnp.float32)
    for ref in (tn, ts):
        ref[:, 7:8] = none
        ref[:, 8 + GROUPS : 9 + GROUPS] = none


def inner_sum(a, te, tw, tn, ts):
    lane = lane_of((GROUPS, LANES))
    here = te[a]
    east = here if a == PLANES - 1 else jnp.where(lane == 0, te[a + 1], here)
    east = drop(turn(east, -1), LAST_OF[a], lane)
    here = tw[a]
    west = here if a == 0 else jnp.where(lane == LANES - 1, tw[a - 1], here)
    west = drop(turn(west, 1), FIRST_OF[a], lane)

    def plane(ref, at):
        down = 8 + (at >= PLANES) - (at < 0)
        return ref[at % PLANES, down : down + GROUPS]

    north = turn(jnp.where(lane >= LANES - 16, plane(tn, a + 1), plane(tn, a + 2)), 16)
    south = turn(jnp.where(lane < 16, plane(ts, a - 1), plane(ts, a - 2)), -16)
    return east + west + north + south


def choose(planes, lane, get):
    value = get(planes[0])
    for j in range(1, GROUP):
        low = (OFF[j] - (32 if planes is LAST else 0)) % LANES
        value = jnp.where(jnp.logical_and(lane >= low, lane < low + 16), get(planes[j]), value)
    return value


def forcing_kernel(
    levels, per, tiles_x, tiles_y,
    pos, temp_in, zonal_in, merid_in, depth_in, ocean_in, diag_in, source_in,
    part_out, own_out, slots_out, table, around,
    temp, zonal, merid, depth, ocean, diag, source, part, own, slots,
    st, sx, sy, pt, te, tw, tn, ts, edges, holder, sems, out_sems,
):
    count = pos.shape[0]
    steps = levels // per
    number_pieces, runs = pieces_of(levels, count)
    slot = RIM_ROWS + number_pieces
    pairs = []
    for step in range(steps):
        chunk = pl.ds(step * per * ROWS, per * ROWS)
        pairs += [
            (a.at[chunk], b.at[chunk]) for a, b in ((temp_in, temp), (zonal_in, zonal), (merid_in, merid))
        ]
    pairs += [
        (a.reshape(ROWS, LANES), b)
        for a, b in ((source_in, source), (ocean_in, ocean), (depth_in, depth), (diag_in, diag))
    ]
    copies = fetching(pairs, sems)
    results = []

    def send(value, target):
        copy = pltpu.make_async_copy(value, target, out_sems.at[len(results)])
        copy.start()
        results.append(copy)

    lane = lane_of((GROUPS, LANES))
    one = lane_of((1, LANES))
    q = lane % 16
    edges[...] = jnp.zeros_like(edges)

    def number(d, carry):
        holder[pos[d]] = d
        return carry

    lax.fori_loop(0, count, number, 0)
    me = lax.axis_index("gx") * tiles_y + lax.axis_index("gy")
    here = pos[me]
    row = here // tiles_x
    column = here % tiles_x
    sides = []
    for c, (dx, dy) in enumerate(SIDES):
        there = row + dy
        inside = jnp.logical_and(there >= 0, there < tiles_y)
        target = jnp.where(inside, there, 0) * tiles_x + (column + dx + tiles_x) % tiles_x
        device = jnp.where(inside, holder[target], -1)
        table[c] = device
        sides.append(device)

    def look(y, carry):
        line = [holder[y * tiles_x + x] for x in range(tiles_x)]
        below = [holder[jnp.maximum(y - 1, 0) * tiles_x + x] for x in range(tiles_x)]
        above = [holder[jnp.minimum(y + 1, tiles_y - 1) * tiles_x + x] for x in range(tiles_x)]
        for x, device in enumerate(line):
            around[device] = line[x - 1]
            around[count + device] = line[(x + 1) % tiles_x]
            around[2 * count + device] = jnp.where(y > 0, below[x], -1)
            around[3 * count + device] = jnp.where(y < tiles_y - 1, above[x], -1)
        return carry

    lax.fori_loop(0, tiles_y, look, 0)
    clear_terms(tn, ts)

    def add(flats, low, size, fresh):
        rows = pl.ds(low, size)
        total = [None] * 3
        for t, u, v in zip(*flats):
            t = t.rows(low, size)
            new = (t, t * u.rows(low, size), t * v.rows(low, size))
            total = [b if a is None else a + b for a, b in zip(total, new)]
        for ref, value in zip((st, sx, sy), total):
            ref[rows, :] = value if fresh else ref[rows, :] + value

    for step in range(steps):
        for copy in copies[3 * step : 3 * step + 3]:
            copy.wait()
        flats = [
            [Level(ref, (step * per + n) * ROWS) for n in range(per)] for ref in (temp, zonal, merid)
        ]

        def some(m, carry):
            add(flats, pl.multiple_of(m * 8, 8), 8, step == 0)
            return carry

        lax.fori_loop(0, ROWS // 8, some, 0, unroll=4)
        if ROWS % 8:
            add(flats, ROWS - ROWS % 8, ROWS % 8, step == 0)

        for n in range(per):
            k = step * per + n
            t, u, v = (flat[n] for flat in flats)

            def term(planes, sign):
                own = choose(planes, lane, t.plane)
                flow = choose(planes, lane, u.plane)
                return DIFFUSE * own + sign * ADVECT * (flow * own)

            edges[0, 0:GROUPS] = jnp.where(q == k, turn(term(START, -1.0), k), edges[0, 0:GROUPS])
            edges[1, 0:GROUPS] = jnp.where(q == k, turn(term(LAST, 1.0), k + 17), edges[1, 0:GROUPS])
            rows = t.rows(0, 2)
            rows = DIFFUSE * rows - ADVECT * (v.rows(0, 2) * rows)
            edges[2, k : k + 1] = rows[0:1]
            edges[2, k + levels : k + levels + 1] = rows[1:2]
            rows = t.rows(ROWS - 2, 2)
            rows = DIFFUSE * rows + ADVECT * (v.rows(ROWS - 2, 2) * rows)
            edges[3, k : k + 1] = turn(jnp.where(one >= 16, rows[0:1], rows[1:2]), -16)
            edges[3, k + levels : k + levels + 1] = turn(rows[1:2], -16)

    for c in range(4):
        for j, device, low, size in runs[c]:
            slots[pl.ds(device * slot + RIM_ROWS + j, size, stride=slot), :] = edges[c, low : low + size]

    for copy in copies[3 * steps :]:
        copy.wait()

    def wet_of(rows):
        return ocean[rows, :].astype(jnp.float32)

    def masked(rows):
        return depth[rows, :] * wet_of(rows)

    for a in range(PLANES):
        total = st[comb(a), :]
        pt[a] = total
        store_terms(a, total, ADVECT * sx[comb(a), :], ADVECT * sy[comb(a), :], te, tw, tn, ts)
    for a in range(PLANES):
        total = pt[a]
        wet = wet_of(comb(a))
        change = inner_sum(a, te, tw, tn, ts) - 4.0 * DIFFUSE * total
        part[comb(a), :] = source[comb(a), :] + (STERIC / levels) * wet * (total + wet * change)
    send(part, part_out)

    def mix(values):
        value = values[4]
        for at, low in ((3, 12), (2, 11), (1, 8), (0, 4)):
            value = jnp.where(q < low, values[at], value)
        return value

    def flat(ref):
        return lambda a: ref[comb(a), :]

    def ends(planes, low):
        value = tn[planes[0], 8 : 8 + GROUPS]
        last = jnp.logical_and(lane >= low, lane < low + 16)
        return jnp.where(last, ts[planes[7], 8 : 8 + GROUPS], value)

    pack_w = mix([
        choose(START, lane, flat(part)),
        turn(choose(START, lane, lambda a: masked(comb(a))), 4),
        turn(choose(START, lane, flat(diag)), 8),
        turn(choose(START, lane, lambda a: te[a]), 11),
        turn(ends(START, OFF[7]), 12),
    ])
    pack_e = mix([
        turn(choose(LAST, lane, flat(part)), 20),
        turn(choose(LAST, lane, lambda a: masked(comb(a))), 24),
        turn(choose(LAST, lane, flat(diag)), 27),
        turn(choose(LAST, lane, lambda a: tw[a]), 28),
        turn(ends(LAST, LANES - 16), 32),
    ])
    own[0:GROUPS] = pack_w
    own[SLABS : SLABS + GROUPS] = pack_e
    north_l = tn[0, 8:9]
    north_r = tn[1, 8:9]
    south_13 = ts[PLANES - 2, 7 + GROUPS : 8 + GROUPS]
    south_14 = ts[PLANES - 1, 7 + GROUPS : 8 + GROUPS]
    south_l = turn(jnp.where(one >= 16, south_13, south_14), -16)
    south_r = turn(south_14, -16)
    own[48:49] = north_l
    own[49:50] = north_r
    own[50:51] = south_l
    own[51:52] = south_r
    send(own, own_out)
    deep = jnp.max(masked(slice(0, ROWS)), axis=(0, 1), keepdims=True)
    top = jnp.max(diag[...], axis=(0, 1), keepdims=True) + 8.0 * deep * deep
    top = jnp.broadcast_to(top, (1, LANES))

    slots[pl.ds(RIM_ROWS - 1, count, stride=slot), :] = jnp.broadcast_to(top, (count, LANES))
    eight = lane_of((8, LANES))
    eighth = row_of((8, LANES))
    for c, first, rows_l, rows_r in ((2, True, north_l, north_r), (3, False, south_l, south_r)):
        base = 0 if first else ROWS - 8
        spare = jnp.logical_and(eighth == 7, eight >= 64) if first else jnp.logical_and(eighth == 0, eight < 64)
        g = 0 if first else GROUPS - 1
        blocks = []
        block = slice(base, base + 8)
        for value, at in ((part[block, :], g), (masked(block), SLABS + g)):
            extra = jnp.broadcast_to(turn(own[at : at + 1], -16), (8, LANES))
            blocks.append(jnp.where(spare, extra, value))
        low = 0 if first else ROWS - 6
        diag_rows = diag[low : low + 6, :]
        last_row = jnp.where(one == LANES - 1, top, rows_r)

        @pl.when(sides[c] >= 0)
        def _(c=c, blocks=blocks, diag_rows=diag_rows, rows_l=rows_l, last_row=last_row):
            at = sides[c] * slot
            slots[pl.ds(at, 8), :] = blocks[0]
            slots[pl.ds(at + 8, 8), :] = blocks[1]
            slots[pl.ds(at + 16, 6), :] = diag_rows
            slots[pl.ds(at + 22, 1), :] = rows_l
            slots[pl.ds(at + 23, 1), :] = last_row

    slots[pl.ds(sides[0] * slot, GROUPS), :] = pack_w
    slots[pl.ds(sides[1] * slot, GROUPS), :] = pack_e
    for c, at in ((4, 0), (5, SLABS), (6, GROUPS - 1), (7, SLABS + GROUPS - 1)):
        @pl.when(sides[c] >= 0)
        def _(c=c, at=at):
            slots[pl.ds(sides[c] * slot, 1), :] = own[at : at + 1]
    send(slots, slots_out.reshape(count * slot, LANES))
    for copy in results:
        copy.wait()


SMEM = pl.BlockSpec(memory_space=pltpu.SMEM)


def solve_kernel(
    levels, tiles_y,
    table, around, rims, own, part, depth, ocean, diag,
    vectors, hands,
    fb, fd, fg, pw, pe, ow, oe, ed, eg, we, wn, last, rows,
):
    count = rims.shape[0]
    number_pieces, _ = pieces_of(levels, count)
    slot = RIM_ROWS + number_pieces
    share = 1 + number_pieces
    came = rims.reshape(count * slot, LANES)
    hand = hands.reshape(count * share, LANES)
    depth, ocean, diag = (ref.reshape(ROWS, LANES) for ref in (depth, ocean, diag))
    lane = lane_of((SLABS, LANES))
    slab = row_of((SLABS, LANES))
    one = lane_of((1, LANES))
    src = [table[c] for c in range(8)]

    def fetch(c, low, high):
        value = came[pl.ds(jnp.maximum(src[c], 0) * slot + low, high - low), :]
        return jnp.where(src[c] >= 0, value, 0.0)

    me = lax.axis_index("gx") * tiles_y + lax.axis_index("gy")
    for n in range(number_pieces):
        side = jnp.minimum((n * count + me) // (2 * levels), 3)
        base = (side + 1 - 2 * (side % 2)) * count

        def relay(d, carry, n=n, base=base):
            row = jnp.maximum(around[base + d], 0) * slot + RIM_ROWS + n
            hand[pl.ds(d * share + 1 + n, 1), :] = came[pl.ds(row, 1), :]
            return carry

        lax.fori_loop(0, count, relay, 0, unroll=4)

    none = jnp.zeros((WIDE - ROWS + 4, LANES), jnp.float32)
    for ref in (fb, fd, fg):
        ref[ROWS - 4 : WIDE] = none
    fb[0:ROWS] = part[...]
    fd[0:ROWS] = depth[...] * ocean[...].astype(jnp.float32)
    fg[0:ROWS] = diag[...]
    for ref, low, high in ((fb, 0, 8), (fd, 8, 16), (fg, 16, 22)):
        ref[ROWS : ROWS + high - low] = fetch(3, low, high)
        ref[WIDE - high + low : WIDE] = fetch(2, low, high)
    empty = jnp.zeros((SLABS, LANES), jnp.float32)
    for ref, side, north, south in ((pw, 0, 6, 4), (pe, 1, 7, 5)):
        ref[...] = empty
        ref[0:GROUPS] = fetch(side, 0, GROUPS)
        ref[GROUPS : GROUPS + 1] = fetch(north, 0, 1)
        ref[SLABS - 1 : SLABS] = fetch(south, 0, 1)
    for ref, at, north, south in ((ow, 0, 7, 0), (oe, SLABS, 15, 8)):
        ref[...] = empty
        ref[0:GROUPS] = own[at : at + GROUPS]
        ref[GROUPS : GROUPS + 1] = turn(fetch(3, north, north + 1), 16)
        ref[SLABS - 1 : SLABS] = turn(fetch(2, south, south + 1), 16)

    def spread(ref, j):
        a = START[j]
        first, second = ref[comb(a, SLABS), :], ref[comb(a + 1, SLABS), :]
        third = ref[comb(a + 2, SLABS), :] if a + 2 < PLANES else second
        left = turn(jnp.where(lane >= OFF[j], first, second), -OFF[j])
        right = turn(jnp.where(lane >= OFF[j], second, third), -OFF[j])
        return left, right

    def seam_row(left, right, slab_at, lanes_at):
        east = turn(pe[slab_at : slab_at + 1], 112 - lanes_at)
        west = turn(pw[slab_at : slab_at + 1], 124 - lanes_at)
        right = jnp.where(one < 112, right, jnp.where(one < 116, east, jnp.where(one >= 124, west, 0.0)))
        return jnp.broadcast_to(left, (SLABS, LANES)), jnp.broadcast_to(right, (SLABS, LANES))

    seams = {
        0: ((0, seam_row(fetch(2, 22, 23), fetch(2, 23, 24), SLABS - 1, 28)),
            (GROUPS, seam_row(own[50:51], own[51:52], GROUPS - 1, 28))),
        GROUP - 1: ((GROUPS - 1, seam_row(fetch(3, 22, 23), fetch(3, 23, 24), GROUPS, 12)),
                    (SLABS - 1, seam_row(own[48:49], own[49:50], 0, 12))),
    }
    weight = STERIC / levels
    for j in range(GROUP):
        o = OFF[j]

        def rim(right, q, width):
            east = turn(pe[...], 112 - o - q)
            west = turn(pw[...], 128 - width - o - q)
            value = jnp.where(lane < 112 + width, east, jnp.where(lane >= 128 - width, west, 0.0))
            return jnp.where(lane < 112, right, value)

        left, right = spread(fd, j)
        right = rim(right, 4, 4)
        wet_l = jnp.where(left > 0, weight, 0.0)
        wet_r = jnp.where(right > 0, weight, 0.0)
        ed[j, :, 0:LANES] = left
        ed[j, :, LANES:] = right
        left, right = spread(fg, j)
        eg[j, :, 0:LANES] = left
        eg[j, :, LANES:] = rim(right, 8, 3)
        left, right = spread(fb, j)
        right = rim(right, 0, 4)
        seam_l = jnp.where(lane == 0, turn(pw[...], -o - 11), 0.0)
        seam_r = jnp.where(lane == 127, turn(ow[...], 127 - o - 11), 0.0)
        seam_r = jnp.where(lane == 111, turn(pe[...], 111 - o - 11), seam_r)
        seam_r = jnp.where(lane == 112, turn(oe[...], 112 - o - 11), seam_r)
        for at, (row_l, row_r) in seams.get(j, ()):
            seam_l = seam_l + jnp.where(slab == at, row_l, 0.0)
            seam_r = seam_r + jnp.where(slab == at, row_r, 0.0)
        vectors[0, j, :, 0:LANES] = left + wet_l * seam_l
        vectors[0, j, :, LANES:] = right + wet_r * seam_r

    for j in range(GROUP):
        d = ed[j]
        we[j] = d * turn(d, -1)
        above = ed[j + 1] if j < GROUP - 1 else turn(ed[0], -1, 0)
        wn[j] = d * above

    top = jnp.max(came[pl.ds(RIM_ROWS - 1, count, stride=slot), :], axis=0, keepdims=True)
    top = jnp.max(jnp.where(one == LANES - 1, top, 0.0), axis=1, keepdims=True)
    scale = STRETCH / top

    big = (SLABS, 2 * LANES)
    mine = jnp.logical_and(row_of(big) < GROUPS, lane_of(big) < SPAN_X)
    pair = 0
    for k in range(5):
        sums = [None] * (k + 1)
        new = last if k == 4 else vectors.at[k]
        if k:
            v = vectors.at[k - 1]
            flow_below = wn[GROUP - 1] * (v[GROUP - 1] - turn(v[0], -1, 0))
            flow_below = turn(flow_below, 1, 0)
        for j in range(GROUP):
            if k:
                here = v[j]
                above = v[j + 1] if j < GROUP - 1 else turn(v[0], -1, 0)
                flow_x = we[j] * (here - turn(here, -1))
                flow_y = wn[j] * (here - above)
                image = eg[j] * here + (flow_x - turn(flow_x, 1)) + (flow_y - flow_below)
                fresh = scale * image - (STRETCH * ROOTS[k - 1]) * here
                flow_below = flow_y
                new[j] = fresh
            else:
                fresh = new[j]
            held = jnp.where(mine, fresh, 0.0)
            for i in range(k + 1):
                other = vectors[i, j] if i < k else held
                value = held * other
                sums[i] = value if sums[i] is None else sums[i] + value
        for i in range(k + 1):
            rows[pair : pair + 1] = jnp.sum(sums[i][:, 0:LANES] + sums[i][:, LANES:], axis=0, keepdims=True)
            pair += 1
    rows[pair : pair + 1] = jnp.where(one == 0, top, 0.0)
    total = jnp.sum(rows[...], axis=1, keepdims=True)
    spot = row_of((16, LANES)) == lane_of((16, LANES))
    line = jnp.sum(jnp.where(spot, total, 0.0), axis=0, keepdims=True)
    hand[pl.ds(0, count, stride=share), :] = jnp.broadcast_to(line, (count, LANES))


def finish_kernel(
    levels, per, table, hands, vectors, edges, inner_in, tracer_out, surface_out,
    cells, flat, left, right, message, sems, out_sems,
):
    count = hands.shape[0]
    number_pieces, runs = pieces_of(levels, count)
    share = 1 + number_pieces
    came = hands.reshape(count * share, LANES)
    steps = levels // per
    chunks = [pl.ds(step * per * ROWS, per * ROWS) for step in range(steps)]
    copies = fetching([(inner_in.at[c], cells.at[c]) for c in chunks], sems)
    row = jnp.sum(came[pl.ds(0, count, stride=share), :], axis=0, keepdims=True)
    one = lane_of((1, LANES))
    entry = {}
    pair = 0
    for k in range(5):
        for i in range(k + 1):
            value = jnp.sum(jnp.where(one == pair, row, 0.0), axis=1, keepdims=True)
            entry[i, k] = entry[k, i] = value
            pair += 1
    top = jnp.sum(jnp.where(one == pair, row, 0.0), axis=1, keepdims=True) * (1.0 / count)

    def image(c):
        out = [None] * 5
        for k in range(4):
            if c[k] is None:
                continue
            low = ROOTS[k] * c[k]
            out[k] = low if out[k] is None else out[k] + low
            out[k + 1] = (1.0 / STRETCH) * c[k]
        return out

    def dot(a, b):
        total = None
        for i in range(5):
            if a[i] is None:
                continue
            inner = None
            for j in range(5):
                if b[j] is not None:
                    value = entry[i, j] * b[j]
                    inner = value if inner is None else inner + value
            total = a[i] * inner if total is None else total + a[i] * inner
        return total

    def axpy(a, s, b):
        return [
            x if y is None else (s * y if x is None else x + s * y) for x, y in zip(a, b)
        ]

    r = [jnp.ones((1, 1), jnp.float32)] + [None] * 4
    p = list(r)
    x = [None] * 5
    rr = entry[0, 0]
    for n in range(ITERS):
        q = image(p)
        step = rr / jnp.maximum(dot(p, q), TINY)
        step = jnp.clip(step, top * (1.0 / HIGH_RATE), top * (1.0 / LOW_RATE))
        x = axpy(x, step, p)
        if n < ITERS - 1:
            r = axpy(r, -step, q)
            fresh = jnp.maximum(dot(r, r), 0.0)
            p = axpy(r, fresh / jnp.maximum(rr, TINY), p)
            rr = fresh
    factors = [c / top for c in x[:4]]
    for j in range(GROUP):
        value = None
        for k in range(4):
            term = factors[k] * vectors[k, j]
            value = term if value is None else value + term
        left[j] = turn(value[:, 0:LANES], OFF[j])
        right[j] = turn(value[:, LANES:], OFF[j])
    lane = lane_of((SLABS, LANES))
    for a in range(PLANES):
        value = None
        for j in range(GROUP):
            for half, ref in ((0, left), (1, right)):
                low = max(SPAN_X * j + LANES * half - LANES * a, 0)
                high = min(SPAN_X * j + (LANES if half == 0 else SPAN_X) - LANES * a, LANES)
                if low >= high:
                    continue
                value = ref[j] if value is None else jnp.where(lane >= low, ref[j], value)
        flat[comb(a), :] = value[0:GROUPS]
    results = [pltpu.make_async_copy(flat, surface_out.reshape(ROWS, LANES), out_sems.at[0])]
    results[0].start()

    for c in range(4):
        for j, device, low, size in runs[c ^ 1]:
            value = came[pl.ds(device * share + 1 + j, size, stride=share), :]
            message[c, low : low + size] = jnp.where(table[c] >= 0, value, 0.0)
    sums = []
    for k in range(levels):
        value = edges[2 * levels - 1] * jnp.concatenate([
            turn(message[0], -k), turn(message[1], -k),
            message[2, k : k + 1], message[2, k + levels : k + levels + 1],
            message[3, k : k + 1], message[3, k + levels : k + levels + 1],
            jnp.zeros((4, LANES), jnp.float32),
        ], axis=0)
        if k:
            value = value + edges[2 * levels + k - 1] * sums[-1]
        sums.append(value * edges[levels - 1 + k])
    for k in range(levels - 2, -1, -1):
        sums[k] = sums[k] + edges[k] * sums[k + 1]
    lane = lane_of((GROUPS, LANES))
    slab = row_of((GROUPS, LANES))
    for k in range(levels):
        if k % per == 0:
            copies[k // per].wait()
        west = sums[k][0:GROUPS]
        east = turn(sums[k][SLABS : SLABS + GROUPS], -17)
        south_l, south_r = sums[k][48:49], sums[k][49:50]
        north_l, north_r = turn(sums[k][50:51], 16), turn(sums[k][51:52], 16)
        for a in range(PLANES):
            rim = None
            for at, source in [(at, west) for at in FIRST_OF[a]] + [(at, east) for at in LAST_OF[a]]:
                rim = jnp.where(lane == at, source, 0.0 if rim is None else rim)
            if rim is None:
                continue
            if a == 0:
                rim = rim + jnp.where(slab == 0, south_l, 0.0)
            if a == 1:
                rim = rim + jnp.where(jnp.logical_and(slab == 0, lane < 112), south_r, 0.0)
            if a == PLANES - 2:
                rim = rim + jnp.where(jnp.logical_and(slab == GROUPS - 1, lane >= 16), north_l, 0.0)
            if a == PLANES - 1:
                rim = rim + jnp.where(slab == GROUPS - 1, jnp.where(lane < 16, north_l, north_r), 0.0)
            rows = comb(k * ROWS + a)
            cells[rows, :] = cells[rows, :] + rim
        if k % per == per - 1:
            step = k // per
            copy = pltpu.make_async_copy(
                cells.at[chunks[step]], tracer_out.at[chunks[step]], out_sems.at[1 + step]
            )
            copy.start()
            results.append(copy)
    for copy in results:
        copy.wait()


def tracer_kernel(
    levels, per, temp_in, zonal_in, merid_in, rates_in, ocean_in,
    inner_out, edges_out,
    temp, zonal, merid, rates, ocean, out, edges,
    te, tw, tn, ts, stepped, border, sems, out_sems,
):
    steps = levels // per
    pairs = [(ocean_in.reshape(ROWS, LANES), ocean)]
    for step in range(steps):
        chunk = pl.ds(step * per * ROWS, per * ROWS)
        pairs += [
            (a.at[chunk], b.at[chunk]) for a, b in ((temp_in, temp), (zonal_in, zonal), (merid_in, merid))
        ]
    copies = fetching(pairs + [(rates_in.reshape((levels - 1) * ROWS, LANES), rates)], sems)
    lane = lane_of((GROUPS, LANES))
    one = lane_of((1, LANES))
    clear_terms(tn, ts)

    copies[0].wait()
    for step in range(steps):
        for copy in copies[1 + 3 * step : 4 + 3 * step]:
            copy.wait()

        def level(k, carry):
            t, u, v = (Level(ref, k * ROWS) for ref in (temp, zonal, merid))
            for a in range(PLANES):
                own = t.plane(a)
                quarter = ADVECT * own
                store_terms(a, own, u.plane(a) * quarter, v.plane(a) * quarter, te, tw, tn, ts)
            for a in range(PLANES):
                own = t.plane(a)
                change = inner_sum(a, te, tw, tn, ts) - 4.0 * DIFFUSE * own
                stepped[k, a] = own + ocean[comb(a), :].astype(jnp.float32) * change
            return carry

        lax.fori_loop(step * per, step * per + per, level, 0)
    copies[-1].wait()

    def block(a, carry):
        for low in range(0, GROUPS, 8):
            size = min(8, GROUPS - low)

            def rows(k):
                return pl.ds(k * ROWS + low * PLANES + a, size, stride=PLANES)

            gains = []
            sums = []
            for k in range(levels):
                value = stepped[k, a, low : low + size]
                pivot = 1.0
                if k > 0:
                    pivot = pivot + upper - upper * gains[-1]
                    value = value + upper * sums[-1]
                if k < levels - 1:
                    lower = rates[rows(k), :]
                    inverse = 1.0 / (pivot + lower)
                    gains.append(lower * inverse)
                    upper = lower
                else:
                    inverse = 1.0 / pivot
                sums.append(value * inverse)
            result = sums[-1]
            out[rows(levels - 1), :] = result
            for k in range(levels - 2, -1, -1):
                result = sums[k] + gains[k] * result
                out[rows(k), :] = result
        return carry

    lax.fori_loop(0, PLANES, block, 0)

    def edge(ref, base, at):
        def get(a):
            return ref[comb(base + a), :].astype(jnp.float32)

        border[0:GROUPS] = choose(START, lane, get)
        border[SLABS : SLABS + GROUPS] = turn(choose(LAST, lane, get), 17)
        border[48:50] = ref[base : base + 2, :].astype(jnp.float32)
        rows = ref[base + ROWS - 2 : base + ROWS, :].astype(jnp.float32)
        border[50:51] = turn(jnp.where(one >= 16, rows[0:1], rows[1:2]), -16)
        border[51:52] = turn(rows[1:2], -16)
        edges[at] = border[...]

    border[...] = jnp.zeros_like(border)
    edge(ocean, 0, 2 * levels - 1)
    gain = None
    for k in range(levels):
        pivot = 1.0
        if k > 0:
            upper = edges[2 * levels + k - 1]
            pivot = pivot + upper - upper * gain
        if k < levels - 1:
            edge(rates, k * ROWS, 2 * levels + k)
            lower = edges[2 * levels + k]
            inverse = 1.0 / (pivot + lower)
            gain = lower * inverse
            edges[k] = gain
        else:
            inverse = 1.0 / pivot
        edges[levels - 1 + k] = inverse
        if k == 0:
            results = fetching([(out, inner_out)], out_sems)
    results.append(pltpu.make_async_copy(edges, edges_out, out_sems.at[1]))
    results[-1].start()
    for copy in results:
        copy.wait()


def on_device(
    thermal_anomaly,
    zonal_flow_ratio,
    meridional_flow_ratio,
    diffusion_rates,
    ocean_bottom_scaled,
    ocean_indicator,
    operator_diagonal,
    elevation_source,
    block_positions,
):
    levels, cells = thermal_anomaly.shape[1:]
    nx = lax.axis_size("gx")
    ny = lax.axis_size("gy")
    count = block_positions.shape[0]
    planes = (ocean_bottom_scaled, ocean_indicator, operator_diagonal, elevation_source)
    depth, ocean, diag, source = planes
    f32 = jnp.float32
    per = next(n for n in (4, 2, 6, levels) if levels % n == 0 and n * ROWS % 8 == 0)
    steps = levels // per
    large = pltpu.CompilerParams(vmem_limit_bytes=BUDGET)
    small = pltpu.CompilerParams(vmem_limit_bytes=BUDGET // 3)
    temp, zonal, merid = (
        array.reshape(levels * ROWS, LANES)
        for array in (thermal_anomaly, zonal_flow_ratio, meridional_flow_ratio)
    )
    rates = diffusion_rates.reshape(levels - 1, 1, cells)
    hbm = pl.BlockSpec(memory_space=pltpu.HBM)
    here = pl.BlockSpec(memory_space=pltpu.VMEM)

    def vmem(*shape, kind=f32):
        return pltpu.VMEM(shape, kind)

    def out(*shape, kind=f32):
        return jax.ShapeDtypeStruct(shape, kind)

    def sems(number):
        return pltpu.SemaphoreType.DMA((number,))

    deep = vmem(levels * ROWS, LANES)
    flat = vmem(ROWS, LANES)
    flat_int = vmem(ROWS, LANES, kind=jnp.int32)
    plane = vmem(PLANES, GROUPS, LANES)
    tall = vmem(PLANES, 40, LANES)
    numbers = pltpu.SMEM((count,), jnp.int32)
    number_pieces, _ = pieces_of(levels, count)
    slot = RIM_ROWS + number_pieces
    share = 1 + number_pieces
    part, own, slots, table, around = pl.pallas_call(
        functools.partial(forcing_kernel, levels, per, nx, ny),
        in_specs=[SMEM] + [hbm] * 7,
        out_specs=[hbm] * 3 + [SMEM] * 2,
        out_shape=[
            out(ROWS, LANES), out(56, LANES), out(count, 1, slot * LANES),
            out(8, kind=jnp.int32), out(4 * count, kind=jnp.int32),
        ],
        scratch_shapes=[deep] * 3 + [flat, flat_int, flat, flat]
        + [flat, vmem(56, LANES), vmem(count * slot, LANES)]
        + [flat] * 3 + [plane] * 3 + [tall] * 2
        + [vmem(4, 2 * levels, LANES), numbers, sems(3 * steps + 4), sems(3)],
        compiler_params=large,
        name="forcing",
    )(block_positions, temp, zonal, merid, depth, ocean, diag, source)
    rims = lax.all_to_all(slots, BOTH, 0, 0, tiled=True)

    inner, edges = pl.pallas_call(
        functools.partial(tracer_kernel, levels, per),
        in_specs=[hbm] * 5,
        out_specs=[hbm] * 2,
        out_shape=[out(levels * ROWS, LANES), out(3 * levels - 1, EDGE, LANES)],
        scratch_shapes=[deep] * 3 + [vmem((levels - 1) * ROWS, LANES), flat_int, deep]
        + [vmem(3 * levels - 1, EDGE, LANES)]
        + [plane] * 2 + [tall] * 2
        + [vmem(levels, PLANES, GROUPS, LANES), vmem(EDGE, LANES), sems(3 * steps + 2), sems(2)],
        compiler_params=large,
        name="tracer",
    )(temp, zonal, merid, rates, ocean)

    rims, edges = lax.optimization_barrier((rims, edges))
    extended = vmem(GROUP, SLABS, 2 * LANES)
    vectors, hand = pl.pallas_call(
        functools.partial(solve_kernel, levels, ny),
        in_specs=[SMEM, SMEM] + [here] * 6,
        out_specs=[here] * 2,
        out_shape=[out(4, GROUP, SLABS, 2 * LANES), out(count, 1, share * LANES)],
        scratch_shapes=[vmem(WIDE, LANES)] * 3 + [vmem(SLABS, LANES)] * 4 + [extended] * 5 + [vmem(16, LANES)],
        compiler_params=small,
        name="vectors",
    )(table, around, rims, own, part, depth, ocean, diag)
    hands = lax.all_to_all(hand, BOTH, 0, 0, tiled=True)

    new_temp, surface = pl.pallas_call(
        functools.partial(finish_kernel, levels, per),
        in_specs=[SMEM] + [here] * 3 + [hbm],
        out_specs=[hbm] * 2,
        out_shape=[out(levels * ROWS, LANES), out(1, cells)],
        input_output_aliases={4: 0},
        scratch_shapes=[
            deep, flat, vmem(GROUP, SLABS, LANES), vmem(GROUP, SLABS, LANES), vmem(4, 2 * levels, LANES),
            sems(steps), sems(1 + steps),
        ],
        compiler_params=small,
        name="finish",
    )(table, hands, vectors, edges, inner)
    return new_temp.reshape(1, levels, cells), surface


def solution(mesh):
    deep = P(BOTH, None, None)
    flat = P(BOTH, None)
    return jax.shard_map(
        on_device,
        mesh=mesh,
        in_specs=(deep, deep, deep, deep, flat, flat, flat, flat, P()),
        out_specs=(deep, flat),
        check_vma=False,
    )
```

```python
import functools

import jax
import jax.numpy as jnp
from jax import lax
from jax.experimental import pallas as pl
from jax.experimental.pallas import tpu as pltpu
from jax.sharding import PartitionSpec as P

ITERS = 4
SPAN_X = 240
SPAN_Y = 160
RIM = 4
ADVECT = 0.25
DIFFUSE = 0.12
STERIC = 0.5
LOW_RATE = 0.05
HIGH_RATE = 32.5
ROOTS = (0.02, 0.35, 0.1, 0.2)
STRETCH = 4.0
TINY = 1e-30
BOTH = ("gx", "gy")
SIDES = ((-1, 0), (1, 0), (0, -1), (0, 1), (-1, -1), (1, -1), (-1, 1), (1, 1))

LANES = 128
GROUP = 8
GROUPS = SPAN_Y // GROUP
PLANES = GROUP * SPAN_X // LANES
ROWS = GROUPS * PLANES
SLABS = GROUPS + 4
WIDE = SLABS * PLANES
START = [SPAN_X * j // LANES for j in range(GROUP)]
OFF = [SPAN_X * j % LANES for j in range(GROUP)]
LAST = [(SPAN_X * j + SPAN_X - 1) // LANES for j in range(GROUP)]
END = [(SPAN_X * j + SPAN_X - 1) % LANES for j in range(GROUP)]
FIRST_OF = [[OFF[j] for j in range(GROUP) if START[j] == a] for a in range(PLANES)]
LAST_OF = [[END[j] for j in range(GROUP) if LAST[j] == a] for a in range(PLANES)]
RIM_ROWS = 24
EDGE = 32
BUDGET = 56 * 1024 * 1024


def turn(value, shift, axis=1):
    shift = shift % value.shape[axis]
    return value if shift == 0 else pltpu.roll(value, shift, axis)


def fetching(pairs, sems):
    copies = [pltpu.make_async_copy(a, b, sems.at[n]) for n, (a, b) in enumerate(pairs)]
    for copy in copies:
        copy.start()
    return copies


def pieces_of(levels, count):
    rows = 2 * levels
    number = -(-4 * rows // count)
    runs = [[] for _ in range(4)]
    for c in range(4):
        for j in range(number):
            low, high = max(c * rows, j * count), min((c + 1) * rows, (j + 1) * count)
            if low < high:
                runs[c].append((j, low - j * count, low - c * rows, high - low))
    return number, runs


class Level:
    def __init__(self, ref, base):
        self.ref, self.base = ref, base

    def plane(self, a):
        return self.ref[comb(self.base + a), :]

    def rows(self, low, size):
        return self.ref[pl.ds(self.base + low, size), :]


def lane_of(shape):
    return lax.broadcasted_iota(jnp.int32, shape, len(shape) - 1)


def row_of(shape):
    return lax.broadcasted_iota(jnp.int32, shape, 0)


def comb(a, count=GROUPS):
    return pl.ds(a, count, stride=PLANES)


def drop(value, lanes, lane):
    for at in lanes:
        value = jnp.where(lane == at, 0.0, value)
    return value


def store_terms(a, temp, flow_x, flow_y, te, tw, tn, ts):
    spread = DIFFUSE * temp
    te[a] = spread - flow_x
    tw[a] = spread + flow_x
    tn[a, 8 : 8 + GROUPS] = spread - flow_y
    ts[a, 8 : 8 + GROUPS] = spread + flow_y


def clear_terms(tn, ts):
    none = jnp.zeros((PLANES, 1, LANES), jnp.float32)
    for ref in (tn, ts):
        ref[:, 7:8] = none
        ref[:, 8 + GROUPS : 9 + GROUPS] = none


def inner_sum(a, te, tw, tn, ts):
    lane = lane_of((GROUPS, LANES))
    here = te[a]
    east = here if a == PLANES - 1 else jnp.where(lane == 0, te[a + 1], here)
    east = drop(turn(east, -1), LAST_OF[a], lane)
    here = tw[a]
    west = here if a == 0 else jnp.where(lane == LANES - 1, tw[a - 1], here)
    west = drop(turn(west, 1), FIRST_OF[a], lane)

    def plane(ref, at):
        down = 8 + (at >= PLANES) - (at < 0)
        return ref[at % PLANES, down : down + GROUPS]

    north = turn(jnp.where(lane >= LANES - 16, plane(tn, a + 1), plane(tn, a + 2)), 16)
    south = turn(jnp.where(lane < 16, plane(ts, a - 1), plane(ts, a - 2)), -16)
    return east + west + north + south


def choose(planes, lane, get):
    value = get(planes[0])
    for j in range(1, GROUP):
        low = (OFF[j] - (32 if planes is LAST else 0)) % LANES
        value = jnp.where(jnp.logical_and(lane >= low, lane < low + 16), get(planes[j]), value)
    return value


def forcing_kernel(
    levels, per, tiles_x, tiles_y,
    pos, temp_in, zonal_in, merid_in, depth_in, ocean_in, diag_in, source_in,
    part_out, own_out, slots_out, table, around,
    temp, zonal, merid, depth, ocean, diag, source, part, own, slots,
    st, sx, sy, pt, te, tw, tn, ts, edges, holder, sems, out_sems,
):
    count = pos.shape[0]
    steps = levels // per
    number_pieces, runs = pieces_of(levels, count)
    slot = RIM_ROWS + number_pieces
    pairs = []
    for step in range(steps):
        chunk = pl.ds(step * per * ROWS, per * ROWS)
        pairs += [
            (a.at[chunk], b.at[chunk]) for a, b in ((temp_in, temp), (zonal_in, zonal), (merid_in, merid))
        ]
    pairs += [
        (a.reshape(ROWS, LANES), b)
        for a, b in ((source_in, source), (ocean_in, ocean), (depth_in, depth), (diag_in, diag))
    ]
    copies = fetching(pairs, sems)
    results = []

    def send(value, target):
        copy = pltpu.make_async_copy(value, target, out_sems.at[len(results)])
        copy.start()
        results.append(copy)

    lane = lane_of((GROUPS, LANES))
    one = lane_of((1, LANES))
    q = lane % 16
    edges[...] = jnp.zeros_like(edges)

    def number(d, carry):
        holder[pos[d]] = d
        return carry

    lax.fori_loop(0, count, number, 0)
    me = lax.axis_index("gx") * tiles_y + lax.axis_index("gy")
    here = pos[me]
    row = here // tiles_x
    column = here % tiles_x
    sides = []
    for c, (dx, dy) in enumerate(SIDES):
        there = row + dy
        inside = jnp.logical_and(there >= 0, there < tiles_y)
        target = jnp.where(inside, there, 0) * tiles_x + (column + dx + tiles_x) % tiles_x
        device = jnp.where(inside, holder[target], -1)
        table[c] = device
        sides.append(device)

    def look(y, carry):
        line = [holder[y * tiles_x + x] for x in range(tiles_x)]
        below = [holder[jnp.maximum(y - 1, 0) * tiles_x + x] for x in range(tiles_x)]
        above = [holder[jnp.minimum(y + 1, tiles_y - 1) * tiles_x + x] for x in range(tiles_x)]
        for x, device in enumerate(line):
            around[device] = line[x - 1]
            around[count + device] = line[(x + 1) % tiles_x]
            around[2 * count + device] = jnp.where(y > 0, below[x], -1)
            around[3 * count + device] = jnp.where(y < tiles_y - 1, above[x], -1)
        return carry

    lax.fori_loop(0, tiles_y, look, 0)
    clear_terms(tn, ts)

    def add(flats, low, size, fresh):
        rows = pl.ds(low, size)
        total = [None] * 3
        for t, u, v in zip(*flats):
            t = t.rows(low, size)
            new = (t, t * u.rows(low, size), t * v.rows(low, size))
            total = [b if a is None else a + b for a, b in zip(total, new)]
        for ref, value in zip((st, sx, sy), total):
            ref[rows, :] = value if fresh else ref[rows, :] + value

    for step in range(steps):
        for copy in copies[3 * step : 3 * step + 3]:
            copy.wait()
        flats = [
            [Level(ref, (step * per + n) * ROWS) for n in range(per)] for ref in (temp, zonal, merid)
        ]

        def some(m, carry):
            add(flats, pl.multiple_of(m * 8, 8), 8, step == 0)
            return carry

        lax.fori_loop(0, ROWS // 8, some, 0, unroll=4)
        if ROWS % 8:
            add(flats, ROWS - ROWS % 8, ROWS % 8, step == 0)

        for n in range(per):
            k = step * per + n
            t, u, v = (flat[n] for flat in flats)

            def term(planes, sign):
                own = choose(planes, lane, t.plane)
                flow = choose(planes, lane, u.plane)
                return DIFFUSE * own + sign * ADVECT * (flow * own)

            edges[0, 0:GROUPS] = jnp.where(q == k, turn(term(START, -1.0), k), edges[0, 0:GROUPS])
            edges[1, 0:GROUPS] = jnp.where(q == k, turn(term(LAST, 1.0), k + 17), edges[1, 0:GROUPS])
            rows = t.rows(0, 2)
            rows = DIFFUSE * rows - ADVECT * (v.rows(0, 2) * rows)
            edges[2, k : k + 1] = rows[0:1]
            edges[2, k + levels : k + levels + 1] = rows[1:2]
            rows = t.rows(ROWS - 2, 2)
            rows = DIFFUSE * rows + ADVECT * (v.rows(ROWS - 2, 2) * rows)
            edges[3, k : k + 1] = turn(jnp.where(one >= 16, rows[0:1], rows[1:2]), -16)
            edges[3, k + levels : k + levels + 1] = turn(rows[1:2], -16)

    for c in range(4):
        for j, device, low, size in runs[c]:
            slots[pl.ds(device * slot + RIM_ROWS + j, size, stride=slot), :] = edges[c, low : low + size]

    for copy in copies[3 * steps :]:
        copy.wait()

    def wet_of(rows):
        return ocean[rows, :].astype(jnp.float32)

    def masked(rows):
        return depth[rows, :] * wet_of(rows)

    for a in range(PLANES):
        total = st[comb(a), :]
        pt[a] = total
        store_terms(a, total, ADVECT * sx[comb(a), :], ADVECT * sy[comb(a), :], te, tw, tn, ts)
    for a in range(PLANES):
        total = pt[a]
        wet = wet_of(comb(a))
        change = inner_sum(a, te, tw, tn, ts) - 4.0 * DIFFUSE * total
        part[comb(a), :] = source[comb(a), :] + (STERIC / levels) * wet * (total + wet * change)
    send(part, part_out)

    def mix(values):
        value = values[4]
        for at, low in ((3, 12), (2, 11), (1, 8), (0, 4)):
            value = jnp.where(q < low, values[at], value)
        return value

    def flat(ref):
        return lambda a: ref[comb(a), :]

    def ends(planes, low):
        value = tn[planes[0], 8 : 8 + GROUPS]
        last = jnp.logical_and(lane >= low, lane < low + 16)
        return jnp.where(last, ts[planes[7], 8 : 8 + GROUPS], value)

    pack_w = mix([
        choose(START, lane, flat(part)),
        turn(choose(START, lane, lambda a: masked(comb(a))), 4),
        turn(choose(START, lane, flat(diag)), 8),
        turn(choose(START, lane, lambda a: te[a]), 11),
        turn(ends(START, OFF[7]), 12),
    ])
    pack_e = mix([
        turn(choose(LAST, lane, flat(part)), 20),
        turn(choose(LAST, lane, lambda a: masked(comb(a))), 24),
        turn(choose(LAST, lane, flat(diag)), 27),
        turn(choose(LAST, lane, lambda a: tw[a]), 28),
        turn(ends(LAST, LANES - 16), 32),
    ])
    own[0:GROUPS] = pack_w
    own[SLABS : SLABS + GROUPS] = pack_e
    north_l = tn[0, 8:9]
    north_r = tn[1, 8:9]
    south_13 = ts[PLANES - 2, 7 + GROUPS : 8 + GROUPS]
    south_14 = ts[PLANES - 1, 7 + GROUPS : 8 + GROUPS]
    south_l = turn(jnp.where(one >= 16, south_13, south_14), -16)
    south_r = turn(south_14, -16)
    own[48:49] = north_l
    own[49:50] = north_r
    own[50:51] = south_l
    own[51:52] = south_r
    send(own, own_out)
    deep = jnp.max(masked(slice(0, ROWS)), axis=(0, 1), keepdims=True)
    top = jnp.max(diag[...], axis=(0, 1), keepdims=True) + 8.0 * deep * deep
    top = jnp.broadcast_to(top, (1, LANES))

    slots[pl.ds(RIM_ROWS - 1, count, stride=slot), :] = jnp.broadcast_to(top, (count, LANES))
    eight = lane_of((8, LANES))
    eighth = row_of((8, LANES))
    for c, first, rows_l, rows_r in ((2, True, north_l, north_r), (3, False, south_l, south_r)):
        base = 0 if first else ROWS - 8
        spare = jnp.logical_and(eighth == 7, eight >= 64) if first else jnp.logical_and(eighth == 0, eight < 64)
        g = 0 if first else GROUPS - 1
        blocks = []
        block = slice(base, base + 8)
        for value, at in ((part[block, :], g), (masked(block), SLABS + g)):
            extra = jnp.broadcast_to(turn(own[at : at + 1], -16), (8, LANES))
            blocks.append(jnp.where(spare, extra, value))
        low = 0 if first else ROWS - 6
        diag_rows = diag[low : low + 6, :]
        last_row = jnp.where(one == LANES - 1, top, rows_r)

        @pl.when(sides[c] >= 0)
        def _(c=c, blocks=blocks, diag_rows=diag_rows, rows_l=rows_l, last_row=last_row):
            at = sides[c] * slot
            slots[pl.ds(at, 8), :] = blocks[0]
            slots[pl.ds(at + 8, 8), :] = blocks[1]
            slots[pl.ds(at + 16, 6), :] = diag_rows
            slots[pl.ds(at + 22, 1), :] = rows_l
            slots[pl.ds(at + 23, 1), :] = last_row

    slots[pl.ds(sides[0] * slot, GROUPS), :] = pack_w
    slots[pl.ds(sides[1] * slot, GROUPS), :] = pack_e
    for c, at in ((4, 0), (5, SLABS), (6, GROUPS - 1), (7, SLABS + GROUPS - 1)):
        @pl.when(sides[c] >= 0)
        def _(c=c, at=at):
            slots[pl.ds(sides[c] * slot, 1), :] = own[at : at + 1]
    send(slots, slots_out.reshape(count * slot, LANES))
    for copy in results:
        copy.wait()


SMEM = pl.BlockSpec(memory_space=pltpu.SMEM)


def solve_kernel(
    levels, tiles_y,
    table, around, rims, own, part, depth, ocean, diag,
    vectors, hands,
    fb, fd, fg, pw, pe, ow, oe, ed, eg, we, wn, last, rows,
):
    count = rims.shape[0]
    number_pieces, _ = pieces_of(levels, count)
    slot = RIM_ROWS + number_pieces
    share = 1 + number_pieces
    came = rims.reshape(count * slot, LANES)
    hand = hands.reshape(count * share, LANES)
    depth, ocean, diag = (ref.reshape(ROWS, LANES) for ref in (depth, ocean, diag))
    lane = lane_of((SLABS, LANES))
    slab = row_of((SLABS, LANES))
    one = lane_of((1, LANES))
    src = [table[c] for c in range(8)]

    def fetch(c, low, high):
        value = came[pl.ds(jnp.maximum(src[c], 0) * slot + low, high - low), :]
        return jnp.where(src[c] >= 0, value, 0.0)

    me = lax.axis_index("gx") * tiles_y + lax.axis_index("gy")
    for n in range(number_pieces):
        side = jnp.minimum((n * count + me) // (2 * levels), 3)
        base = (side + 1 - 2 * (side % 2)) * count

        def relay(d, carry, n=n, base=base):
            row = jnp.maximum(around[base + d], 0) * slot + RIM_ROWS + n
            hand[pl.ds(d * share + 1 + n, 1), :] = came[pl.ds(row, 1), :]
            return carry

        lax.fori_loop(0, count, relay, 0, unroll=4)

    none = jnp.zeros((WIDE - ROWS + 4, LANES), jnp.float32)
    for ref in (fb, fd, fg):
        ref[ROWS - 4 : WIDE] = none
    fb[0:ROWS] = part[...]
    fd[0:ROWS] = depth[...] * ocean[...].astype(jnp.float32)
    fg[0:ROWS] = diag[...]
    for ref, low, high in ((fb, 0, 8), (fd, 8, 16), (fg, 16, 22)):
        ref[ROWS : ROWS + high - low] = fetch(3, low, high)
        ref[WIDE - high + low : WIDE] = fetch(2, low, high)
    empty = jnp.zeros((SLABS, LANES), jnp.float32)
    for ref, side, north, south in ((pw, 0, 6, 4), (pe, 1, 7, 5)):
        ref[...] = empty
        ref[0:GROUPS] = fetch(side, 0, GROUPS)
        ref[GROUPS : GROUPS + 1] = fetch(north, 0, 1)
        ref[SLABS - 1 : SLABS] = fetch(south, 0, 1)
    for ref, at, north, south in ((ow, 0, 7, 0), (oe, SLABS, 15, 8)):
        ref[...] = empty
        ref[0:GROUPS] = own[at : at + GROUPS]
        ref[GROUPS : GROUPS + 1] = turn(fetch(3, north, north + 1), 16)
        ref[SLABS - 1 : SLABS] = turn(fetch(2, south, south + 1), 16)

    def spread(ref, j):
        a = START[j]
        first, second = ref[comb(a, SLABS), :], ref[comb(a + 1, SLABS), :]
        third = ref[comb(a + 2, SLABS), :] if a + 2 < PLANES else second
        left = turn(jnp.where(lane >= OFF[j], first, second), -OFF[j])
        right = turn(jnp.where(lane >= OFF[j], second, third), -OFF[j])
        return left, right

    def seam_row(left, right, slab_at, lanes_at):
        east = turn(pe[slab_at : slab_at + 1], 112 - lanes_at)
        west = turn(pw[slab_at : slab_at + 1], 124 - lanes_at)
        right = jnp.where(one < 112, right, jnp.where(one < 116, east, jnp.where(one >= 124, west, 0.0)))
        return jnp.broadcast_to(left, (SLABS, LANES)), jnp.broadcast_to(right, (SLABS, LANES))

    seams = {
        0: ((0, seam_row(fetch(2, 22, 23), fetch(2, 23, 24), SLABS - 1, 28)),
            (GROUPS, seam_row(own[50:51], own[51:52], GROUPS - 1, 28))),
        GROUP - 1: ((GROUPS - 1, seam_row(fetch(3, 22, 23), fetch(3, 23, 24), GROUPS, 12)),
                    (SLABS - 1, seam_row(own[48:49], own[49:50], 0, 12))),
    }
    weight = STERIC / levels
    for j in range(GROUP):
        o = OFF[j]

        def rim(right, q, width):
            east = turn(pe[...], 112 - o - q)
            west = turn(pw[...], 128 - width - o - q)
            value = jnp.where(lane < 112 + width, east, jnp.where(lane >= 128 - width, west, 0.0))
            return jnp.where(lane < 112, right, value)

        left, right = spread(fd, j)
        right = rim(right, 4, 4)
        wet_l = jnp.where(left > 0, weight, 0.0)
        wet_r = jnp.where(right > 0, weight, 0.0)
        ed[j, :, 0:LANES] = left
        ed[j, :, LANES:] = right
        left, right = spread(fg, j)
        eg[j, :, 0:LANES] = left
        eg[j, :, LANES:] = rim(right, 8, 3)
        left, right = spread(fb, j)
        right = rim(right, 0, 4)
        seam_l = jnp.where(lane == 0, turn(pw[...], -o - 11), 0.0)
        seam_r = jnp.where(lane == 127, turn(ow[...], 127 - o - 11), 0.0)
        seam_r = jnp.where(lane == 111, turn(pe[...], 111 - o - 11), seam_r)
        seam_r = jnp.where(lane == 112, turn(oe[...], 112 - o - 11), seam_r)
        for at, (row_l, row_r) in seams.get(j, ()):
            seam_l = seam_l + jnp.where(slab == at, row_l, 0.0)
            seam_r = seam_r + jnp.where(slab == at, row_r, 0.0)
        vectors[0, j, :, 0:LANES] = left + wet_l * seam_l
        vectors[0, j, :, LANES:] = right + wet_r * seam_r

    for j in range(GROUP):
        d = ed[j]
        we[j] = d * turn(d, -1)
        above = ed[j + 1] if j < GROUP - 1 else turn(ed[0], -1, 0)
        wn[j] = d * above

    top = jnp.max(came[pl.ds(RIM_ROWS - 1, count, stride=slot), :], axis=0, keepdims=True)
    top = jnp.max(jnp.where(one == LANES - 1, top, 0.0), axis=1, keepdims=True)
    scale = STRETCH / top

    big = (SLABS, 2 * LANES)
    mine = jnp.logical_and(row_of(big) < GROUPS, lane_of(big) < SPAN_X)
    pair = 0
    for k in range(5):
        sums = [None] * (k + 1)
        new = last if k == 4 else vectors.at[k]
        if k:
            v = vectors.at[k - 1]
            flow_below = wn[GROUP - 1] * (v[GROUP - 1] - turn(v[0], -1, 0))
            flow_below = turn(flow_below, 1, 0)
        for j in range(GROUP):
            if k:
                here = v[j]
                above = v[j + 1] if j < GROUP - 1 else turn(v[0], -1, 0)
                flow_x = we[j] * (here - turn(here, -1))
                flow_y = wn[j] * (here - above)
                image = eg[j] * here + (flow_x - turn(flow_x, 1)) + (flow_y - flow_below)
                fresh = scale * image - (STRETCH * ROOTS[k - 1]) * here
                flow_below = flow_y
                new[j] = fresh
            else:
                fresh = new[j]
            held = jnp.where(mine, fresh, 0.0)
            for i in range(k + 1):
                other = vectors[i, j] if i < k else held
                value = held * other
                sums[i] = value if sums[i] is None else sums[i] + value
        for i in range(k + 1):
            rows[pair : pair + 1] = jnp.sum(sums[i][:, 0:LANES] + sums[i][:, LANES:], axis=0, keepdims=True)
            pair += 1
    rows[pair : pair + 1] = jnp.where(one == 0, top, 0.0)
    total = jnp.sum(rows[...], axis=1, keepdims=True)
    spot = row_of((16, LANES)) == lane_of((16, LANES))
    line = jnp.sum(jnp.where(spot, total, 0.0), axis=0, keepdims=True)
    hand[pl.ds(0, count, stride=share), :] = jnp.broadcast_to(line, (count, LANES))


def finish_kernel(
    levels, per, table, hands, vectors, edges, inner, tracer_out, surface_out,
    cells, flat, left, right, message, out_sems,
):
    count = hands.shape[0]
    number_pieces, runs = pieces_of(levels, count)
    share = 1 + number_pieces
    came = hands.reshape(count * share, LANES)
    steps = levels // per
    chunks = [pl.ds(step * per * ROWS, per * ROWS) for step in range(steps)]
    row = jnp.sum(came[pl.ds(0, count, stride=share), :], axis=0, keepdims=True)
    one = lane_of((1, LANES))
    entry = {}
    pair = 0
    for k in range(5):
        for i in range(k + 1):
            value = jnp.sum(jnp.where(one == pair, row, 0.0), axis=1, keepdims=True)
            entry[i, k] = entry[k, i] = value
            pair += 1
    top = jnp.sum(jnp.where(one == pair, row, 0.0), axis=1, keepdims=True) * (1.0 / count)

    def image(c):
        out = [None] * 5
        for k in range(4):
            if c[k] is None:
                continue
            low = ROOTS[k] * c[k]
            out[k] = low if out[k] is None else out[k] + low
            out[k + 1] = (1.0 / STRETCH) * c[k]
        return out

    def dot(a, b):
        total = None
        for i in range(5):
            if a[i] is None:
                continue
            inner = None
            for j in range(5):
                if b[j] is not None:
                    value = entry[i, j] * b[j]
                    inner = value if inner is None else inner + value
            total = a[i] * inner if total is None else total + a[i] * inner
        return total

    def axpy(a, s, b):
        return [
            x if y is None else (s * y if x is None else x + s * y) for x, y in zip(a, b)
        ]

    r = [jnp.ones((1, 1), jnp.float32)] + [None] * 4
    p = list(r)
    x = [None] * 5
    rr = entry[0, 0]
    for n in range(ITERS):
        q = image(p)
        step = rr / jnp.maximum(dot(p, q), TINY)
        step = jnp.clip(step, top * (1.0 / HIGH_RATE), top * (1.0 / LOW_RATE))
        x = axpy(x, step, p)
        if n < ITERS - 1:
            r = axpy(r, -step, q)
            fresh = jnp.maximum(dot(r, r), 0.0)
            p = axpy(r, fresh / jnp.maximum(rr, TINY), p)
            rr = fresh
    factors = [c / top for c in x[:4]]
    for j in range(GROUP):
        value = None
        for k in range(4):
            term = factors[k] * vectors[k, j]
            value = term if value is None else value + term
        left[j] = turn(value[:, 0:LANES], OFF[j])
        right[j] = turn(value[:, LANES:], OFF[j])
    lane = lane_of((SLABS, LANES))
    for a in range(PLANES):
        value = None
        for j in range(GROUP):
            for half, ref in ((0, left), (1, right)):
                low = max(SPAN_X * j + LANES * half - LANES * a, 0)
                high = min(SPAN_X * j + (LANES if half == 0 else SPAN_X) - LANES * a, LANES)
                if low >= high:
                    continue
                value = ref[j] if value is None else jnp.where(lane >= low, ref[j], value)
        flat[comb(a), :] = value[0:GROUPS]
    results = [pltpu.make_async_copy(flat, surface_out.reshape(ROWS, LANES), out_sems.at[0])]
    results[0].start()

    for c in range(4):
        for j, device, low, size in runs[c ^ 1]:
            value = came[pl.ds(device * share + 1 + j, size, stride=share), :]
            message[c, low : low + size] = jnp.where(table[c] >= 0, value, 0.0)
    second = lane_of((SLABS, LANES)) % 16 == 1
    sums = []
    for k in range(levels):
        value = edges[2 * levels - 1] * jnp.concatenate([
            jnp.where(second, turn(message[1], 1 - k), turn(message[0], -k)),
            message[2, k : k + 1], message[2, k + levels : k + levels + 1],
            message[3, k : k + 1], message[3, k + levels : k + levels + 1],
            jnp.zeros((EDGE - SLABS - 4, LANES), jnp.float32),
        ], axis=0)
        if k:
            value = value + edges[2 * levels + k - 1] * sums[-1]
        sums.append(value * edges[levels - 1 + k])
    for k in range(levels - 2, -1, -1):
        sums[k] = sums[k] + edges[k] * sums[k + 1]
    lane = lane_of((GROUPS, LANES))
    slab = row_of((GROUPS, LANES))
    for k in range(levels):
        west = sums[k][0:GROUPS]
        east = turn(west, -18)
        south_l, south_r = sums[k][SLABS : SLABS + 1], sums[k][SLABS + 1 : SLABS + 2]
        north_l = turn(sums[k][SLABS + 2 : SLABS + 3], 16)
        north_r = turn(sums[k][SLABS + 3 : SLABS + 4], 16)
        for a in range(PLANES):
            rim = None
            for at, source in [(at, west) for at in FIRST_OF[a]] + [(at, east) for at in LAST_OF[a]]:
                rim = jnp.where(lane == at, source, 0.0 if rim is None else rim)
            rows = comb(k * ROWS + a)
            if rim is None:
                cells[rows, :] = inner[rows, :]
                continue
            if a == 0:
                rim = rim + jnp.where(slab == 0, south_l, 0.0)
            if a == 1:
                rim = rim + jnp.where(jnp.logical_and(slab == 0, lane < 112), south_r, 0.0)
            if a == PLANES - 2:
                rim = rim + jnp.where(jnp.logical_and(slab == GROUPS - 1, lane >= 16), north_l, 0.0)
            if a == PLANES - 1:
                rim = rim + jnp.where(slab == GROUPS - 1, jnp.where(lane < 16, north_l, north_r), 0.0)
            cells[rows, :] = inner[rows, :] + rim
        if k % per == per - 1:
            step = k // per
            copy = pltpu.make_async_copy(
                cells.at[chunks[step]], tracer_out.at[chunks[step]], out_sems.at[1 + step]
            )
            copy.start()
            results.append(copy)
    for copy in results:
        copy.wait()


def tracer_kernel(
    levels, per, temp_in, zonal_in, merid_in, rates_in, ocean_in,
    out, edges,
    temp, zonal, merid, rates, ocean,
    te, tw, tn, ts, stepped, border, sems,
):
    steps = levels // per
    pairs = [(ocean_in.reshape(ROWS, LANES), ocean)]
    for step in range(steps):
        chunk = pl.ds(step * per * ROWS, per * ROWS)
        pairs += [
            (a.at[chunk], b.at[chunk]) for a, b in ((temp_in, temp), (zonal_in, zonal), (merid_in, merid))
        ]
    copies = fetching(pairs + [(rates_in.reshape((levels - 1) * ROWS, LANES), rates)], sems)
    lane = lane_of((GROUPS, LANES))
    one = lane_of((1, LANES))
    clear_terms(tn, ts)

    copies[0].wait()
    for step in range(steps):
        for copy in copies[1 + 3 * step : 4 + 3 * step]:
            copy.wait()

        def level(k, carry):
            t, u, v = (Level(ref, k * ROWS) for ref in (temp, zonal, merid))
            for a in range(PLANES):
                own = t.plane(a)
                quarter = ADVECT * own
                store_terms(a, own, u.plane(a) * quarter, v.plane(a) * quarter, te, tw, tn, ts)
            for a in range(PLANES):
                own = t.plane(a)
                change = inner_sum(a, te, tw, tn, ts) - 4.0 * DIFFUSE * own
                stepped[k, a] = own + ocean[comb(a), :].astype(jnp.float32) * change
            return carry

        lax.fori_loop(step * per, step * per + per, level, 0)
    copies[-1].wait()

    def block(a, carry):
        for low in range(0, GROUPS, 8):
            size = min(8, GROUPS - low)

            def rows(k):
                return pl.ds(k * ROWS + low * PLANES + a, size, stride=PLANES)

            gains = []
            sums = []
            for k in range(levels):
                value = stepped[k, a, low : low + size]
                pivot = 1.0
                if k > 0:
                    pivot = pivot + upper - upper * gains[-1]
                    value = value + upper * sums[-1]
                if k < levels - 1:
                    lower = rates[rows(k), :]
                    inverse = 1.0 / (pivot + lower)
                    gains.append(lower * inverse)
                    upper = lower
                else:
                    inverse = 1.0 / pivot
                sums.append(value * inverse)
            result = sums[-1]
            out[rows(levels - 1), :] = result
            for k in range(levels - 2, -1, -1):
                result = sums[k] + gains[k] * result
                out[rows(k), :] = result
        return carry

    lax.fori_loop(0, PLANES, block, 0)

    def edge(ref, base, at):
        def get(a):
            return ref[comb(base + a), :].astype(jnp.float32)

        border[0:GROUPS] = jnp.where(
            lane % 16 == 1, turn(choose(LAST, lane, get), 18), choose(START, lane, get)
        )
        border[SLABS : SLABS + 2] = ref[base : base + 2, :].astype(jnp.float32)
        rows = ref[base + ROWS - 2 : base + ROWS, :].astype(jnp.float32)
        border[SLABS + 2 : SLABS + 3] = turn(jnp.where(one >= 16, rows[0:1], rows[1:2]), -16)
        border[SLABS + 3 : SLABS + 4] = turn(rows[1:2], -16)
        edges[at] = border[...]

    border[...] = jnp.zeros_like(border)
    edge(ocean, 0, 2 * levels - 1)
    gain = None
    for k in range(levels):
        pivot = 1.0
        if k > 0:
            upper = edges[2 * levels + k - 1]
            pivot = pivot + upper - upper * gain
        if k < levels - 1:
            edge(rates, k * ROWS, 2 * levels + k)
            lower = edges[2 * levels + k]
            inverse = 1.0 / (pivot + lower)
            gain = lower * inverse
            edges[k] = gain
        else:
            inverse = 1.0 / pivot
        edges[levels - 1 + k] = inverse


def on_device(
    thermal_anomaly,
    zonal_flow_ratio,
    meridional_flow_ratio,
    diffusion_rates,
    ocean_bottom_scaled,
    ocean_indicator,
    operator_diagonal,
    elevation_source,
    block_positions,
):
    levels, cells = thermal_anomaly.shape[1:]
    nx = lax.axis_size("gx")
    ny = lax.axis_size("gy")
    count = block_positions.shape[0]
    planes = (ocean_bottom_scaled, ocean_indicator, operator_diagonal, elevation_source)
    depth, ocean, diag, source = planes
    f32 = jnp.float32
    per = next(n for n in (4, 2, 6, levels) if levels % n == 0 and n * ROWS % 8 == 0)
    steps = levels // per
    large = pltpu.CompilerParams(vmem_limit_bytes=BUDGET)
    middle = pltpu.CompilerParams(vmem_limit_bytes=BUDGET * 7 // 8)
    small = pltpu.CompilerParams(vmem_limit_bytes=BUDGET // 3)
    temp, zonal, merid = (
        array.reshape(levels * ROWS, LANES)
        for array in (thermal_anomaly, zonal_flow_ratio, meridional_flow_ratio)
    )
    rates = diffusion_rates.reshape(levels - 1, 1, cells)
    hbm = pl.BlockSpec(memory_space=pltpu.HBM)
    here = pl.BlockSpec(memory_space=pltpu.VMEM)

    def vmem(*shape, kind=f32):
        return pltpu.VMEM(shape, kind)

    def out(*shape, kind=f32):
        return jax.ShapeDtypeStruct(shape, kind)

    def sems(number):
        return pltpu.SemaphoreType.DMA((number,))

    deep = vmem(levels * ROWS, LANES)
    flat = vmem(ROWS, LANES)
    flat_int = vmem(ROWS, LANES, kind=jnp.int32)
    plane = vmem(PLANES, GROUPS, LANES)
    tall = vmem(PLANES, 40, LANES)
    numbers = pltpu.SMEM((count,), jnp.int32)
    number_pieces, _ = pieces_of(levels, count)
    slot = RIM_ROWS + number_pieces
    share = 1 + number_pieces
    part, own, slots, table, around = pl.pallas_call(
        functools.partial(forcing_kernel, levels, per, nx, ny),
        in_specs=[SMEM] + [hbm] * 7,
        out_specs=[hbm] * 3 + [SMEM] * 2,
        out_shape=[
            out(ROWS, LANES), out(56, LANES), out(count, 1, slot * LANES),
            out(8, kind=jnp.int32), out(4 * count, kind=jnp.int32),
        ],
        scratch_shapes=[deep] * 3 + [flat, flat_int, flat, flat]
        + [flat, vmem(56, LANES), vmem(count * slot, LANES)]
        + [flat] * 3 + [plane] * 3 + [tall] * 2
        + [vmem(4, 2 * levels, LANES), numbers, sems(3 * steps + 4), sems(3)],
        compiler_params=large,
        name="forcing",
    )(block_positions, temp, zonal, merid, depth, ocean, diag, source)
    rims = lax.all_to_all(slots, BOTH, 0, 0, tiled=True)

    inner, edges = pl.pallas_call(
        functools.partial(tracer_kernel, levels, per),
        in_specs=[hbm] * 5,
        out_specs=[here] * 2,
        out_shape=[out(levels * ROWS, LANES), out(3 * levels - 1, EDGE, LANES)],
        scratch_shapes=[deep] * 3 + [vmem((levels - 1) * ROWS, LANES), flat_int]
        + [plane] * 2 + [tall] * 2
        + [vmem(levels, PLANES, GROUPS, LANES), vmem(EDGE, LANES), sems(3 * steps + 2)],
        compiler_params=middle,
        name="tracer",
    )(temp, zonal, merid, rates, ocean)

    rims, edges = lax.optimization_barrier((rims, edges))
    extended = vmem(GROUP, SLABS, 2 * LANES)
    vectors, hand = pl.pallas_call(
        functools.partial(solve_kernel, levels, ny),
        in_specs=[SMEM, SMEM] + [here] * 6,
        out_specs=[here] * 2,
        out_shape=[out(4, GROUP, SLABS, 2 * LANES), out(count, 1, share * LANES)],
        scratch_shapes=[vmem(WIDE, LANES)] * 3 + [vmem(SLABS, LANES)] * 4 + [extended] * 5 + [vmem(16, LANES)],
        compiler_params=small,
        name="vectors",
    )(table, around, rims, own, part, depth, ocean, diag)
    hands = lax.all_to_all(hand, BOTH, 0, 0, tiled=True)

    new_temp, surface = pl.pallas_call(
        functools.partial(finish_kernel, levels, per),
        in_specs=[SMEM] + [here] * 4,
        out_specs=[hbm] * 2,
        out_shape=[out(levels * ROWS, LANES), out(1, cells)],
        scratch_shapes=[
            deep, flat, vmem(GROUP, SLABS, LANES), vmem(GROUP, SLABS, LANES), vmem(4, 2 * levels, LANES),
            sems(1 + steps),
        ],
        compiler_params=small,
        name="finish",
    )(table, hands, vectors, edges, inner)
    return new_temp.reshape(1, levels, cells), surface


def solution(mesh):
    deep = P(BOTH, None, None)
    flat = P(BOTH, None)
    return jax.shard_map(
        on_device,
        mesh=mesh,
        in_specs=(deep, deep, deep, deep, flat, flat, flat, flat, P()),
        out_specs=(deep, flat),
        check_vma=False,
    )
```

```python
import functools

import jax
import jax.numpy as jnp
from jax import lax
from jax.experimental import pallas as pl
from jax.experimental.pallas import tpu as pltpu
from jax.sharding import PartitionSpec as P

ITERS = 4
SPAN_X = 240
SPAN_Y = 160
RIM = 4
ADVECT = 0.25
DIFFUSE = 0.12
STERIC = 0.5
LOW_RATE = 0.05
HIGH_RATE = 32.5
ROOTS = (0.02, 0.35, 0.1, 0.2)
STRETCH = 4.0
TINY = 1e-30
BOTH = ("gx", "gy")
SIDES = ((-1, 0), (1, 0), (0, -1), (0, 1), (-1, -1), (1, -1), (-1, 1), (1, 1))

LANES = 128
GROUP = 8
GROUPS = SPAN_Y // GROUP
PLANES = GROUP * SPAN_X // LANES
ROWS = GROUPS * PLANES
SLABS = GROUPS + 4
WIDE = SLABS * PLANES
START = [SPAN_X * j // LANES for j in range(GROUP)]
OFF = [SPAN_X * j % LANES for j in range(GROUP)]
LAST = [(SPAN_X * j + SPAN_X - 1) // LANES for j in range(GROUP)]
END = [(SPAN_X * j + SPAN_X - 1) % LANES for j in range(GROUP)]
FIRST_OF = [[OFF[j] for j in range(GROUP) if START[j] == a] for a in range(PLANES)]
LAST_OF = [[END[j] for j in range(GROUP) if LAST[j] == a] for a in range(PLANES)]
RIM_ROWS = 20
EDGE = 32
BUDGET = 56 * 1024 * 1024


def turn(value, shift, axis=1):
    shift = shift % value.shape[axis]
    return value if shift == 0 else pltpu.roll(value, shift, axis)


def fetching(pairs, sems):
    copies = [pltpu.make_async_copy(a, b, sems.at[n]) for n, (a, b) in enumerate(pairs)]
    for copy in copies:
        copy.start()
    return copies


def pieces_of(levels, count):
    rows = 2 * levels
    number = -(-4 * rows // count)
    runs = [[] for _ in range(4)]
    for c in range(4):
        for j in range(number):
            low, high = max(c * rows, j * count), min((c + 1) * rows, (j + 1) * count)
            if low < high:
                runs[c].append((j, low - j * count, low - c * rows, high - low))
    return number, runs


class Level:
    def __init__(self, ref, base):
        self.ref, self.base = ref, base

    def plane(self, a):
        return self.ref[comb(self.base + a), :]

    def rows(self, low, size):
        return self.ref[pl.ds(self.base + low, size), :]


def lane_of(shape):
    return lax.broadcasted_iota(jnp.int32, shape, len(shape) - 1)


def row_of(shape):
    return lax.broadcasted_iota(jnp.int32, shape, 0)


def comb(a, count=GROUPS):
    return pl.ds(a, count, stride=PLANES)


def line_of(get, y):
    lane = lane_of((1, LANES))
    j = y % GROUP
    row = y // GROUP * PLANES + START[j]
    first, second = get(row), get(row + 1)
    third = get(row + 2) if START[j] + 2 < PLANES else second
    left = turn(jnp.where(lane >= OFF[j], first, second), -OFF[j])
    right = turn(jnp.where(lane >= OFF[j], second, third), -OFF[j])
    return left, right


def drop(value, lanes, lane):
    for at in lanes:
        value = jnp.where(lane == at, 0.0, value)
    return value


def store_terms(a, temp, flow_x, flow_y, te, tw, tn, ts):
    spread = DIFFUSE * temp
    te[a] = spread - flow_x
    tw[a] = spread + flow_x
    tn[a, 8 : 8 + GROUPS] = spread - flow_y
    ts[a, 8 : 8 + GROUPS] = spread + flow_y


def clear_terms(tn, ts):
    none = jnp.zeros((PLANES, 1, LANES), jnp.float32)
    for ref in (tn, ts):
        ref[:, 7:8] = none
        ref[:, 8 + GROUPS : 9 + GROUPS] = none


def inner_sum(a, te, tw, tn, ts):
    lane = lane_of((GROUPS, LANES))
    here = te[a]
    east = here if a == PLANES - 1 else jnp.where(lane == 0, te[a + 1], here)
    east = drop(turn(east, -1), LAST_OF[a], lane)
    here = tw[a]
    west = here if a == 0 else jnp.where(lane == LANES - 1, tw[a - 1], here)
    west = drop(turn(west, 1), FIRST_OF[a], lane)

    def plane(ref, at):
        down = 8 + (at >= PLANES) - (at < 0)
        return ref[at % PLANES, down : down + GROUPS]

    north = turn(jnp.where(lane >= LANES - 16, plane(tn, a + 1), plane(tn, a + 2)), 16)
    south = turn(jnp.where(lane < 16, plane(ts, a - 1), plane(ts, a - 2)), -16)
    return east + west + north + south


def choose(planes, lane, get):
    value = get(planes[0])
    for j in range(1, GROUP):
        low = (OFF[j] - (32 if planes is LAST else 0)) % LANES
        value = jnp.where(jnp.logical_and(lane >= low, lane < low + 16), get(planes[j]), value)
    return value


def forcing_kernel(
    levels, per, tiles_x, tiles_y,
    pos, temp_in, zonal_in, merid_in, depth_in, ocean_in, diag_in, source_in,
    part_out, own_out, slots_out, table, around,
    temp, zonal, merid, depth, ocean, diag, source, part, own, slots,
    st, sx, sy, pt, te, tw, tn, ts, edges, holder, sems, out_sems,
):
    count = pos.shape[0]
    steps = levels // per
    number_pieces, runs = pieces_of(levels, count)
    slot = RIM_ROWS + number_pieces
    pairs = []
    for step in range(steps):
        chunk = pl.ds(step * per * ROWS, per * ROWS)
        pairs += [
            (a.at[chunk], b.at[chunk]) for a, b in ((temp_in, temp), (zonal_in, zonal), (merid_in, merid))
        ]
    pairs += [
        (a.reshape(ROWS, LANES), b)
        for a, b in ((source_in, source), (ocean_in, ocean), (depth_in, depth), (diag_in, diag))
    ]
    copies = fetching(pairs, sems)
    results = []

    def send(value, target):
        copy = pltpu.make_async_copy(value, target, out_sems.at[len(results)])
        copy.start()
        results.append(copy)

    lane = lane_of((GROUPS, LANES))
    one = lane_of((1, LANES))
    q = lane % 16
    edges[...] = jnp.zeros_like(edges)

    def number(d, carry):
        holder[pos[d]] = d
        return carry

    lax.fori_loop(0, count, number, 0)
    me = lax.axis_index("gx") * tiles_y + lax.axis_index("gy")
    here = pos[me]
    row = here // tiles_x
    column = here % tiles_x
    sides = []
    for c, (dx, dy) in enumerate(SIDES):
        there = row + dy
        inside = jnp.logical_and(there >= 0, there < tiles_y)
        target = jnp.where(inside, there, 0) * tiles_x + (column + dx + tiles_x) % tiles_x
        device = jnp.where(inside, holder[target], -1)
        table[c] = device
        sides.append(device)

    def look(y, carry):
        line = [holder[y * tiles_x + x] for x in range(tiles_x)]
        below = [holder[jnp.maximum(y - 1, 0) * tiles_x + x] for x in range(tiles_x)]
        above = [holder[jnp.minimum(y + 1, tiles_y - 1) * tiles_x + x] for x in range(tiles_x)]
        for x, device in enumerate(line):
            around[device] = line[x - 1]
            around[count + device] = line[(x + 1) % tiles_x]
            around[2 * count + device] = jnp.where(y > 0, below[x], -1)
            around[3 * count + device] = jnp.where(y < tiles_y - 1, above[x], -1)
        return carry

    lax.fori_loop(0, tiles_y, look, 0)
    clear_terms(tn, ts)

    def add(flats, low, size, fresh):
        rows = pl.ds(low, size)
        total = [None] * 3
        for t, u, v in zip(*flats):
            t = t.rows(low, size)
            new = (t, t * u.rows(low, size), t * v.rows(low, size))
            total = [b if a is None else a + b for a, b in zip(total, new)]
        for ref, value in zip((st, sx, sy), total):
            ref[rows, :] = value if fresh else ref[rows, :] + value

    for step in range(steps):
        for copy in copies[3 * step : 3 * step + 3]:
            copy.wait()
        flats = [
            [Level(ref, (step * per + n) * ROWS) for n in range(per)] for ref in (temp, zonal, merid)
        ]

        def some(m, carry):
            add(flats, pl.multiple_of(m * 8, 8), 8, step == 0)
            return carry

        lax.fori_loop(0, ROWS // 8, some, 0, unroll=4)
        if ROWS % 8:
            add(flats, ROWS - ROWS % 8, ROWS % 8, step == 0)

        for n in range(per):
            k = step * per + n
            t, u, v = (flat[n] for flat in flats)

            loaded = {a: (t.plane(a), u.plane(a)) for a in sorted(set(START + LAST))}

            def term(planes, sign):
                own = choose(planes, lane, lambda a: loaded[a][0])
                flow = choose(planes, lane, lambda a: loaded[a][1])
                return DIFFUSE * own + sign * ADVECT * (flow * own)

            edges[0, 0:GROUPS] = jnp.where(q == k, turn(term(START, -1.0), k), edges[0, 0:GROUPS])
            edges[1, 0:GROUPS] = jnp.where(q == k, turn(term(LAST, 1.0), k + 17), edges[1, 0:GROUPS])
            rows = t.rows(0, 2)
            rows = DIFFUSE * rows - ADVECT * (v.rows(0, 2) * rows)
            edges[2, k : k + 1] = rows[0:1]
            edges[2, k + levels : k + levels + 1] = rows[1:2]
            rows = t.rows(ROWS - 2, 2)
            rows = DIFFUSE * rows + ADVECT * (v.rows(ROWS - 2, 2) * rows)
            edges[3, k : k + 1] = turn(jnp.where(one >= 16, rows[0:1], rows[1:2]), -16)
            edges[3, k + levels : k + levels + 1] = turn(rows[1:2], -16)

    for c in range(4):
        for j, device, low, size in runs[c]:
            slots[pl.ds(device * slot + RIM_ROWS + j, size, stride=slot), :] = edges[c, low : low + size]

    for copy in copies[3 * steps :]:
        copy.wait()

    def wet_of(rows):
        return ocean[rows, :].astype(jnp.float32)

    def masked(rows):
        return depth[rows, :] * wet_of(rows)

    for a in range(PLANES):
        total = st[comb(a), :]
        pt[a] = total
        store_terms(a, total, ADVECT * sx[comb(a), :], ADVECT * sy[comb(a), :], te, tw, tn, ts)
    for a in range(PLANES):
        total = pt[a]
        wet = wet_of(comb(a))
        change = inner_sum(a, te, tw, tn, ts) - 4.0 * DIFFUSE * total
        part[comb(a), :] = source[comb(a), :] + (STERIC / levels) * wet * (total + wet * change)
    send(part, part_out)

    def mix(*values):
        value = values[-1]
        for at, low in ((6, 12), (5, 11), (4, 10), (3, 9), (2, 8), (1, 6), (0, 3)):
            value = jnp.where(q < low, values[at], value)
        return value

    def ends(planes, low):
        value = tn[planes[0], 8 : 8 + GROUPS]
        last = jnp.logical_and(lane >= low, lane < low + 16)
        return jnp.where(last, ts[planes[7], 8 : 8 + GROUPS], value)

    def beside(b, d, g, b_out, d_out):
        return g * b + d * d_out * (b - b_out)

    bp = choose(START, lane, lambda a: part[comb(a), :])
    dp = choose(START, lane, lambda a: masked(comb(a)))
    gp = choose(START, lane, lambda a: diag[comb(a), :])
    pp = beside(bp, dp, gp, turn(bp, -1), turn(dp, -1))
    pack_w = mix(
        bp, turn(dp, 3), turn(gp, 6), turn(pp, 6), turn(choose(START, lane, lambda a: te[a]), 9),
        turn(gp, 8), turn(dp, 8), turn(ends(START, OFF[7]), 12),
    )
    bp = choose(LAST, lane, lambda a: part[comb(a), :])
    dp = choose(LAST, lane, lambda a: masked(comb(a)))
    gp = choose(LAST, lane, lambda a: diag[comb(a), :])
    pp = beside(bp, dp, gp, turn(bp, 1), turn(dp, 1))
    pack_e = mix(
        turn(bp, 19), turn(dp, 22), turn(gp, 24), turn(pp, 27),
        turn(choose(LAST, lane, lambda a: tw[a]), 26),
        turn(gp, 29), turn(dp, 31), turn(ends(LAST, LANES - 16), 32),
    )
    own[0:GROUPS] = pack_w
    own[SLABS : SLABS + GROUPS] = pack_e
    north_l = tn[0, 8:9]
    north_r = tn[1, 8:9]
    south_13 = ts[PLANES - 2, 7 + GROUPS : 8 + GROUPS]
    south_14 = ts[PLANES - 1, 7 + GROUPS : 8 + GROUPS]
    south_l = turn(jnp.where(one >= 16, south_13, south_14), -16)
    south_r = turn(south_14, -16)
    own[48:49] = north_l
    own[49:50] = north_r
    own[50:51] = south_l
    own[51:52] = south_r
    send(own, own_out)
    deep = jnp.max(masked(slice(0, ROWS)), axis=(0, 1), keepdims=True)
    top = jnp.max(diag[...], axis=(0, 1), keepdims=True) + 8.0 * deep * deep
    top = jnp.broadcast_to(top, (1, LANES))

    slots[pl.ds(RIM_ROWS - 1, count, stride=slot), :] = jnp.broadcast_to(top, (count, LANES))
    block_lane = lane_of((6, LANES))
    block_row = row_of((6, LANES))
    for c, first, rows_l, rows_r in ((2, True, north_l, north_r), (3, False, south_l, south_r)):
        base = 0 if first else ROWS - 6
        if first:
            spare = jnp.logical_and(block_row == 5, block_lane >= 80)
        else:
            spare = jnp.logical_and(block_row == 0, block_lane < 48)
        g = 0 if first else GROUPS - 1
        blocks = []
        block = slice(base, base + 6)
        for value, at in ((part[block, :], g), (masked(block), SLABS + g)):
            extra = jnp.broadcast_to(turn(own[at : at + 1], -16), (6, LANES))
            blocks.append(jnp.where(spare, extra, value))
        low = 0 if first else ROWS - 4
        diag_rows = diag[low : low + 4, :]
        third, fourth = (2, 3) if first else (SPAN_Y - 3, SPAN_Y - 4)
        b_l, b_r = line_of(lambda n: part[n : n + 1, :], third)
        d_l, d_r = line_of(lambda n: masked(slice(n, n + 1)), third)
        g_l, g_r = line_of(lambda n: diag[n : n + 1, :], third)
        bo_l, bo_r = line_of(lambda n: part[n : n + 1, :], fourth)
        do_l, do_r = line_of(lambda n: masked(slice(n, n + 1)), fourth)
        out_l = beside(b_l, d_l, g_l, bo_l, do_l)
        out_r = beside(b_r, d_r, g_r, bo_r, do_r)
        for at, value in ((112, turn(g_l, 112)), (113, turn(do_l, 113)), (114, turn(g_r, 3)), (115, turn(do_r, 4))):
            out_r = jnp.where(one == at, value, out_r)
        last_row = jnp.where(one == LANES - 1, top, rows_r)

        @pl.when(sides[c] >= 0)
        def _(c=c, blocks=blocks, diag_rows=diag_rows, singles=(out_l, out_r, rows_l, last_row)):
            at = sides[c] * slot
            slots[pl.ds(at, 6), :] = blocks[0]
            slots[pl.ds(at + 6, 6), :] = blocks[1]
            slots[pl.ds(at + 12, 4), :] = diag_rows
            for n, value in enumerate(singles):
                slots[pl.ds(at + 16 + n, 1), :] = value

    corner = jnp.logical_and(row_of((GROUPS, LANES)) == RIM_ROWS - 1, lane == LANES - 1)
    for c, pack in ((0, pack_w), (1, pack_e)):
        slots[pl.ds(sides[c] * slot, GROUPS), :] = jnp.where(corner, top, pack)
    for c, at in ((4, 0), (5, SLABS), (6, GROUPS - 1), (7, SLABS + GROUPS - 1)):
        @pl.when(sides[c] >= 0)
        def _(c=c, at=at):
            slots[pl.ds(sides[c] * slot, 1), :] = own[at : at + 1]
    send(slots, slots_out.reshape(count * slot, LANES))
    for copy in results:
        copy.wait()


SMEM = pl.BlockSpec(memory_space=pltpu.SMEM)


def solve_kernel(
    levels, tiles_y,
    table, around, rims, own, part, depth, ocean, diag,
    vectors, hands,
    fb, fd, fg, pw, pe, ow, oe, ed, eg, ex, we, wn, last, rows,
):
    count = rims.shape[0]
    number_pieces, _ = pieces_of(levels, count)
    slot = RIM_ROWS + number_pieces
    share = 1 + number_pieces
    came = rims.reshape(count * slot, LANES)
    hand = hands.reshape(count * share, LANES)
    depth, ocean, diag = (ref.reshape(ROWS, LANES) for ref in (depth, ocean, diag))
    lane = lane_of((SLABS, LANES))
    slab = row_of((SLABS, LANES))
    one = lane_of((1, LANES))
    src = [table[c] for c in range(8)]

    def fetch(c, low, high):
        value = came[pl.ds(jnp.maximum(src[c], 0) * slot + low, high - low), :]
        return jnp.where(src[c] >= 0, value, 0.0)

    me = lax.axis_index("gx") * tiles_y + lax.axis_index("gy")
    for n in range(number_pieces):
        side = jnp.minimum((n * count + me) // (2 * levels), 3)
        base = (side + 1 - 2 * (side % 2)) * count

        def relay(d, carry, n=n, base=base):
            row = jnp.maximum(around[base + d], 0) * slot + RIM_ROWS + n
            hand[pl.ds(d * share + 1 + n, 1), :] = came[pl.ds(row, 1), :]
            return carry

        lax.fori_loop(0, count, relay, 0, unroll=4)

    none = jnp.zeros((WIDE - ROWS + 4, LANES), jnp.float32)
    for ref in (fb, fd, fg):
        ref[ROWS - 4 : WIDE] = none
    fb[0:ROWS] = part[...]
    fd[0:ROWS] = depth[...] * ocean[...].astype(jnp.float32)
    fg[0:ROWS] = diag[...]
    for ref, low, high, n_lane, s_lane in ((fb, 0, 6, 80, 48), (fd, 6, 12, 80, 48), (fg, 12, 16, 96, 32)):
        size = high - low
        row, column = row_of((size, LANES)), lane_of((size, LANES))
        beyond = jnp.logical_and(row == size - 1, column >= n_lane)
        ref[ROWS : ROWS + size] = jnp.where(beyond, 0.0, fetch(3, low, high))
        beyond = jnp.logical_and(row == 0, column < s_lane)
        ref[WIDE - size : WIDE] = jnp.where(beyond, 0.0, fetch(2, low, high))
    empty = jnp.zeros((SLABS, LANES), jnp.float32)
    for ref, side, north, south in ((pw, 0, 6, 4), (pe, 1, 7, 5)):
        ref[...] = empty
        ref[0:GROUPS] = fetch(side, 0, GROUPS)
        ref[GROUPS : GROUPS + 1] = fetch(north, 0, 1)
        ref[SLABS - 1 : SLABS] = fetch(south, 0, 1)
    for ref, at, north, south in ((ow, 0, 5, 0), (oe, SLABS, 11, 6)):
        ref[...] = empty
        ref[0:GROUPS] = own[at : at + GROUPS]
        ref[GROUPS : GROUPS + 1] = turn(fetch(3, north, north + 1), 16)
        ref[SLABS - 1 : SLABS] = turn(fetch(2, south, south + 1), 16)

    def spread(ref, j):
        a = START[j]
        first, second = ref[comb(a, SLABS), :], ref[comb(a + 1, SLABS), :]
        third = ref[comb(a + 2, SLABS), :] if a + 2 < PLANES else second
        left = turn(jnp.where(lane >= OFF[j], first, second), -OFF[j])
        right = turn(jnp.where(lane >= OFF[j], second, third), -OFF[j])
        return left, right

    def seam_row(left, right, slab_at, lanes_at):
        east = turn(pe[slab_at : slab_at + 1], 112 - lanes_at)
        west = turn(pw[slab_at : slab_at + 1], 124 - lanes_at)
        right = jnp.where(one < 112, right, jnp.where(one < 116, east, jnp.where(one >= 124, west, 0.0)))
        return jnp.broadcast_to(left, (SLABS, LANES)), jnp.broadcast_to(right, (SLABS, LANES))

    seams = {
        0: ((0, seam_row(fetch(2, 18, 19), fetch(2, 19, 20), SLABS - 1, 28)),
            (GROUPS, seam_row(own[50:51], own[51:52], GROUPS - 1, 28))),
        GROUP - 1: ((GROUPS - 1, seam_row(fetch(3, 18, 19), fetch(3, 19, 20), GROUPS, 12)),
                    (SLABS - 1, seam_row(own[48:49], own[49:50], 0, 12))),
    }
    weight = STERIC / levels

    def missing(target, term, term_out, d, d_out, g):
        term, term_out, d, d_out, g = (
            turn(value[0], target - value[1]) for value in (term, term_out, d, d_out, g)
        )
        term = jnp.where(d > 0, weight * term, 0.0)
        term_out = jnp.where(d_out > 0, weight * term_out, 0.0)
        return jnp.where(one == target, g * term + d * d_out * (term - term_out), 0.0)

    def ring(ref, at):
        return ref[at : at + 1]

    outer = {j: [] for j in range(GROUP)}
    for j, at, beyond, o, lanes in ((0, 0, SLABS - 1, 0, 28), (GROUP - 1, GROUPS - 1, GROUPS, 16, 12)):
        own_row, corner = ring(pe, at), ring(pe, beyond)
        outer[j].append((1, at, missing(
            114, (corner, lanes + 2), (corner, lanes + 3), (own_row, o + 5), (own_row, o + 11), (own_row, o + 10),
        )))
        own_row, corner = ring(pw, at), ring(pw, beyond)
        outer[j].append((1, at, missing(
            125, (corner, lanes + 1), (corner, lanes), (own_row, o + 3), (own_row, o + 11), (own_row, o + 10),
        )))
    for j, at, c, j_out, d_l, d_r in ((2, GROUPS, 3, 3, (9, 96), (11, 79)), (5, SLABS - 1, 2, 4, (6, 48), (8, 31))):
        line_l, line_r = fetch(c, 16, 17), fetch(c, 17, 18)
        corner = ring(pw, at)
        outer[j].append((0, at, line_l + missing(
            0, (corner, OFF[j] + 9), (corner, OFF[j_out] + 9), (fetch(c, d_l[0], d_l[0] + 1), d_l[1]),
            (line_r, 113), (line_r, 112),
        )))
        corner = ring(pe, at)
        outer[j].append((1, at, jnp.where(one < 112, line_r, 0.0) + missing(
            111, (corner, OFF[j] + 9), (corner, OFF[j_out] + 9), (fetch(c, d_r[0], d_r[0] + 1), d_r[1]),
            (line_r, 115), (line_r, 114),
        )))
    for j in range(GROUP):
        o = OFF[j]
        inside = slab < GROUPS
        halves = [
            jnp.zeros((SLABS, LANES), jnp.float32),
            jnp.where(
                jnp.logical_and(inside, lane == 114), turn(pe[...], 114 - o - 8),
                jnp.where(jnp.logical_and(inside, lane == 125), turn(pw[...], 125 - o - 8), 0.0),
            ),
        ]
        for half, at, line in outer[j]:
            halves[half] = halves[half] + jnp.where(slab == at, line, 0.0)
        ex[j, :, 0:LANES] = halves[0]
        ex[j, :, LANES:] = halves[1]

        def rim(right, q, width):
            east = turn(pe[...], 112 - o - q)
            west = turn(pw[...], 128 - width - o - q)
            value = jnp.where(lane < 112 + width, east, jnp.where(lane >= 128 - width, west, 0.0))
            return jnp.where(lane < 112, right, value)

        left, right = spread(fd, j)
        right = rim(right, 3, 3)
        wet_l = jnp.where(left > 0, weight, 0.0)
        wet_r = jnp.where(right > 0, weight, 0.0)
        ed[j, :, 0:LANES] = left
        ed[j, :, LANES:] = right
        left, right = spread(fg, j)
        eg[j, :, 0:LANES] = left
        eg[j, :, LANES:] = rim(right, 6, 2)
        left, right = spread(fb, j)
        right = rim(right, 0, 3)
        seam_l = jnp.where(lane == 0, turn(pw[...], -o - 9), 0.0)
        seam_r = jnp.where(lane == 127, turn(ow[...], 127 - o - 9), 0.0)
        seam_r = jnp.where(lane == 111, turn(pe[...], 111 - o - 9), seam_r)
        seam_r = jnp.where(lane == 112, turn(oe[...], 112 - o - 9), seam_r)
        for at, (row_l, row_r) in seams.get(j, ()):
            seam_l = seam_l + jnp.where(slab == at, row_l, 0.0)
            seam_r = seam_r + jnp.where(slab == at, row_r, 0.0)
        vectors[0, j, :, 0:LANES] = left + wet_l * seam_l
        vectors[0, j, :, LANES:] = right + wet_r * seam_r

    for j in range(GROUP):
        d = ed[j]
        we[j] = d * turn(d, -1)
        above = ed[j + 1] if j < GROUP - 1 else turn(ed[0], -1, 0)
        wn[j] = d * above

    top = jnp.max(came[pl.ds(RIM_ROWS - 1, count, stride=slot), :], axis=0, keepdims=True)
    top = jnp.max(jnp.where(one == LANES - 1, top, 0.0), axis=1, keepdims=True)
    scale = STRETCH / top

    big = (SLABS, 2 * LANES)
    mine = jnp.logical_and(row_of(big) < GROUPS, lane_of(big) < SPAN_X)
    pair = 0
    for k in range(5):
        sums = [None] * (k + 1)
        new = last if k == 4 else vectors.at[k]
        if k:
            v = vectors.at[k - 1]
            flow_below = wn[GROUP - 1] * (v[GROUP - 1] - turn(v[0], -1, 0))
            flow_below = turn(flow_below, 1, 0)
        for j in range(GROUP):
            if k:
                here = v[j]
                above = v[j + 1] if j < GROUP - 1 else turn(v[0], -1, 0)
                flow_x = we[j] * (here - turn(here, -1))
                flow_y = wn[j] * (here - above)
                image = eg[j] * here + (flow_x - turn(flow_x, 1)) + (flow_y - flow_below)
                if k == 1:
                    image = image + ex[j]
                fresh = scale * image - (STRETCH * ROOTS[k - 1]) * here
                flow_below = flow_y
                new[j] = fresh
            else:
                fresh = new[j]
            held = jnp.where(mine, fresh, 0.0)
            for i in range(k + 1):
                other = vectors[i, j] if i < k else held
                value = held * other
                sums[i] = value if sums[i] is None else sums[i] + value
        for i in range(k + 1):
            rows[pair : pair + 1] = jnp.sum(sums[i][:, 0:LANES] + sums[i][:, LANES:], axis=0, keepdims=True)
            pair += 1
    rows[pair : pair + 1] = jnp.where(one == 0, top, 0.0)
    total = jnp.sum(rows[...], axis=1, keepdims=True)
    spot = row_of((16, LANES)) == lane_of((16, LANES))
    line = jnp.sum(jnp.where(spot, total, 0.0), axis=0, keepdims=True)
    hand[pl.ds(0, count, stride=share), :] = jnp.broadcast_to(line, (count, LANES))


def finish_kernel(
    levels, per, table, hands, vectors, edges, inner, tracer_out, surface_out,
    cells, flat, left, right, message, out_sems,
):
    count = hands.shape[0]
    number_pieces, runs = pieces_of(levels, count)
    share = 1 + number_pieces
    came = hands.reshape(count * share, LANES)
    steps = levels // per
    chunks = [pl.ds(step * per * ROWS, per * ROWS) for step in range(steps)]
    row = jnp.sum(came[pl.ds(0, count, stride=share), :], axis=0, keepdims=True)
    one = lane_of((1, LANES))
    entry = {}
    pair = 0
    for k in range(5):
        for i in range(k + 1):
            value = jnp.sum(jnp.where(one == pair, row, 0.0), axis=1, keepdims=True)
            entry[i, k] = entry[k, i] = value
            pair += 1
    top = jnp.sum(jnp.where(one == pair, row, 0.0), axis=1, keepdims=True) * (1.0 / count)

    def image(c):
        out = [None] * 5
        for k in range(4):
            if c[k] is None:
                continue
            low = ROOTS[k] * c[k]
            out[k] = low if out[k] is None else out[k] + low
            out[k + 1] = (1.0 / STRETCH) * c[k]
        return out

    def dot(a, b):
        total = None
        for i in range(5):
            if a[i] is None:
                continue
            inner = None
            for j in range(5):
                if b[j] is not None:
                    value = entry[i, j] * b[j]
                    inner = value if inner is None else inner + value
            total = a[i] * inner if total is None else total + a[i] * inner
        return total

    def axpy(a, s, b):
        return [
            x if y is None else (s * y if x is None else x + s * y) for x, y in zip(a, b)
        ]

    r = [jnp.ones((1, 1), jnp.float32)] + [None] * 4
    p = list(r)
    x = [None] * 5
    rr = entry[0, 0]
    for n in range(ITERS):
        q = image(p)
        step = rr / jnp.maximum(dot(p, q), TINY)
        step = jnp.clip(step, top * (1.0 / HIGH_RATE), top * (1.0 / LOW_RATE))
        x = axpy(x, step, p)
        if n < ITERS - 1:
            r = axpy(r, -step, q)
            fresh = jnp.maximum(dot(r, r), 0.0)
            p = axpy(r, fresh / jnp.maximum(rr, TINY), p)
            rr = fresh
    factors = [c / top for c in x[:4]]
    for j in range(GROUP):
        value = None
        for k in range(4):
            term = factors[k] * vectors[k, j]
            value = term if value is None else value + term
        left[j] = turn(value[:, 0:LANES], OFF[j])
        right[j] = turn(value[:, LANES:], OFF[j])
    lane = lane_of((SLABS, LANES))
    for a in range(PLANES):
        value = None
        for j in range(GROUP):
            for half, ref in ((0, left), (1, right)):
                low = max(SPAN_X * j + LANES * half - LANES * a, 0)
                high = min(SPAN_X * j + (LANES if half == 0 else SPAN_X) - LANES * a, LANES)
                if low >= high:
                    continue
                value = ref[j] if value is None else jnp.where(lane >= low, ref[j], value)
        flat[comb(a), :] = value[0:GROUPS]
    results = [pltpu.make_async_copy(flat, surface_out.reshape(ROWS, LANES), out_sems.at[0])]
    results[0].start()

    for c in range(4):
        for j, device, low, size in runs[c ^ 1]:
            value = came[pl.ds(device * share + 1 + j, size, stride=share), :]
            message[c, low : low + size] = jnp.where(table[c] >= 0, value, 0.0)
    second = lane_of((SLABS, LANES)) % 16 == 1
    sums = []
    for k in range(levels):
        value = edges[2 * levels - 1] * jnp.concatenate([
            jnp.where(second, turn(message[1], 1 - k), turn(message[0], -k)),
            message[2, k : k + 1], message[2, k + levels : k + levels + 1],
            message[3, k : k + 1], message[3, k + levels : k + levels + 1],
            jnp.zeros((EDGE - SLABS - 4, LANES), jnp.float32),
        ], axis=0)
        if k:
            value = value + edges[2 * levels + k - 1] * sums[-1]
        sums.append(value * edges[levels - 1 + k])
    for k in range(levels - 2, -1, -1):
        sums[k] = sums[k] + edges[k] * sums[k + 1]
    lane = lane_of((GROUPS, LANES))
    slab = row_of((GROUPS, LANES))
    for k in range(levels):
        west = sums[k][0:GROUPS]
        east = turn(west, -18)
        south_l, south_r = sums[k][SLABS : SLABS + 1], sums[k][SLABS + 1 : SLABS + 2]
        north_l = turn(sums[k][SLABS + 2 : SLABS + 3], 16)
        north_r = turn(sums[k][SLABS + 3 : SLABS + 4], 16)
        for a in range(PLANES):
            rim = None
            for at, source in [(at, west) for at in FIRST_OF[a]] + [(at, east) for at in LAST_OF[a]]:
                rim = jnp.where(lane == at, source, 0.0 if rim is None else rim)
            rows = comb(k * ROWS + a)
            if rim is None:
                cells[rows, :] = inner[rows, :]
                continue
            if a == 0:
                rim = rim + jnp.where(slab == 0, south_l, 0.0)
            if a == 1:
                rim = rim + jnp.where(jnp.logical_and(slab == 0, lane < 112), south_r, 0.0)
            if a == PLANES - 2:
                rim = rim + jnp.where(jnp.logical_and(slab == GROUPS - 1, lane >= 16), north_l, 0.0)
            if a == PLANES - 1:
                rim = rim + jnp.where(slab == GROUPS - 1, jnp.where(lane < 16, north_l, north_r), 0.0)
            cells[rows, :] = inner[rows, :] + rim
        if k % per == per - 1:
            step = k // per
            copy = pltpu.make_async_copy(
                cells.at[chunks[step]], tracer_out.at[chunks[step]], out_sems.at[1 + step]
            )
            copy.start()
            results.append(copy)
    for copy in results:
        copy.wait()


def tracer_kernel(
    levels, per, temp_in, zonal_in, merid_in, rates_in, ocean_in,
    out, edges,
    temp, zonal, merid, rates, ocean,
    te, tw, tn, ts, stepped, border, sems,
):
    steps = levels // per
    pairs = [(ocean_in.reshape(ROWS, LANES), ocean)]
    for step in range(steps):
        chunk = pl.ds(step * per * ROWS, per * ROWS)
        pairs += [
            (a.at[chunk], b.at[chunk]) for a, b in ((temp_in, temp), (zonal_in, zonal), (merid_in, merid))
        ]
    copies = fetching(pairs + [(rates_in.reshape((levels - 1) * ROWS, LANES), rates)], sems)
    lane = lane_of((GROUPS, LANES))
    one = lane_of((1, LANES))
    clear_terms(tn, ts)

    copies[0].wait()
    for step in range(steps):
        for copy in copies[1 + 3 * step : 4 + 3 * step]:
            copy.wait()

        def level(k, carry):
            t, u, v = (Level(ref, k * ROWS) for ref in (temp, zonal, merid))
            for a in range(PLANES):
                own = t.plane(a)
                quarter = ADVECT * own
                store_terms(a, own, u.plane(a) * quarter, v.plane(a) * quarter, te, tw, tn, ts)
            for a in range(PLANES):
                own = t.plane(a)
                change = inner_sum(a, te, tw, tn, ts) - 4.0 * DIFFUSE * own
                stepped[k, a] = own + ocean[comb(a), :].astype(jnp.float32) * change
            return carry

        lax.fori_loop(step * per, step * per + per, level, 0)
    copies[-1].wait()

    def block(a, carry):
        for low in range(0, GROUPS, 8):
            size = min(8, GROUPS - low)

            def rows(k):
                return pl.ds(k * ROWS + low * PLANES + a, size, stride=PLANES)

            gains = []
            sums = []
            for k in range(levels):
                value = stepped[k, a, low : low + size]
                pivot = 1.0
                if k > 0:
                    pivot = pivot + upper - upper * gains[-1]
                    value = value + upper * sums[-1]
                if k < levels - 1:
                    lower = rates[rows(k), :]
                    inverse = 1.0 / (pivot + lower)
                    gains.append(lower * inverse)
                    upper = lower
                else:
                    inverse = 1.0 / pivot
                sums.append(value * inverse)
            result = sums[-1]
            out[rows(levels - 1), :] = result
            for k in range(levels - 2, -1, -1):
                result = sums[k] + gains[k] * result
                out[rows(k), :] = result
        return carry

    lax.fori_loop(0, PLANES, block, 0)

    def edge(ref, base, at):
        def get(a):
            return ref[comb(base + a), :].astype(jnp.float32)

        border[0:GROUPS] = jnp.where(
            lane % 16 == 1, turn(choose(LAST, lane, get), 18), choose(START, lane, get)
        )
        border[SLABS : SLABS + 2] = ref[base : base + 2, :].astype(jnp.float32)
        rows = ref[base + ROWS - 2 : base + ROWS, :].astype(jnp.float32)
        border[SLABS + 2 : SLABS + 3] = turn(jnp.where(one >= 16, rows[0:1], rows[1:2]), -16)
        border[SLABS + 3 : SLABS + 4] = turn(rows[1:2], -16)
        edges[at] = border[...]

    border[...] = jnp.zeros_like(border)
    edge(ocean, 0, 2 * levels - 1)
    gain = None
    for k in range(levels):
        pivot = 1.0
        if k > 0:
            upper = edges[2 * levels + k - 1]
            pivot = pivot + upper - upper * gain
        if k < levels - 1:
            edge(rates, k * ROWS, 2 * levels + k)
            lower = edges[2 * levels + k]
            inverse = 1.0 / (pivot + lower)
            gain = lower * inverse
            edges[k] = gain
        else:
            inverse = 1.0 / pivot
        edges[levels - 1 + k] = inverse


def on_device(
    thermal_anomaly,
    zonal_flow_ratio,
    meridional_flow_ratio,
    diffusion_rates,
    ocean_bottom_scaled,
    ocean_indicator,
    operator_diagonal,
    elevation_source,
    block_positions,
):
    levels, cells = thermal_anomaly.shape[1:]
    nx = lax.axis_size("gx")
    ny = lax.axis_size("gy")
    count = block_positions.shape[0]
    planes = (ocean_bottom_scaled, ocean_indicator, operator_diagonal, elevation_source)
    depth, ocean, diag, source = planes
    f32 = jnp.float32
    per = next(n for n in (4, 2, 6, levels) if levels % n == 0 and n * ROWS % 8 == 0)
    steps = levels // per
    few = next(n for n in (2, 4, 6, levels) if levels % n == 0 and n * ROWS % 8 == 0)
    large = pltpu.CompilerParams(vmem_limit_bytes=BUDGET)
    middle = pltpu.CompilerParams(vmem_limit_bytes=BUDGET * 7 // 8)
    small = pltpu.CompilerParams(vmem_limit_bytes=BUDGET // 3)
    temp, zonal, merid = (
        array.reshape(levels * ROWS, LANES)
        for array in (thermal_anomaly, zonal_flow_ratio, meridional_flow_ratio)
    )
    rates = diffusion_rates.reshape(levels - 1, 1, cells)
    hbm = pl.BlockSpec(memory_space=pltpu.HBM)
    here = pl.BlockSpec(memory_space=pltpu.VMEM)

    def vmem(*shape, kind=f32):
        return pltpu.VMEM(shape, kind)

    def out(*shape, kind=f32):
        return jax.ShapeDtypeStruct(shape, kind)

    def sems(number):
        return pltpu.SemaphoreType.DMA((number,))

    deep = vmem(levels * ROWS, LANES)
    flat = vmem(ROWS, LANES)
    flat_int = vmem(ROWS, LANES, kind=jnp.int32)
    plane = vmem(PLANES, GROUPS, LANES)
    tall = vmem(PLANES, 40, LANES)
    numbers = pltpu.SMEM((count,), jnp.int32)
    number_pieces, _ = pieces_of(levels, count)
    slot = RIM_ROWS + number_pieces
    share = 1 + number_pieces
    part, own, slots, table, around = pl.pallas_call(
        functools.partial(forcing_kernel, levels, few, nx, ny),
        in_specs=[SMEM] + [hbm] * 7,
        out_specs=[hbm] * 3 + [SMEM] * 2,
        out_shape=[
            out(ROWS, LANES), out(56, LANES), out(count, 1, slot * LANES),
            out(8, kind=jnp.int32), out(4 * count, kind=jnp.int32),
        ],
        scratch_shapes=[deep] * 3 + [flat, flat_int, flat, flat]
        + [flat, vmem(56, LANES), vmem(count * slot, LANES)]
        + [flat] * 3 + [plane] * 3 + [tall] * 2
        + [vmem(4, 2 * levels, LANES), numbers, sems(3 * (levels // few) + 4), sems(3)],
        compiler_params=large,
        name="forcing",
    )(block_positions, temp, zonal, merid, depth, ocean, diag, source)
    rims = lax.all_to_all(slots, BOTH, 0, 0, tiled=True)

    inner, edges = pl.pallas_call(
        functools.partial(tracer_kernel, levels, per),
        in_specs=[hbm] * 5,
        out_specs=[here] * 2,
        out_shape=[out(levels * ROWS, LANES), out(3 * levels - 1, EDGE, LANES)],
        scratch_shapes=[deep] * 3 + [vmem((levels - 1) * ROWS, LANES), flat_int]
        + [plane] * 2 + [tall] * 2
        + [vmem(levels, PLANES, GROUPS, LANES), vmem(EDGE, LANES), sems(3 * steps + 2)],
        compiler_params=middle,
        name="tracer",
    )(temp, zonal, merid, rates, ocean)

    rims, edges = lax.optimization_barrier((rims, edges))
    extended = vmem(GROUP, SLABS, 2 * LANES)
    vectors, hand = pl.pallas_call(
        functools.partial(solve_kernel, levels, ny),
        in_specs=[SMEM, SMEM] + [here] * 6,
        out_specs=[here] * 2,
        out_shape=[out(4, GROUP, SLABS, 2 * LANES), out(count, 1, share * LANES)],
        scratch_shapes=[vmem(WIDE, LANES)] * 3 + [vmem(SLABS, LANES)] * 4 + [extended] * 6 + [vmem(16, LANES)],
        compiler_params=small,
        name="vectors",
    )(table, around, rims, own, part, depth, ocean, diag)
    hands = lax.all_to_all(hand, BOTH, 0, 0, tiled=True)

    new_temp, surface = pl.pallas_call(
        functools.partial(finish_kernel, levels, per),
        in_specs=[SMEM] + [here] * 4,
        out_specs=[hbm] * 2,
        out_shape=[out(levels * ROWS, LANES), out(1, cells)],
        scratch_shapes=[
            deep, flat, vmem(GROUP, SLABS, LANES), vmem(GROUP, SLABS, LANES), vmem(4, 2 * levels, LANES),
            sems(1 + steps),
        ],
        compiler_params=small,
        name="finish",
    )(table, hands, vectors, edges, inner)
    return new_temp.reshape(1, levels, cells), surface


def solution(mesh):
    deep = P(BOTH, None, None)
    flat = P(BOTH, None)
    return jax.shard_map(
        on_device,
        mesh=mesh,
        in_specs=(deep, deep, deep, deep, flat, flat, flat, flat, P()),
        out_specs=(deep, flat),
        check_vma=False,
    )
```

```python
import functools

import jax
import jax.numpy as jnp
from jax import lax
from jax.experimental import pallas as pl
from jax.experimental.pallas import tpu as pltpu
from jax.sharding import PartitionSpec as P

ITERS = 4
SPAN_X = 240
SPAN_Y = 160
RIM = 4
ADVECT = 0.25
DIFFUSE = 0.12
STERIC = 0.5
LOW_RATE = 0.05
HIGH_RATE = 32.5
ROOTS = (0.02, 0.35, 0.1, 0.2)
STRETCH = 4.0
TINY = 1e-30
BOTH = ("gx", "gy")
SIDES = ((-1, 0), (1, 0), (0, -1), (0, 1), (-1, -1), (1, -1), (-1, 1), (1, 1))

LANES = 128
GROUP = 8
GROUPS = SPAN_Y // GROUP
PLANES = GROUP * SPAN_X // LANES
ROWS = GROUPS * PLANES
SLABS = GROUPS + 4
WIDE = SLABS * PLANES
START = [SPAN_X * j // LANES for j in range(GROUP)]
OFF = [SPAN_X * j % LANES for j in range(GROUP)]
LAST = [(SPAN_X * j + SPAN_X - 1) // LANES for j in range(GROUP)]
END = [(SPAN_X * j + SPAN_X - 1) % LANES for j in range(GROUP)]
FIRST_OF = [[OFF[j] for j in range(GROUP) if START[j] == a] for a in range(PLANES)]
LAST_OF = [[END[j] for j in range(GROUP) if LAST[j] == a] for a in range(PLANES)]
RIM_ROWS = 20
HELD = -(-ROWS // 8) * 8
PACKS = 3 * HELD
FIELDS = PACKS + 56
EDGE = 32
BUDGET = 56 * 1024 * 1024


def turn(value, shift, axis=1):
    shift = shift % value.shape[axis]
    return value if shift == 0 else pltpu.roll(value, shift, axis)


def fetching(pairs, sems):
    copies = [pltpu.make_async_copy(a, b, sems.at[n]) for n, (a, b) in enumerate(pairs)]
    for copy in copies:
        copy.start()
    return copies


def pieces_of(levels, count):
    rows = 2 * levels
    number = -(-4 * rows // count)
    runs = [[] for _ in range(4)]
    for c in range(4):
        for j in range(number):
            low, high = max(c * rows, j * count), min((c + 1) * rows, (j + 1) * count)
            if low < high:
                runs[c].append((j, low - j * count, low - c * rows, high - low))
    return number, runs


class Level:
    def __init__(self, ref, base):
        self.ref, self.base = ref, base

    def plane(self, a):
        return self.ref[comb(self.base + a), :]

    def rows(self, low, size):
        return self.ref[pl.ds(self.base + low, size), :]


def lane_of(shape):
    return lax.broadcasted_iota(jnp.int32, shape, len(shape) - 1)


def row_of(shape):
    return lax.broadcasted_iota(jnp.int32, shape, 0)


def comb(a, count=GROUPS):
    return pl.ds(a, count, stride=PLANES)


def line_of(get, y):
    lane = lane_of((1, LANES))
    j = y % GROUP
    row = y // GROUP * PLANES + START[j]
    first, second = get(row), get(row + 1)
    third = get(row + 2) if START[j] + 2 < PLANES else second
    left = turn(jnp.where(lane >= OFF[j], first, second), -OFF[j])
    right = turn(jnp.where(lane >= OFF[j], second, third), -OFF[j])
    return left, right


def drop(value, lanes, lane):
    for at in lanes:
        value = jnp.where(lane == at, 0.0, value)
    return value


def store_terms(a, temp, flow_x, flow_y, te, tw, tn, ts):
    spread = DIFFUSE * temp
    te[a] = spread - flow_x
    tw[a] = spread + flow_x
    tn[a, 8 : 8 + GROUPS] = spread - flow_y
    ts[a, 8 : 8 + GROUPS] = spread + flow_y


def clear_terms(tn, ts):
    none = jnp.zeros((PLANES, 1, LANES), jnp.float32)
    for ref in (tn, ts):
        ref[:, 7:8] = none
        ref[:, 8 + GROUPS : 9 + GROUPS] = none


def inner_sum(a, te, tw, tn, ts):
    lane = lane_of((GROUPS, LANES))
    here = te[a]
    east = here if a == PLANES - 1 else jnp.where(lane == 0, te[a + 1], here)
    east = drop(turn(east, -1), LAST_OF[a], lane)
    here = tw[a]
    west = here if a == 0 else jnp.where(lane == LANES - 1, tw[a - 1], here)
    west = drop(turn(west, 1), FIRST_OF[a], lane)

    def plane(ref, at):
        down = 8 + (at >= PLANES) - (at < 0)
        return ref[at % PLANES, down : down + GROUPS]

    north = turn(jnp.where(lane >= LANES - 16, plane(tn, a + 1), plane(tn, a + 2)), 16)
    south = turn(jnp.where(lane < 16, plane(ts, a - 1), plane(ts, a - 2)), -16)
    return east + west + north + south


def choose(planes, lane, get):
    value = get(planes[0])
    for j in range(1, GROUP):
        low = (OFF[j] - (32 if planes is LAST else 0)) % LANES
        value = jnp.where(jnp.logical_and(lane >= low, lane < low + 16), get(planes[j]), value)
    return value


def forcing_kernel(
    levels, per, tiles_x, tiles_y,
    pos, temp_in, zonal_in, merid_in, depth_in, ocean_in, diag_in, source_in,
    fields_out, slots_out, around,
    temp, zonal, merid, depth, ocean, source, fields, slots,
    st, sx, sy, pt, te, tw, tn, ts, edges, holder, sems, out_sems,
):
    count = pos.shape[0]
    steps = levels // per
    number_pieces, runs = pieces_of(levels, count)
    slot = RIM_ROWS + number_pieces
    pairs = []
    for step in range(steps):
        chunk = pl.ds(step * per * ROWS, per * ROWS)
        pairs += [
            (a.at[chunk], b.at[chunk]) for a, b in ((temp_in, temp), (zonal_in, zonal), (merid_in, merid))
        ]
    pairs += [
        (a.reshape(ROWS, LANES), b)
        for a, b in (
            (source_in, source), (ocean_in, ocean), (depth_in, depth),
            (diag_in, fields.at[pl.ds(2 * HELD, ROWS)]),
        )
    ]
    copies = fetching(pairs, sems)
    results = []

    def send(value, target):
        copy = pltpu.make_async_copy(value, target, out_sems.at[len(results)])
        copy.start()
        results.append(copy)

    lane = lane_of((GROUPS, LANES))
    one = lane_of((1, LANES))
    q = lane % 16
    edges[...] = jnp.zeros_like(edges)

    def number(d, carry):
        holder[pos[d]] = d
        return carry

    lax.fori_loop(0, count, number, 0)
    me = lax.axis_index("gx") * tiles_y + lax.axis_index("gy")
    here = pos[me]
    row = here // tiles_x
    column = here % tiles_x
    sides = []
    for c, (dx, dy) in enumerate(SIDES):
        there = row + dy
        inside = jnp.logical_and(there >= 0, there < tiles_y)
        target = jnp.where(inside, there, 0) * tiles_x + (column + dx + tiles_x) % tiles_x
        device = jnp.where(inside, holder[target], -1)
        around[4 * count + c] = device
        sides.append(device)

    def look(y, carry):
        line = [holder[y * tiles_x + x] for x in range(tiles_x)]
        below = [holder[jnp.maximum(y - 1, 0) * tiles_x + x] for x in range(tiles_x)]
        above = [holder[jnp.minimum(y + 1, tiles_y - 1) * tiles_x + x] for x in range(tiles_x)]
        for x, device in enumerate(line):
            for c, other in enumerate((line[x - 1], line[(x + 1) % tiles_x], below[x], above[x])):
                around[c * count + device] = other * slot + RIM_ROWS
        return carry

    lax.fori_loop(0, tiles_y, look, 0)
    clear_terms(tn, ts)

    def add(flats, low, size, fresh):
        rows = pl.ds(low, size)
        total = [None] * 3
        for t, u, v in zip(*flats):
            t = t.rows(low, size)
            new = (t, t * u.rows(low, size), t * v.rows(low, size))
            total = [b if a is None else a + b for a, b in zip(total, new)]
        for ref, value in zip((st, sx, sy), total):
            ref[rows, :] = value if fresh else ref[rows, :] + value

    for step in range(steps):
        for copy in copies[3 * step : 3 * step + 3]:
            copy.wait()
        flats = [
            [Level(ref, (step * per + n) * ROWS) for n in range(per)] for ref in (temp, zonal, merid)
        ]

        def some(m, carry):
            add(flats, pl.multiple_of(m * 8, 8), 8, step == 0)
            return carry

        lax.fori_loop(0, ROWS // 8, some, 0, unroll=4)
        if ROWS % 8:
            add(flats, ROWS - ROWS % 8, ROWS % 8, step == 0)

        for n in range(per):
            k = step * per + n
            t, u, v = (flat[n] for flat in flats)

            loaded = {a: (t.plane(a), u.plane(a)) for a in sorted(set(START + LAST))}

            def term(planes, sign):
                own = choose(planes, lane, lambda a: loaded[a][0])
                flow = choose(planes, lane, lambda a: loaded[a][1])
                return DIFFUSE * own + sign * ADVECT * (flow * own)

            edges[0, 0:GROUPS] = jnp.where(q == k, turn(term(START, -1.0), k), edges[0, 0:GROUPS])
            edges[1, 0:GROUPS] = jnp.where(q == k, turn(term(LAST, 1.0), k + 17), edges[1, 0:GROUPS])
            rows = t.rows(0, 2)
            rows = DIFFUSE * rows - ADVECT * (v.rows(0, 2) * rows)
            edges[2, k : k + 1] = rows[0:1]
            edges[2, k + levels : k + levels + 1] = rows[1:2]
            rows = t.rows(ROWS - 2, 2)
            rows = DIFFUSE * rows + ADVECT * (v.rows(ROWS - 2, 2) * rows)
            edges[3, k : k + 1] = turn(jnp.where(one >= 16, rows[0:1], rows[1:2]), -16)
            edges[3, k + levels : k + levels + 1] = turn(rows[1:2], -16)

    for c in range(4):
        for j, device, low, size in runs[c]:
            slots[pl.ds(device * slot + RIM_ROWS + j, size, stride=slot), :] = edges[c, low : low + size]

    for copy in copies[3 * steps :]:
        copy.wait()

    part = fields.at[pl.ds(0, HELD)]
    mask = fields.at[pl.ds(HELD, HELD)]
    diag = fields.at[pl.ds(2 * HELD, HELD)]
    own = fields.at[pl.ds(PACKS, 56)]
    mask[0:ROWS] = depth[...] * ocean[...].astype(jnp.float32)

    def wet_of(rows):
        return ocean[rows, :].astype(jnp.float32)

    def masked(rows):
        return mask[rows, :]

    for a in range(PLANES):
        total = st[comb(a), :]
        pt[a] = total
        store_terms(a, total, ADVECT * sx[comb(a), :], ADVECT * sy[comb(a), :], te, tw, tn, ts)
    for a in range(PLANES):
        total = pt[a]
        wet = wet_of(comb(a))
        change = inner_sum(a, te, tw, tn, ts) - 4.0 * DIFFUSE * total
        part[comb(a), :] = source[comb(a), :] + (STERIC / levels) * wet * (total + wet * change)

    def mix(*values):
        value = values[-1]
        for at, low in ((6, 12), (5, 11), (4, 10), (3, 9), (2, 8), (1, 6), (0, 3)):
            value = jnp.where(q < low, values[at], value)
        return value

    def ends(planes, low):
        value = tn[planes[0], 8 : 8 + GROUPS]
        last = jnp.logical_and(lane >= low, lane < low + 16)
        return jnp.where(last, ts[planes[7], 8 : 8 + GROUPS], value)

    def beside(b, d, g, b_out, d_out):
        return g * b + d * d_out * (b - b_out)

    bp = choose(START, lane, lambda a: part[comb(a), :])
    dp = choose(START, lane, lambda a: masked(comb(a)))
    gp = choose(START, lane, lambda a: diag[comb(a), :])
    pp = beside(bp, dp, gp, turn(bp, -1), turn(dp, -1))
    pack_w = mix(
        bp, turn(dp, 3), turn(gp, 6), turn(pp, 6), turn(choose(START, lane, lambda a: te[a]), 9),
        turn(gp, 8), turn(dp, 8), turn(ends(START, OFF[7]), 12),
    )
    bp = choose(LAST, lane, lambda a: part[comb(a), :])
    dp = choose(LAST, lane, lambda a: masked(comb(a)))
    gp = choose(LAST, lane, lambda a: diag[comb(a), :])
    pp = beside(bp, dp, gp, turn(bp, 1), turn(dp, 1))
    pack_e = mix(
        turn(bp, 19), turn(dp, 22), turn(gp, 24), turn(pp, 27),
        turn(choose(LAST, lane, lambda a: tw[a]), 26),
        turn(gp, 29), turn(dp, 31), turn(ends(LAST, LANES - 16), 32),
    )
    own[0:GROUPS] = pack_w
    own[SLABS : SLABS + GROUPS] = pack_e
    north_l = tn[0, 8:9]
    north_r = tn[1, 8:9]
    south_13 = ts[PLANES - 2, 7 + GROUPS : 8 + GROUPS]
    south_14 = ts[PLANES - 1, 7 + GROUPS : 8 + GROUPS]
    south_l = turn(jnp.where(one >= 16, south_13, south_14), -16)
    south_r = turn(south_14, -16)
    own[48:49] = north_l
    own[49:50] = north_r
    own[50:51] = south_l
    own[51:52] = south_r
    send(fields, fields_out)
    deep = jnp.max(masked(slice(0, ROWS)), axis=(0, 1), keepdims=True)
    top = jnp.max(diag[0:ROWS], axis=(0, 1), keepdims=True) + 8.0 * deep * deep
    top = jnp.broadcast_to(top, (1, LANES))

    slots[pl.ds(RIM_ROWS - 1, count, stride=slot), :] = jnp.broadcast_to(top, (count, LANES))
    block_lane = lane_of((6, LANES))
    block_row = row_of((6, LANES))
    for c, first, rows_l, rows_r in ((2, True, north_l, north_r), (3, False, south_l, south_r)):
        base = 0 if first else ROWS - 6
        if first:
            spare = jnp.logical_and(block_row == 5, block_lane >= 80)
        else:
            spare = jnp.logical_and(block_row == 0, block_lane < 48)
        g = 0 if first else GROUPS - 1
        blocks = []
        block = slice(base, base + 6)
        for value, at in ((part[block, :], g), (masked(block), SLABS + g)):
            extra = jnp.broadcast_to(turn(own[at : at + 1], -16), (6, LANES))
            blocks.append(jnp.where(spare, extra, value))
        low = 0 if first else ROWS - 4
        diag_rows = diag[low : low + 4, :]
        third, fourth = (2, 3) if first else (SPAN_Y - 3, SPAN_Y - 4)
        b_l, b_r = line_of(lambda n: part[n : n + 1, :], third)
        d_l, d_r = line_of(lambda n: masked(slice(n, n + 1)), third)
        g_l, g_r = line_of(lambda n: diag[n : n + 1, :], third)
        bo_l, bo_r = line_of(lambda n: part[n : n + 1, :], fourth)
        do_l, do_r = line_of(lambda n: masked(slice(n, n + 1)), fourth)
        out_l = beside(b_l, d_l, g_l, bo_l, do_l)
        out_r = beside(b_r, d_r, g_r, bo_r, do_r)
        for at, value in ((112, turn(g_l, 112)), (113, turn(do_l, 113)), (114, turn(g_r, 3)), (115, turn(do_r, 4))):
            out_r = jnp.where(one == at, value, out_r)
        last_row = jnp.where(one == LANES - 1, top, rows_r)

        @pl.when(sides[c] >= 0)
        def _(c=c, blocks=blocks, diag_rows=diag_rows, singles=(out_l, out_r, rows_l, last_row)):
            at = sides[c] * slot
            slots[pl.ds(at, 6), :] = blocks[0]
            slots[pl.ds(at + 6, 6), :] = blocks[1]
            slots[pl.ds(at + 12, 4), :] = diag_rows
            for n, value in enumerate(singles):
                slots[pl.ds(at + 16 + n, 1), :] = value

    corner = jnp.logical_and(row_of((GROUPS, LANES)) == RIM_ROWS - 1, lane == LANES - 1)
    for c, pack in ((0, pack_w), (1, pack_e)):
        slots[pl.ds(sides[c] * slot, GROUPS), :] = jnp.where(corner, top, pack)
    for c, at in ((4, 0), (5, SLABS), (6, GROUPS - 1), (7, SLABS + GROUPS - 1)):
        @pl.when(sides[c] >= 0)
        def _(c=c, at=at):
            slots[pl.ds(sides[c] * slot, 1), :] = own[at : at + 1]
    send(slots, slots_out.reshape(count * slot, LANES))
    for copy in results:
        copy.wait()


SMEM = pl.BlockSpec(memory_space=pltpu.SMEM)


def solve_kernel(
    levels, tiles_y,
    around, rims, fields,
    vectors, hands,
    north_in, south_in, fb, fd, fg, pw, pe, ow, oe, ed, eg, ex, we, wn, last, rows,
):
    count = rims.shape[0]
    number_pieces, _ = pieces_of(levels, count)
    slot = RIM_ROWS + number_pieces
    share = 1 + number_pieces
    came = rims.reshape(count * slot, LANES)
    hand = hands.reshape(count * share, LANES)
    own = fields.at[pl.ds(PACKS, 56)]
    lane = lane_of((SLABS, LANES))
    slab = row_of((SLABS, LANES))
    one = lane_of((1, LANES))
    src = [around[4 * count + c] for c in range(8)]

    def fetch(c, low, high):
        value = came[pl.ds(jnp.maximum(src[c], 0) * slot + low, high - low), :]
        return jnp.where(src[c] >= 0, value, 0.0)

    me = lax.axis_index("gx") * tiles_y + lax.axis_index("gy")
    for n in range(number_pieces):
        side = jnp.minimum((n * count + me) // (2 * levels), 3)
        base = (side + 1 - 2 * (side % 2)) * count

        def relay(d, carry, n=n, base=base):
            row = around[base + d] + n
            hand[pl.ds(d * share + 1 + n, 1), :] = came[pl.ds(row, 1), :]
            return carry

        for d in range(count):
            relay(d, 0)

    north_in[0:RIM_ROWS] = fetch(3, 0, RIM_ROWS)
    south_in[0:RIM_ROWS] = fetch(2, 0, RIM_ROWS)
    strips = {2: south_in, 3: north_in}
    none = jnp.zeros((WIDE - ROWS + 4, LANES), jnp.float32)
    for ref in (fb, fd, fg):
        ref[ROWS - 4 : WIDE] = none
    for n, ref in enumerate((fb, fd, fg)):
        ref[0:ROWS] = fields[n * HELD : n * HELD + ROWS]
    for ref, low, high, n_lane, s_lane in ((fb, 0, 6, 80, 48), (fd, 6, 12, 80, 48), (fg, 12, 16, 96, 32)):
        size = high - low
        row, column = row_of((size, LANES)), lane_of((size, LANES))
        beyond = jnp.logical_and(row == size - 1, column >= n_lane)
        ref[ROWS : ROWS + size] = jnp.where(beyond, 0.0, strips[3][low:high])
        beyond = jnp.logical_and(row == 0, column < s_lane)
        ref[WIDE - size : WIDE] = jnp.where(beyond, 0.0, strips[2][low:high])
    empty = jnp.zeros((SLABS, LANES), jnp.float32)
    for ref, side, north, south in ((pw, 0, 6, 4), (pe, 1, 7, 5)):
        ref[...] = empty
        ref[0:GROUPS] = fetch(side, 0, GROUPS)
        ref[GROUPS : GROUPS + 1] = fetch(north, 0, 1)
        ref[SLABS - 1 : SLABS] = fetch(south, 0, 1)
    for ref, at, north, south in ((ow, 0, 5, 0), (oe, SLABS, 11, 6)):
        ref[...] = empty
        ref[0:GROUPS] = own[at : at + GROUPS]
        ref[GROUPS : GROUPS + 1] = turn(strips[3][north:north + 1], 16)
        ref[SLABS - 1 : SLABS] = turn(strips[2][south:south + 1], 16)

    def spread(ref, j):
        a = START[j]
        first, second = ref[comb(a, SLABS), :], ref[comb(a + 1, SLABS), :]
        third = ref[comb(a + 2, SLABS), :] if a + 2 < PLANES else second
        left = turn(jnp.where(lane >= OFF[j], first, second), -OFF[j])
        right = turn(jnp.where(lane >= OFF[j], second, third), -OFF[j])
        return left, right

    def seam_row(left, right, slab_at, lanes_at):
        east = turn(pe[slab_at : slab_at + 1], 112 - lanes_at)
        west = turn(pw[slab_at : slab_at + 1], 124 - lanes_at)
        right = jnp.where(one < 112, right, jnp.where(one < 116, east, jnp.where(one >= 124, west, 0.0)))
        return jnp.broadcast_to(left, (SLABS, LANES)), jnp.broadcast_to(right, (SLABS, LANES))

    seams = {
        0: ((0, seam_row(strips[2][18:19], strips[2][19:20], SLABS - 1, 28)),
            (GROUPS, seam_row(own[50:51], own[51:52], GROUPS - 1, 28))),
        GROUP - 1: ((GROUPS - 1, seam_row(strips[3][18:19], strips[3][19:20], GROUPS, 12)),
                    (SLABS - 1, seam_row(own[48:49], own[49:50], 0, 12))),
    }
    weight = STERIC / levels

    def missing(target, term, term_out, d, d_out, g):
        term, term_out, d, d_out, g = (
            turn(value[0], target - value[1]) for value in (term, term_out, d, d_out, g)
        )
        term = jnp.where(d > 0, weight * term, 0.0)
        term_out = jnp.where(d_out > 0, weight * term_out, 0.0)
        return jnp.where(one == target, g * term + d * d_out * (term - term_out), 0.0)

    def ring(ref, at):
        return ref[at : at + 1]

    outer = {j: [] for j in range(GROUP)}
    for j, at, beyond, o, lanes in ((0, 0, SLABS - 1, 0, 28), (GROUP - 1, GROUPS - 1, GROUPS, 16, 12)):
        own_row, corner = ring(pe, at), ring(pe, beyond)
        outer[j].append((1, at, missing(
            114, (corner, lanes + 2), (corner, lanes + 3), (own_row, o + 5), (own_row, o + 11), (own_row, o + 10),
        )))
        own_row, corner = ring(pw, at), ring(pw, beyond)
        outer[j].append((1, at, missing(
            125, (corner, lanes + 1), (corner, lanes), (own_row, o + 3), (own_row, o + 11), (own_row, o + 10),
        )))
    for j, at, c, j_out, d_l, d_r in ((2, GROUPS, 3, 3, (9, 96), (11, 79)), (5, SLABS - 1, 2, 4, (6, 48), (8, 31))):
        line_l, line_r = strips[c][16:17], strips[c][17:18]
        corner = ring(pw, at)
        outer[j].append((0, at, line_l + missing(
            0, (corner, OFF[j] + 9), (corner, OFF[j_out] + 9), (strips[c][d_l[0]:d_l[0] + 1], d_l[1]),
            (line_r, 113), (line_r, 112),
        )))
        corner = ring(pe, at)
        outer[j].append((1, at, jnp.where(one < 112, line_r, 0.0) + missing(
            111, (corner, OFF[j] + 9), (corner, OFF[j_out] + 9), (strips[c][d_r[0]:d_r[0] + 1], d_r[1]),
            (line_r, 115), (line_r, 114),
        )))
    for j in range(GROUP):
        o = OFF[j]
        inside = slab < GROUPS
        halves = [
            jnp.zeros((SLABS, LANES), jnp.float32),
            jnp.where(
                jnp.logical_and(inside, lane == 114), turn(pe[...], 114 - o - 8),
                jnp.where(jnp.logical_and(inside, lane == 125), turn(pw[...], 125 - o - 8), 0.0),
            ),
        ]
        for half, at, line in outer[j]:
            halves[half] = halves[half] + jnp.where(slab == at, line, 0.0)
        ex[j, :, 0:LANES] = halves[0]
        ex[j, :, LANES:] = halves[1]

        def rim(right, q, width):
            east = turn(pe[...], 112 - o - q)
            west = turn(pw[...], 128 - width - o - q)
            value = jnp.where(lane < 112 + width, east, jnp.where(lane >= 128 - width, west, 0.0))
            return jnp.where(lane < 112, right, value)

        left, right = spread(fd, j)
        right = rim(right, 3, 3)
        wet_l = jnp.where(left > 0, weight, 0.0)
        wet_r = jnp.where(right > 0, weight, 0.0)
        ed[j, :, 0:LANES] = left
        ed[j, :, LANES:] = right
        left, right = spread(fg, j)
        eg[j, :, 0:LANES] = left
        eg[j, :, LANES:] = rim(right, 6, 2)
        left, right = spread(fb, j)
        right = rim(right, 0, 3)
        seam_l = jnp.where(lane == 0, turn(pw[...], -o - 9), 0.0)
        seam_r = jnp.where(lane == 127, turn(ow[...], 127 - o - 9), 0.0)
        seam_r = jnp.where(lane == 111, turn(pe[...], 111 - o - 9), seam_r)
        seam_r = jnp.where(lane == 112, turn(oe[...], 112 - o - 9), seam_r)
        for at, (row_l, row_r) in seams.get(j, ()):
            seam_l = seam_l + jnp.where(slab == at, row_l, 0.0)
            seam_r = seam_r + jnp.where(slab == at, row_r, 0.0)
        vectors[0, j, :, 0:LANES] = left + wet_l * seam_l
        vectors[0, j, :, LANES:] = right + wet_r * seam_r

    for j in range(GROUP):
        d = ed[j]
        we[j] = d * turn(d, -1)
        above = ed[j + 1] if j < GROUP - 1 else turn(ed[0], -1, 0)
        wn[j] = d * above

    top = jnp.max(came[pl.ds(RIM_ROWS - 1, count, stride=slot), :], axis=0, keepdims=True)
    top = jnp.max(jnp.where(one == LANES - 1, top, 0.0), axis=1, keepdims=True)
    scale = STRETCH / top

    big = (SLABS, 2 * LANES)
    mine = jnp.logical_and(row_of(big) < GROUPS, lane_of(big) < SPAN_X)
    pair = 0
    for k in range(5):
        sums = [None] * (k + 1)
        new = last if k == 4 else vectors.at[k]
        if k:
            v = vectors.at[k - 1]
            flow_below = wn[GROUP - 1] * (v[GROUP - 1] - turn(v[0], -1, 0))
            flow_below = turn(flow_below, 1, 0)
        for j in range(GROUP):
            if k:
                here = v[j]
                above = v[j + 1] if j < GROUP - 1 else turn(v[0], -1, 0)
                flow_x = we[j] * (here - turn(here, -1))
                flow_y = wn[j] * (here - above)
                image = eg[j] * here + (flow_x - turn(flow_x, 1)) + (flow_y - flow_below)
                if k == 1:
                    image = image + ex[j]
                fresh = scale * image - (STRETCH * ROOTS[k - 1]) * here
                flow_below = flow_y
                new[j] = fresh
            else:
                fresh = new[j]
            held = jnp.where(mine, fresh, 0.0)
            for i in range(k + 1):
                other = vectors[i, j] if i < k else held
                value = held * other
                sums[i] = value if sums[i] is None else sums[i] + value
        for i in range(k + 1):
            rows[pair : pair + 1] = jnp.sum(sums[i][:, 0:LANES] + sums[i][:, LANES:], axis=0, keepdims=True)
            pair += 1
    rows[pair : pair + 1] = jnp.where(one == 0, top, 0.0)
    total = jnp.sum(rows[...], axis=1, keepdims=True)
    spot = row_of((16, LANES)) == lane_of((16, LANES))
    line = jnp.sum(jnp.where(spot, total, 0.0), axis=0, keepdims=True)
    hand[pl.ds(0, count, stride=share), :] = jnp.broadcast_to(line, (count, LANES))


def finish_kernel(
    levels, per, around, hands, vectors, edges, inner, tracer_out, surface_out,
    cells, flat, left, right, message, out_sems,
):
    count = hands.shape[0]
    number_pieces, runs = pieces_of(levels, count)
    share = 1 + number_pieces
    came = hands.reshape(count * share, LANES)
    steps = levels // per
    chunks = [pl.ds(step * per * ROWS, per * ROWS) for step in range(steps)]
    row = jnp.sum(came[pl.ds(0, count, stride=share), :], axis=0, keepdims=True)
    one = lane_of((1, LANES))
    entry = {}
    pair = 0
    for k in range(5):
        for i in range(k + 1):
            value = jnp.sum(jnp.where(one == pair, row, 0.0), axis=1, keepdims=True)
            entry[i, k] = entry[k, i] = value
            pair += 1
    top = jnp.sum(jnp.where(one == pair, row, 0.0), axis=1, keepdims=True) * (1.0 / count)

    def image(c):
        out = [None] * 5
        for k in range(4):
            if c[k] is None:
                continue
            low = ROOTS[k] * c[k]
            out[k] = low if out[k] is None else out[k] + low
            out[k + 1] = (1.0 / STRETCH) * c[k]
        return out

    def dot(a, b):
        total = None
        for i in range(5):
            if a[i] is None:
                continue
            inner = None
            for j in range(5):
                if b[j] is not None:
                    value = entry[i, j] * b[j]
                    inner = value if inner is None else inner + value
            total = a[i] * inner if total is None else total + a[i] * inner
        return total

    def axpy(a, s, b):
        return [
            x if y is None else (s * y if x is None else x + s * y) for x, y in zip(a, b)
        ]

    r = [jnp.ones((1, 1), jnp.float32)] + [None] * 4
    p = list(r)
    x = [None] * 5
    rr = entry[0, 0]
    for n in range(ITERS):
        q = image(p)
        step = rr / jnp.maximum(dot(p, q), TINY)
        step = jnp.clip(step, top * (1.0 / HIGH_RATE), top * (1.0 / LOW_RATE))
        x = axpy(x, step, p)
        if n < ITERS - 1:
            r = axpy(r, -step, q)
            fresh = jnp.maximum(dot(r, r), 0.0)
            p = axpy(r, fresh / jnp.maximum(rr, TINY), p)
            rr = fresh
    factors = [c / top for c in x[:4]]
    for j in range(GROUP):
        value = None
        for k in range(4):
            term = factors[k] * vectors[k, j]
            value = term if value is None else value + term
        left[j] = turn(value[:, 0:LANES], OFF[j])
        right[j] = turn(value[:, LANES:], OFF[j])
    lane = lane_of((SLABS, LANES))
    for a in range(PLANES):
        value = None
        for j in range(GROUP):
            for half, ref in ((0, left), (1, right)):
                low = max(SPAN_X * j + LANES * half - LANES * a, 0)
                high = min(SPAN_X * j + (LANES if half == 0 else SPAN_X) - LANES * a, LANES)
                if low >= high:
                    continue
                value = ref[j] if value is None else jnp.where(lane >= low, ref[j], value)
        flat[comb(a), :] = value[0:GROUPS]
    results = [pltpu.make_async_copy(flat, surface_out.reshape(ROWS, LANES), out_sems.at[0])]
    results[0].start()

    for c in range(4):
        for j, device, low, size in runs[c ^ 1]:
            value = came[pl.ds(device * share + 1 + j, size, stride=share), :]
            message[c, low : low + size] = jnp.where(around[4 * count + c] >= 0, value, 0.0)
    second = lane_of((SLABS, LANES)) % 16 == 1
    sums = []
    for k in range(levels):
        value = edges[2 * levels - 1] * jnp.concatenate([
            jnp.where(second, turn(message[1], 1 - k), turn(message[0], -k)),
            message[2, k : k + 1], message[2, k + levels : k + levels + 1],
            message[3, k : k + 1], message[3, k + levels : k + levels + 1],
            jnp.zeros((EDGE - SLABS - 4, LANES), jnp.float32),
        ], axis=0)
        if k:
            value = value + edges[2 * levels + k - 1] * sums[-1]
        sums.append(value * edges[levels - 1 + k])
    for k in range(levels - 2, -1, -1):
        sums[k] = sums[k] + edges[k] * sums[k + 1]
    lane = lane_of((GROUPS, LANES))
    slab = row_of((GROUPS, LANES))
    for k in range(levels):
        west = sums[k][0:GROUPS]
        east = turn(west, -18)
        south_l, south_r = sums[k][SLABS : SLABS + 1], sums[k][SLABS + 1 : SLABS + 2]
        north_l = turn(sums[k][SLABS + 2 : SLABS + 3], 16)
        north_r = turn(sums[k][SLABS + 3 : SLABS + 4], 16)
        for a in range(PLANES):
            rim = None
            for at, source in [(at, west) for at in FIRST_OF[a]] + [(at, east) for at in LAST_OF[a]]:
                rim = jnp.where(lane == at, source, 0.0 if rim is None else rim)
            rows = comb(k * ROWS + a)
            if rim is None:
                cells[rows, :] = inner[rows, :]
                continue
            if a == 0:
                rim = rim + jnp.where(slab == 0, south_l, 0.0)
            if a == 1:
                rim = rim + jnp.where(jnp.logical_and(slab == 0, lane < 112), south_r, 0.0)
            if a == PLANES - 2:
                rim = rim + jnp.where(jnp.logical_and(slab == GROUPS - 1, lane >= 16), north_l, 0.0)
            if a == PLANES - 1:
                rim = rim + jnp.where(slab == GROUPS - 1, jnp.where(lane < 16, north_l, north_r), 0.0)
            cells[rows, :] = inner[rows, :] + rim
        if k % per == per - 1:
            step = k // per
            copy = pltpu.make_async_copy(
                cells.at[chunks[step]], tracer_out.at[chunks[step]], out_sems.at[1 + step]
            )
            copy.start()
            results.append(copy)
    for copy in results:
        copy.wait()


def tracer_kernel(
    levels, per, temp_in, zonal_in, merid_in, rates_in, fields_in,
    out, edges,
    temp, zonal, merid, rates, depth, ocean,
    te, tw, tn, ts, stepped, border, sems,
):
    steps = levels // per
    pairs = [(fields_in.at[pl.ds(HELD, HELD)], depth)]
    for step in range(steps):
        chunk = pl.ds(step * per * ROWS, per * ROWS)
        pairs += [
            (a.at[chunk], b.at[chunk]) for a, b in ((temp_in, temp), (zonal_in, zonal), (merid_in, merid))
        ]
    copies = fetching(pairs + [(rates_in.reshape((levels - 1) * ROWS, LANES), rates)], sems)
    lane = lane_of((GROUPS, LANES))
    one = lane_of((1, LANES))
    clear_terms(tn, ts)

    copies[0].wait()
    ocean[...] = jnp.where(depth[0:ROWS] > 0, 1.0, 0.0)
    for step in range(steps):
        for copy in copies[1 + 3 * step : 4 + 3 * step]:
            copy.wait()

        def level(k, carry):
            t, u, v = (Level(ref, k * ROWS) for ref in (temp, zonal, merid))
            for a in range(PLANES):
                own = t.plane(a)
                quarter = ADVECT * own
                store_terms(a, own, u.plane(a) * quarter, v.plane(a) * quarter, te, tw, tn, ts)
            for a in range(PLANES):
                own = t.plane(a)
                change = inner_sum(a, te, tw, tn, ts) - 4.0 * DIFFUSE * own
                stepped[k, a] = own + ocean[comb(a), :] * change
            return carry

        lax.fori_loop(step * per, step * per + per, level, 0)
    copies[-1].wait()

    def block(a, carry):
        for low in range(0, GROUPS, 8):
            size = min(8, GROUPS - low)

            def rows(k):
                return pl.ds(k * ROWS + low * PLANES + a, size, stride=PLANES)

            gains = []
            sums = []
            for k in range(levels):
                value = stepped[k, a, low : low + size]
                pivot = 1.0
                if k > 0:
                    pivot = pivot + upper - upper * gains[-1]
                    value = value + upper * sums[-1]
                if k < levels - 1:
                    lower = rates[rows(k), :]
                    inverse = 1.0 / (pivot + lower)
                    gains.append(lower * inverse)
                    upper = lower
                else:
                    inverse = 1.0 / pivot
                sums.append(value * inverse)
            result = sums[-1]
            out[rows(levels - 1), :] = result
            for k in range(levels - 2, -1, -1):
                result = sums[k] + gains[k] * result
                out[rows(k), :] = result
        return carry

    lax.fori_loop(0, PLANES, block, 0)

    def edge(ref, base, at):
        def get(a):
            return ref[comb(base + a), :].astype(jnp.float32)

        border[0:GROUPS] = jnp.where(
            lane % 16 == 1, turn(choose(LAST, lane, get), 18), choose(START, lane, get)
        )
        border[SLABS : SLABS + 2] = ref[base : base + 2, :].astype(jnp.float32)
        rows = ref[base + ROWS - 2 : base + ROWS, :].astype(jnp.float32)
        border[SLABS + 2 : SLABS + 3] = turn(jnp.where(one >= 16, rows[0:1], rows[1:2]), -16)
        border[SLABS + 3 : SLABS + 4] = turn(rows[1:2], -16)
        edges[at] = border[...]

    border[...] = jnp.zeros_like(border)
    edge(ocean, 0, 2 * levels - 1)
    gain = None
    for k in range(levels):
        pivot = 1.0
        if k > 0:
            upper = edges[2 * levels + k - 1]
            pivot = pivot + upper - upper * gain
        if k < levels - 1:
            edge(rates, k * ROWS, 2 * levels + k)
            lower = edges[2 * levels + k]
            inverse = 1.0 / (pivot + lower)
            gain = lower * inverse
            edges[k] = gain
        else:
            inverse = 1.0 / pivot
        edges[levels - 1 + k] = inverse


def on_device(
    thermal_anomaly,
    zonal_flow_ratio,
    meridional_flow_ratio,
    diffusion_rates,
    ocean_bottom_scaled,
    ocean_indicator,
    operator_diagonal,
    elevation_source,
    block_positions,
):
    levels, cells = thermal_anomaly.shape[1:]
    nx = lax.axis_size("gx")
    ny = lax.axis_size("gy")
    count = block_positions.shape[0]
    planes = (ocean_bottom_scaled, ocean_indicator, operator_diagonal, elevation_source)
    depth, ocean, diag, source = planes
    f32 = jnp.float32
    per = next(n for n in (4, 2, 6, levels) if levels % n == 0 and n * ROWS % 8 == 0)
    steps = levels // per
    few = next(n for n in (2, 4, 6, levels) if levels % n == 0 and n * ROWS % 8 == 0)
    large = pltpu.CompilerParams(vmem_limit_bytes=BUDGET)
    middle = pltpu.CompilerParams(vmem_limit_bytes=BUDGET * 7 // 8)
    small = pltpu.CompilerParams(vmem_limit_bytes=BUDGET // 3)
    temp, zonal, merid = (
        array.reshape(levels * ROWS, LANES)
        for array in (thermal_anomaly, zonal_flow_ratio, meridional_flow_ratio)
    )
    rates = diffusion_rates.reshape(levels - 1, 1, cells)
    hbm = pl.BlockSpec(memory_space=pltpu.HBM)
    here = pl.BlockSpec(memory_space=pltpu.VMEM)

    def vmem(*shape, kind=f32):
        return pltpu.VMEM(shape, kind)

    def out(*shape, kind=f32):
        return jax.ShapeDtypeStruct(shape, kind)

    def sems(number):
        return pltpu.SemaphoreType.DMA((number,))

    deep = vmem(levels * ROWS, LANES)
    flat = vmem(ROWS, LANES)
    flat_int = vmem(ROWS, LANES, kind=jnp.int32)
    plane = vmem(PLANES, GROUPS, LANES)
    tall = vmem(PLANES, 40, LANES)
    numbers = pltpu.SMEM((count,), jnp.int32)
    number_pieces, _ = pieces_of(levels, count)
    slot = RIM_ROWS + number_pieces
    share = 1 + number_pieces
    fields, slots, around = pl.pallas_call(
        functools.partial(forcing_kernel, levels, few, nx, ny),
        in_specs=[SMEM] + [hbm] * 7,
        out_specs=[hbm] * 2 + [SMEM],
        out_shape=[
            out(FIELDS, LANES), out(count, 1, slot * LANES), out(4 * count + 8, kind=jnp.int32),
        ],
        scratch_shapes=[deep] * 3 + [flat, flat_int, flat]
        + [vmem(FIELDS, LANES), vmem(count * slot, LANES)]
        + [flat] * 3 + [plane] * 3 + [tall] * 2
        + [vmem(4, 2 * levels, LANES), numbers, sems(3 * (levels // few) + 4), sems(2)],
        compiler_params=large,
        name="forcing",
    )(block_positions, temp, zonal, merid, depth, ocean, diag, source)
    rims = lax.all_to_all(slots, BOTH, 0, 0, tiled=True)

    inner, edges = pl.pallas_call(
        functools.partial(tracer_kernel, levels, per),
        in_specs=[hbm] * 5,
        out_specs=[here] * 2,
        out_shape=[out(levels * ROWS, LANES), out(3 * levels - 1, EDGE, LANES)],
        scratch_shapes=[deep] * 3 + [vmem((levels - 1) * ROWS, LANES), vmem(HELD, LANES), flat]
        + [plane] * 2 + [tall] * 2
        + [vmem(levels, PLANES, GROUPS, LANES), vmem(EDGE, LANES), sems(3 * steps + 2)],
        compiler_params=middle,
        name="tracer",
    )(temp, zonal, merid, rates, fields)

    rims, edges = lax.optimization_barrier((rims, edges))
    extended = vmem(GROUP, SLABS, 2 * LANES)
    vectors, hand = pl.pallas_call(
        functools.partial(solve_kernel, levels, ny),
        in_specs=[SMEM] + [here] * 2,
        out_specs=[here] * 2,
        out_shape=[out(4, GROUP, SLABS, 2 * LANES), out(count, 1, share * LANES)],
        scratch_shapes=[vmem(SLABS, LANES)] * 2 + [vmem(WIDE, LANES)] * 3 + [vmem(SLABS, LANES)] * 4 + [extended] * 6 + [vmem(16, LANES)],
        compiler_params=small,
        name="vectors",
    )(around, rims, fields)
    hands = lax.all_to_all(hand, BOTH, 0, 0, tiled=True)

    new_temp, surface = pl.pallas_call(
        functools.partial(finish_kernel, levels, per),
        in_specs=[SMEM] + [here] * 4,
        out_specs=[hbm] * 2,
        out_shape=[out(levels * ROWS, LANES), out(1, cells)],
        scratch_shapes=[
            deep, flat, vmem(GROUP, SLABS, LANES), vmem(GROUP, SLABS, LANES), vmem(4, 2 * levels, LANES),
            sems(1 + steps),
        ],
        compiler_params=small,
        name="finish",
    )(around, hands, vectors, edges, inner)
    return new_temp.reshape(1, levels, cells), surface


def solution(mesh):
    deep = P(BOTH, None, None)
    flat = P(BOTH, None)
    return jax.shard_map(
        on_device,
        mesh=mesh,
        in_specs=(deep, deep, deep, deep, flat, flat, flat, flat, P()),
        out_specs=(deep, flat),
        check_vma=False,
    )
```

```python
import functools

import jax
import jax.numpy as jnp
from jax import lax
from jax.experimental import pallas as pl
from jax.experimental.pallas import tpu as pltpu
from jax.sharding import PartitionSpec as P

ITERS = 4
SPAN_X = 240
SPAN_Y = 160
RIM = 4
ADVECT = 0.25
DIFFUSE = 0.12
STERIC = 0.5
LOW_RATE = 0.05
HIGH_RATE = 32.5
ROOTS = (0.02, 0.35, 0.1, 0.2)
STRETCH = 4.0
TINY = 1e-30
BOTH = ("gx", "gy")
SIDES = ((-1, 0), (1, 0), (0, -1), (0, 1), (-1, -1), (1, -1), (-1, 1), (1, 1))

LANES = 128
GROUP = 8
GROUPS = SPAN_Y // GROUP
PLANES = GROUP * SPAN_X // LANES
ROWS = GROUPS * PLANES
SLABS = GROUPS + 4
WIDE = SLABS * PLANES
START = [SPAN_X * j // LANES for j in range(GROUP)]
OFF = [SPAN_X * j % LANES for j in range(GROUP)]
LAST = [(SPAN_X * j + SPAN_X - 1) // LANES for j in range(GROUP)]
END = [(SPAN_X * j + SPAN_X - 1) % LANES for j in range(GROUP)]
FIRST_OF = [[OFF[j] for j in range(GROUP) if START[j] == a] for a in range(PLANES)]
LAST_OF = [[END[j] for j in range(GROUP) if LAST[j] == a] for a in range(PLANES)]
RIM_ROWS = 20
HELD = -(-ROWS // 8) * 8
PACKS = 3 * HELD
FIELDS = PACKS + 56
EDGE = 32
BUDGET = 32 * 1024 * 1024


def turn(value, shift, axis=1):
    shift = shift % value.shape[axis]
    return value if shift == 0 else pltpu.roll(value, shift, axis)


def fetching(pairs, sems):
    copies = [pltpu.make_async_copy(a, b, sems.at[n]) for n, (a, b) in enumerate(pairs)]
    for copy in copies:
        copy.start()
    return copies


def pieces_of(levels, count):
    rows = 2 * levels
    number = -(-4 * rows // count)
    runs = [[] for _ in range(4)]
    for c in range(4):
        for j in range(number):
            low, high = max(c * rows, j * count), min((c + 1) * rows, (j + 1) * count)
            if low < high:
                runs[c].append((j, low - j * count, low - c * rows, high - low))
    return number, runs


class Level:
    def __init__(self, ref, base):
        self.ref, self.base = ref, base

    def plane(self, a):
        return self.ref[comb(self.base + a), :]

    def rows(self, low, size):
        return self.ref[pl.ds(self.base + low, size), :]


def lane_of(shape):
    return lax.broadcasted_iota(jnp.int32, shape, len(shape) - 1)


def row_of(shape):
    return lax.broadcasted_iota(jnp.int32, shape, 0)


def comb(a, count=GROUPS):
    return pl.ds(a, count, stride=PLANES)


def line_of(get, y):
    lane = lane_of((1, LANES))
    j = y % GROUP
    row = y // GROUP * PLANES + START[j]
    first, second = get(row), get(row + 1)
    third = get(row + 2) if START[j] + 2 < PLANES else second
    left = turn(jnp.where(lane >= OFF[j], first, second), -OFF[j])
    right = turn(jnp.where(lane >= OFF[j], second, third), -OFF[j])
    return left, right


def drop(value, lanes, lane):
    for at in lanes:
        value = jnp.where(lane == at, 0.0, value)
    return value


def store_terms(a, temp, flow_x, flow_y, te, tw, tn, ts):
    spread = DIFFUSE * temp
    te[a] = spread - flow_x
    tw[a] = spread + flow_x
    tn[a, 8 : 8 + GROUPS] = spread - flow_y
    ts[a, 8 : 8 + GROUPS] = spread + flow_y


def clear_terms(tn, ts):
    none = jnp.zeros((PLANES, 1, LANES), jnp.float32)
    for ref in (tn, ts):
        ref[:, 7:8] = none
        ref[:, 8 + GROUPS : 9 + GROUPS] = none


def inner_sum(a, te, tw, tn, ts):
    lane = lane_of((GROUPS, LANES))
    here = te[a]
    east = here if a == PLANES - 1 else jnp.where(lane == 0, te[a + 1], here)
    east = drop(turn(east, -1), LAST_OF[a], lane)
    here = tw[a]
    west = here if a == 0 else jnp.where(lane == LANES - 1, tw[a - 1], here)
    west = drop(turn(west, 1), FIRST_OF[a], lane)

    def plane(ref, at):
        down = 8 + (at >= PLANES) - (at < 0)
        return ref[at % PLANES, down : down + GROUPS]

    north = turn(jnp.where(lane >= LANES - 16, plane(tn, a + 1), plane(tn, a + 2)), 16)
    south = turn(jnp.where(lane < 16, plane(ts, a - 1), plane(ts, a - 2)), -16)
    return east + west + north + south


def choose(planes, lane, get):
    value = get(planes[0])
    for j in range(1, GROUP):
        low = (OFF[j] - (32 if planes is LAST else 0)) % LANES
        value = jnp.where(jnp.logical_and(lane >= low, lane < low + 16), get(planes[j]), value)
    return value


def forcing_kernel(
    levels, per, tiles_x, tiles_y,
    pos_in, temp_in, zonal_in, merid_in, depth_in, ocean_in, diag_in, source_in,
    fields, slots_out, around,
    temp, zonal, merid, depth, ocean, source, slots,
    st, sx, sy, pt, te, tw, tn, ts, edges, pos, holder, sems, out_sems,
):
    count = pos.shape[0]
    steps = levels // per
    number_pieces, runs = pieces_of(levels, count)
    slot = RIM_ROWS + number_pieces
    pairs = []
    for step in range(steps):
        chunk = pl.ds(step * per * ROWS, per * ROWS)
        pairs += [
            (a.at[chunk], b.at[chunk]) for a, b in ((temp_in, temp), (zonal_in, zonal), (merid_in, merid))
        ]
    pairs += [
        (a.reshape(ROWS, LANES), b)
        for a, b in (
            (source_in, source), (ocean_in, ocean), (depth_in, depth),
            (diag_in, fields.at[pl.ds(2 * HELD, ROWS)]),
        )
    ]
    copies = fetching([(pos_in, pos)] + pairs, sems)
    copies.pop(0).wait()
    results = []

    def send(value, target):
        copy = pltpu.make_async_copy(value, target, out_sems.at[len(results)])
        copy.start()
        results.append(copy)

    lane = lane_of((GROUPS, LANES))
    one = lane_of((1, LANES))
    q = lane % 16
    edges[...] = jnp.zeros_like(edges)

    def number(d, carry):
        holder[pos[d]] = d
        return carry

    lax.fori_loop(0, count, number, 0)
    me = lax.axis_index("gx") * tiles_y + lax.axis_index("gy")
    here = pos[me]
    row = here // tiles_x
    column = here % tiles_x
    sides = []
    for c, (dx, dy) in enumerate(SIDES):
        there = row + dy
        inside = jnp.logical_and(there >= 0, there < tiles_y)
        target = jnp.where(inside, there, 0) * tiles_x + (column + dx + tiles_x) % tiles_x
        device = jnp.where(inside, holder[target], -1)
        around[4 * count + c] = device
        sides.append(device)

    def look(y, carry):
        line = [holder[y * tiles_x + x] for x in range(tiles_x)]
        below = [holder[jnp.maximum(y - 1, 0) * tiles_x + x] for x in range(tiles_x)]
        above = [holder[jnp.minimum(y + 1, tiles_y - 1) * tiles_x + x] for x in range(tiles_x)]
        for x, device in enumerate(line):
            for c, other in enumerate((line[x - 1], line[(x + 1) % tiles_x], below[x], above[x])):
                around[c * count + device] = other * slot + RIM_ROWS
        return carry

    lax.fori_loop(0, tiles_y, look, 0)
    clear_terms(tn, ts)

    def add(flats, low, size, fresh):
        rows = pl.ds(low, size)
        total = [None] * 3
        for t, u, v in zip(*flats):
            t = t.rows(low, size)
            new = (t, t * u.rows(low, size), t * v.rows(low, size))
            total = [b if a is None else a + b for a, b in zip(total, new)]
        for ref, value in zip((st, sx, sy), total):
            ref[rows, :] = value if fresh else ref[rows, :] + value

    for step in range(steps):
        for copy in copies[3 * step : 3 * step + 3]:
            copy.wait()
        flats = [
            [Level(ref, (step * per + n) * ROWS) for n in range(per)] for ref in (temp, zonal, merid)
        ]

        def some(m, carry):
            add(flats, pl.multiple_of(m * 8, 8), 8, step == 0)
            return carry

        lax.fori_loop(0, ROWS // 8, some, 0, unroll=4)
        if ROWS % 8:
            add(flats, ROWS - ROWS % 8, ROWS % 8, step == 0)

        for n in range(per):
            k = step * per + n
            t, u, v = (flat[n] for flat in flats)

            loaded = {a: (t.plane(a), u.plane(a)) for a in sorted(set(START + LAST))}

            def term(planes, sign):
                own = choose(planes, lane, lambda a: loaded[a][0])
                flow = choose(planes, lane, lambda a: loaded[a][1])
                return DIFFUSE * own + sign * ADVECT * (flow * own)

            edges[0, 0:GROUPS] = jnp.where(q == k, turn(term(START, -1.0), k), edges[0, 0:GROUPS])
            edges[1, 0:GROUPS] = jnp.where(q == k, turn(term(LAST, 1.0), k + 17), edges[1, 0:GROUPS])
            rows = t.rows(0, 2)
            rows = DIFFUSE * rows - ADVECT * (v.rows(0, 2) * rows)
            edges[2, k : k + 1] = rows[0:1]
            edges[2, k + levels : k + levels + 1] = rows[1:2]
            rows = t.rows(ROWS - 2, 2)
            rows = DIFFUSE * rows + ADVECT * (v.rows(ROWS - 2, 2) * rows)
            edges[3, k : k + 1] = turn(jnp.where(one >= 16, rows[0:1], rows[1:2]), -16)
            edges[3, k + levels : k + levels + 1] = turn(rows[1:2], -16)

    for c in range(4):
        for j, device, low, size in runs[c]:
            slots[pl.ds(device * slot + RIM_ROWS + j, size, stride=slot), :] = edges[c, low : low + size]

    for copy in copies[3 * steps :]:
        copy.wait()

    part = fields.at[pl.ds(0, HELD)]
    mask = fields.at[pl.ds(HELD, HELD)]
    diag = fields.at[pl.ds(2 * HELD, HELD)]
    own = fields.at[pl.ds(PACKS, 56)]
    mask[0:ROWS] = depth[...] * ocean[...].astype(jnp.float32)

    def wet_of(rows):
        return ocean[rows, :].astype(jnp.float32)

    def masked(rows):
        return mask[rows, :]

    for a in range(PLANES):
        total = st[comb(a), :]
        pt[a] = total
        store_terms(a, total, ADVECT * sx[comb(a), :], ADVECT * sy[comb(a), :], te, tw, tn, ts)
    for a in range(PLANES):
        total = pt[a]
        wet = wet_of(comb(a))
        change = inner_sum(a, te, tw, tn, ts) - 4.0 * DIFFUSE * total
        part[comb(a), :] = source[comb(a), :] + (STERIC / levels) * wet * (total + wet * change)

    def mix(*values):
        value = values[-1]
        for at, low in ((6, 12), (5, 11), (4, 10), (3, 9), (2, 8), (1, 6), (0, 3)):
            value = jnp.where(q < low, values[at], value)
        return value

    def ends(planes, low):
        value = tn[planes[0], 8 : 8 + GROUPS]
        last = jnp.logical_and(lane >= low, lane < low + 16)
        return jnp.where(last, ts[planes[7], 8 : 8 + GROUPS], value)

    def beside(b, d, g, b_out, d_out):
        return g * b + d * d_out * (b - b_out)

    bp = choose(START, lane, lambda a: part[comb(a), :])
    dp = choose(START, lane, lambda a: masked(comb(a)))
    gp = choose(START, lane, lambda a: diag[comb(a), :])
    pp = beside(bp, dp, gp, turn(bp, -1), turn(dp, -1))
    pack_w = mix(
        bp, turn(dp, 3), turn(gp, 6), turn(pp, 6), turn(choose(START, lane, lambda a: te[a]), 9),
        turn(gp, 8), turn(dp, 8), turn(ends(START, OFF[7]), 12),
    )
    bp = choose(LAST, lane, lambda a: part[comb(a), :])
    dp = choose(LAST, lane, lambda a: masked(comb(a)))
    gp = choose(LAST, lane, lambda a: diag[comb(a), :])
    pp = beside(bp, dp, gp, turn(bp, 1), turn(dp, 1))
    pack_e = mix(
        turn(bp, 19), turn(dp, 22), turn(gp, 24), turn(pp, 27),
        turn(choose(LAST, lane, lambda a: tw[a]), 26),
        turn(gp, 29), turn(dp, 31), turn(ends(LAST, LANES - 16), 32),
    )
    own[0:GROUPS] = pack_w
    own[SLABS : SLABS + GROUPS] = pack_e
    north_l = tn[0, 8:9]
    north_r = tn[1, 8:9]
    south_13 = ts[PLANES - 2, 7 + GROUPS : 8 + GROUPS]
    south_14 = ts[PLANES - 1, 7 + GROUPS : 8 + GROUPS]
    south_l = turn(jnp.where(one >= 16, south_13, south_14), -16)
    south_r = turn(south_14, -16)
    own[48:49] = north_l
    own[49:50] = north_r
    own[50:51] = south_l
    own[51:52] = south_r
    deep = jnp.max(masked(slice(0, ROWS)), axis=(0, 1), keepdims=True)
    top = jnp.max(diag[0:ROWS], axis=(0, 1), keepdims=True) + 8.0 * deep * deep
    top = jnp.broadcast_to(top, (1, LANES))

    slots[pl.ds(RIM_ROWS - 1, count, stride=slot), :] = jnp.broadcast_to(top, (count, LANES))
    block_lane = lane_of((6, LANES))
    block_row = row_of((6, LANES))
    for c, first, rows_l, rows_r in ((2, True, north_l, north_r), (3, False, south_l, south_r)):
        base = 0 if first else ROWS - 6
        if first:
            spare = jnp.logical_and(block_row == 5, block_lane >= 80)
        else:
            spare = jnp.logical_and(block_row == 0, block_lane < 48)
        g = 0 if first else GROUPS - 1
        blocks = []
        block = slice(base, base + 6)
        for value, at in ((part[block, :], g), (masked(block), SLABS + g)):
            extra = jnp.broadcast_to(turn(own[at : at + 1], -16), (6, LANES))
            blocks.append(jnp.where(spare, extra, value))
        low = 0 if first else ROWS - 4
        diag_rows = diag[low : low + 4, :]
        third, fourth = (2, 3) if first else (SPAN_Y - 3, SPAN_Y - 4)
        b_l, b_r = line_of(lambda n: part[n : n + 1, :], third)
        d_l, d_r = line_of(lambda n: masked(slice(n, n + 1)), third)
        g_l, g_r = line_of(lambda n: diag[n : n + 1, :], third)
        bo_l, bo_r = line_of(lambda n: part[n : n + 1, :], fourth)
        do_l, do_r = line_of(lambda n: masked(slice(n, n + 1)), fourth)
        out_l = beside(b_l, d_l, g_l, bo_l, do_l)
        out_r = beside(b_r, d_r, g_r, bo_r, do_r)
        for at, value in ((112, turn(g_l, 112)), (113, turn(do_l, 113)), (114, turn(g_r, 3)), (115, turn(do_r, 4))):
            out_r = jnp.where(one == at, value, out_r)
        last_row = jnp.where(one == LANES - 1, top, rows_r)

        @pl.when(sides[c] >= 0)
        def _(c=c, blocks=blocks, diag_rows=diag_rows, singles=(out_l, out_r, rows_l, last_row)):
            at = sides[c] * slot
            slots[pl.ds(at, 6), :] = blocks[0]
            slots[pl.ds(at + 6, 6), :] = blocks[1]
            slots[pl.ds(at + 12, 4), :] = diag_rows
            for n, value in enumerate(singles):
                slots[pl.ds(at + 16 + n, 1), :] = value

    corner = jnp.logical_and(row_of((GROUPS, LANES)) == RIM_ROWS - 1, lane == LANES - 1)
    for c, pack in ((0, pack_w), (1, pack_e)):
        slots[pl.ds(sides[c] * slot, GROUPS), :] = jnp.where(corner, top, pack)
    for c, at in ((4, 0), (5, SLABS), (6, GROUPS - 1), (7, SLABS + GROUPS - 1)):
        @pl.when(sides[c] >= 0)
        def _(c=c, at=at):
            slots[pl.ds(sides[c] * slot, 1), :] = own[at : at + 1]
    send(slots, slots_out.reshape(count * slot, LANES))
    for copy in results:
        copy.wait()


SMEM = pl.BlockSpec(memory_space=pltpu.SMEM)


def solve_kernel(
    levels, tiles_y,
    around_in, rims, fields,
    vectors, hands,
    around, sem, north_in, south_in, fb, fd, fg, pw, pe, ow, oe, ed, eg, ex, we, wn, last, rows,
):
    copies = fetching([(around_in, around)], sem)
    count = rims.shape[0]
    number_pieces, _ = pieces_of(levels, count)
    slot = RIM_ROWS + number_pieces
    share = 1 + number_pieces
    came = rims.reshape(count * slot, LANES)
    hand = hands.reshape(count * share, LANES)
    own = fields.at[pl.ds(PACKS, 56)]
    lane = lane_of((SLABS, LANES))
    slab = row_of((SLABS, LANES))
    one = lane_of((1, LANES))

    none = jnp.zeros((WIDE - ROWS + 4, LANES), jnp.float32)
    for ref in (fb, fd, fg):
        ref[ROWS - 4 : WIDE] = none
    for n, ref in enumerate((fb, fd, fg)):
        ref[0:ROWS] = fields[n * HELD : n * HELD + ROWS]
    copies[0].wait()
    src = [around[4 * count + c] for c in range(8)]

    def fetch(c, low, high):
        value = came[pl.ds(jnp.maximum(src[c], 0) * slot + low, high - low), :]
        return jnp.where(src[c] >= 0, value, 0.0)

    me = lax.axis_index("gx") * tiles_y + lax.axis_index("gy")
    for n in range(number_pieces):
        side = jnp.minimum((n * count + me) // (2 * levels), 3)
        base = (side + 1 - 2 * (side % 2)) * count

        def relay(d, carry, n=n, base=base):
            row = around[base + d] + n
            hand[pl.ds(d * share + 1 + n, 1), :] = came[pl.ds(row, 1), :]
            return carry

        for d in range(count):
            relay(d, 0)

    north_in[0:RIM_ROWS] = fetch(3, 0, RIM_ROWS)
    south_in[0:RIM_ROWS] = fetch(2, 0, RIM_ROWS)
    strips = {2: south_in, 3: north_in}
    for ref, low, high, n_lane, s_lane in ((fb, 0, 6, 80, 48), (fd, 6, 12, 80, 48), (fg, 12, 16, 96, 32)):
        size = high - low
        row, column = row_of((size, LANES)), lane_of((size, LANES))
        beyond = jnp.logical_and(row == size - 1, column >= n_lane)
        ref[ROWS : ROWS + size] = jnp.where(beyond, 0.0, strips[3][low:high])
        beyond = jnp.logical_and(row == 0, column < s_lane)
        ref[WIDE - size : WIDE] = jnp.where(beyond, 0.0, strips[2][low:high])
    empty = jnp.zeros((SLABS, LANES), jnp.float32)
    for ref, side, north, south in ((pw, 0, 6, 4), (pe, 1, 7, 5)):
        ref[...] = empty
        ref[0:GROUPS] = fetch(side, 0, GROUPS)
        ref[GROUPS : GROUPS + 1] = fetch(north, 0, 1)
        ref[SLABS - 1 : SLABS] = fetch(south, 0, 1)
    for ref, at, north, south in ((ow, 0, 5, 0), (oe, SLABS, 11, 6)):
        ref[...] = empty
        ref[0:GROUPS] = own[at : at + GROUPS]
        ref[GROUPS : GROUPS + 1] = turn(strips[3][north:north + 1], 16)
        ref[SLABS - 1 : SLABS] = turn(strips[2][south:south + 1], 16)

    def spread(ref, j):
        a = START[j]
        first, second = ref[comb(a, SLABS), :], ref[comb(a + 1, SLABS), :]
        third = ref[comb(a + 2, SLABS), :] if a + 2 < PLANES else second
        left = turn(jnp.where(lane >= OFF[j], first, second), -OFF[j])
        right = turn(jnp.where(lane >= OFF[j], second, third), -OFF[j])
        return left, right

    def seam_row(left, right, slab_at, lanes_at):
        east = turn(pe[slab_at : slab_at + 1], 112 - lanes_at)
        west = turn(pw[slab_at : slab_at + 1], 124 - lanes_at)
        right = jnp.where(one < 112, right, jnp.where(one < 116, east, jnp.where(one >= 124, west, 0.0)))
        return jnp.broadcast_to(left, (SLABS, LANES)), jnp.broadcast_to(right, (SLABS, LANES))

    seams = {
        0: ((0, seam_row(strips[2][18:19], strips[2][19:20], SLABS - 1, 28)),
            (GROUPS, seam_row(own[50:51], own[51:52], GROUPS - 1, 28))),
        GROUP - 1: ((GROUPS - 1, seam_row(strips[3][18:19], strips[3][19:20], GROUPS, 12)),
                    (SLABS - 1, seam_row(own[48:49], own[49:50], 0, 12))),
    }
    weight = STERIC / levels

    def missing(target, term, term_out, d, d_out, g):
        term, term_out, d, d_out, g = (
            turn(value[0], target - value[1]) for value in (term, term_out, d, d_out, g)
        )
        term = jnp.where(d > 0, weight * term, 0.0)
        term_out = jnp.where(d_out > 0, weight * term_out, 0.0)
        return jnp.where(one == target, g * term + d * d_out * (term - term_out), 0.0)

    def ring(ref, at):
        return ref[at : at + 1]

    outer = {j: [] for j in range(GROUP)}
    for j, at, beyond, o, lanes in ((0, 0, SLABS - 1, 0, 28), (GROUP - 1, GROUPS - 1, GROUPS, 16, 12)):
        own_row, corner = ring(pe, at), ring(pe, beyond)
        outer[j].append((1, at, missing(
            114, (corner, lanes + 2), (corner, lanes + 3), (own_row, o + 5), (own_row, o + 11), (own_row, o + 10),
        )))
        own_row, corner = ring(pw, at), ring(pw, beyond)
        outer[j].append((1, at, missing(
            125, (corner, lanes + 1), (corner, lanes), (own_row, o + 3), (own_row, o + 11), (own_row, o + 10),
        )))
    for j, at, c, j_out, d_l, d_r in ((2, GROUPS, 3, 3, (9, 96), (11, 79)), (5, SLABS - 1, 2, 4, (6, 48), (8, 31))):
        line_l, line_r = strips[c][16:17], strips[c][17:18]
        corner = ring(pw, at)
        outer[j].append((0, at, line_l + missing(
            0, (corner, OFF[j] + 9), (corner, OFF[j_out] + 9), (strips[c][d_l[0]:d_l[0] + 1], d_l[1]),
            (line_r, 113), (line_r, 112),
        )))
        corner = ring(pe, at)
        outer[j].append((1, at, jnp.where(one < 112, line_r, 0.0) + missing(
            111, (corner, OFF[j] + 9), (corner, OFF[j_out] + 9), (strips[c][d_r[0]:d_r[0] + 1], d_r[1]),
            (line_r, 115), (line_r, 114),
        )))
    for j in range(GROUP):
        o = OFF[j]
        inside = slab < GROUPS
        halves = [
            jnp.zeros((SLABS, LANES), jnp.float32),
            jnp.where(
                jnp.logical_and(inside, lane == 114), turn(pe[...], 114 - o - 8),
                jnp.where(jnp.logical_and(inside, lane == 125), turn(pw[...], 125 - o - 8), 0.0),
            ),
        ]
        for half, at, line in outer[j]:
            halves[half] = halves[half] + jnp.where(slab == at, line, 0.0)
        ex[j, :, 0:LANES] = halves[0]
        ex[j, :, LANES:] = halves[1]

        def rim(right, q, width):
            east = turn(pe[...], 112 - o - q)
            west = turn(pw[...], 128 - width - o - q)
            value = jnp.where(lane < 112 + width, east, jnp.where(lane >= 128 - width, west, 0.0))
            return jnp.where(lane < 112, right, value)

        left, right = spread(fd, j)
        right = rim(right, 3, 3)
        wet_l = jnp.where(left > 0, weight, 0.0)
        wet_r = jnp.where(right > 0, weight, 0.0)
        ed[j, :, 0:LANES] = left
        ed[j, :, LANES:] = right
        left, right = spread(fg, j)
        eg[j, :, 0:LANES] = left
        eg[j, :, LANES:] = rim(right, 6, 2)
        left, right = spread(fb, j)
        right = rim(right, 0, 3)
        seam_l = jnp.where(lane == 0, turn(pw[...], -o - 9), 0.0)
        seam_r = jnp.where(lane == 127, turn(ow[...], 127 - o - 9), 0.0)
        seam_r = jnp.where(lane == 111, turn(pe[...], 111 - o - 9), seam_r)
        seam_r = jnp.where(lane == 112, turn(oe[...], 112 - o - 9), seam_r)
        for at, (row_l, row_r) in seams.get(j, ()):
            seam_l = seam_l + jnp.where(slab == at, row_l, 0.0)
            seam_r = seam_r + jnp.where(slab == at, row_r, 0.0)
        vectors[0, j, :, 0:LANES] = left + wet_l * seam_l
        vectors[0, j, :, LANES:] = right + wet_r * seam_r

    for j in range(GROUP):
        d = ed[j]
        we[j] = d * turn(d, -1)
        above = ed[j + 1] if j < GROUP - 1 else turn(ed[0], -1, 0)
        wn[j] = d * above

    top = jnp.max(came[pl.ds(RIM_ROWS - 1, count, stride=slot), :], axis=0, keepdims=True)
    top = jnp.max(jnp.where(one == LANES - 1, top, 0.0), axis=1, keepdims=True)
    scale = STRETCH / top

    big = (SLABS, 2 * LANES)
    mine = jnp.logical_and(row_of(big) < GROUPS, lane_of(big) < SPAN_X)
    pair = 0
    for k in range(5):
        sums = [None] * (k + 1)
        new = last if k == 4 else vectors.at[k]
        if k:
            v = vectors.at[k - 1]
            flow_below = wn[GROUP - 1] * (v[GROUP - 1] - turn(v[0], -1, 0))
            flow_below = turn(flow_below, 1, 0)
        for j in range(GROUP):
            if k:
                here = v[j]
                above = v[j + 1] if j < GROUP - 1 else turn(v[0], -1, 0)
                flow_x = we[j] * (here - turn(here, -1))
                flow_y = wn[j] * (here - above)
                image = eg[j] * here + (flow_x - turn(flow_x, 1)) + (flow_y - flow_below)
                if k == 1:
                    image = image + ex[j]
                fresh = scale * image - (STRETCH * ROOTS[k - 1]) * here
                flow_below = flow_y
                new[j] = fresh
            else:
                fresh = new[j]
            held = jnp.where(mine, fresh, 0.0)
            for i in range(k + 1):
                other = vectors[i, j] if i < k else held
                value = held * other
                sums[i] = value if sums[i] is None else sums[i] + value
        for i in range(k + 1):
            rows[pair : pair + 1] = jnp.sum(sums[i][:, 0:LANES] + sums[i][:, LANES:], axis=0, keepdims=True)
            pair += 1
    rows[pair : pair + 1] = jnp.where(one == 0, top, 0.0)
    total = jnp.sum(rows[...], axis=1, keepdims=True)
    spot = row_of((16, LANES)) == lane_of((16, LANES))
    line = jnp.sum(jnp.where(spot, total, 0.0), axis=0, keepdims=True)
    hand[pl.ds(0, count, stride=share), :] = jnp.broadcast_to(line, (count, LANES))


def finish_kernel(
    levels, per, hands, vectors, edges, inner, tracer_out, surface_out,
    cells, flat, left, right, message, out_sems,
):
    count = hands.shape[0]
    number_pieces, runs = pieces_of(levels, count)
    share = 1 + number_pieces
    came = hands.reshape(count * share, LANES)
    steps = levels // per
    chunks = [pl.ds(step * per * ROWS, per * ROWS) for step in range(steps)]
    row = jnp.sum(came[pl.ds(0, count, stride=share), :], axis=0, keepdims=True)
    one = lane_of((1, LANES))
    entry = {}
    pair = 0
    for k in range(5):
        for i in range(k + 1):
            value = jnp.sum(jnp.where(one == pair, row, 0.0), axis=1, keepdims=True)
            entry[i, k] = entry[k, i] = value
            pair += 1
    top = jnp.sum(jnp.where(one == pair, row, 0.0), axis=1, keepdims=True) * (1.0 / count)

    def image(c):
        out = [None] * 5
        for k in range(4):
            if c[k] is None:
                continue
            low = ROOTS[k] * c[k]
            out[k] = low if out[k] is None else out[k] + low
            out[k + 1] = (1.0 / STRETCH) * c[k]
        return out

    def dot(a, b):
        total = None
        for i in range(5):
            if a[i] is None:
                continue
            inner = None
            for j in range(5):
                if b[j] is not None:
                    value = entry[i, j] * b[j]
                    inner = value if inner is None else inner + value
            total = a[i] * inner if total is None else total + a[i] * inner
        return total

    def axpy(a, s, b):
        return [
            x if y is None else (s * y if x is None else x + s * y) for x, y in zip(a, b)
        ]

    r = [jnp.ones((1, 1), jnp.float32)] + [None] * 4
    p = list(r)
    x = [None] * 5
    rr = entry[0, 0]
    for n in range(ITERS):
        q = image(p)
        step = rr / jnp.maximum(dot(p, q), TINY)
        step = jnp.clip(step, top * (1.0 / HIGH_RATE), top * (1.0 / LOW_RATE))
        x = axpy(x, step, p)
        if n < ITERS - 1:
            r = axpy(r, -step, q)
            fresh = jnp.maximum(dot(r, r), 0.0)
            p = axpy(r, fresh / jnp.maximum(rr, TINY), p)
            rr = fresh
    factors = [c / top for c in x[:4]]
    for j in range(GROUP):
        value = None
        for k in range(4):
            term = factors[k] * vectors[k, j]
            value = term if value is None else value + term
        left[j] = turn(value[:, 0:LANES], OFF[j])
        right[j] = turn(value[:, LANES:], OFF[j])
    lane = lane_of((SLABS, LANES))
    for a in range(PLANES):
        value = None
        for j in range(GROUP):
            for half, ref in ((0, left), (1, right)):
                low = max(SPAN_X * j + LANES * half - LANES * a, 0)
                high = min(SPAN_X * j + (LANES if half == 0 else SPAN_X) - LANES * a, LANES)
                if low >= high:
                    continue
                value = ref[j] if value is None else jnp.where(lane >= low, ref[j], value)
        flat[comb(a), :] = value[0:GROUPS]
    results = [pltpu.make_async_copy(flat, surface_out.reshape(ROWS, LANES), out_sems.at[0])]
    results[0].start()

    for c in range(4):
        for j, device, low, size in runs[c ^ 1]:
            value = came[pl.ds(device * share + 1 + j, size, stride=share), :]
            message[c, low : low + size] = value
    second = lane_of((SLABS, LANES)) % 16 == 1
    sums = []
    for k in range(levels):
        value = edges[2 * levels - 1] * jnp.concatenate([
            jnp.where(second, turn(message[1], 1 - k), turn(message[0], -k)),
            message[2, k : k + 1], message[2, k + levels : k + levels + 1],
            message[3, k : k + 1], message[3, k + levels : k + levels + 1],
            jnp.zeros((EDGE - SLABS - 4, LANES), jnp.float32),
        ], axis=0)
        if k:
            value = value + edges[2 * levels + k - 1] * sums[-1]
        sums.append(value * edges[levels - 1 + k])
    for k in range(levels - 2, -1, -1):
        sums[k] = sums[k] + edges[k] * sums[k + 1]
    lane = lane_of((GROUPS, LANES))
    slab = row_of((GROUPS, LANES))
    for k in range(levels):
        west = sums[k][0:GROUPS]
        east = turn(west, -18)
        south_l, south_r = sums[k][SLABS : SLABS + 1], sums[k][SLABS + 1 : SLABS + 2]
        north_l = turn(sums[k][SLABS + 2 : SLABS + 3], 16)
        north_r = turn(sums[k][SLABS + 3 : SLABS + 4], 16)
        for a in range(PLANES):
            rim = None
            for at, source in [(at, west) for at in FIRST_OF[a]] + [(at, east) for at in LAST_OF[a]]:
                rim = jnp.where(lane == at, source, 0.0 if rim is None else rim)
            rows = comb(k * ROWS + a)
            if rim is None:
                cells[rows, :] = inner[rows, :]
                continue
            if a == 0:
                rim = rim + jnp.where(slab == 0, south_l, 0.0)
            if a == 1:
                rim = rim + jnp.where(jnp.logical_and(slab == 0, lane < 112), south_r, 0.0)
            if a == PLANES - 2:
                rim = rim + jnp.where(jnp.logical_and(slab == GROUPS - 1, lane >= 16), north_l, 0.0)
            if a == PLANES - 1:
                rim = rim + jnp.where(slab == GROUPS - 1, jnp.where(lane < 16, north_l, north_r), 0.0)
            cells[rows, :] = inner[rows, :] + rim
        if k % per == per - 1:
            step = k // per
            copy = pltpu.make_async_copy(
                cells.at[chunks[step]], tracer_out.at[chunks[step]], out_sems.at[1 + step]
            )
            copy.start()
            results.append(copy)
    for copy in results:
        copy.wait()


def tracer_kernel(
    levels, per, sides, around, temp_in, zonal_in, merid_in, rates_in, fields,
    out, edges,
    temp, zonal, merid, rates, ocean,
    te, tw, tn, ts, stepped, border, sems,
):
    steps = levels // per
    pairs = []
    for step in range(steps):
        chunk = pl.ds(step * per * ROWS, per * ROWS)
        pairs += [
            (a.at[chunk], b.at[chunk]) for a, b in ((temp_in, temp), (zonal_in, zonal), (merid_in, merid))
        ]
    copies = fetching(pairs + [(rates_in.reshape((levels - 1) * ROWS, LANES), rates)], sems)
    lane = lane_of((GROUPS, LANES))
    one = lane_of((1, LANES))
    clear_terms(tn, ts)

    ocean[...] = jnp.where(fields[HELD : HELD + ROWS] > 0, 1.0, 0.0)
    for step in range(steps):
        for copy in copies[3 * step : 3 * step + 3]:
            copy.wait()

        def level(k, carry):
            t, u, v = (Level(ref, k * ROWS) for ref in (temp, zonal, merid))
            for a in range(PLANES):
                own = t.plane(a)
                quarter = ADVECT * own
                store_terms(a, own, u.plane(a) * quarter, v.plane(a) * quarter, te, tw, tn, ts)
            for a in range(PLANES):
                own = t.plane(a)
                change = inner_sum(a, te, tw, tn, ts) - 4.0 * DIFFUSE * own
                stepped[k, a] = own + ocean[comb(a), :] * change
            return carry

        lax.fori_loop(step * per, step * per + per, level, 0)
    copies[-1].wait()

    def block(a, carry):
        for low in range(0, GROUPS, 8):
            size = min(8, GROUPS - low)

            def rows(k):
                return pl.ds(k * ROWS + low * PLANES + a, size, stride=PLANES)

            gains = []
            sums = []
            for k in range(levels):
                value = stepped[k, a, low : low + size]
                pivot = 1.0
                if k > 0:
                    pivot = pivot + upper - upper * gains[-1]
                    value = value + upper * sums[-1]
                if k < levels - 1:
                    lower = rates[rows(k), :]
                    inverse = 1.0 / (pivot + lower)
                    gains.append(lower * inverse)
                    upper = lower
                else:
                    inverse = 1.0 / pivot
                sums.append(value * inverse)
            result = sums[-1]
            out[rows(levels - 1), :] = result
            for k in range(levels - 2, -1, -1):
                result = sums[k] + gains[k] * result
                out[rows(k), :] = result
        return carry

    lax.fori_loop(0, PLANES, block, 0)

    def edge(ref, base, at):
        def get(a):
            return ref[comb(base + a), :].astype(jnp.float32)

        border[0:GROUPS] = jnp.where(
            lane % 16 == 1, turn(choose(LAST, lane, get), 18), choose(START, lane, get)
        )
        border[SLABS : SLABS + 2] = ref[base : base + 2, :].astype(jnp.float32)
        rows = ref[base + ROWS - 2 : base + ROWS, :].astype(jnp.float32)
        border[SLABS + 2 : SLABS + 3] = turn(jnp.where(one >= 16, rows[0:1], rows[1:2]), -16)
        border[SLABS + 3 : SLABS + 4] = turn(rows[1:2], -16)
        edges[at] = border[...]

    border[...] = jnp.zeros_like(border)
    edge(ocean, 0, 2 * levels - 1)
    for c in (2, 3):
        rows = pl.ds(SLABS + 2 * (c - 2), 2)
        value = edges[2 * levels - 1, rows]
        edges[2 * levels - 1, rows] = jnp.where(around[sides + c] >= 0, value, 0.0)
    gain = None
    for k in range(levels):
        pivot = 1.0
        if k > 0:
            upper = edges[2 * levels + k - 1]
            pivot = pivot + upper - upper * gain
        if k < levels - 1:
            edge(rates, k * ROWS, 2 * levels + k)
            lower = edges[2 * levels + k]
            inverse = 1.0 / (pivot + lower)
            gain = lower * inverse
            edges[k] = gain
        else:
            inverse = 1.0 / pivot
        edges[levels - 1 + k] = inverse


def on_device(
    thermal_anomaly,
    zonal_flow_ratio,
    meridional_flow_ratio,
    diffusion_rates,
    ocean_bottom_scaled,
    ocean_indicator,
    operator_diagonal,
    elevation_source,
    block_positions,
):
    levels, cells = thermal_anomaly.shape[1:]
    nx = lax.axis_size("gx")
    ny = lax.axis_size("gy")
    count = block_positions.shape[0]
    planes = (ocean_bottom_scaled, ocean_indicator, operator_diagonal, elevation_source)
    depth, ocean, diag, source = planes
    f32 = jnp.float32
    per = next(n for n in (4, 2, 6, levels) if levels % n == 0 and n * ROWS % 8 == 0)
    steps = levels // per
    few = next(n for n in (2, 4, 6, levels) if levels % n == 0 and n * ROWS % 8 == 0)
    params = pltpu.CompilerParams(vmem_limit_bytes=BUDGET)
    temp, zonal, merid = (
        array.reshape(levels * ROWS, LANES)
        for array in (thermal_anomaly, zonal_flow_ratio, meridional_flow_ratio)
    )
    rates = diffusion_rates.reshape(levels - 1, 1, cells)
    temp, zonal, merid, rates, depth, ocean, diag, source, positions = (
        pltpu.with_memory_space_constraint(array, pltpu.HBM)
        for array in (temp, zonal, merid, rates, depth, ocean, diag, source, block_positions)
    )
    hbm = pl.BlockSpec(memory_space=pltpu.HBM)
    here = pl.BlockSpec(memory_space=pltpu.VMEM)

    def vmem(*shape, kind=f32):
        return pltpu.VMEM(shape, kind)

    def out(*shape, kind=f32):
        return jax.ShapeDtypeStruct(shape, kind)

    def sems(number):
        return pltpu.SemaphoreType.DMA((number,))

    deep = vmem(levels * ROWS, LANES)
    flat = vmem(ROWS, LANES)
    flat_int = vmem(ROWS, LANES, kind=jnp.int32)
    plane = vmem(PLANES, GROUPS, LANES)
    tall = vmem(PLANES, 40, LANES)
    numbers = pltpu.SMEM((count,), jnp.int32)
    number_pieces, _ = pieces_of(levels, count)
    slot = RIM_ROWS + number_pieces
    share = 1 + number_pieces
    fields, slots, around = pl.pallas_call(
        functools.partial(forcing_kernel, levels, few, nx, ny),
        in_specs=[hbm] * 8,
        out_specs=[here, hbm, SMEM],
        out_shape=[
            out(FIELDS, LANES), pltpu.HBM((count, 1, slot * LANES), f32), out(4 * count + 8, kind=jnp.int32),
        ],
        scratch_shapes=[deep] * 3 + [flat, flat_int, flat]
        + [vmem(count * slot, LANES)]
        + [flat] * 3 + [plane] * 3 + [tall] * 2
        + [vmem(4, 2 * levels, LANES), numbers, numbers, sems(3 * (levels // few) + 5), sems(1)],
        compiler_params=params,
        name="forcing",
    )(positions, temp, zonal, merid, depth, ocean, diag, source)
    rims = lax.all_to_all(slots, BOTH, 0, 0, tiled=True)

    inner, edges = pl.pallas_call(
        functools.partial(tracer_kernel, levels, per, 4 * count),
        in_specs=[SMEM] + [hbm] * 4 + [here],
        out_specs=[here] * 2,
        out_shape=[out(levels * ROWS, LANES), out(3 * levels - 1, EDGE, LANES)],
        scratch_shapes=[deep] * 3 + [vmem((levels - 1) * ROWS, LANES), flat]
        + [plane] * 2 + [tall] * 2
        + [vmem(levels, PLANES, GROUPS, LANES), vmem(EDGE, LANES), sems(3 * steps + 1)],
        compiler_params=params,
        name="tracer",
    )(around, temp, zonal, merid, rates, fields)

    rims, edges = lax.optimization_barrier((rims, edges))
    extended = vmem(GROUP, SLABS, 2 * LANES)
    vectors, hand = pl.pallas_call(
        functools.partial(solve_kernel, levels, ny),
        in_specs=[pl.BlockSpec(memory_space=pl.ANY)] + [here] * 2,
        out_specs=[here] * 2,
        out_shape=[out(4, GROUP, SLABS, 2 * LANES), out(count, 1, share * LANES)],
        scratch_shapes=[pltpu.SMEM((4 * count + 8,), jnp.int32), sems(1)]
        + [vmem(SLABS, LANES)] * 2 + [vmem(WIDE, LANES)] * 3 + [vmem(SLABS, LANES)] * 4 + [extended] * 6 + [vmem(16, LANES)],
        compiler_params=params,
        name="vectors",
    )(around, rims, fields)
    hands = lax.all_to_all(hand, BOTH, 0, 0, tiled=True)

    new_temp, surface = pl.pallas_call(
        functools.partial(finish_kernel, levels, per),
        in_specs=[here] * 4,
        out_specs=[hbm] * 2,
        out_shape=[out(levels * ROWS, LANES), out(1, cells)],
        scratch_shapes=[
            deep, flat, vmem(GROUP, SLABS, LANES), vmem(GROUP, SLABS, LANES), vmem(4, 2 * levels, LANES),
            sems(1 + steps),
        ],
        compiler_params=params,
        name="finish",
    )(hands, vectors, edges, inner)
    return new_temp.reshape(1, levels, cells), surface


def solution(mesh):
    deep = P(BOTH, None, None)
    flat = P(BOTH, None)
    return jax.shard_map(
        on_device,
        mesh=mesh,
        in_specs=(deep, deep, deep, deep, flat, flat, flat, flat, P()),
        out_specs=(deep, flat),
        check_vma=False,
    )
```

```python
import functools

import jax
import jax.numpy as jnp
from jax import lax
from jax.experimental import pallas as pl
from jax.experimental.pallas import tpu as pltpu
from jax.sharding import PartitionSpec as P

ITERS = 4
SPAN_X = 240
SPAN_Y = 160
RIM = 4
ADVECT = 0.25
DIFFUSE = 0.12
STERIC = 0.5
LOW_RATE = 0.05
HIGH_RATE = 32.5
ROOTS = (0.02, 0.35, 0.1, 0.2)
STRETCH = 4.0
TINY = 1e-30
BOTH = ("gx", "gy")
SIDES = ((-1, 0), (1, 0), (0, -1), (0, 1), (-1, -1), (1, -1), (-1, 1), (1, 1))

LANES = 128
GROUP = 8
GROUPS = SPAN_Y // GROUP
PLANES = GROUP * SPAN_X // LANES
ROWS = GROUPS * PLANES
SLABS = GROUPS + 4
WIDE = SLABS * PLANES
START = [SPAN_X * j // LANES for j in range(GROUP)]
OFF = [SPAN_X * j % LANES for j in range(GROUP)]
LAST = [(SPAN_X * j + SPAN_X - 1) // LANES for j in range(GROUP)]
END = [(SPAN_X * j + SPAN_X - 1) % LANES for j in range(GROUP)]
FIRST_OF = [[OFF[j] for j in range(GROUP) if START[j] == a] for a in range(PLANES)]
LAST_OF = [[END[j] for j in range(GROUP) if LAST[j] == a] for a in range(PLANES)]
RIM_ROWS = 20
HELD = -(-ROWS // 8) * 8
PACKS = 3 * HELD
FIELDS = PACKS + 56
EDGE = 32
BUDGET = 32 * 1024 * 1024


def turn(value, shift, axis=1):
    shift = shift % value.shape[axis]
    return value if shift == 0 else pltpu.roll(value, shift, axis)


def fetching(pairs, sems):
    copies = [pltpu.make_async_copy(a, b, sems.at[n]) for n, (a, b) in enumerate(pairs)]
    for copy in copies:
        copy.start()
    return copies


def pieces_of(levels, count):
    rows = 2 * levels
    number = -(-4 * rows // count)
    runs = [[] for _ in range(4)]
    for c in range(4):
        for j in range(number):
            low, high = max(c * rows, j * count), min((c + 1) * rows, (j + 1) * count)
            if low < high:
                runs[c].append((j, low - j * count, low - c * rows, high - low))
    merged = count <= 2 * rows and levels <= 12
    return number, runs, number + (0 if merged else 1), 0 if merged else 1


def gram_lane(n):
    return 16 * (n // 4) + 12 + n % 4


class Level:
    def __init__(self, ref, base):
        self.ref, self.base = ref, base

    def plane(self, a):
        return self.ref[comb(self.base + a), :]

    def rows(self, low, size):
        return self.ref[pl.ds(self.base + low, size), :]


def lane_of(shape):
    return lax.broadcasted_iota(jnp.int32, shape, len(shape) - 1)


def row_of(shape):
    return lax.broadcasted_iota(jnp.int32, shape, 0)


def comb(a, count=GROUPS):
    return pl.ds(a, count, stride=PLANES)


def line_of(get, y):
    lane = lane_of((1, LANES))
    j = y % GROUP
    row = y // GROUP * PLANES + START[j]
    first, second = get(row), get(row + 1)
    third = get(row + 2) if START[j] + 2 < PLANES else second
    left = turn(jnp.where(lane >= OFF[j], first, second), -OFF[j])
    right = turn(jnp.where(lane >= OFF[j], second, third), -OFF[j])
    return left, right


def drop(value, lanes, lane):
    for at in lanes:
        value = jnp.where(lane == at, 0.0, value)
    return value


def store_terms(a, temp, flow_x, flow_y, te, tw, tn, ts):
    spread = DIFFUSE * temp
    te[a] = spread - flow_x
    tw[a] = spread + flow_x
    tn[a, 8 : 8 + GROUPS] = spread - flow_y
    ts[a, 8 : 8 + GROUPS] = spread + flow_y


def clear_terms(tn, ts):
    none = jnp.zeros((PLANES, 1, LANES), jnp.float32)
    for ref in (tn, ts):
        ref[:, 7:8] = none
        ref[:, 8 + GROUPS : 9 + GROUPS] = none


def inner_sum(a, te, tw, tn, ts):
    lane = lane_of((GROUPS, LANES))
    here = te[a]
    east = here if a == PLANES - 1 else jnp.where(lane == 0, te[a + 1], here)
    east = drop(turn(east, -1), LAST_OF[a], lane)
    here = tw[a]
    west = here if a == 0 else jnp.where(lane == LANES - 1, tw[a - 1], here)
    west = drop(turn(west, 1), FIRST_OF[a], lane)

    def plane(ref, at):
        down = 8 + (at >= PLANES) - (at < 0)
        return ref[at % PLANES, down : down + GROUPS]

    north = turn(jnp.where(lane >= LANES - 16, plane(tn, a + 1), plane(tn, a + 2)), 16)
    south = turn(jnp.where(lane < 16, plane(ts, a - 1), plane(ts, a - 2)), -16)
    return east + west + north + south


def choose(planes, lane, get):
    shift = 32 if planes is LAST else 0
    lows = sorted(((OFF[j] - shift) % LANES, planes[j]) for j in range(GROUP))
    value = get(lows[-1][1])
    for low, a in reversed(lows[:-1]):
        value = jnp.where(lane < low + 16, get(a), value)
    return value


def forcing_kernel(
    levels, per, tiles_x, tiles_y,
    pos_in, temp_in, zonal_in, merid_in, depth_in, ocean_in, diag_in, source_in,
    fields, slots_out, around,
    temp, zonal, merid, depth, ocean, source, slots,
    st, sx, sy, pt, te, tw, tn, ts, edges, pos, holder, sems, out_sems,
):
    count = pos.shape[0]
    steps = levels // per
    number_pieces, runs, _, _ = pieces_of(levels, count)
    slot = RIM_ROWS + number_pieces
    pairs = []
    for step in range(steps):
        chunk = pl.ds(step * per * ROWS, per * ROWS)
        pairs += [
            (a.at[chunk], b.at[chunk]) for a, b in ((temp_in, temp), (zonal_in, zonal), (merid_in, merid))
        ]
    pairs += [
        (a.reshape(ROWS, LANES), b)
        for a, b in (
            (source_in, source), (ocean_in, ocean), (depth_in, depth),
            (diag_in, fields.at[pl.ds(2 * HELD, ROWS)]),
        )
    ]
    copies = fetching([(pos_in, pos)] + pairs, sems)
    copies.pop(0).wait()
    results = []

    def send(value, target):
        copy = pltpu.make_async_copy(value, target, out_sems.at[len(results)])
        copy.start()
        results.append(copy)

    lane = lane_of((GROUPS, LANES))
    one = lane_of((1, LANES))
    q = lane % 16
    edges[...] = jnp.zeros_like(edges)

    def number(d, carry):
        holder[pos[d]] = d
        return carry

    lax.fori_loop(0, count, number, 0)
    me = lax.axis_index("gx") * tiles_y + lax.axis_index("gy")
    here = pos[me]
    row = here // tiles_x
    column = here % tiles_x
    sides = []
    for c, (dx, dy) in enumerate(SIDES):
        there = row + dy
        inside = jnp.logical_and(there >= 0, there < tiles_y)
        target = jnp.where(inside, there, 0) * tiles_x + (column + dx + tiles_x) % tiles_x
        device = jnp.where(inside, holder[target], -1)
        around[4 * count + c] = device
        sides.append(device)

    def look(y, carry):
        line = [holder[y * tiles_x + x] for x in range(tiles_x)]
        below = [holder[jnp.maximum(y - 1, 0) * tiles_x + x] for x in range(tiles_x)]
        above = [holder[jnp.minimum(y + 1, tiles_y - 1) * tiles_x + x] for x in range(tiles_x)]
        for x, device in enumerate(line):
            for c, other in enumerate((line[x - 1], line[(x + 1) % tiles_x], below[x], above[x])):
                around[c * count + device] = other * slot + RIM_ROWS
        return carry

    lax.fori_loop(0, tiles_y, look, 0)
    clear_terms(tn, ts)

    def add(flats, low, size, fresh):
        rows = pl.ds(low, size)
        total = [None] * 3
        for t, u, v in zip(*flats):
            t = t.rows(low, size)
            new = (t, t * u.rows(low, size), t * v.rows(low, size))
            total = [b if a is None else a + b for a, b in zip(total, new)]
        for ref, value in zip((st, sx, sy), total):
            ref[rows, :] = value if fresh else ref[rows, :] + value

    for step in range(steps):
        for copy in copies[3 * step : 3 * step + 3]:
            copy.wait()
        flats = [
            [Level(ref, (step * per + n) * ROWS) for n in range(per)] for ref in (temp, zonal, merid)
        ]

        def some(m, carry):
            add(flats, pl.multiple_of(m * 8, 8), 8, step == 0)
            return carry

        lax.fori_loop(0, ROWS // 8, some, 0, unroll=4)
        if ROWS % 8:
            add(flats, ROWS - ROWS % 8, ROWS % 8, step == 0)

        for n in range(per):
            k = step * per + n
            t, u, v = (flat[n] for flat in flats)

            loaded = {a: (t.plane(a), u.plane(a)) for a in sorted(set(START + LAST))}

            def term(planes, sign):
                own = choose(planes, lane, lambda a: loaded[a][0])
                flow = choose(planes, lane, lambda a: loaded[a][1])
                return DIFFUSE * own + sign * ADVECT * (flow * own)

            edges[0, 0:GROUPS] = jnp.where(q == k, turn(term(START, -1.0), k), edges[0, 0:GROUPS])
            edges[1, 0:GROUPS] = jnp.where(q == k, turn(term(LAST, 1.0), k + 17), edges[1, 0:GROUPS])
            rows = t.rows(0, 2)
            rows = DIFFUSE * rows - ADVECT * (v.rows(0, 2) * rows)
            edges[2, k : k + 1] = rows[0:1]
            edges[2, k + levels : k + levels + 1] = rows[1:2]
            rows = t.rows(ROWS - 2, 2)
            rows = DIFFUSE * rows + ADVECT * (v.rows(ROWS - 2, 2) * rows)
            edges[3, k : k + 1] = turn(jnp.where(one >= 16, rows[0:1], rows[1:2]), -16)
            edges[3, k + levels : k + levels + 1] = turn(rows[1:2], -16)

    for c in range(4):
        for j, device, low, size in runs[c]:
            slots[pl.ds(device * slot + RIM_ROWS + j, size, stride=slot), :] = edges[c, low : low + size]

    for copy in copies[3 * steps :]:
        copy.wait()

    part = fields.at[pl.ds(0, HELD)]
    mask = fields.at[pl.ds(HELD, HELD)]
    diag = fields.at[pl.ds(2 * HELD, HELD)]
    own = fields.at[pl.ds(PACKS, 56)]
    mask[0:ROWS] = depth[...] * ocean[...].astype(jnp.float32)

    def wet_of(rows):
        return ocean[rows, :].astype(jnp.float32)

    def masked(rows):
        return mask[rows, :]

    for a in range(PLANES):
        total = st[comb(a), :]
        pt[a] = total
        store_terms(a, total, ADVECT * sx[comb(a), :], ADVECT * sy[comb(a), :], te, tw, tn, ts)
    for a in range(PLANES):
        total = pt[a]
        wet = wet_of(comb(a))
        change = inner_sum(a, te, tw, tn, ts) - 4.0 * DIFFUSE * total
        part[comb(a), :] = source[comb(a), :] + (STERIC / levels) * wet * (total + wet * change)

    def mix(*values):
        value = values[-1]
        for at, low in ((6, 12), (5, 11), (4, 10), (3, 9), (2, 8), (1, 6), (0, 3)):
            value = jnp.where(q < low, values[at], value)
        return value

    def ends(planes, low):
        value = tn[planes[0], 8 : 8 + GROUPS]
        last = jnp.logical_and(lane >= low, lane < low + 16)
        return jnp.where(last, ts[planes[7], 8 : 8 + GROUPS], value)

    def beside(b, d, g, b_out, d_out):
        return g * b + d * d_out * (b - b_out)

    bp = choose(START, lane, lambda a: part[comb(a), :])
    dp = choose(START, lane, lambda a: masked(comb(a)))
    gp = choose(START, lane, lambda a: diag[comb(a), :])
    pp = beside(bp, dp, gp, turn(bp, -1), turn(dp, -1))
    pack_w = mix(
        bp, turn(dp, 3), turn(gp, 6), turn(pp, 6), turn(choose(START, lane, lambda a: te[a]), 9),
        turn(gp, 8), turn(dp, 8), turn(ends(START, OFF[7]), 12),
    )
    bp = choose(LAST, lane, lambda a: part[comb(a), :])
    dp = choose(LAST, lane, lambda a: masked(comb(a)))
    gp = choose(LAST, lane, lambda a: diag[comb(a), :])
    pp = beside(bp, dp, gp, turn(bp, 1), turn(dp, 1))
    pack_e = mix(
        turn(bp, 19), turn(dp, 22), turn(gp, 24), turn(pp, 27),
        turn(choose(LAST, lane, lambda a: tw[a]), 26),
        turn(gp, 29), turn(dp, 31), turn(ends(LAST, LANES - 16), 32),
    )
    own[0:GROUPS] = pack_w
    own[SLABS : SLABS + GROUPS] = pack_e
    north_l = tn[0, 8:9]
    north_r = tn[1, 8:9]
    south_13 = ts[PLANES - 2, 7 + GROUPS : 8 + GROUPS]
    south_14 = ts[PLANES - 1, 7 + GROUPS : 8 + GROUPS]
    south_l = turn(jnp.where(one >= 16, south_13, south_14), -16)
    south_r = turn(south_14, -16)
    own[48:49] = north_l
    own[49:50] = north_r
    own[50:51] = south_l
    own[51:52] = south_r
    deep = jnp.max(masked(slice(0, ROWS)), axis=(0, 1), keepdims=True)
    top = jnp.max(diag[0:ROWS], axis=(0, 1), keepdims=True) + 8.0 * deep * deep
    top = jnp.broadcast_to(top, (1, LANES))

    slots[pl.ds(RIM_ROWS - 1, count, stride=slot), :] = jnp.broadcast_to(top, (count, LANES))
    block_lane = lane_of((6, LANES))
    block_row = row_of((6, LANES))
    for c, first, rows_l, rows_r in ((2, True, north_l, north_r), (3, False, south_l, south_r)):
        base = 0 if first else ROWS - 6
        if first:
            spare = jnp.logical_and(block_row == 5, block_lane >= 80)
        else:
            spare = jnp.logical_and(block_row == 0, block_lane < 48)
        g = 0 if first else GROUPS - 1
        blocks = []
        block = slice(base, base + 6)
        for value, at in ((part[block, :], g), (masked(block), SLABS + g)):
            extra = jnp.broadcast_to(turn(own[at : at + 1], -16), (6, LANES))
            blocks.append(jnp.where(spare, extra, value))
        low = 0 if first else ROWS - 4
        diag_rows = diag[low : low + 4, :]
        third, fourth = (2, 3) if first else (SPAN_Y - 3, SPAN_Y - 4)
        b_l, b_r = line_of(lambda n: part[n : n + 1, :], third)
        d_l, d_r = line_of(lambda n: masked(slice(n, n + 1)), third)
        g_l, g_r = line_of(lambda n: diag[n : n + 1, :], third)
        bo_l, bo_r = line_of(lambda n: part[n : n + 1, :], fourth)
        do_l, do_r = line_of(lambda n: masked(slice(n, n + 1)), fourth)
        out_l = beside(b_l, d_l, g_l, bo_l, do_l)
        out_r = beside(b_r, d_r, g_r, bo_r, do_r)
        for at, value in ((112, turn(g_l, 112)), (113, turn(do_l, 113)), (114, turn(g_r, 3)), (115, turn(do_r, 4))):
            out_r = jnp.where(one == at, value, out_r)
        last_row = jnp.where(one == LANES - 1, top, rows_r)

        @pl.when(sides[c] >= 0)
        def _(c=c, blocks=blocks, diag_rows=diag_rows, singles=(out_l, out_r, rows_l, last_row)):
            at = sides[c] * slot
            slots[pl.ds(at, 6), :] = blocks[0]
            slots[pl.ds(at + 6, 6), :] = blocks[1]
            slots[pl.ds(at + 12, 4), :] = diag_rows
            for n, value in enumerate(singles):
                slots[pl.ds(at + 16 + n, 1), :] = value

    corner = jnp.logical_and(row_of((GROUPS, LANES)) == RIM_ROWS - 1, lane == LANES - 1)
    for c, pack in ((0, pack_w), (1, pack_e)):
        slots[pl.ds(sides[c] * slot, GROUPS), :] = jnp.where(corner, top, pack)
    for c, at in ((4, 0), (5, SLABS), (6, GROUPS - 1), (7, SLABS + GROUPS - 1)):
        @pl.when(sides[c] >= 0)
        def _(c=c, at=at):
            slots[pl.ds(sides[c] * slot, 1), :] = own[at : at + 1]
    send(slots, slots_out.reshape(count * slot, LANES))
    for copy in results:
        copy.wait()


SMEM = pl.BlockSpec(memory_space=pltpu.SMEM)


def solve_kernel(
    levels, tiles_y,
    around_in, rims, fields,
    vectors, hands,
    around, sem, north_in, south_in, fb, fd, fg, pw, pe, ow, oe, ed, eg, ex, we, wn, last, rows,
):
    copies = fetching([(around_in, around)], sem)
    count = rims.shape[0]
    number_pieces, _, share, first = pieces_of(levels, count)
    slot = RIM_ROWS + number_pieces
    came = rims.reshape(count * slot, LANES)
    hand = hands.reshape(count * share, LANES)
    own = fields.at[pl.ds(PACKS, 56)]
    lane = lane_of((SLABS, LANES))
    slab = row_of((SLABS, LANES))
    one = lane_of((1, LANES))

    none = jnp.zeros((WIDE - ROWS + 4, LANES), jnp.float32)
    for ref in (fb, fd, fg):
        ref[ROWS - 4 : WIDE] = none
    for n, ref in enumerate((fb, fd, fg)):
        ref[0:ROWS] = fields[n * HELD : n * HELD + ROWS]
    copies[0].wait()
    src = [around[4 * count + c] for c in range(8)]

    def fetch(c, low, high):
        value = came[pl.ds(jnp.maximum(src[c], 0) * slot + low, high - low), :]
        return jnp.where(src[c] >= 0, value, 0.0)

    me = lax.axis_index("gx") * tiles_y + lax.axis_index("gy")
    for n in range(number_pieces):
        side = jnp.minimum((n * count + me) // (2 * levels), 3)
        base = (side + 1 - 2 * (side % 2)) * count

        def relay(d, carry, n=n, base=base):
            row = around[base + d] + n
            hand[pl.ds(d * share + first + n, 1), :] = came[pl.ds(row, 1), :]
            return carry

        for d in range(count):
            relay(d, 0)

    north_in[0:RIM_ROWS] = fetch(3, 0, RIM_ROWS)
    south_in[0:RIM_ROWS] = fetch(2, 0, RIM_ROWS)
    strips = {2: south_in, 3: north_in}
    for ref, low, high, n_lane, s_lane in ((fb, 0, 6, 80, 48), (fd, 6, 12, 80, 48), (fg, 12, 16, 96, 32)):
        size = high - low
        row, column = row_of((size, LANES)), lane_of((size, LANES))
        beyond = jnp.logical_and(row == size - 1, column >= n_lane)
        ref[ROWS : ROWS + size] = jnp.where(beyond, 0.0, strips[3][low:high])
        beyond = jnp.logical_and(row == 0, column < s_lane)
        ref[WIDE - size : WIDE] = jnp.where(beyond, 0.0, strips[2][low:high])
    empty = jnp.zeros((SLABS, LANES), jnp.float32)
    for ref, side, north, south in ((pw, 0, 6, 4), (pe, 1, 7, 5)):
        ref[...] = empty
        ref[0:GROUPS] = fetch(side, 0, GROUPS)
        ref[GROUPS : GROUPS + 1] = fetch(north, 0, 1)
        ref[SLABS - 1 : SLABS] = fetch(south, 0, 1)
    for ref, at, north, south in ((ow, 0, 5, 0), (oe, SLABS, 11, 6)):
        ref[...] = empty
        ref[0:GROUPS] = own[at : at + GROUPS]
        ref[GROUPS : GROUPS + 1] = turn(strips[3][north:north + 1], 16)
        ref[SLABS - 1 : SLABS] = turn(strips[2][south:south + 1], 16)

    def spread(ref, j):
        a = START[j]
        first, second = ref[comb(a, SLABS), :], ref[comb(a + 1, SLABS), :]
        third = ref[comb(a + 2, SLABS), :] if a + 2 < PLANES else second
        left = turn(jnp.where(lane >= OFF[j], first, second), -OFF[j])
        right = turn(jnp.where(lane >= OFF[j], second, third), -OFF[j])
        return left, right

    def seam_row(left, right, slab_at, lanes_at):
        east = turn(pe[slab_at : slab_at + 1], 112 - lanes_at)
        west = turn(pw[slab_at : slab_at + 1], 124 - lanes_at)
        right = jnp.where(one < 112, right, jnp.where(one < 116, east, jnp.where(one >= 124, west, 0.0)))
        return jnp.broadcast_to(left, (SLABS, LANES)), jnp.broadcast_to(right, (SLABS, LANES))

    seams = {
        0: ((0, seam_row(strips[2][18:19], strips[2][19:20], SLABS - 1, 28)),
            (GROUPS, seam_row(own[50:51], own[51:52], GROUPS - 1, 28))),
        GROUP - 1: ((GROUPS - 1, seam_row(strips[3][18:19], strips[3][19:20], GROUPS, 12)),
                    (SLABS - 1, seam_row(own[48:49], own[49:50], 0, 12))),
    }
    weight = STERIC / levels

    def missing(target, term, term_out, d, d_out, g):
        term, term_out, d, d_out, g = (
            turn(value[0], target - value[1]) for value in (term, term_out, d, d_out, g)
        )
        term = jnp.where(d > 0, weight * term, 0.0)
        term_out = jnp.where(d_out > 0, weight * term_out, 0.0)
        return jnp.where(one == target, g * term + d * d_out * (term - term_out), 0.0)

    def ring(ref, at):
        return ref[at : at + 1]

    outer = {j: [] for j in range(GROUP)}
    for j, at, beyond, o, lanes in ((0, 0, SLABS - 1, 0, 28), (GROUP - 1, GROUPS - 1, GROUPS, 16, 12)):
        own_row, corner = ring(pe, at), ring(pe, beyond)
        outer[j].append((1, at, missing(
            114, (corner, lanes + 2), (corner, lanes + 3), (own_row, o + 5), (own_row, o + 11), (own_row, o + 10),
        )))
        own_row, corner = ring(pw, at), ring(pw, beyond)
        outer[j].append((1, at, missing(
            125, (corner, lanes + 1), (corner, lanes), (own_row, o + 3), (own_row, o + 11), (own_row, o + 10),
        )))
    for j, at, c, j_out, d_l, d_r in ((2, GROUPS, 3, 3, (9, 96), (11, 79)), (5, SLABS - 1, 2, 4, (6, 48), (8, 31))):
        line_l, line_r = strips[c][16:17], strips[c][17:18]
        corner = ring(pw, at)
        outer[j].append((0, at, line_l + missing(
            0, (corner, OFF[j] + 9), (corner, OFF[j_out] + 9), (strips[c][d_l[0]:d_l[0] + 1], d_l[1]),
            (line_r, 113), (line_r, 112),
        )))
        corner = ring(pe, at)
        outer[j].append((1, at, jnp.where(one < 112, line_r, 0.0) + missing(
            111, (corner, OFF[j] + 9), (corner, OFF[j_out] + 9), (strips[c][d_r[0]:d_r[0] + 1], d_r[1]),
            (line_r, 115), (line_r, 114),
        )))
    for j in range(GROUP):
        o = OFF[j]
        inside = slab < GROUPS
        halves = [
            jnp.zeros((SLABS, LANES), jnp.float32),
            jnp.where(
                jnp.logical_and(inside, lane == 114), turn(pe[...], 114 - o - 8),
                jnp.where(jnp.logical_and(inside, lane == 125), turn(pw[...], 125 - o - 8), 0.0),
            ),
        ]
        for half, at, line in outer[j]:
            halves[half] = halves[half] + jnp.where(slab == at, line, 0.0)
        ex[j, :, 0:LANES] = halves[0]
        ex[j, :, LANES:] = halves[1]

        def rim(right, q, width):
            east = turn(pe[...], 112 - o - q)
            west = turn(pw[...], 128 - width - o - q)
            value = jnp.where(lane < 112 + width, east, jnp.where(lane >= 128 - width, west, 0.0))
            return jnp.where(lane < 112, right, value)

        left, right = spread(fd, j)
        right = rim(right, 3, 3)
        wet_l = jnp.where(left > 0, weight, 0.0)
        wet_r = jnp.where(right > 0, weight, 0.0)
        ed[j, :, 0:LANES] = left
        ed[j, :, LANES:] = right
        left, right = spread(fg, j)
        eg[j, :, 0:LANES] = left
        eg[j, :, LANES:] = rim(right, 6, 2)
        left, right = spread(fb, j)
        right = rim(right, 0, 3)
        seam_l = jnp.where(lane == 0, turn(pw[...], -o - 9), 0.0)
        seam_r = jnp.where(lane == 127, turn(ow[...], 127 - o - 9), 0.0)
        seam_r = jnp.where(lane == 111, turn(pe[...], 111 - o - 9), seam_r)
        seam_r = jnp.where(lane == 112, turn(oe[...], 112 - o - 9), seam_r)
        for at, (row_l, row_r) in seams.get(j, ()):
            seam_l = seam_l + jnp.where(slab == at, row_l, 0.0)
            seam_r = seam_r + jnp.where(slab == at, row_r, 0.0)
        vectors[0, j, :, 0:LANES] = left + wet_l * seam_l
        vectors[0, j, :, LANES:] = right + wet_r * seam_r

    for j in range(GROUP):
        d = ed[j]
        we[j] = d * turn(d, -1)
        above = ed[j + 1] if j < GROUP - 1 else turn(ed[0], -1, 0)
        wn[j] = d * above

    top = jnp.max(came[pl.ds(RIM_ROWS - 1, count, stride=slot), :], axis=0, keepdims=True)
    top = jnp.max(jnp.where(one == LANES - 1, top, 0.0), axis=1, keepdims=True)
    scale = STRETCH / top

    big = (SLABS, 2 * LANES)
    mine = jnp.logical_and(row_of(big) < GROUPS, lane_of(big) < SPAN_X)
    pair = 0
    for k in range(5):
        sums = [None] * (k + 1)
        new = last if k == 4 else vectors.at[k]
        if k:
            v = vectors.at[k - 1]
            flow_below = wn[GROUP - 1] * (v[GROUP - 1] - turn(v[0], -1, 0))
            flow_below = turn(flow_below, 1, 0)
        for j in range(GROUP):
            if k:
                here = v[j]
                above = v[j + 1] if j < GROUP - 1 else turn(v[0], -1, 0)
                flow_x = we[j] * (here - turn(here, -1))
                flow_y = wn[j] * (here - above)
                image = eg[j] * here + (flow_x - turn(flow_x, 1)) + (flow_y - flow_below)
                if k == 1:
                    image = image + ex[j]
                fresh = scale * image - (STRETCH * ROOTS[k - 1]) * here
                flow_below = flow_y
                new[j] = fresh
            else:
                fresh = new[j]
            held = jnp.where(mine, fresh, 0.0)
            for i in range(k + 1):
                other = vectors[i, j] if i < k else held
                value = held * other
                sums[i] = value if sums[i] is None else sums[i] + value
        for i in range(k + 1):
            rows[pair : pair + 1] = jnp.sum(sums[i][:, 0:LANES] + sums[i][:, LANES:], axis=0, keepdims=True)
            pair += 1
    rows[pair : pair + 1] = jnp.where(one == 0, top, 0.0)
    total = jnp.sum(rows[...], axis=1, keepdims=True)
    spot = lane_of((16, LANES)) == gram_lane(row_of((16, LANES)))
    line = jnp.sum(jnp.where(spot, total, 0.0), axis=0, keepdims=True)
    line = jnp.broadcast_to(line, (count, LANES))
    if first == 0:
        line = jnp.where(lane_of((count, LANES)) % 16 < 12, hand[pl.ds(0, count, stride=share), :], line)
    hand[pl.ds(0, count, stride=share), :] = line


def finish_kernel(
    levels, per, hands, vectors, edges, inner, tracer_out, surface_out,
    cells, flat, left, right, message, out_sems,
):
    count = hands.shape[0]
    _, runs, share, first = pieces_of(levels, count)
    came = hands.reshape(count * share, LANES)
    steps = levels // per
    chunks = [pl.ds(step * per * ROWS, per * ROWS) for step in range(steps)]
    row = jnp.sum(came[pl.ds(0, count, stride=share), :], axis=0, keepdims=True)
    one = lane_of((1, LANES))
    entry = {}
    pair = 0
    for k in range(5):
        for i in range(k + 1):
            value = jnp.sum(jnp.where(one == gram_lane(pair), row, 0.0), axis=1, keepdims=True)
            entry[i, k] = entry[k, i] = value
            pair += 1
    top = jnp.sum(jnp.where(one == gram_lane(pair), row, 0.0), axis=1, keepdims=True) * (1.0 / count)

    def image(c):
        out = [None] * 5
        for k in range(4):
            if c[k] is None:
                continue
            low = ROOTS[k] * c[k]
            out[k] = low if out[k] is None else out[k] + low
            out[k + 1] = (1.0 / STRETCH) * c[k]
        return out

    def dot(a, b):
        total = None
        for i in range(5):
            if a[i] is None:
                continue
            inner = None
            for j in range(5):
                if b[j] is not None:
                    value = entry[i, j] * b[j]
                    inner = value if inner is None else inner + value
            total = a[i] * inner if total is None else total + a[i] * inner
        return total

    def axpy(a, s, b):
        return [
            x if y is None else (s * y if x is None else x + s * y) for x, y in zip(a, b)
        ]

    r = [jnp.ones((1, 1), jnp.float32)] + [None] * 4
    p = list(r)
    x = [None] * 5
    rr = entry[0, 0]
    for n in range(ITERS):
        q = image(p)
        step = rr / jnp.maximum(dot(p, q), TINY)
        step = jnp.clip(step, top * (1.0 / HIGH_RATE), top * (1.0 / LOW_RATE))
        x = axpy(x, step, p)
        if n < ITERS - 1:
            r = axpy(r, -step, q)
            fresh = jnp.maximum(dot(r, r), 0.0)
            p = axpy(r, fresh / jnp.maximum(rr, TINY), p)
            rr = fresh
    factors = [c / top for c in x[:4]]
    for j in range(GROUP):
        value = None
        for k in range(4):
            term = factors[k] * vectors[k, j]
            value = term if value is None else value + term
        left[j] = turn(value[:, 0:LANES], OFF[j])
        right[j] = turn(value[:, LANES:], OFF[j])
    lane = lane_of((SLABS, LANES))
    for a in range(PLANES):
        value = None
        for j in range(GROUP):
            for half, ref in ((0, left), (1, right)):
                low = max(SPAN_X * j + LANES * half - LANES * a, 0)
                high = min(SPAN_X * j + (LANES if half == 0 else SPAN_X) - LANES * a, LANES)
                if low >= high:
                    continue
                value = ref[j] if value is None else jnp.where(lane >= low, ref[j], value)
        flat[comb(a), :] = value[0:GROUPS]
    results = [pltpu.make_async_copy(flat, surface_out.reshape(ROWS, LANES), out_sems.at[0])]
    results[0].start()

    for c in range(4):
        for j, device, low, size in runs[c ^ 1]:
            value = came[pl.ds(device * share + first + j, size, stride=share), :]
            message[c, low : low + size] = value
    second = lane_of((SLABS, LANES)) % 16 == 1
    sums = []
    for k in range(levels):
        value = edges[2 * levels - 1] * jnp.concatenate([
            jnp.where(second, turn(message[1], 1 - k), turn(message[0], -k)),
            message[2, k : k + 1], message[2, k + levels : k + levels + 1],
            message[3, k : k + 1], message[3, k + levels : k + levels + 1],
            jnp.zeros((EDGE - SLABS - 4, LANES), jnp.float32),
        ], axis=0)
        if k:
            value = value + edges[2 * levels + k - 1] * sums[-1]
        sums.append(value * edges[levels - 1 + k])
    for k in range(levels - 2, -1, -1):
        sums[k] = sums[k] + edges[k] * sums[k + 1]
    lane = lane_of((GROUPS, LANES))
    slab = row_of((GROUPS, LANES))
    for k in range(levels):
        west = sums[k][0:GROUPS]
        east = turn(west, -18)
        south_l, south_r = sums[k][SLABS : SLABS + 1], sums[k][SLABS + 1 : SLABS + 2]
        north_l = turn(sums[k][SLABS + 2 : SLABS + 3], 16)
        north_r = turn(sums[k][SLABS + 3 : SLABS + 4], 16)
        for a in range(PLANES):
            rim = None
            for at, source in [(at, west) for at in FIRST_OF[a]] + [(at, east) for at in LAST_OF[a]]:
                rim = jnp.where(lane == at, source, 0.0 if rim is None else rim)
            rows = comb(k * ROWS + a)
            if rim is None:
                cells[rows, :] = inner[rows, :]
                continue
            if a == 0:
                rim = rim + jnp.where(slab == 0, south_l, 0.0)
            if a == 1:
                rim = rim + jnp.where(jnp.logical_and(slab == 0, lane < 112), south_r, 0.0)
            if a == PLANES - 2:
                rim = rim + jnp.where(jnp.logical_and(slab == GROUPS - 1, lane >= 16), north_l, 0.0)
            if a == PLANES - 1:
                rim = rim + jnp.where(slab == GROUPS - 1, jnp.where(lane < 16, north_l, north_r), 0.0)
            cells[rows, :] = inner[rows, :] + rim
        if k % per == per - 1:
            step = k // per
            copy = pltpu.make_async_copy(
                cells.at[chunks[step]], tracer_out.at[chunks[step]], out_sems.at[1 + step]
            )
            copy.start()
            results.append(copy)
    for copy in results:
        copy.wait()


def tracer_kernel(
    levels, per, sides, around, temp_in, zonal_in, merid_in, rates_in, fields,
    out, edges,
    temp, zonal, merid, rates, ocean,
    te, tw, tn, ts, stepped, border, sems,
):
    steps = levels // per
    pairs = []
    for step in range(steps):
        chunk = pl.ds(step * per * ROWS, per * ROWS)
        pairs += [
            (a.at[chunk], b.at[chunk]) for a, b in ((temp_in, temp), (zonal_in, zonal), (merid_in, merid))
        ]
    copies = fetching(pairs + [(rates_in.reshape((levels - 1) * ROWS, LANES), rates)], sems)
    lane = lane_of((GROUPS, LANES))
    one = lane_of((1, LANES))
    clear_terms(tn, ts)

    ocean[...] = jnp.where(fields[HELD : HELD + ROWS] > 0, 1.0, 0.0)
    for step in range(steps):
        for copy in copies[3 * step : 3 * step + 3]:
            copy.wait()

        def level(k, carry):
            t, u, v = (Level(ref, k * ROWS) for ref in (temp, zonal, merid))
            for a in range(PLANES):
                own = t.plane(a)
                quarter = ADVECT * own
                store_terms(a, own, u.plane(a) * quarter, v.plane(a) * quarter, te, tw, tn, ts)
            for a in range(PLANES):
                own = t.plane(a)
                change = inner_sum(a, te, tw, tn, ts) - 4.0 * DIFFUSE * own
                stepped[k, a] = own + ocean[comb(a), :] * change
            return carry

        lax.fori_loop(step * per, step * per + per, level, 0)
    copies[-1].wait()

    def block(a, carry):
        for low in range(0, GROUPS, 8):
            size = min(8, GROUPS - low)

            def rows(k):
                return pl.ds(k * ROWS + low * PLANES + a, size, stride=PLANES)

            gains = []
            sums = []
            for k in range(levels):
                value = stepped[k, a, low : low + size]
                pivot = 1.0
                if k > 0:
                    pivot = pivot + upper - upper * gains[-1]
                    value = value + upper * sums[-1]
                if k < levels - 1:
                    lower = rates[rows(k), :]
                    inverse = 1.0 / (pivot + lower)
                    gains.append(lower * inverse)
                    upper = lower
                else:
                    inverse = 1.0 / pivot
                sums.append(value * inverse)
            result = sums[-1]
            out[rows(levels - 1), :] = result
            for k in range(levels - 2, -1, -1):
                result = sums[k] + gains[k] * result
                out[rows(k), :] = result
        return carry

    lax.fori_loop(0, PLANES, block, 0)

    def edge(ref, base, at):
        def get(a):
            return ref[comb(base + a), :].astype(jnp.float32)

        border[0:GROUPS] = jnp.where(
            lane % 16 == 1, turn(choose(LAST, lane, get), 18), choose(START, lane, get)
        )
        border[SLABS : SLABS + 2] = ref[base : base + 2, :].astype(jnp.float32)
        rows = ref[base + ROWS - 2 : base + ROWS, :].astype(jnp.float32)
        border[SLABS + 2 : SLABS + 3] = turn(jnp.where(one >= 16, rows[0:1], rows[1:2]), -16)
        border[SLABS + 3 : SLABS + 4] = turn(rows[1:2], -16)
        edges[at] = border[...]

    border[...] = jnp.zeros_like(border)
    edge(ocean, 0, 2 * levels - 1)
    for c in (2, 3):
        rows = pl.ds(SLABS + 2 * (c - 2), 2)
        value = edges[2 * levels - 1, rows]
        edges[2 * levels - 1, rows] = jnp.where(around[sides + c] >= 0, value, 0.0)
    gain = None
    for k in range(levels):
        pivot = 1.0
        if k > 0:
            upper = edges[2 * levels + k - 1]
            pivot = pivot + upper - upper * gain
        if k < levels - 1:
            edge(rates, k * ROWS, 2 * levels + k)
            lower = edges[2 * levels + k]
            inverse = 1.0 / (pivot + lower)
            gain = lower * inverse
            edges[k] = gain
        else:
            inverse = 1.0 / pivot
        edges[levels - 1 + k] = inverse


def on_device(
    thermal_anomaly,
    zonal_flow_ratio,
    meridional_flow_ratio,
    diffusion_rates,
    ocean_bottom_scaled,
    ocean_indicator,
    operator_diagonal,
    elevation_source,
    block_positions,
):
    levels, cells = thermal_anomaly.shape[1:]
    nx = lax.axis_size("gx")
    ny = lax.axis_size("gy")
    count = block_positions.shape[0]
    planes = (ocean_bottom_scaled, ocean_indicator, operator_diagonal, elevation_source)
    depth, ocean, diag, source = planes
    f32 = jnp.float32
    per = next(n for n in (4, 2, 6, levels) if levels % n == 0 and n * ROWS % 8 == 0)
    steps = levels // per
    few = next(n for n in (2, 4, 6, levels) if levels % n == 0 and n * ROWS % 8 == 0)
    params = pltpu.CompilerParams(vmem_limit_bytes=BUDGET)
    temp, zonal, merid = (
        array.reshape(levels * ROWS, LANES)
        for array in (thermal_anomaly, zonal_flow_ratio, meridional_flow_ratio)
    )
    rates = diffusion_rates.reshape(levels - 1, 1, cells)
    temp, zonal, merid, rates, depth, ocean, diag, source, positions = (
        pltpu.with_memory_space_constraint(array, pltpu.HBM)
        for array in (temp, zonal, merid, rates, depth, ocean, diag, source, block_positions)
    )
    hbm = pl.BlockSpec(memory_space=pltpu.HBM)
    here = pl.BlockSpec(memory_space=pltpu.VMEM)

    def vmem(*shape, kind=f32):
        return pltpu.VMEM(shape, kind)

    def out(*shape, kind=f32):
        return jax.ShapeDtypeStruct(shape, kind)

    def sems(number):
        return pltpu.SemaphoreType.DMA((number,))

    deep = vmem(levels * ROWS, LANES)
    flat = vmem(ROWS, LANES)
    flat_int = vmem(ROWS, LANES, kind=jnp.int32)
    plane = vmem(PLANES, GROUPS, LANES)
    tall = vmem(PLANES, 40, LANES)
    numbers = pltpu.SMEM((count,), jnp.int32)
    number_pieces, _, share, _ = pieces_of(levels, count)
    slot = RIM_ROWS + number_pieces
    fields, slots, around = pl.pallas_call(
        functools.partial(forcing_kernel, levels, few, nx, ny),
        in_specs=[hbm] * 8,
        out_specs=[here, hbm, SMEM],
        out_shape=[
            out(FIELDS, LANES), pltpu.HBM((count, 1, slot * LANES), f32), out(4 * count + 8, kind=jnp.int32),
        ],
        scratch_shapes=[deep] * 3 + [flat, flat_int, flat]
        + [vmem(count * slot, LANES)]
        + [flat] * 3 + [plane] * 3 + [tall] * 2
        + [vmem(4, 2 * levels, LANES), numbers, numbers, sems(3 * (levels // few) + 5), sems(1)],
        compiler_params=params,
        name="forcing",
    )(positions, temp, zonal, merid, depth, ocean, diag, source)
    rims = lax.all_to_all(slots, BOTH, 0, 0, tiled=True)

    inner, edges = pl.pallas_call(
        functools.partial(tracer_kernel, levels, per, 4 * count),
        in_specs=[SMEM] + [hbm] * 4 + [here],
        out_specs=[here] * 2,
        out_shape=[out(levels * ROWS, LANES), out(3 * levels - 1, EDGE, LANES)],
        scratch_shapes=[deep] * 3 + [vmem((levels - 1) * ROWS, LANES), flat]
        + [plane] * 2 + [tall] * 2
        + [vmem(levels, PLANES, GROUPS, LANES), vmem(EDGE, LANES), sems(3 * steps + 1)],
        compiler_params=params,
        name="tracer",
    )(around, temp, zonal, merid, rates, fields)

    rims, edges = lax.optimization_barrier((rims, edges))
    extended = vmem(GROUP, SLABS, 2 * LANES)
    vectors, hand = pl.pallas_call(
        functools.partial(solve_kernel, levels, ny),
        in_specs=[pl.BlockSpec(memory_space=pl.ANY)] + [here] * 2,
        out_specs=[here] * 2,
        out_shape=[out(4, GROUP, SLABS, 2 * LANES), out(count, 1, share * LANES)],
        scratch_shapes=[pltpu.SMEM((4 * count + 8,), jnp.int32), sems(1)]
        + [vmem(SLABS, LANES)] * 2 + [vmem(WIDE, LANES)] * 3 + [vmem(SLABS, LANES)] * 4 + [extended] * 6 + [vmem(16, LANES)],
        compiler_params=params,
        name="vectors",
    )(around, rims, fields)
    hands = lax.all_to_all(hand, BOTH, 0, 0, tiled=True)

    new_temp, surface = pl.pallas_call(
        functools.partial(finish_kernel, levels, per),
        in_specs=[here] * 4,
        out_specs=[hbm] * 2,
        out_shape=[out(levels * ROWS, LANES), out(1, cells)],
        scratch_shapes=[
            deep, flat, vmem(GROUP, SLABS, LANES), vmem(GROUP, SLABS, LANES), vmem(4, 2 * levels, LANES),
            sems(1 + steps),
        ],
        compiler_params=params,
        name="finish",
    )(hands, vectors, edges, inner)
    return new_temp.reshape(1, levels, cells), surface


def solution(mesh):
    deep = P(BOTH, None, None)
    flat = P(BOTH, None)
    return jax.shard_map(
        on_device,
        mesh=mesh,
        in_specs=(deep, deep, deep, deep, flat, flat, flat, flat, P()),
        out_specs=(deep, flat),
        check_vma=False,
    )
```

```python
import functools

import jax
import jax.numpy as jnp
from jax import lax
from jax.experimental import pallas as pl
from jax.experimental.pallas import tpu as pltpu
from jax.sharding import PartitionSpec as P

ITERS = 4
SPAN_X = 240
SPAN_Y = 160
RIM = 4
ADVECT = 0.25
DIFFUSE = 0.12
STERIC = 0.5
LOW_RATE = 0.05
HIGH_RATE = 32.5
ROOTS = (0.02, 0.35, 0.1, 0.2)
STRETCH = 4.0
TINY = 1e-30
BOTH = ("gx", "gy")
SIDES = ((-1, 0), (1, 0), (0, -1), (0, 1), (-1, -1), (1, -1), (-1, 1), (1, 1))

LANES = 128
GROUP = 8
GROUPS = SPAN_Y // GROUP
PLANES = GROUP * SPAN_X // LANES
ROWS = GROUPS * PLANES
SLABS = GROUPS + 4
WIDE = SLABS * PLANES
START = [SPAN_X * j // LANES for j in range(GROUP)]
OFF = [SPAN_X * j % LANES for j in range(GROUP)]
LAST = [(SPAN_X * j + SPAN_X - 1) // LANES for j in range(GROUP)]
END = [(SPAN_X * j + SPAN_X - 1) % LANES for j in range(GROUP)]
FIRST_OF = [[OFF[j] for j in range(GROUP) if START[j] == a] for a in range(PLANES)]
LAST_OF = [[END[j] for j in range(GROUP) if LAST[j] == a] for a in range(PLANES)]
RIM_ROWS = 20
HELD = -(-ROWS // 8) * 8
PACKS = 3 * HELD
FIELDS = PACKS + 56
EDGE = 32
BUDGET = 32 * 1024 * 1024


def turn(value, shift, axis=1):
    shift = shift % value.shape[axis]
    return value if shift == 0 else pltpu.roll(value, shift, axis)


def fetching(pairs, sems):
    copies = [pltpu.make_async_copy(a, b, sems.at[n]) for n, (a, b) in enumerate(pairs)]
    for copy in copies:
        copy.start()
    return copies


def pieces_of(levels, count):
    rows = 2 * levels
    number = -(-4 * rows // count)
    runs = [[] for _ in range(4)]
    for c in range(4):
        for j in range(number):
            low, high = max(c * rows, j * count), min((c + 1) * rows, (j + 1) * count)
            if low < high:
                runs[c].append((j, low - j * count, low - c * rows, high - low))
    merged = count <= 2 * rows and levels <= 12
    return number, runs, number + (0 if merged else 1), 0 if merged else 1


def gram_lane(n):
    return 16 * (n // 4) + 12 + n % 4


class Level:
    def __init__(self, ref, base):
        self.ref, self.base = ref, base

    def plane(self, a, low=0, size=GROUPS):
        return self.ref[comb(self.base + a, size, low), :]

    def rows(self, low, size):
        return self.ref[pl.ds(self.base + low, size), :]


def lane_of(shape):
    return lax.broadcasted_iota(jnp.int32, shape, len(shape) - 1)


def row_of(shape):
    return lax.broadcasted_iota(jnp.int32, shape, 0)


def comb(a, count=GROUPS, low=0):
    return pl.ds(low * PLANES + a, count, stride=PLANES)


def line_of(get, y):
    lane = lane_of((1, LANES))
    j = y % GROUP
    row = y // GROUP * PLANES + START[j]
    first, second = get(row), get(row + 1)
    third = get(row + 2) if START[j] + 2 < PLANES else second
    left = turn(jnp.where(lane >= OFF[j], first, second), -OFF[j])
    right = turn(jnp.where(lane >= OFF[j], second, third), -OFF[j])
    return left, right


def drop(value, lanes, lane):
    for at in lanes:
        value = jnp.where(lane == at, 0.0, value)
    return value


def store_terms(a, temp, flow_x, flow_y, te, tw, tn, ts, low=0, size=GROUPS):
    spread = DIFFUSE * temp
    te[a, low : low + size] = spread - flow_x
    tw[a, low : low + size] = spread + flow_x
    tn[a, 8 + low : 8 + low + size] = spread - flow_y
    ts[a, 8 + low : 8 + low + size] = spread + flow_y


def clear_terms(tn, ts):
    none = jnp.zeros((PLANES, 1, LANES), jnp.float32)
    for ref in (tn, ts):
        ref[:, 7:8] = none
        ref[:, 8 + GROUPS : 9 + GROUPS] = none


def inner_sum(a, te, tw, tn, ts, low=0, size=GROUPS):
    lane = lane_of((size, LANES))
    rows = slice(low, low + size)
    here = te[a, rows]
    east = here if a == PLANES - 1 else jnp.where(lane == 0, te[a + 1, rows], here)
    east = drop(turn(east, -1), LAST_OF[a], lane)
    here = tw[a, rows]
    west = here if a == 0 else jnp.where(lane == LANES - 1, tw[a - 1, rows], here)
    west = drop(turn(west, 1), FIRST_OF[a], lane)

    def plane(ref, at):
        down = 8 + low + (at >= PLANES) - (at < 0)
        return ref[at % PLANES, down : down + size]

    north = turn(jnp.where(lane >= LANES - 16, plane(tn, a + 1), plane(tn, a + 2)), 16)
    south = turn(jnp.where(lane < 16, plane(ts, a - 1), plane(ts, a - 2)), -16)
    return east + west + north + south


def choose(planes, lane, get):
    shift = 32 if planes is LAST else 0
    lows = sorted(((OFF[j] - shift) % LANES, planes[j]) for j in range(GROUP))
    value = get(lows[-1][1])
    for low, a in reversed(lows[:-1]):
        value = jnp.where(lane < low + 16, get(a), value)
    return value


def forcing_kernel(
    levels, tiles_x, tiles_y,
    pos_in, temp_in, zonal_in, merid_in, depth_in, ocean_in, diag_in, source_in,
    fields, slots_out, around,
    temp_at, zonal_at, merid_at, depth, ocean, source, slots,
    st, sx, sy, pt, te, tw, tn, ts, edges, pos, holder, sems, out_sems,
):
    count = pos.shape[0]
    number_pieces, runs, _, _ = pieces_of(levels, count)
    slot = RIM_ROWS + number_pieces
    blocks = [(low, min(8, GROUPS - low)) for low in range(0, GROUPS, 8)]
    pairs = [(pos_in, pos)]
    for n, (low, size) in enumerate(blocks):
        cells = pl.ds(low * PLANES * LANES, size * PLANES * LANES)
        pairs += [
            (a.at[:, :, cells], b.at[:, :, cells])
            for a, b in ((temp_in, temp_at), (zonal_in, zonal_at), (merid_in, merid_at))
        ]
        if n == 0:
            pairs += [
                (a.reshape(ROWS, LANES), b)
                for a, b in (
                    (source_in, source), (ocean_in, ocean), (depth_in, depth),
                    (diag_in, fields.at[pl.ds(2 * HELD, ROWS)]),
                )
            ]
    copies = fetching(pairs, sems)
    temp, zonal, merid = (ref.reshape(levels * ROWS, LANES) for ref in (temp_at, zonal_at, merid_at))
    copies.pop(0).wait()
    results = []

    def send(value, target):
        copy = pltpu.make_async_copy(value, target, out_sems.at[len(results)])
        copy.start()
        results.append(copy)

    lane = lane_of((GROUPS, LANES))
    one = lane_of((1, LANES))
    q = lane % 16
    edges[...] = jnp.zeros_like(edges)

    def number(d, carry):
        holder[pos[d]] = d
        return carry

    lax.fori_loop(0, count, number, 0)
    me = lax.axis_index("gx") * tiles_y + lax.axis_index("gy")
    here = pos[me]
    row = here // tiles_x
    column = here % tiles_x
    sides = []
    for c, (dx, dy) in enumerate(SIDES):
        there = row + dy
        inside = jnp.logical_and(there >= 0, there < tiles_y)
        target = jnp.where(inside, there, 0) * tiles_x + (column + dx + tiles_x) % tiles_x
        device = jnp.where(inside, holder[target], -1)
        around[4 * count + c] = device
        sides.append(device)

    def look(y, carry):
        line = [holder[y * tiles_x + x] for x in range(tiles_x)]
        below = [holder[jnp.maximum(y - 1, 0) * tiles_x + x] for x in range(tiles_x)]
        above = [holder[jnp.minimum(y + 1, tiles_y - 1) * tiles_x + x] for x in range(tiles_x)]
        for x, device in enumerate(line):
            for c, other in enumerate((line[x - 1], line[(x + 1) % tiles_x], below[x], above[x])):
                around[c * count + device] = other * slot + RIM_ROWS
        return carry

    lax.fori_loop(0, tiles_y, look, 0)
    clear_terms(tn, ts)

    part = fields.at[pl.ds(0, HELD)]
    mask = fields.at[pl.ds(HELD, HELD)]
    diag = fields.at[pl.ds(2 * HELD, HELD)]
    own = fields.at[pl.ds(PACKS, 56)]

    def wet_of(rows):
        return ocean[rows, :].astype(jnp.float32)

    def masked(rows):
        return mask[rows, :]

    def add(low, size):
        total = [None] * 3
        for k in range(levels):
            rows = pl.ds(k * ROWS + low, size)
            t = temp[rows, :]
            new = (t, t * zonal[rows, :], t * merid[rows, :])
            total = [b if a is None else a + b for a, b in zip(total, new)]
        for ref, value in zip((st, sx, sy), total):
            ref[pl.ds(low, size), :] = value

    def finish_part(low, size):
        for a in range(PLANES):
            rows = comb(a, size, low)
            total = pt[a, low : low + size]
            wet = wet_of(rows)
            change = inner_sum(a, te, tw, tn, ts, low, size) - 4.0 * DIFFUSE * total
            part[rows, :] = source[rows, :] + (STERIC / levels) * wet * (total + wet * change)

    for n, (low, size) in enumerate(blocks):
        for copy in copies[:3]:
            copy.wait()
        del copies[:3]

        def some(m, carry, low=low):
            add(low * PLANES + m * 8, 8)
            return carry

        lax.fori_loop(0, size * PLANES // 8, some, 0)
        if size * PLANES % 8:
            rest = size * PLANES % 8
            add((low + size) * PLANES - rest, rest)
        for a in range(PLANES):
            rows = comb(a, size, low)
            total = st[rows, :]
            pt[a, low : low + size] = total
            store_terms(
                a, total, ADVECT * sx[rows, :], ADVECT * sy[rows, :], te, tw, tn, ts, low, size
            )

        some_lanes = lane_of((size, LANES))
        some_q = some_lanes % 16
        for c, planes, sign, more in ((0, START, -1.0, 0), (1, LAST, 1.0, 17)):
            pack = jnp.zeros((size, LANES), jnp.float32)
            for k in range(levels):
                t, u = Level(temp, k * ROWS), Level(zonal, k * ROWS)
                value = choose(planes, some_lanes, lambda a: t.plane(a, low, size))
                flow = choose(planes, some_lanes, lambda a: u.plane(a, low, size))
                value = DIFFUSE * value + sign * ADVECT * (flow * value)
                pack = jnp.where(some_q == k, turn(value, k + more), pack)
            edges[c, low : low + size] = pack
        for c, at, sign in ((2, 0, -1.0), (3, ROWS - 2, 1.0)):
            if n != (0 if c == 2 else len(blocks) - 1):
                continue
            for k in range(levels):
                rows = pl.ds(k * ROWS + at, 2)
                value = temp[rows, :]
                value = DIFFUSE * value + sign * ADVECT * (merid[rows, :] * value)
                left, right = value[0:1], value[1:2]
                if c == 3:
                    left, right = turn(jnp.where(one >= 16, left, right), -16), turn(right, -16)
                edges[c, k : k + 1] = left
                edges[c, k + levels : k + levels + 1] = right

        if n == 0:
            for copy in copies[:4]:
                copy.wait()
            del copies[:4]
            mask[0:ROWS] = depth[...] * ocean[...].astype(jnp.float32)
        else:
            finish_part(*blocks[n - 1])

    for c in range(4):
        for j, device, low, size in runs[c]:
            slots[pl.ds(device * slot + RIM_ROWS + j, size, stride=slot), :] = edges[c, low : low + size]
    finish_part(*blocks[-1])

    def mix(*values):
        value = values[-1]
        for at, low in ((6, 12), (5, 11), (4, 10), (3, 9), (2, 8), (1, 6), (0, 3)):
            value = jnp.where(q < low, values[at], value)
        return value

    def ends(planes, low):
        value = tn[planes[0], 8 : 8 + GROUPS]
        last = jnp.logical_and(lane >= low, lane < low + 16)
        return jnp.where(last, ts[planes[7], 8 : 8 + GROUPS], value)

    def beside(b, d, g, b_out, d_out):
        return g * b + d * d_out * (b - b_out)

    bp = choose(START, lane, lambda a: part[comb(a), :])
    dp = choose(START, lane, lambda a: masked(comb(a)))
    gp = choose(START, lane, lambda a: diag[comb(a), :])
    pp = beside(bp, dp, gp, turn(bp, -1), turn(dp, -1))
    pack_w = mix(
        bp, turn(dp, 3), turn(gp, 6), turn(pp, 6), turn(choose(START, lane, lambda a: te[a]), 9),
        turn(gp, 8), turn(dp, 8), turn(ends(START, OFF[7]), 12),
    )
    bp = choose(LAST, lane, lambda a: part[comb(a), :])
    dp = choose(LAST, lane, lambda a: masked(comb(a)))
    gp = choose(LAST, lane, lambda a: diag[comb(a), :])
    pp = beside(bp, dp, gp, turn(bp, 1), turn(dp, 1))
    pack_e = mix(
        turn(bp, 19), turn(dp, 22), turn(gp, 24), turn(pp, 27),
        turn(choose(LAST, lane, lambda a: tw[a]), 26),
        turn(gp, 29), turn(dp, 31), turn(ends(LAST, LANES - 16), 32),
    )
    own[0:GROUPS] = pack_w
    own[SLABS : SLABS + GROUPS] = pack_e
    north_l = tn[0, 8:9]
    north_r = tn[1, 8:9]
    south_13 = ts[PLANES - 2, 7 + GROUPS : 8 + GROUPS]
    south_14 = ts[PLANES - 1, 7 + GROUPS : 8 + GROUPS]
    south_l = turn(jnp.where(one >= 16, south_13, south_14), -16)
    south_r = turn(south_14, -16)
    own[48:49] = north_l
    own[49:50] = north_r
    own[50:51] = south_l
    own[51:52] = south_r
    deep = jnp.max(masked(slice(0, ROWS)), axis=(0, 1), keepdims=True)
    top = jnp.max(diag[0:ROWS], axis=(0, 1), keepdims=True) + 8.0 * deep * deep
    top = jnp.broadcast_to(top, (1, LANES))

    slots[pl.ds(RIM_ROWS - 1, count, stride=slot), :] = jnp.broadcast_to(top, (count, LANES))
    block_lane = lane_of((6, LANES))
    block_row = row_of((6, LANES))
    for c, first, rows_l, rows_r in ((2, True, north_l, north_r), (3, False, south_l, south_r)):
        base = 0 if first else ROWS - 6
        if first:
            spare = jnp.logical_and(block_row == 5, block_lane >= 80)
        else:
            spare = jnp.logical_and(block_row == 0, block_lane < 48)
        g = 0 if first else GROUPS - 1
        blocks = []
        block = slice(base, base + 6)
        for value, at in ((part[block, :], g), (masked(block), SLABS + g)):
            extra = jnp.broadcast_to(turn(own[at : at + 1], -16), (6, LANES))
            blocks.append(jnp.where(spare, extra, value))
        low = 0 if first else ROWS - 4
        diag_rows = diag[low : low + 4, :]
        third, fourth = (2, 3) if first else (SPAN_Y - 3, SPAN_Y - 4)
        b_l, b_r = line_of(lambda n: part[n : n + 1, :], third)
        d_l, d_r = line_of(lambda n: masked(slice(n, n + 1)), third)
        g_l, g_r = line_of(lambda n: diag[n : n + 1, :], third)
        bo_l, bo_r = line_of(lambda n: part[n : n + 1, :], fourth)
        do_l, do_r = line_of(lambda n: masked(slice(n, n + 1)), fourth)
        out_l = beside(b_l, d_l, g_l, bo_l, do_l)
        out_r = beside(b_r, d_r, g_r, bo_r, do_r)
        for at, value in ((112, turn(g_l, 112)), (113, turn(do_l, 113)), (114, turn(g_r, 3)), (115, turn(do_r, 4))):
            out_r = jnp.where(one == at, value, out_r)
        last_row = jnp.where(one == LANES - 1, top, rows_r)

        @pl.when(sides[c] >= 0)
        def _(c=c, blocks=blocks, diag_rows=diag_rows, singles=(out_l, out_r, rows_l, last_row)):
            at = sides[c] * slot
            slots[pl.ds(at, 6), :] = blocks[0]
            slots[pl.ds(at + 6, 6), :] = blocks[1]
            slots[pl.ds(at + 12, 4), :] = diag_rows
            for n, value in enumerate(singles):
                slots[pl.ds(at + 16 + n, 1), :] = value

    corner = jnp.logical_and(row_of((GROUPS, LANES)) == RIM_ROWS - 1, lane == LANES - 1)
    for c, pack in ((0, pack_w), (1, pack_e)):
        slots[pl.ds(sides[c] * slot, GROUPS), :] = jnp.where(corner, top, pack)
    for c, at in ((4, 0), (5, SLABS), (6, GROUPS - 1), (7, SLABS + GROUPS - 1)):
        @pl.when(sides[c] >= 0)
        def _(c=c, at=at):
            slots[pl.ds(sides[c] * slot, 1), :] = own[at : at + 1]
    send(slots, slots_out.reshape(count * slot, LANES))
    for copy in results:
        copy.wait()


SMEM = pl.BlockSpec(memory_space=pltpu.SMEM)


def solve_kernel(
    levels, tiles_y,
    around_in, rims, fields,
    vectors, hands,
    around, sem, north_in, south_in, fb, fd, fg, pw, pe, ow, oe, ed, eg, ex, we, wn, last, rows,
):
    copies = fetching([(around_in, around)], sem)
    count = rims.shape[0]
    number_pieces, _, share, first = pieces_of(levels, count)
    slot = RIM_ROWS + number_pieces
    came = rims.reshape(count * slot, LANES)
    hand = hands.reshape(count * share, LANES)
    own = fields.at[pl.ds(PACKS, 56)]
    lane = lane_of((SLABS, LANES))
    slab = row_of((SLABS, LANES))
    one = lane_of((1, LANES))

    none = jnp.zeros((WIDE - ROWS + 4, LANES), jnp.float32)
    for ref in (fb, fd, fg):
        ref[ROWS - 4 : WIDE] = none
    for n, ref in enumerate((fb, fd, fg)):
        ref[0:ROWS] = fields[n * HELD : n * HELD + ROWS]
    copies[0].wait()
    src = [around[4 * count + c] for c in range(8)]

    def fetch(c, low, high):
        value = came[pl.ds(jnp.maximum(src[c], 0) * slot + low, high - low), :]
        return jnp.where(src[c] >= 0, value, 0.0)

    me = lax.axis_index("gx") * tiles_y + lax.axis_index("gy")
    for n in range(number_pieces):
        side = jnp.minimum((n * count + me) // (2 * levels), 3)
        base = (side + 1 - 2 * (side % 2)) * count

        def relay(d, carry, n=n, base=base):
            row = around[base + d] + n
            hand[pl.ds(d * share + first + n, 1), :] = came[pl.ds(row, 1), :]
            return carry

        for d in range(count):
            relay(d, 0)

    north_in[0:RIM_ROWS] = fetch(3, 0, RIM_ROWS)
    south_in[0:RIM_ROWS] = fetch(2, 0, RIM_ROWS)
    strips = {2: south_in, 3: north_in}
    for ref, low, high, n_lane, s_lane in ((fb, 0, 6, 80, 48), (fd, 6, 12, 80, 48), (fg, 12, 16, 96, 32)):
        size = high - low
        row, column = row_of((size, LANES)), lane_of((size, LANES))
        beyond = jnp.logical_and(row == size - 1, column >= n_lane)
        ref[ROWS : ROWS + size] = jnp.where(beyond, 0.0, strips[3][low:high])
        beyond = jnp.logical_and(row == 0, column < s_lane)
        ref[WIDE - size : WIDE] = jnp.where(beyond, 0.0, strips[2][low:high])
    empty = jnp.zeros((SLABS, LANES), jnp.float32)
    for ref, side, north, south in ((pw, 0, 6, 4), (pe, 1, 7, 5)):
        ref[...] = empty
        ref[0:GROUPS] = fetch(side, 0, GROUPS)
        ref[GROUPS : GROUPS + 1] = fetch(north, 0, 1)
        ref[SLABS - 1 : SLABS] = fetch(south, 0, 1)
    for ref, at, north, south in ((ow, 0, 5, 0), (oe, SLABS, 11, 6)):
        ref[...] = empty
        ref[0:GROUPS] = own[at : at + GROUPS]
        ref[GROUPS : GROUPS + 1] = turn(strips[3][north:north + 1], 16)
        ref[SLABS - 1 : SLABS] = turn(strips[2][south:south + 1], 16)

    def spread(ref, j):
        a = START[j]
        first, second = ref[comb(a, SLABS), :], ref[comb(a + 1, SLABS), :]
        third = ref[comb(a + 2, SLABS), :] if a + 2 < PLANES else second
        left = turn(jnp.where(lane >= OFF[j], first, second), -OFF[j])
        right = turn(jnp.where(lane >= OFF[j], second, third), -OFF[j])
        return left, right

    def seam_row(left, right, slab_at, lanes_at):
        east = turn(pe[slab_at : slab_at + 1], 112 - lanes_at)
        west = turn(pw[slab_at : slab_at + 1], 124 - lanes_at)
        right = jnp.where(one < 112, right, jnp.where(one < 116, east, jnp.where(one >= 124, west, 0.0)))
        return jnp.broadcast_to(left, (SLABS, LANES)), jnp.broadcast_to(right, (SLABS, LANES))

    seams = {
        0: ((0, seam_row(strips[2][18:19], strips[2][19:20], SLABS - 1, 28)),
            (GROUPS, seam_row(own[50:51], own[51:52], GROUPS - 1, 28))),
        GROUP - 1: ((GROUPS - 1, seam_row(strips[3][18:19], strips[3][19:20], GROUPS, 12)),
                    (SLABS - 1, seam_row(own[48:49], own[49:50], 0, 12))),
    }
    weight = STERIC / levels

    def missing(target, term, term_out, d, d_out, g):
        term, term_out, d, d_out, g = (
            turn(value[0], target - value[1]) for value in (term, term_out, d, d_out, g)
        )
        term = jnp.where(d > 0, weight * term, 0.0)
        term_out = jnp.where(d_out > 0, weight * term_out, 0.0)
        return jnp.where(one == target, g * term + d * d_out * (term - term_out), 0.0)

    def ring(ref, at):
        return ref[at : at + 1]

    outer = {j: [] for j in range(GROUP)}
    for j, at, beyond, o, lanes in ((0, 0, SLABS - 1, 0, 28), (GROUP - 1, GROUPS - 1, GROUPS, 16, 12)):
        own_row, corner = ring(pe, at), ring(pe, beyond)
        outer[j].append((1, at, missing(
            114, (corner, lanes + 2), (corner, lanes + 3), (own_row, o + 5), (own_row, o + 11), (own_row, o + 10),
        )))
        own_row, corner = ring(pw, at), ring(pw, beyond)
        outer[j].append((1, at, missing(
            125, (corner, lanes + 1), (corner, lanes), (own_row, o + 3), (own_row, o + 11), (own_row, o + 10),
        )))
    for j, at, c, j_out, d_l, d_r in ((2, GROUPS, 3, 3, (9, 96), (11, 79)), (5, SLABS - 1, 2, 4, (6, 48), (8, 31))):
        line_l, line_r = strips[c][16:17], strips[c][17:18]
        corner = ring(pw, at)
        outer[j].append((0, at, line_l + missing(
            0, (corner, OFF[j] + 9), (corner, OFF[j_out] + 9), (strips[c][d_l[0]:d_l[0] + 1], d_l[1]),
            (line_r, 113), (line_r, 112),
        )))
        corner = ring(pe, at)
        outer[j].append((1, at, jnp.where(one < 112, line_r, 0.0) + missing(
            111, (corner, OFF[j] + 9), (corner, OFF[j_out] + 9), (strips[c][d_r[0]:d_r[0] + 1], d_r[1]),
            (line_r, 115), (line_r, 114),
        )))
    for j in range(GROUP):
        o = OFF[j]
        inside = slab < GROUPS
        halves = [
            jnp.zeros((SLABS, LANES), jnp.float32),
            jnp.where(
                jnp.logical_and(inside, lane == 114), turn(pe[...], 114 - o - 8),
                jnp.where(jnp.logical_and(inside, lane == 125), turn(pw[...], 125 - o - 8), 0.0),
            ),
        ]
        for half, at, line in outer[j]:
            halves[half] = halves[half] + jnp.where(slab == at, line, 0.0)
        ex[j, :, 0:LANES] = halves[0]
        ex[j, :, LANES:] = halves[1]

        def rim(right, q, width):
            east = turn(pe[...], 112 - o - q)
            west = turn(pw[...], 128 - width - o - q)
            value = jnp.where(lane < 112 + width, east, jnp.where(lane >= 128 - width, west, 0.0))
            return jnp.where(lane < 112, right, value)

        left, right = spread(fd, j)
        right = rim(right, 3, 3)
        wet_l = jnp.where(left > 0, weight, 0.0)
        wet_r = jnp.where(right > 0, weight, 0.0)
        ed[j, :, 0:LANES] = left
        ed[j, :, LANES:] = right
        left, right = spread(fg, j)
        eg[j, :, 0:LANES] = left
        eg[j, :, LANES:] = rim(right, 6, 2)
        left, right = spread(fb, j)
        right = rim(right, 0, 3)
        seam_l = jnp.where(lane == 0, turn(pw[...], -o - 9), 0.0)
        seam_r = jnp.where(lane == 127, turn(ow[...], 127 - o - 9), 0.0)
        seam_r = jnp.where(lane == 111, turn(pe[...], 111 - o - 9), seam_r)
        seam_r = jnp.where(lane == 112, turn(oe[...], 112 - o - 9), seam_r)
        for at, (row_l, row_r) in seams.get(j, ()):
            seam_l = seam_l + jnp.where(slab == at, row_l, 0.0)
            seam_r = seam_r + jnp.where(slab == at, row_r, 0.0)
        vectors[0, j, :, 0:LANES] = left + wet_l * seam_l
        vectors[0, j, :, LANES:] = right + wet_r * seam_r

    for j in range(GROUP):
        d = ed[j]
        we[j] = d * turn(d, -1)
        above = ed[j + 1] if j < GROUP - 1 else turn(ed[0], -1, 0)
        wn[j] = d * above

    top = jnp.max(came[pl.ds(RIM_ROWS - 1, count, stride=slot), :], axis=0, keepdims=True)
    top = jnp.max(jnp.where(one == LANES - 1, top, 0.0), axis=1, keepdims=True)
    scale = STRETCH / top

    big = (SLABS, 2 * LANES)
    mine = jnp.logical_and(row_of(big) < GROUPS, lane_of(big) < SPAN_X)
    pair = 0
    for k in range(5):
        sums = [None] * (k + 1)
        new = last if k == 4 else vectors.at[k]
        if k:
            v = vectors.at[k - 1]
            flow_below = wn[GROUP - 1] * (v[GROUP - 1] - turn(v[0], -1, 0))
            flow_below = turn(flow_below, 1, 0)
        for j in range(GROUP):
            if k:
                here = v[j]
                above = v[j + 1] if j < GROUP - 1 else turn(v[0], -1, 0)
                flow_x = we[j] * (here - turn(here, -1))
                flow_y = wn[j] * (here - above)
                image = eg[j] * here + (flow_x - turn(flow_x, 1)) + (flow_y - flow_below)
                if k == 1:
                    image = image + ex[j]
                fresh = scale * image - (STRETCH * ROOTS[k - 1]) * here
                flow_below = flow_y
                new[j] = fresh
            else:
                fresh = new[j]
            held = jnp.where(mine, fresh, 0.0)
            for i in range(k + 1):
                other = vectors[i, j] if i < k else held
                value = held * other
                sums[i] = value if sums[i] is None else sums[i] + value
        for i in range(k + 1):
            rows[pair : pair + 1] = jnp.sum(sums[i][:, 0:LANES] + sums[i][:, LANES:], axis=0, keepdims=True)
            pair += 1
    rows[pair : pair + 1] = jnp.where(one == 0, top, 0.0)
    total = jnp.sum(rows[...], axis=1, keepdims=True)
    spot = lane_of((16, LANES)) == gram_lane(row_of((16, LANES)))
    line = jnp.sum(jnp.where(spot, total, 0.0), axis=0, keepdims=True)
    line = jnp.broadcast_to(line, (count, LANES))
    if first == 0:
        line = jnp.where(lane_of((count, LANES)) % 16 < 12, hand[pl.ds(0, count, stride=share), :], line)
    hand[pl.ds(0, count, stride=share), :] = line


def finish_kernel(
    levels, per, hands, vectors, edges, inner, tracer_out, surface_out,
    cells, flat, left, right, message, out_sems,
):
    count = hands.shape[0]
    _, runs, share, first = pieces_of(levels, count)
    came = hands.reshape(count * share, LANES)
    steps = levels // per
    chunks = [pl.ds(step * per * ROWS, per * ROWS) for step in range(steps)]
    row = jnp.sum(came[pl.ds(0, count, stride=share), :], axis=0, keepdims=True)
    one = lane_of((1, LANES))
    entry = {}
    pair = 0
    for k in range(5):
        for i in range(k + 1):
            value = jnp.sum(jnp.where(one == gram_lane(pair), row, 0.0), axis=1, keepdims=True)
            entry[i, k] = entry[k, i] = value
            pair += 1
    top = jnp.sum(jnp.where(one == gram_lane(pair), row, 0.0), axis=1, keepdims=True) * (1.0 / count)

    def image(c):
        out = [None] * 5
        for k in range(4):
            if c[k] is None:
                continue
            low = ROOTS[k] * c[k]
            out[k] = low if out[k] is None else out[k] + low
            out[k + 1] = (1.0 / STRETCH) * c[k]
        return out

    def dot(a, b):
        total = None
        for i in range(5):
            if a[i] is None:
                continue
            inner = None
            for j in range(5):
                if b[j] is not None:
                    value = entry[i, j] * b[j]
                    inner = value if inner is None else inner + value
            total = a[i] * inner if total is None else total + a[i] * inner
        return total

    def axpy(a, s, b):
        return [
            x if y is None else (s * y if x is None else x + s * y) for x, y in zip(a, b)
        ]

    r = [jnp.ones((1, 1), jnp.float32)] + [None] * 4
    p = list(r)
    x = [None] * 5
    rr = entry[0, 0]
    for n in range(ITERS):
        q = image(p)
        step = rr / jnp.maximum(dot(p, q), TINY)
        step = jnp.clip(step, top * (1.0 / HIGH_RATE), top * (1.0 / LOW_RATE))
        x = axpy(x, step, p)
        if n < ITERS - 1:
            r = axpy(r, -step, q)
            fresh = jnp.maximum(dot(r, r), 0.0)
            p = axpy(r, fresh / jnp.maximum(rr, TINY), p)
            rr = fresh
    factors = [c / top for c in x[:4]]
    for j in range(GROUP):
        value = None
        for k in range(4):
            term = factors[k] * vectors[k, j]
            value = term if value is None else value + term
        left[j] = turn(value[:, 0:LANES], OFF[j])
        right[j] = turn(value[:, LANES:], OFF[j])
    lane = lane_of((SLABS, LANES))
    for a in range(PLANES):
        value = None
        for j in range(GROUP):
            for half, ref in ((0, left), (1, right)):
                low = max(SPAN_X * j + LANES * half - LANES * a, 0)
                high = min(SPAN_X * j + (LANES if half == 0 else SPAN_X) - LANES * a, LANES)
                if low >= high:
                    continue
                value = ref[j] if value is None else jnp.where(lane >= low, ref[j], value)
        flat[comb(a), :] = value[0:GROUPS]
    results = [pltpu.make_async_copy(flat, surface_out.reshape(ROWS, LANES), out_sems.at[0])]
    results[0].start()

    for c in range(4):
        for j, device, low, size in runs[c ^ 1]:
            value = came[pl.ds(device * share + first + j, size, stride=share), :]
            message[c, low : low + size] = value
    second = lane_of((SLABS, LANES)) % 16 == 1
    sums = []
    for k in range(levels):
        value = edges[2 * levels - 1] * jnp.concatenate([
            jnp.where(second, turn(message[1], 1 - k), turn(message[0], -k)),
            message[2, k : k + 1], message[2, k + levels : k + levels + 1],
            message[3, k : k + 1], message[3, k + levels : k + levels + 1],
            jnp.zeros((EDGE - SLABS - 4, LANES), jnp.float32),
        ], axis=0)
        if k:
            value = value + edges[2 * levels + k - 1] * sums[-1]
        sums.append(value * edges[levels - 1 + k])
    for k in range(levels - 2, -1, -1):
        sums[k] = sums[k] + edges[k] * sums[k + 1]
    lane = lane_of((GROUPS, LANES))
    slab = row_of((GROUPS, LANES))
    for k in range(levels):
        west = sums[k][0:GROUPS]
        east = turn(west, -18)
        south_l, south_r = sums[k][SLABS : SLABS + 1], sums[k][SLABS + 1 : SLABS + 2]
        north_l = turn(sums[k][SLABS + 2 : SLABS + 3], 16)
        north_r = turn(sums[k][SLABS + 3 : SLABS + 4], 16)
        for a in range(PLANES):
            rim = None
            for at, source in [(at, west) for at in FIRST_OF[a]] + [(at, east) for at in LAST_OF[a]]:
                rim = jnp.where(lane == at, source, 0.0 if rim is None else rim)
            rows = comb(k * ROWS + a)
            if rim is None:
                cells[rows, :] = inner[rows, :]
                continue
            if a == 0:
                rim = rim + jnp.where(slab == 0, south_l, 0.0)
            if a == 1:
                rim = rim + jnp.where(jnp.logical_and(slab == 0, lane < 112), south_r, 0.0)
            if a == PLANES - 2:
                rim = rim + jnp.where(jnp.logical_and(slab == GROUPS - 1, lane >= 16), north_l, 0.0)
            if a == PLANES - 1:
                rim = rim + jnp.where(slab == GROUPS - 1, jnp.where(lane < 16, north_l, north_r), 0.0)
            cells[rows, :] = inner[rows, :] + rim
        if k % per == per - 1:
            step = k // per
            copy = pltpu.make_async_copy(
                cells.at[chunks[step]], tracer_out.at[chunks[step]], out_sems.at[1 + step]
            )
            copy.start()
            results.append(copy)
    for copy in results:
        copy.wait()


def tracer_kernel(
    levels, per, sides, around, temp_in, zonal_in, merid_in, rates_in, fields,
    out, edges,
    temp, zonal, merid, rates, ocean,
    te, tw, tn, ts, stepped, border, sems,
):
    steps = levels // per
    pairs = []
    for step in range(steps):
        chunk = pl.ds(step * per * ROWS, per * ROWS)
        pairs += [
            (a.at[chunk], b.at[chunk]) for a, b in ((temp_in, temp), (zonal_in, zonal), (merid_in, merid))
        ]
    copies = fetching(pairs + [(rates_in.reshape((levels - 1) * ROWS, LANES), rates)], sems)
    lane = lane_of((GROUPS, LANES))
    one = lane_of((1, LANES))
    clear_terms(tn, ts)

    ocean[...] = jnp.where(fields[HELD : HELD + ROWS] > 0, 1.0, 0.0)
    for step in range(steps):
        for copy in copies[3 * step : 3 * step + 3]:
            copy.wait()

        def level(k, carry):
            t, u, v = (Level(ref, k * ROWS) for ref in (temp, zonal, merid))
            for a in range(PLANES):
                own = t.plane(a)
                quarter = ADVECT * own
                store_terms(a, own, u.plane(a) * quarter, v.plane(a) * quarter, te, tw, tn, ts)
            for a in range(PLANES):
                own = t.plane(a)
                change = inner_sum(a, te, tw, tn, ts) - 4.0 * DIFFUSE * own
                stepped[k, a] = own + ocean[comb(a), :] * change
            return carry

        lax.fori_loop(step * per, step * per + per, level, 0)
    copies[-1].wait()

    def block(a, carry):
        for low in range(0, GROUPS, 8):
            size = min(8, GROUPS - low)

            def rows(k):
                return pl.ds(k * ROWS + low * PLANES + a, size, stride=PLANES)

            gains = []
            sums = []
            for k in range(levels):
                value = stepped[k, a, low : low + size]
                pivot = 1.0
                if k > 0:
                    pivot = pivot + upper - upper * gains[-1]
                    value = value + upper * sums[-1]
                if k < levels - 1:
                    lower = rates[rows(k), :]
                    inverse = 1.0 / (pivot + lower)
                    gains.append(lower * inverse)
                    upper = lower
                else:
                    inverse = 1.0 / pivot
                sums.append(value * inverse)
            result = sums[-1]
            out[rows(levels - 1), :] = result
            for k in range(levels - 2, -1, -1):
                result = sums[k] + gains[k] * result
                out[rows(k), :] = result
        return carry

    lax.fori_loop(0, PLANES, block, 0)

    def edge(ref, base, at):
        def get(a):
            return ref[comb(base + a), :].astype(jnp.float32)

        border[0:GROUPS] = jnp.where(
            lane % 16 == 1, turn(choose(LAST, lane, get), 18), choose(START, lane, get)
        )
        border[SLABS : SLABS + 2] = ref[base : base + 2, :].astype(jnp.float32)
        rows = ref[base + ROWS - 2 : base + ROWS, :].astype(jnp.float32)
        border[SLABS + 2 : SLABS + 3] = turn(jnp.where(one >= 16, rows[0:1], rows[1:2]), -16)
        border[SLABS + 3 : SLABS + 4] = turn(rows[1:2], -16)
        edges[at] = border[...]

    border[...] = jnp.zeros_like(border)
    edge(ocean, 0, 2 * levels - 1)
    for c in (2, 3):
        rows = pl.ds(SLABS + 2 * (c - 2), 2)
        value = edges[2 * levels - 1, rows]
        edges[2 * levels - 1, rows] = jnp.where(around[sides + c] >= 0, value, 0.0)
    gain = None
    for k in range(levels):
        pivot = 1.0
        if k > 0:
            upper = edges[2 * levels + k - 1]
            pivot = pivot + upper - upper * gain
        if k < levels - 1:
            edge(rates, k * ROWS, 2 * levels + k)
            lower = edges[2 * levels + k]
            inverse = 1.0 / (pivot + lower)
            gain = lower * inverse
            edges[k] = gain
        else:
            inverse = 1.0 / pivot
        edges[levels - 1 + k] = inverse


def on_device(
    thermal_anomaly,
    zonal_flow_ratio,
    meridional_flow_ratio,
    diffusion_rates,
    ocean_bottom_scaled,
    ocean_indicator,
    operator_diagonal,
    elevation_source,
    block_positions,
):
    levels, cells = thermal_anomaly.shape[1:]
    nx = lax.axis_size("gx")
    ny = lax.axis_size("gy")
    count = block_positions.shape[0]
    planes = (ocean_bottom_scaled, ocean_indicator, operator_diagonal, elevation_source)
    depth, ocean, diag, source = planes
    f32 = jnp.float32
    per = next(n for n in (4, 2, 6, levels) if levels % n == 0 and n * ROWS % 8 == 0)
    steps = levels // per
    params = pltpu.CompilerParams(vmem_limit_bytes=BUDGET)
    temp, zonal, merid = (
        array.reshape(levels * ROWS, LANES)
        for array in (thermal_anomaly, zonal_flow_ratio, meridional_flow_ratio)
    )
    rates = diffusion_rates.reshape(levels - 1, 1, cells)
    by_cells = [
        pltpu.with_memory_space_constraint(array.reshape(levels, 1, cells), pltpu.HBM)
        for array in (temp, zonal, merid)
    ]
    temp, zonal, merid, rates, depth, ocean, diag, source, positions = (
        pltpu.with_memory_space_constraint(array, pltpu.HBM)
        for array in (temp, zonal, merid, rates, depth, ocean, diag, source, block_positions)
    )
    hbm = pl.BlockSpec(memory_space=pltpu.HBM)
    here = pl.BlockSpec(memory_space=pltpu.VMEM)

    def vmem(*shape, kind=f32):
        return pltpu.VMEM(shape, kind)

    def out(*shape, kind=f32):
        return jax.ShapeDtypeStruct(shape, kind)

    def sems(number):
        return pltpu.SemaphoreType.DMA((number,))

    deep = vmem(levels * ROWS, LANES)
    flat = vmem(ROWS, LANES)
    flat_int = vmem(ROWS, LANES, kind=jnp.int32)
    plane = vmem(PLANES, GROUPS, LANES)
    tall = vmem(PLANES, 40, LANES)
    numbers = pltpu.SMEM((count,), jnp.int32)
    number_pieces, _, share, _ = pieces_of(levels, count)
    slot = RIM_ROWS + number_pieces
    fields, slots, around = pl.pallas_call(
        functools.partial(forcing_kernel, levels, nx, ny),
        in_specs=[hbm] * 8,
        out_specs=[here, hbm, SMEM],
        out_shape=[
            out(FIELDS, LANES), pltpu.HBM((count, 1, slot * LANES), f32), out(4 * count + 8, kind=jnp.int32),
        ],
        scratch_shapes=[vmem(levels, 1, cells)] * 3 + [flat, flat_int, flat]
        + [vmem(count * slot, LANES)]
        + [flat] * 3 + [plane] * 3 + [tall] * 2
        + [vmem(4, 2 * levels, LANES), numbers, numbers, sems(3 * len(range(0, GROUPS, 8)) + 5), sems(1)],
        compiler_params=params,
        name="forcing",
    )(positions, *by_cells, depth, ocean, diag, source)
    rims = lax.all_to_all(slots, BOTH, 0, 0, tiled=True)

    inner, edges = pl.pallas_call(
        functools.partial(tracer_kernel, levels, per, 4 * count),
        in_specs=[SMEM] + [hbm] * 4 + [here],
        out_specs=[here] * 2,
        out_shape=[out(levels * ROWS, LANES), out(3 * levels - 1, EDGE, LANES)],
        scratch_shapes=[deep] * 3 + [vmem((levels - 1) * ROWS, LANES), flat]
        + [plane] * 2 + [tall] * 2
        + [vmem(levels, PLANES, GROUPS, LANES), vmem(EDGE, LANES), sems(3 * steps + 1)],
        compiler_params=params,
        name="tracer",
    )(around, temp, zonal, merid, rates, fields)

    rims, edges = lax.optimization_barrier((rims, edges))
    extended = vmem(GROUP, SLABS, 2 * LANES)
    vectors, hand = pl.pallas_call(
        functools.partial(solve_kernel, levels, ny),
        in_specs=[pl.BlockSpec(memory_space=pl.ANY)] + [here] * 2,
        out_specs=[here] * 2,
        out_shape=[out(4, GROUP, SLABS, 2 * LANES), out(count, 1, share * LANES)],
        scratch_shapes=[pltpu.SMEM((4 * count + 8,), jnp.int32), sems(1)]
        + [vmem(SLABS, LANES)] * 2 + [vmem(WIDE, LANES)] * 3 + [vmem(SLABS, LANES)] * 4 + [extended] * 6 + [vmem(16, LANES)],
        compiler_params=params,
        name="vectors",
    )(around, rims, fields)
    hands = lax.all_to_all(hand, BOTH, 0, 0, tiled=True)

    new_temp, surface = pl.pallas_call(
        functools.partial(finish_kernel, levels, per),
        in_specs=[here] * 4,
        out_specs=[hbm] * 2,
        out_shape=[out(levels * ROWS, LANES), out(1, cells)],
        scratch_shapes=[
            deep, flat, vmem(GROUP, SLABS, LANES), vmem(GROUP, SLABS, LANES), vmem(4, 2 * levels, LANES),
            sems(1 + steps),
        ],
        compiler_params=params,
        name="finish",
    )(hands, vectors, edges, inner)
    return new_temp.reshape(1, levels, cells), surface


def solution(mesh):
    deep = P(BOTH, None, None)
    flat = P(BOTH, None)
    return jax.shard_map(
        on_device,
        mesh=mesh,
        in_specs=(deep, deep, deep, deep, flat, flat, flat, flat, P()),
        out_specs=(deep, flat),
        check_vma=False,
    )
```

```python
import functools

import jax
import jax.numpy as jnp
from jax import lax
from jax.experimental import pallas as pl
from jax.experimental.pallas import tpu as pltpu
from jax.sharding import PartitionSpec as P

ITERS = 4
SPAN_X = 240
SPAN_Y = 160
RIM = 4
ADVECT = 0.25
DIFFUSE = 0.12
STERIC = 0.5
LOW_RATE = 0.05
HIGH_RATE = 32.5
ROOTS = (0.02, 0.35, 0.1, 0.2)
STRETCH = 4.0
TINY = 1e-30
BOTH = ("gx", "gy")
SIDES = ((-1, 0), (1, 0), (0, -1), (0, 1), (-1, -1), (1, -1), (-1, 1), (1, 1))

LANES = 128
GROUP = 8
GROUPS = SPAN_Y // GROUP
PLANES = GROUP * SPAN_X // LANES
ROWS = GROUPS * PLANES
SLABS = GROUPS + 4
WIDE = SLABS * PLANES
START = [SPAN_X * j // LANES for j in range(GROUP)]
OFF = [SPAN_X * j % LANES for j in range(GROUP)]
LAST = [(SPAN_X * j + SPAN_X - 1) // LANES for j in range(GROUP)]
END = [(SPAN_X * j + SPAN_X - 1) % LANES for j in range(GROUP)]
FIRST_OF = [[OFF[j] for j in range(GROUP) if START[j] == a] for a in range(PLANES)]
LAST_OF = [[END[j] for j in range(GROUP) if LAST[j] == a] for a in range(PLANES)]
RIM_ROWS = 20
HELD = -(-ROWS // 8) * 8
PACKS = 3 * HELD
FIELDS = PACKS + 56
EDGE = 32
BUDGET = 32 * 1024 * 1024


def turn(value, shift, axis=1):
    shift = shift % value.shape[axis]
    return value if shift == 0 else pltpu.roll(value, shift, axis)


def fetching(pairs, sems):
    copies = [pltpu.make_async_copy(a, b, sems.at[n]) for n, (a, b) in enumerate(pairs)]
    for copy in copies:
        copy.start()
    return copies


def pieces_of(levels, count):
    rows = 2 * levels
    number = -(-4 * rows // count)
    runs = [[] for _ in range(4)]
    for c in range(4):
        for j in range(number):
            low, high = max(c * rows, j * count), min((c + 1) * rows, (j + 1) * count)
            if low < high:
                runs[c].append((j, low - j * count, low - c * rows, high - low))
    merged = count <= 2 * rows and levels <= 12
    return number, runs, number + (0 if merged else 1), 0 if merged else 1


def gram_lane(n):
    return 16 * (n // 4) + 12 + n % 4


class Level:
    def __init__(self, ref, base):
        self.ref, self.base = ref, base

    def plane(self, a):
        return self.ref[comb(self.base + a), :]

    def rows(self, low, size):
        return self.ref[pl.ds(self.base + low, size), :]


def lane_of(shape):
    return lax.broadcasted_iota(jnp.int32, shape, len(shape) - 1)


def row_of(shape):
    return lax.broadcasted_iota(jnp.int32, shape, 0)


def comb(a, count=GROUPS):
    return pl.ds(a, count, stride=PLANES)


def line_of(get, y):
    lane = lane_of((1, LANES))
    j = y % GROUP
    row = y // GROUP * PLANES + START[j]
    first, second = get(row), get(row + 1)
    third = get(row + 2) if START[j] + 2 < PLANES else second
    left = turn(jnp.where(lane >= OFF[j], first, second), -OFF[j])
    right = turn(jnp.where(lane >= OFF[j], second, third), -OFF[j])
    return left, right


def drop(value, lanes, lane):
    for at in lanes:
        value = jnp.where(lane == at, 0.0, value)
    return value


def store_terms(a, temp, flow_x, flow_y, te, tw, tn, ts):
    spread = DIFFUSE * temp
    te[a] = spread - flow_x
    tw[a] = spread + flow_x
    tn[a, 8 : 8 + GROUPS] = spread - flow_y
    ts[a, 8 : 8 + GROUPS] = spread + flow_y


def clear_terms(tn, ts):
    none = jnp.zeros((PLANES, 1, LANES), jnp.float32)
    for ref in (tn, ts):
        ref[:, 7:8] = none
        ref[:, 8 + GROUPS : 9 + GROUPS] = none


def inner_sum(a, te, tw, tn, ts):
    lane = lane_of((GROUPS, LANES))
    here = te[a]
    east = here if a == PLANES - 1 else jnp.where(lane == 0, te[a + 1], here)
    east = drop(turn(east, -1), LAST_OF[a], lane)
    here = tw[a]
    west = here if a == 0 else jnp.where(lane == LANES - 1, tw[a - 1], here)
    west = drop(turn(west, 1), FIRST_OF[a], lane)

    def plane(ref, at):
        down = 8 + (at >= PLANES) - (at < 0)
        return ref[at % PLANES, down : down + GROUPS]

    north = turn(jnp.where(lane >= LANES - 16, plane(tn, a + 1), plane(tn, a + 2)), 16)
    south = turn(jnp.where(lane < 16, plane(ts, a - 1), plane(ts, a - 2)), -16)
    return east + west + north + south


def choose(planes, lane, get):
    shift = 32 if planes is LAST else 0
    lows = sorted(((OFF[j] - shift) % LANES, planes[j]) for j in range(GROUP))
    value = get(lows[-1][1])
    for low, a in reversed(lows[:-1]):
        value = jnp.where(lane < low + 16, get(a), value)
    return value


def forcing_kernel(
    levels, per, tiles_x, tiles_y,
    pos_in, temp_in, zonal_in, merid_in, depth_in, ocean_in, diag_in, source_in,
    fields, slots_out, around_out,
    temp, zonal, merid, depth, ocean, source, slots,
    st, sx, sy, pt, te, tw, tn, ts, edges, pos, holder, around, sems, out_sems,
):
    count = pos.shape[0]
    steps = levels // per
    number_pieces, runs, _, _ = pieces_of(levels, count)
    slot = RIM_ROWS + number_pieces
    pairs = []
    for step in range(steps):
        chunk = pl.ds(step * per * ROWS, per * ROWS)
        pairs += [
            (a.at[chunk], b.at[chunk]) for a, b in ((temp_in, temp), (zonal_in, zonal), (merid_in, merid))
        ]
    pairs += [
        (a.reshape(ROWS, LANES), b)
        for a, b in (
            (source_in, source), (ocean_in, ocean), (depth_in, depth),
            (diag_in, fields.at[pl.ds(2 * HELD, ROWS)]),
        )
    ]
    copies = fetching([(pos_in, pos)] + pairs, sems)
    copies.pop(0).wait()
    results = []

    def send(value, target):
        copy = pltpu.make_async_copy(value, target, out_sems.at[len(results)])
        copy.start()
        results.append(copy)

    lane = lane_of((GROUPS, LANES))
    one = lane_of((1, LANES))
    q = lane % 16
    edges[...] = jnp.zeros_like(edges)

    def number(d, carry):
        holder[pos[d]] = d
        return carry

    lax.fori_loop(0, count, number, 0)
    me = lax.axis_index("gx") * tiles_y + lax.axis_index("gy")
    here = pos[me]
    row = here // tiles_x
    column = here % tiles_x
    sides = []
    for c, (dx, dy) in enumerate(SIDES):
        there = row + dy
        inside = jnp.logical_and(there >= 0, there < tiles_y)
        target = jnp.where(inside, there, 0) * tiles_x + (column + dx + tiles_x) % tiles_x
        device = jnp.where(inside, holder[target], -1)
        around[4 * count + c] = device
        sides.append(device)

    def look(y, carry):
        line = [holder[y * tiles_x + x] for x in range(tiles_x)]
        below = [holder[jnp.maximum(y - 1, 0) * tiles_x + x] for x in range(tiles_x)]
        above = [holder[jnp.minimum(y + 1, tiles_y - 1) * tiles_x + x] for x in range(tiles_x)]
        for x, device in enumerate(line):
            for c, other in enumerate((line[x - 1], line[(x + 1) % tiles_x], below[x], above[x])):
                around[c * count + device] = other * slot + RIM_ROWS
        return carry

    lax.fori_loop(0, tiles_y, look, 0)
    send(around, around_out)
    clear_terms(tn, ts)

    def add(flats, low, size, fresh):
        rows = pl.ds(low, size)
        total = [None] * 3
        for t, u, v in zip(*flats):
            t = t.rows(low, size)
            new = (t, t * u.rows(low, size), t * v.rows(low, size))
            total = [b if a is None else a + b for a, b in zip(total, new)]
        for ref, value in zip((st, sx, sy), total):
            ref[rows, :] = value if fresh else ref[rows, :] + value

    for step in range(steps):
        for copy in copies[3 * step : 3 * step + 3]:
            copy.wait()
        flats = [
            [Level(ref, (step * per + n) * ROWS) for n in range(per)] for ref in (temp, zonal, merid)
        ]

        def some(m, carry):
            add(flats, pl.multiple_of(m * 8, 8), 8, step == 0)
            return carry

        lax.fori_loop(0, ROWS // 8, some, 0, unroll=4)
        if ROWS % 8:
            add(flats, ROWS - ROWS % 8, ROWS % 8, step == 0)

        for n in range(per):
            k = step * per + n
            t, u, v = (flat[n] for flat in flats)

            loaded = {a: (t.plane(a), u.plane(a)) for a in sorted(set(START + LAST))}

            def term(planes, sign):
                own = choose(planes, lane, lambda a: loaded[a][0])
                flow = choose(planes, lane, lambda a: loaded[a][1])
                return DIFFUSE * own + sign * ADVECT * (flow * own)

            edges[0, 0:GROUPS] = jnp.where(q == k, turn(term(START, -1.0), k), edges[0, 0:GROUPS])
            edges[1, 0:GROUPS] = jnp.where(q == k, turn(term(LAST, 1.0), k + 17), edges[1, 0:GROUPS])
            rows = t.rows(0, 2)
            rows = DIFFUSE * rows - ADVECT * (v.rows(0, 2) * rows)
            edges[2, k : k + 1] = rows[0:1]
            edges[2, k + levels : k + levels + 1] = rows[1:2]
            rows = t.rows(ROWS - 2, 2)
            rows = DIFFUSE * rows + ADVECT * (v.rows(ROWS - 2, 2) * rows)
            edges[3, k : k + 1] = turn(jnp.where(one >= 16, rows[0:1], rows[1:2]), -16)
            edges[3, k + levels : k + levels + 1] = turn(rows[1:2], -16)

    for c in range(4):
        for j, device, low, size in runs[c]:
            slots[pl.ds(device * slot + RIM_ROWS + j, size, stride=slot), :] = edges[c, low : low + size]

    for copy in copies[3 * steps :]:
        copy.wait()

    part = fields.at[pl.ds(0, HELD)]
    mask = fields.at[pl.ds(HELD, HELD)]
    diag = fields.at[pl.ds(2 * HELD, HELD)]
    own = fields.at[pl.ds(PACKS, 56)]
    mask[0:ROWS] = depth[...] * ocean[...].astype(jnp.float32)

    def wet_of(rows):
        return ocean[rows, :].astype(jnp.float32)

    def masked(rows):
        return mask[rows, :]

    for a in range(PLANES):
        total = st[comb(a), :]
        pt[a] = total
        store_terms(a, total, ADVECT * sx[comb(a), :], ADVECT * sy[comb(a), :], te, tw, tn, ts)
    for a in range(PLANES):
        total = pt[a]
        wet = wet_of(comb(a))
        change = inner_sum(a, te, tw, tn, ts) - 4.0 * DIFFUSE * total
        part[comb(a), :] = source[comb(a), :] + (STERIC / levels) * wet * (total + wet * change)

    def mix(*values):
        value = values[-1]
        for at, low in ((6, 12), (5, 11), (4, 10), (3, 9), (2, 8), (1, 6), (0, 3)):
            value = jnp.where(q < low, values[at], value)
        return value

    def ends(planes, low):
        value = tn[planes[0], 8 : 8 + GROUPS]
        last = jnp.logical_and(lane >= low, lane < low + 16)
        return jnp.where(last, ts[planes[7], 8 : 8 + GROUPS], value)

    def beside(b, d, g, b_out, d_out):
        return g * b + d * d_out * (b - b_out)

    bp = choose(START, lane, lambda a: part[comb(a), :])
    dp = choose(START, lane, lambda a: masked(comb(a)))
    gp = choose(START, lane, lambda a: diag[comb(a), :])
    pp = beside(bp, dp, gp, turn(bp, -1), turn(dp, -1))
    pack_w = mix(
        bp, turn(dp, 3), turn(gp, 6), turn(pp, 6), turn(choose(START, lane, lambda a: te[a]), 9),
        turn(gp, 8), turn(dp, 8), turn(ends(START, OFF[7]), 12),
    )
    bp = choose(LAST, lane, lambda a: part[comb(a), :])
    dp = choose(LAST, lane, lambda a: masked(comb(a)))
    gp = choose(LAST, lane, lambda a: diag[comb(a), :])
    pp = beside(bp, dp, gp, turn(bp, 1), turn(dp, 1))
    pack_e = mix(
        turn(bp, 19), turn(dp, 22), turn(gp, 24), turn(pp, 27),
        turn(choose(LAST, lane, lambda a: tw[a]), 26),
        turn(gp, 29), turn(dp, 31), turn(ends(LAST, LANES - 16), 32),
    )
    own[0:GROUPS] = pack_w
    own[SLABS : SLABS + GROUPS] = pack_e
    north_l = tn[0, 8:9]
    north_r = tn[1, 8:9]
    south_13 = ts[PLANES - 2, 7 + GROUPS : 8 + GROUPS]
    south_14 = ts[PLANES - 1, 7 + GROUPS : 8 + GROUPS]
    south_l = turn(jnp.where(one >= 16, south_13, south_14), -16)
    south_r = turn(south_14, -16)
    own[48:49] = north_l
    own[49:50] = north_r
    own[50:51] = south_l
    own[51:52] = south_r
    deep = jnp.max(masked(slice(0, ROWS)), axis=(0, 1), keepdims=True)
    top = jnp.max(diag[0:ROWS], axis=(0, 1), keepdims=True) + 8.0 * deep * deep
    top = jnp.broadcast_to(top, (1, LANES))

    slots[pl.ds(RIM_ROWS - 1, count, stride=slot), :] = jnp.broadcast_to(top, (count, LANES))
    block_lane = lane_of((6, LANES))
    block_row = row_of((6, LANES))
    for c, first, rows_l, rows_r in ((2, True, north_l, north_r), (3, False, south_l, south_r)):
        base = 0 if first else ROWS - 6
        if first:
            spare = jnp.logical_and(block_row == 5, block_lane >= 80)
        else:
            spare = jnp.logical_and(block_row == 0, block_lane < 48)
        g = 0 if first else GROUPS - 1
        blocks = []
        block = slice(base, base + 6)
        for value, at in ((part[block, :], g), (masked(block), SLABS + g)):
            extra = jnp.broadcast_to(turn(own[at : at + 1], -16), (6, LANES))
            blocks.append(jnp.where(spare, extra, value))
        low = 0 if first else ROWS - 4
        diag_rows = diag[low : low + 4, :]
        third, fourth = (2, 3) if first else (SPAN_Y - 3, SPAN_Y - 4)
        b_l, b_r = line_of(lambda n: part[n : n + 1, :], third)
        d_l, d_r = line_of(lambda n: masked(slice(n, n + 1)), third)
        g_l, g_r = line_of(lambda n: diag[n : n + 1, :], third)
        bo_l, bo_r = line_of(lambda n: part[n : n + 1, :], fourth)
        do_l, do_r = line_of(lambda n: masked(slice(n, n + 1)), fourth)
        out_l = beside(b_l, d_l, g_l, bo_l, do_l)
        out_r = beside(b_r, d_r, g_r, bo_r, do_r)
        for at, value in ((112, turn(g_l, 112)), (113, turn(do_l, 113)), (114, turn(g_r, 3)), (115, turn(do_r, 4))):
            out_r = jnp.where(one == at, value, out_r)
        last_row = jnp.where(one == LANES - 1, top, rows_r)

        @pl.when(sides[c] >= 0)
        def _(c=c, blocks=blocks, diag_rows=diag_rows, singles=(out_l, out_r, rows_l, last_row)):
            at = sides[c] * slot
            slots[pl.ds(at, 6), :] = blocks[0]
            slots[pl.ds(at + 6, 6), :] = blocks[1]
            slots[pl.ds(at + 12, 4), :] = diag_rows
            for n, value in enumerate(singles):
                slots[pl.ds(at + 16 + n, 1), :] = value

    corner = jnp.logical_and(row_of((GROUPS, LANES)) == RIM_ROWS - 1, lane == LANES - 1)
    for c, pack in ((0, pack_w), (1, pack_e)):
        slots[pl.ds(sides[c] * slot, GROUPS), :] = jnp.where(corner, top, pack)
    for c, at in ((4, 0), (5, SLABS), (6, GROUPS - 1), (7, SLABS + GROUPS - 1)):
        @pl.when(sides[c] >= 0)
        def _(c=c, at=at):
            slots[pl.ds(sides[c] * slot, 1), :] = own[at : at + 1]
    send(slots, slots_out.reshape(count * slot, LANES))
    for copy in results:
        copy.wait()


SMEM = pl.BlockSpec(memory_space=pltpu.SMEM)


def solve_kernel(
    levels, tiles_y,
    around_in, rims, fields,
    vectors, hands,
    around, sem, north_in, south_in, fb, fd, fg, pw, pe, ow, oe, ed, eg, ex, we, wn, last, rows,
):
    copies = fetching([(around_in, around)], sem)
    count = rims.shape[0]
    number_pieces, _, share, first = pieces_of(levels, count)
    slot = RIM_ROWS + number_pieces
    came = rims.reshape(count * slot, LANES)
    hand = hands.reshape(count * share, LANES)
    own = fields.at[pl.ds(PACKS, 56)]
    lane = lane_of((SLABS, LANES))
    slab = row_of((SLABS, LANES))
    one = lane_of((1, LANES))

    none = jnp.zeros((WIDE - ROWS + 4, LANES), jnp.float32)
    for ref in (fb, fd, fg):
        ref[ROWS - 4 : WIDE] = none
    for n, ref in enumerate((fb, fd, fg)):
        ref[0:ROWS] = fields[n * HELD : n * HELD + ROWS]
    copies[0].wait()
    src = [around[4 * count + c] for c in range(8)]

    def fetch(c, low, high):
        value = came[pl.ds(jnp.maximum(src[c], 0) * slot + low, high - low), :]
        return jnp.where(src[c] >= 0, value, 0.0)

    me = lax.axis_index("gx") * tiles_y + lax.axis_index("gy")
    for n in range(number_pieces):
        side = jnp.minimum((n * count + me) // (2 * levels), 3)
        base = (side + 1 - 2 * (side % 2)) * count

        def relay(d, carry, n=n, base=base):
            row = around[base + d] + n
            hand[pl.ds(d * share + first + n, 1), :] = came[pl.ds(row, 1), :]
            return carry

        for d in range(count):
            relay(d, 0)

    north_in[0:RIM_ROWS] = fetch(3, 0, RIM_ROWS)
    south_in[0:RIM_ROWS] = fetch(2, 0, RIM_ROWS)
    strips = {2: south_in, 3: north_in}
    for ref, low, high, n_lane, s_lane in ((fb, 0, 6, 80, 48), (fd, 6, 12, 80, 48), (fg, 12, 16, 96, 32)):
        size = high - low
        row, column = row_of((size, LANES)), lane_of((size, LANES))
        beyond = jnp.logical_and(row == size - 1, column >= n_lane)
        ref[ROWS : ROWS + size] = jnp.where(beyond, 0.0, strips[3][low:high])
        beyond = jnp.logical_and(row == 0, column < s_lane)
        ref[WIDE - size : WIDE] = jnp.where(beyond, 0.0, strips[2][low:high])
    empty = jnp.zeros((SLABS, LANES), jnp.float32)
    for ref, side, north, south in ((pw, 0, 6, 4), (pe, 1, 7, 5)):
        ref[...] = empty
        ref[0:GROUPS] = fetch(side, 0, GROUPS)
        ref[GROUPS : GROUPS + 1] = fetch(north, 0, 1)
        ref[SLABS - 1 : SLABS] = fetch(south, 0, 1)
    for ref, at, north, south in ((ow, 0, 5, 0), (oe, SLABS, 11, 6)):
        ref[...] = empty
        ref[0:GROUPS] = own[at : at + GROUPS]
        ref[GROUPS : GROUPS + 1] = turn(strips[3][north:north + 1], 16)
        ref[SLABS - 1 : SLABS] = turn(strips[2][south:south + 1], 16)

    def spread(ref, j):
        a = START[j]
        first, second = ref[comb(a, SLABS), :], ref[comb(a + 1, SLABS), :]
        third = ref[comb(a + 2, SLABS), :] if a + 2 < PLANES else second
        left = turn(jnp.where(lane >= OFF[j], first, second), -OFF[j])
        right = turn(jnp.where(lane >= OFF[j], second, third), -OFF[j])
        return left, right

    def seam_row(left, right, slab_at, lanes_at):
        east = turn(pe[slab_at : slab_at + 1], 112 - lanes_at)
        west = turn(pw[slab_at : slab_at + 1], 124 - lanes_at)
        right = jnp.where(one < 112, right, jnp.where(one < 116, east, jnp.where(one >= 124, west, 0.0)))
        return jnp.broadcast_to(left, (SLABS, LANES)), jnp.broadcast_to(right, (SLABS, LANES))

    seams = {
        0: ((0, seam_row(strips[2][18:19], strips[2][19:20], SLABS - 1, 28)),
            (GROUPS, seam_row(own[50:51], own[51:52], GROUPS - 1, 28))),
        GROUP - 1: ((GROUPS - 1, seam_row(strips[3][18:19], strips[3][19:20], GROUPS, 12)),
                    (SLABS - 1, seam_row(own[48:49], own[49:50], 0, 12))),
    }
    weight = STERIC / levels

    def missing(target, term, term_out, d, d_out, g):
        term, term_out, d, d_out, g = (
            turn(value[0], target - value[1]) for value in (term, term_out, d, d_out, g)
        )
        term = jnp.where(d > 0, weight * term, 0.0)
        term_out = jnp.where(d_out > 0, weight * term_out, 0.0)
        return jnp.where(one == target, g * term + d * d_out * (term - term_out), 0.0)

    def ring(ref, at):
        return ref[at : at + 1]

    outer = {j: [] for j in range(GROUP)}
    for j, at, beyond, o, lanes in ((0, 0, SLABS - 1, 0, 28), (GROUP - 1, GROUPS - 1, GROUPS, 16, 12)):
        own_row, corner = ring(pe, at), ring(pe, beyond)
        outer[j].append((1, at, missing(
            114, (corner, lanes + 2), (corner, lanes + 3), (own_row, o + 5), (own_row, o + 11), (own_row, o + 10),
        )))
        own_row, corner = ring(pw, at), ring(pw, beyond)
        outer[j].append((1, at, missing(
            125, (corner, lanes + 1), (corner, lanes), (own_row, o + 3), (own_row, o + 11), (own_row, o + 10),
        )))
    for j, at, c, j_out, d_l, d_r in ((2, GROUPS, 3, 3, (9, 96), (11, 79)), (5, SLABS - 1, 2, 4, (6, 48), (8, 31))):
        line_l, line_r = strips[c][16:17], strips[c][17:18]
        corner = ring(pw, at)
        outer[j].append((0, at, line_l + missing(
            0, (corner, OFF[j] + 9), (corner, OFF[j_out] + 9), (strips[c][d_l[0]:d_l[0] + 1], d_l[1]),
            (line_r, 113), (line_r, 112),
        )))
        corner = ring(pe, at)
        outer[j].append((1, at, jnp.where(one < 112, line_r, 0.0) + missing(
            111, (corner, OFF[j] + 9), (corner, OFF[j_out] + 9), (strips[c][d_r[0]:d_r[0] + 1], d_r[1]),
            (line_r, 115), (line_r, 114),
        )))
    for j in range(GROUP):
        o = OFF[j]
        inside = slab < GROUPS
        halves = [
            jnp.zeros((SLABS, LANES), jnp.float32),
            jnp.where(
                jnp.logical_and(inside, lane == 114), turn(pe[...], 114 - o - 8),
                jnp.where(jnp.logical_and(inside, lane == 125), turn(pw[...], 125 - o - 8), 0.0),
            ),
        ]
        for half, at, line in outer[j]:
            halves[half] = halves[half] + jnp.where(slab == at, line, 0.0)
        ex[j, :, 0:LANES] = halves[0]
        ex[j, :, LANES:] = halves[1]

        def rim(right, q, width):
            east = turn(pe[...], 112 - o - q)
            west = turn(pw[...], 128 - width - o - q)
            value = jnp.where(lane < 112 + width, east, jnp.where(lane >= 128 - width, west, 0.0))
            return jnp.where(lane < 112, right, value)

        left, right = spread(fd, j)
        right = rim(right, 3, 3)
        wet_l = jnp.where(left > 0, weight, 0.0)
        wet_r = jnp.where(right > 0, weight, 0.0)
        ed[j, :, 0:LANES] = left
        ed[j, :, LANES:] = right
        left, right = spread(fg, j)
        eg[j, :, 0:LANES] = left
        eg[j, :, LANES:] = rim(right, 6, 2)
        left, right = spread(fb, j)
        right = rim(right, 0, 3)
        seam_l = jnp.where(lane == 0, turn(pw[...], -o - 9), 0.0)
        seam_r = jnp.where(lane == 127, turn(ow[...], 127 - o - 9), 0.0)
        seam_r = jnp.where(lane == 111, turn(pe[...], 111 - o - 9), seam_r)
        seam_r = jnp.where(lane == 112, turn(oe[...], 112 - o - 9), seam_r)
        for at, (row_l, row_r) in seams.get(j, ()):
            seam_l = seam_l + jnp.where(slab == at, row_l, 0.0)
            seam_r = seam_r + jnp.where(slab == at, row_r, 0.0)
        vectors[0, j, :, 0:LANES] = left + wet_l * seam_l
        vectors[0, j, :, LANES:] = right + wet_r * seam_r

    for j in range(GROUP):
        d = ed[j]
        we[j] = d * turn(d, -1)
        above = ed[j + 1] if j < GROUP - 1 else turn(ed[0], -1, 0)
        wn[j] = d * above

    top = jnp.max(came[pl.ds(RIM_ROWS - 1, count, stride=slot), :], axis=0, keepdims=True)
    top = jnp.max(jnp.where(one == LANES - 1, top, 0.0), axis=1, keepdims=True)
    scale = STRETCH / top

    big = (SLABS, 2 * LANES)
    mine = jnp.logical_and(row_of(big) < GROUPS, lane_of(big) < SPAN_X)
    pair = 0
    for k in range(5):
        sums = [None] * (k + 1)
        new = last if k == 4 else vectors.at[k]
        if k:
            v = vectors.at[k - 1]
            flow_below = wn[GROUP - 1] * (v[GROUP - 1] - turn(v[0], -1, 0))
            flow_below = turn(flow_below, 1, 0)
        for j in range(GROUP):
            if k:
                here = v[j]
                above = v[j + 1] if j < GROUP - 1 else turn(v[0], -1, 0)
                flow_x = we[j] * (here - turn(here, -1))
                flow_y = wn[j] * (here - above)
                image = eg[j] * here + (flow_x - turn(flow_x, 1)) + (flow_y - flow_below)
                if k == 1:
                    image = image + ex[j]
                fresh = scale * image - (STRETCH * ROOTS[k - 1]) * here
                flow_below = flow_y
                new[j] = fresh
            else:
                fresh = new[j]
            held = jnp.where(mine, fresh, 0.0)
            for i in range(k + 1):
                other = vectors[i, j] if i < k else held
                value = held * other
                sums[i] = value if sums[i] is None else sums[i] + value
        for i in range(k + 1):
            rows[pair : pair + 1] = jnp.sum(sums[i][:, 0:LANES] + sums[i][:, LANES:], axis=0, keepdims=True)
            pair += 1
    rows[pair : pair + 1] = jnp.where(one == 0, top, 0.0)
    total = jnp.sum(rows[...], axis=1, keepdims=True)
    spot = lane_of((16, LANES)) == gram_lane(row_of((16, LANES)))
    line = jnp.sum(jnp.where(spot, total, 0.0), axis=0, keepdims=True)
    line = jnp.broadcast_to(line, (count, LANES))
    if first == 0:
        line = jnp.where(lane_of((count, LANES)) % 16 < 12, hand[pl.ds(0, count, stride=share), :], line)
    hand[pl.ds(0, count, stride=share), :] = line


def finish_kernel(
    levels, per, hands, vectors, edges, inner, tracer_out, surface_out,
    cells, flat, left, right, message, out_sems,
):
    count = hands.shape[0]
    _, runs, share, first = pieces_of(levels, count)
    came = hands.reshape(count * share, LANES)
    steps = levels // per
    chunks = [pl.ds(step * per * ROWS, per * ROWS) for step in range(steps)]
    row = jnp.sum(came[pl.ds(0, count, stride=share), :], axis=0, keepdims=True)
    one = lane_of((1, LANES))
    entry = {}
    pair = 0
    for k in range(5):
        for i in range(k + 1):
            value = jnp.sum(jnp.where(one == gram_lane(pair), row, 0.0), axis=1, keepdims=True)
            entry[i, k] = entry[k, i] = value
            pair += 1
    top = jnp.sum(jnp.where(one == gram_lane(pair), row, 0.0), axis=1, keepdims=True) * (1.0 / count)

    def image(c):
        out = [None] * 5
        for k in range(4):
            if c[k] is None:
                continue
            low = ROOTS[k] * c[k]
            out[k] = low if out[k] is None else out[k] + low
            out[k + 1] = (1.0 / STRETCH) * c[k]
        return out

    def dot(a, b):
        total = None
        for i in range(5):
            if a[i] is None:
                continue
            inner = None
            for j in range(5):
                if b[j] is not None:
                    value = entry[i, j] * b[j]
                    inner = value if inner is None else inner + value
            total = a[i] * inner if total is None else total + a[i] * inner
        return total

    def axpy(a, s, b):
        return [
            x if y is None else (s * y if x is None else x + s * y) for x, y in zip(a, b)
        ]

    r = [jnp.ones((1, 1), jnp.float32)] + [None] * 4
    p = list(r)
    x = [None] * 5
    rr = entry[0, 0]
    for n in range(ITERS):
        q = image(p)
        step = rr / jnp.maximum(dot(p, q), TINY)
        step = jnp.clip(step, top * (1.0 / HIGH_RATE), top * (1.0 / LOW_RATE))
        x = axpy(x, step, p)
        if n < ITERS - 1:
            r = axpy(r, -step, q)
            fresh = jnp.maximum(dot(r, r), 0.0)
            p = axpy(r, fresh / jnp.maximum(rr, TINY), p)
            rr = fresh
    factors = [c / top for c in x[:4]]
    for j in range(GROUP):
        value = None
        for k in range(4):
            term = factors[k] * vectors[k, j]
            value = term if value is None else value + term
        left[j] = turn(value[:, 0:LANES], OFF[j])
        right[j] = turn(value[:, LANES:], OFF[j])
    lane = lane_of((SLABS, LANES))
    for a in range(PLANES):
        value = None
        for j in range(GROUP):
            for half, ref in ((0, left), (1, right)):
                low = max(SPAN_X * j + LANES * half - LANES * a, 0)
                high = min(SPAN_X * j + (LANES if half == 0 else SPAN_X) - LANES * a, LANES)
                if low >= high:
                    continue
                value = ref[j] if value is None else jnp.where(lane >= low, ref[j], value)
        flat[comb(a), :] = value[0:GROUPS]
    results = [pltpu.make_async_copy(flat, surface_out.reshape(ROWS, LANES), out_sems.at[0])]
    results[0].start()

    for c in range(4):
        for j, device, low, size in runs[c ^ 1]:
            value = came[pl.ds(device * share + first + j, size, stride=share), :]
            message[c, low : low + size] = value
    second = lane_of((SLABS, LANES)) % 16 == 1
    sums = []
    for k in range(levels):
        value = edges[2 * levels - 1] * jnp.concatenate([
            jnp.where(second, turn(message[1], 1 - k), turn(message[0], -k)),
            message[2, k : k + 1], message[2, k + levels : k + levels + 1],
            message[3, k : k + 1], message[3, k + levels : k + levels + 1],
            jnp.zeros((EDGE - SLABS - 4, LANES), jnp.float32),
        ], axis=0)
        if k:
            value = value + edges[2 * levels + k - 1] * sums[-1]
        sums.append(value * edges[levels - 1 + k])
    for k in range(levels - 2, -1, -1):
        sums[k] = sums[k] + edges[k] * sums[k + 1]
    lane = lane_of((GROUPS, LANES))
    slab = row_of((GROUPS, LANES))
    for k in range(levels):
        west = sums[k][0:GROUPS]
        east = turn(west, -18)
        south_l, south_r = sums[k][SLABS : SLABS + 1], sums[k][SLABS + 1 : SLABS + 2]
        north_l = turn(sums[k][SLABS + 2 : SLABS + 3], 16)
        north_r = turn(sums[k][SLABS + 3 : SLABS + 4], 16)
        for a in range(PLANES):
            rim = None
            for at, source in [(at, west) for at in FIRST_OF[a]] + [(at, east) for at in LAST_OF[a]]:
                rim = jnp.where(lane == at, source, 0.0 if rim is None else rim)
            rows = comb(k * ROWS + a)
            if rim is None:
                cells[rows, :] = inner[rows, :]
                continue
            if a == 0:
                rim = rim + jnp.where(slab == 0, south_l, 0.0)
            if a == 1:
                rim = rim + jnp.where(jnp.logical_and(slab == 0, lane < 112), south_r, 0.0)
            if a == PLANES - 2:
                rim = rim + jnp.where(jnp.logical_and(slab == GROUPS - 1, lane >= 16), north_l, 0.0)
            if a == PLANES - 1:
                rim = rim + jnp.where(slab == GROUPS - 1, jnp.where(lane < 16, north_l, north_r), 0.0)
            cells[rows, :] = inner[rows, :] + rim
        if k % per == per - 1:
            step = k // per
            copy = pltpu.make_async_copy(
                cells.at[chunks[step]], tracer_out.at[chunks[step]], out_sems.at[1 + step]
            )
            copy.start()
            results.append(copy)
    for copy in results:
        copy.wait()


def tracer_kernel(
    levels, per, sides, around, temp_in, zonal_in, merid_in, rates_in, fields,
    out, edges,
    temp, zonal, merid, rates, ocean,
    te, tw, tn, ts, stepped, border, sems,
):
    steps = levels // per
    pairs = []
    for step in range(steps):
        chunk = pl.ds(step * per * ROWS, per * ROWS)
        pairs += [
            (a.at[chunk], b.at[chunk]) for a, b in ((temp_in, temp), (zonal_in, zonal), (merid_in, merid))
        ]
    copies = fetching(pairs + [(rates_in.reshape((levels - 1) * ROWS, LANES), rates)], sems)
    lane = lane_of((GROUPS, LANES))
    one = lane_of((1, LANES))
    clear_terms(tn, ts)

    ocean[...] = jnp.where(fields[HELD : HELD + ROWS] > 0, 1.0, 0.0)
    for step in range(steps):
        for copy in copies[3 * step : 3 * step + 3]:
            copy.wait()

        def level(k, carry):
            t, u, v = (Level(ref, k * ROWS) for ref in (temp, zonal, merid))
            for a in range(PLANES):
                own = t.plane(a)
                quarter = ADVECT * own
                store_terms(a, own, u.plane(a) * quarter, v.plane(a) * quarter, te, tw, tn, ts)
            for a in range(PLANES):
                own = t.plane(a)
                change = inner_sum(a, te, tw, tn, ts) - 4.0 * DIFFUSE * own
                stepped[k, a] = own + ocean[comb(a), :] * change
            return carry

        lax.fori_loop(step * per, step * per + per, level, 0)
    copies[-1].wait()

    def block(a, carry):
        for low in range(0, GROUPS, 8):
            size = min(8, GROUPS - low)

            def rows(k):
                return pl.ds(k * ROWS + low * PLANES + a, size, stride=PLANES)

            gains = []
            sums = []
            for k in range(levels):
                value = stepped[k, a, low : low + size]
                pivot = 1.0
                if k > 0:
                    pivot = pivot + upper - upper * gains[-1]
                    value = value + upper * sums[-1]
                if k < levels - 1:
                    lower = rates[rows(k), :]
                    inverse = 1.0 / (pivot + lower)
                    gains.append(lower * inverse)
                    upper = lower
                else:
                    inverse = 1.0 / pivot
                sums.append(value * inverse)
            result = sums[-1]
            out[rows(levels - 1), :] = result
            for k in range(levels - 2, -1, -1):
                result = sums[k] + gains[k] * result
                out[rows(k), :] = result
        return carry

    lax.fori_loop(0, PLANES, block, 0)

    def edge(ref, base, at):
        def get(a):
            return ref[comb(base + a), :].astype(jnp.float32)

        border[0:GROUPS] = jnp.where(
            lane % 16 == 1, turn(choose(LAST, lane, get), 18), choose(START, lane, get)
        )
        border[SLABS : SLABS + 2] = ref[base : base + 2, :].astype(jnp.float32)
        rows = ref[base + ROWS - 2 : base + ROWS, :].astype(jnp.float32)
        border[SLABS + 2 : SLABS + 3] = turn(jnp.where(one >= 16, rows[0:1], rows[1:2]), -16)
        border[SLABS + 3 : SLABS + 4] = turn(rows[1:2], -16)
        edges[at] = border[...]

    border[...] = jnp.zeros_like(border)
    edge(ocean, 0, 2 * levels - 1)
    for c in (2, 3):
        rows = pl.ds(SLABS + 2 * (c - 2), 2)
        value = edges[2 * levels - 1, rows]
        edges[2 * levels - 1, rows] = jnp.where(around[sides + c] >= 0, value, 0.0)
    gain = None
    for k in range(levels):
        pivot = 1.0
        if k > 0:
            upper = edges[2 * levels + k - 1]
            pivot = pivot + upper - upper * gain
        if k < levels - 1:
            edge(rates, k * ROWS, 2 * levels + k)
            lower = edges[2 * levels + k]
            inverse = 1.0 / (pivot + lower)
            gain = lower * inverse
            edges[k] = gain
        else:
            inverse = 1.0 / pivot
        edges[levels - 1 + k] = inverse


def on_device(
    thermal_anomaly,
    zonal_flow_ratio,
    meridional_flow_ratio,
    diffusion_rates,
    ocean_bottom_scaled,
    ocean_indicator,
    operator_diagonal,
    elevation_source,
    block_positions,
):
    levels, cells = thermal_anomaly.shape[1:]
    nx = lax.axis_size("gx")
    ny = lax.axis_size("gy")
    count = block_positions.shape[0]
    planes = (ocean_bottom_scaled, ocean_indicator, operator_diagonal, elevation_source)
    depth, ocean, diag, source = planes
    f32 = jnp.float32
    per = next(n for n in (4, 2, 6, levels) if levels % n == 0 and n * ROWS % 8 == 0)
    steps = levels // per
    few = next(n for n in (2, 4, 6, levels) if levels % n == 0 and n * ROWS % 8 == 0)
    params = pltpu.CompilerParams(vmem_limit_bytes=BUDGET)
    temp, zonal, merid = (
        array.reshape(levels * ROWS, LANES)
        for array in (thermal_anomaly, zonal_flow_ratio, meridional_flow_ratio)
    )
    rates = diffusion_rates.reshape(levels - 1, 1, cells)
    temp, zonal, merid, rates, depth, ocean, diag, source, positions = (
        pltpu.with_memory_space_constraint(array, pltpu.HBM)
        for array in (temp, zonal, merid, rates, depth, ocean, diag, source, block_positions)
    )
    hbm = pl.BlockSpec(memory_space=pltpu.HBM)
    here = pl.BlockSpec(memory_space=pltpu.VMEM)

    def vmem(*shape, kind=f32):
        return pltpu.VMEM(shape, kind)

    def out(*shape, kind=f32):
        return jax.ShapeDtypeStruct(shape, kind)

    def sems(number):
        return pltpu.SemaphoreType.DMA((number,))

    deep = vmem(levels * ROWS, LANES)
    flat = vmem(ROWS, LANES)
    flat_int = vmem(ROWS, LANES, kind=jnp.int32)
    plane = vmem(PLANES, GROUPS, LANES)
    tall = vmem(PLANES, 40, LANES)
    numbers = pltpu.SMEM((count,), jnp.int32)
    number_pieces, _, share, _ = pieces_of(levels, count)
    slot = RIM_ROWS + number_pieces
    fields, slots, around = pl.pallas_call(
        functools.partial(forcing_kernel, levels, few, nx, ny),
        in_specs=[hbm] * 8,
        out_specs=[here, hbm, hbm],
        out_shape=[
            out(FIELDS, LANES), pltpu.HBM((count, 1, slot * LANES), f32), out(4 * count + 8, kind=jnp.int32),
        ],
        scratch_shapes=[deep] * 3 + [flat, flat_int, flat]
        + [vmem(count * slot, LANES)]
        + [flat] * 3 + [plane] * 3 + [tall] * 2
        + [vmem(4, 2 * levels, LANES), numbers, numbers]
        + [pltpu.SMEM((4 * count + 8,), jnp.int32), sems(3 * (levels // few) + 5), sems(2)],
        compiler_params=params,
        name="forcing",
    )(positions, temp, zonal, merid, depth, ocean, diag, source)
    rims = lax.all_to_all(slots, BOTH, 0, 0, tiled=True)

    inner, edges = pl.pallas_call(
        functools.partial(tracer_kernel, levels, per, 4 * count),
        in_specs=[SMEM] + [hbm] * 4 + [here],
        out_specs=[here] * 2,
        out_shape=[out(levels * ROWS, LANES), out(3 * levels - 1, EDGE, LANES)],
        scratch_shapes=[deep] * 3 + [vmem((levels - 1) * ROWS, LANES), flat]
        + [plane] * 2 + [tall] * 2
        + [vmem(levels, PLANES, GROUPS, LANES), vmem(EDGE, LANES), sems(3 * steps + 1)],
        compiler_params=params,
        name="tracer",
    )(around, temp, zonal, merid, rates, fields)

    rims, edges = lax.optimization_barrier((rims, edges))
    extended = vmem(GROUP, SLABS, 2 * LANES)
    vectors, hand = pl.pallas_call(
        functools.partial(solve_kernel, levels, ny),
        in_specs=[pl.BlockSpec(memory_space=pl.ANY)] + [here] * 2,
        out_specs=[here] * 2,
        out_shape=[out(4, GROUP, SLABS, 2 * LANES), out(count, 1, share * LANES)],
        scratch_shapes=[pltpu.SMEM((4 * count + 8,), jnp.int32), sems(1)]
        + [vmem(SLABS, LANES)] * 2 + [vmem(WIDE, LANES)] * 3 + [vmem(SLABS, LANES)] * 4 + [extended] * 6 + [vmem(16, LANES)],
        compiler_params=params,
        name="vectors",
    )(around, rims, fields)
    hands = lax.all_to_all(hand, BOTH, 0, 0, tiled=True)

    new_temp, surface = pl.pallas_call(
        functools.partial(finish_kernel, levels, per),
        in_specs=[here] * 4,
        out_specs=[hbm] * 2,
        out_shape=[out(levels * ROWS, LANES), out(1, cells)],
        scratch_shapes=[
            deep, flat, vmem(GROUP, SLABS, LANES), vmem(GROUP, SLABS, LANES), vmem(4, 2 * levels, LANES),
            sems(1 + steps),
        ],
        compiler_params=params,
        name="finish",
    )(hands, vectors, edges, inner)
    return new_temp.reshape(1, levels, cells), surface


def solution(mesh):
    deep = P(BOTH, None, None)
    flat = P(BOTH, None)
    return jax.shard_map(
        on_device,
        mesh=mesh,
        in_specs=(deep, deep, deep, deep, flat, flat, flat, flat, P()),
        out_specs=(deep, flat),
        check_vma=False,
    )
```

```python
import functools

import jax
import jax.numpy as jnp
from jax import lax
from jax.experimental import pallas as pl
from jax.experimental.pallas import tpu as pltpu
from jax.sharding import PartitionSpec as P

ITERS = 4
SPAN_X = 240
SPAN_Y = 160
RIM = 4
ADVECT = 0.25
DIFFUSE = 0.12
STERIC = 0.5
LOW_RATE = 0.05
HIGH_RATE = 32.5
ROOTS = (0.02, 0.35, 0.1, 0.2)
STRETCH = 4.0
TINY = 1e-30
BOTH = ("gx", "gy")
SIDES = ((-1, 0), (1, 0), (0, -1), (0, 1), (-1, -1), (1, -1), (-1, 1), (1, 1))

LANES = 128
GROUP = 8
GROUPS = SPAN_Y // GROUP
PLANES = GROUP * SPAN_X // LANES
ROWS = GROUPS * PLANES
SLABS = GROUPS + 4
WIDE = SLABS * PLANES
START = [SPAN_X * j // LANES for j in range(GROUP)]
OFF = [SPAN_X * j % LANES for j in range(GROUP)]
LAST = [(SPAN_X * j + SPAN_X - 1) // LANES for j in range(GROUP)]
END = [(SPAN_X * j + SPAN_X - 1) % LANES for j in range(GROUP)]
FIRST_OF = [[OFF[j] for j in range(GROUP) if START[j] == a] for a in range(PLANES)]
LAST_OF = [[END[j] for j in range(GROUP) if LAST[j] == a] for a in range(PLANES)]
RIM_ROWS = 20
HELD = -(-ROWS // 8) * 8
PACKS = 3 * HELD
FIELDS = PACKS + 56
EDGE = 32
BUDGET = 32 * 1024 * 1024


def turn(value, shift, axis=1):
    shift = shift % value.shape[axis]
    return value if shift == 0 else pltpu.roll(value, shift, axis)


def fetching(pairs, sems):
    copies = [pltpu.make_async_copy(a, b, sems.at[n]) for n, (a, b) in enumerate(pairs)]
    for copy in copies:
        copy.start()
    return copies


def pieces_of(levels, count):
    rows = 2 * levels
    number = -(-4 * rows // count)
    runs = [[] for _ in range(4)]
    for c in range(4):
        for j in range(number):
            low, high = max(c * rows, j * count), min((c + 1) * rows, (j + 1) * count)
            if low < high:
                runs[c].append((j, low - j * count, low - c * rows, high - low))
    merged = count <= 2 * rows and levels <= 12
    return number, runs, number + (0 if merged else 1), 0 if merged else 1


def gram_lane(n):
    return 16 * (n // 4) + 12 + n % 4


class Level:
    def __init__(self, ref, base):
        self.ref, self.base = ref, base

    def plane(self, a):
        return self.ref[comb(self.base + a), :]

    def rows(self, low, size):
        return self.ref[pl.ds(self.base + low, size), :]


def lane_of(shape):
    return lax.broadcasted_iota(jnp.int32, shape, len(shape) - 1)


def row_of(shape):
    return lax.broadcasted_iota(jnp.int32, shape, 0)


def comb(a, count=GROUPS):
    return pl.ds(a, count, stride=PLANES)


def line_of(get, y):
    lane = lane_of((1, LANES))
    j = y % GROUP
    row = y // GROUP * PLANES + START[j]
    first, second = get(row), get(row + 1)
    third = get(row + 2) if START[j] + 2 < PLANES else second
    left = turn(jnp.where(lane >= OFF[j], first, second), -OFF[j])
    right = turn(jnp.where(lane >= OFF[j], second, third), -OFF[j])
    return left, right


def drop(value, lanes, lane):
    for at in lanes:
        value = jnp.where(lane == at, 0.0, value)
    return value


def store_terms(a, temp, flow_x, flow_y, te, tw, tn, ts):
    spread = DIFFUSE * temp
    te[a] = spread - flow_x
    tw[a] = spread + flow_x
    tn[a, 8 : 8 + GROUPS] = spread - flow_y
    ts[a, 8 : 8 + GROUPS] = spread + flow_y


def clear_terms(tn, ts):
    none = jnp.zeros((PLANES, 1, LANES), jnp.float32)
    for ref in (tn, ts):
        ref[:, 7:8] = none
        ref[:, 8 + GROUPS : 9 + GROUPS] = none


def inner_sum(a, te, tw, tn, ts):
    lane = lane_of((GROUPS, LANES))
    here = te[a]
    east = here if a == PLANES - 1 else jnp.where(lane == 0, te[a + 1], here)
    east = drop(turn(east, -1), LAST_OF[a], lane)
    here = tw[a]
    west = here if a == 0 else jnp.where(lane == LANES - 1, tw[a - 1], here)
    west = drop(turn(west, 1), FIRST_OF[a], lane)

    def plane(ref, at):
        down = 8 + (at >= PLANES) - (at < 0)
        return ref[at % PLANES, down : down + GROUPS]

    north = turn(jnp.where(lane >= LANES - 16, plane(tn, a + 1), plane(tn, a + 2)), 16)
    south = turn(jnp.where(lane < 16, plane(ts, a - 1), plane(ts, a - 2)), -16)
    return east + west + north + south


def choose(planes, lane, get):
    shift = 32 if planes is LAST else 0
    lows = sorted(((OFF[j] - shift) % LANES, planes[j]) for j in range(GROUP))
    value = get(lows[-1][1])
    for low, a in reversed(lows[:-1]):
        value = jnp.where(lane < low + 16, get(a), value)
    return value


def forcing_kernel(
    levels, per, tiles_x, tiles_y,
    pos_in, temp_in, zonal_in, merid_in, depth_in, ocean_in, diag_in, source_in,
    fields, slots_out, around_out,
    temp, zonal, merid, depth, ocean, source, slots,
    st, sx, sy, pt, te, tw, tn, ts, edges, pos, holder, around, sems, out_sems,
):
    count = pos.shape[0]
    steps = levels // per
    number_pieces, runs, _, _ = pieces_of(levels, count)
    slot = RIM_ROWS + number_pieces
    pairs = []
    for step in range(steps):
        chunk = pl.ds(step * per * ROWS, per * ROWS)
        pairs += [
            (a.at[chunk], b.at[chunk]) for a, b in ((temp_in, temp), (zonal_in, zonal), (merid_in, merid))
        ]
    pairs += [
        (a.reshape(ROWS, LANES), b)
        for a, b in (
            (source_in, source), (ocean_in, ocean), (depth_in, depth),
            (diag_in, fields.at[pl.ds(2 * HELD, ROWS)]),
        )
    ]
    copies = fetching([(pos_in, pos)] + pairs, sems)
    copies.pop(0).wait()
    results = []

    def send(value, target):
        copy = pltpu.make_async_copy(value, target, out_sems.at[len(results)])
        copy.start()
        results.append(copy)

    lane = lane_of((GROUPS, LANES))
    one = lane_of((1, LANES))
    q = lane % 16
    edges[...] = jnp.zeros_like(edges)

    def number(d, carry):
        holder[pos[d]] = d
        return carry

    lax.fori_loop(0, count, number, 0)
    me = lax.axis_index("gx") * tiles_y + lax.axis_index("gy")
    here = pos[me]
    row = here // tiles_x
    column = here % tiles_x
    sides = []
    for c, (dx, dy) in enumerate(SIDES):
        there = row + dy
        inside = jnp.logical_and(there >= 0, there < tiles_y)
        target = jnp.where(inside, there, 0) * tiles_x + (column + dx + tiles_x) % tiles_x
        device = jnp.where(inside, holder[target], -1)
        around[4 * count + c] = device
        sides.append(device)

    def look(y, carry):
        line = [holder[y * tiles_x + x] for x in range(tiles_x)]
        below = [holder[jnp.maximum(y - 1, 0) * tiles_x + x] for x in range(tiles_x)]
        above = [holder[jnp.minimum(y + 1, tiles_y - 1) * tiles_x + x] for x in range(tiles_x)]
        for x, device in enumerate(line):
            for c, other in enumerate((line[x - 1], line[(x + 1) % tiles_x], below[x], above[x])):
                around[c * count + device] = other * slot + RIM_ROWS
        return carry

    lax.fori_loop(0, tiles_y, look, 0)
    send(around, around_out)
    clear_terms(tn, ts)

    def add(flats, low, size, fresh):
        rows = pl.ds(low, size)
        total = [None] * 3
        for t, u, v in zip(*flats):
            t = t.rows(low, size)
            new = (t, t * u.rows(low, size), t * v.rows(low, size))
            total = [b if a is None else a + b for a, b in zip(total, new)]
        for ref, value in zip((st, sx, sy), total):
            ref[rows, :] = value if fresh else ref[rows, :] + value

    for step in range(steps):
        for copy in copies[3 * step : 3 * step + 3]:
            copy.wait()
        flats = [
            [Level(ref, (step * per + n) * ROWS) for n in range(per)] for ref in (temp, zonal, merid)
        ]

        def some(m, carry):
            add(flats, pl.multiple_of(m * 8, 8), 8, step == 0)
            return carry

        lax.fori_loop(0, ROWS // 8, some, 0, unroll=4)
        if ROWS % 8:
            add(flats, ROWS - ROWS % 8, ROWS % 8, step == 0)

        for n in range(per):
            k = step * per + n
            t, u, v = (flat[n] for flat in flats)

            def term(planes, sign):
                own = choose(planes, lane, t.plane)
                flow = choose(planes, lane, u.plane)
                return DIFFUSE * own + sign * ADVECT * (flow * own)

            edges[0, 0:GROUPS] = jnp.where(q == k, turn(term(START, -1.0), k), edges[0, 0:GROUPS])
            edges[1, 0:GROUPS] = jnp.where(q == k, turn(term(LAST, 1.0), k + 17), edges[1, 0:GROUPS])
            rows = t.rows(0, 2)
            rows = DIFFUSE * rows - ADVECT * (v.rows(0, 2) * rows)
            edges[2, k : k + 1] = rows[0:1]
            edges[2, k + levels : k + levels + 1] = rows[1:2]
            rows = t.rows(ROWS - 2, 2)
            rows = DIFFUSE * rows + ADVECT * (v.rows(ROWS - 2, 2) * rows)
            edges[3, k : k + 1] = turn(jnp.where(one >= 16, rows[0:1], rows[1:2]), -16)
            edges[3, k + levels : k + levels + 1] = turn(rows[1:2], -16)

    for c in range(4):
        for j, device, low, size in runs[c]:
            slots[pl.ds(device * slot + RIM_ROWS + j, size, stride=slot), :] = edges[c, low : low + size]

    for copy in copies[3 * steps :]:
        copy.wait()

    part = fields.at[pl.ds(0, HELD)]
    mask = fields.at[pl.ds(HELD, HELD)]
    diag = fields.at[pl.ds(2 * HELD, HELD)]
    own = fields.at[pl.ds(PACKS, 56)]
    mask[0:ROWS] = depth[...] * ocean[...].astype(jnp.float32)

    def wet_of(rows):
        return ocean[rows, :].astype(jnp.float32)

    def masked(rows):
        return mask[rows, :]

    for a in range(PLANES):
        total = st[comb(a), :]
        pt[a] = total
        store_terms(a, total, ADVECT * sx[comb(a), :], ADVECT * sy[comb(a), :], te, tw, tn, ts)
    for a in range(PLANES):
        total = pt[a]
        wet = wet_of(comb(a))
        change = inner_sum(a, te, tw, tn, ts) - 4.0 * DIFFUSE * total
        part[comb(a), :] = source[comb(a), :] + (STERIC / levels) * wet * (total + wet * change)

    def mix(*values):
        value = values[-1]
        for at, low in ((6, 12), (5, 11), (4, 10), (3, 9), (2, 8), (1, 6), (0, 3)):
            value = jnp.where(q < low, values[at], value)
        return value

    def ends(planes, low):
        value = tn[planes[0], 8 : 8 + GROUPS]
        last = jnp.logical_and(lane >= low, lane < low + 16)
        return jnp.where(last, ts[planes[7], 8 : 8 + GROUPS], value)

    def beside(b, d, g, b_out, d_out):
        return g * b + d * d_out * (b - b_out)

    bp = choose(START, lane, lambda a: part[comb(a), :])
    dp = choose(START, lane, lambda a: masked(comb(a)))
    gp = choose(START, lane, lambda a: diag[comb(a), :])
    pp = beside(bp, dp, gp, turn(bp, -1), turn(dp, -1))
    pack_w = mix(
        bp, turn(dp, 3), turn(gp, 6), turn(pp, 6), turn(choose(START, lane, lambda a: te[a]), 9),
        turn(gp, 8), turn(dp, 8), turn(ends(START, OFF[7]), 12),
    )
    bp = choose(LAST, lane, lambda a: part[comb(a), :])
    dp = choose(LAST, lane, lambda a: masked(comb(a)))
    gp = choose(LAST, lane, lambda a: diag[comb(a), :])
    pp = beside(bp, dp, gp, turn(bp, 1), turn(dp, 1))
    pack_e = mix(
        turn(bp, 19), turn(dp, 22), turn(gp, 24), turn(pp, 27),
        turn(choose(LAST, lane, lambda a: tw[a]), 26),
        turn(gp, 29), turn(dp, 31), turn(ends(LAST, LANES - 16), 32),
    )
    own[0:GROUPS] = pack_w
    own[SLABS : SLABS + GROUPS] = pack_e
    north_l = tn[0, 8:9]
    north_r = tn[1, 8:9]
    south_13 = ts[PLANES - 2, 7 + GROUPS : 8 + GROUPS]
    south_14 = ts[PLANES - 1, 7 + GROUPS : 8 + GROUPS]
    south_l = turn(jnp.where(one >= 16, south_13, south_14), -16)
    south_r = turn(south_14, -16)
    own[48:49] = north_l
    own[49:50] = north_r
    own[50:51] = south_l
    own[51:52] = south_r
    deep = jnp.max(masked(slice(0, ROWS)), axis=(0, 1), keepdims=True)
    top = jnp.max(diag[0:ROWS], axis=(0, 1), keepdims=True) + 8.0 * deep * deep
    top = jnp.broadcast_to(top, (1, LANES))

    slots[pl.ds(RIM_ROWS - 1, count, stride=slot), :] = jnp.broadcast_to(top, (count, LANES))
    block_lane = lane_of((6, LANES))
    block_row = row_of((6, LANES))
    for c, first, rows_l, rows_r in ((2, True, north_l, north_r), (3, False, south_l, south_r)):
        base = 0 if first else ROWS - 6
        if first:
            spare = jnp.logical_and(block_row == 5, block_lane >= 80)
        else:
            spare = jnp.logical_and(block_row == 0, block_lane < 48)
        g = 0 if first else GROUPS - 1
        blocks = []
        block = slice(base, base + 6)
        for value, at in ((part[block, :], g), (masked(block), SLABS + g)):
            extra = jnp.broadcast_to(turn(own[at : at + 1], -16), (6, LANES))
            blocks.append(jnp.where(spare, extra, value))
        low = 0 if first else ROWS - 4
        diag_rows = diag[low : low + 4, :]
        third, fourth = (2, 3) if first else (SPAN_Y - 3, SPAN_Y - 4)
        b_l, b_r = line_of(lambda n: part[n : n + 1, :], third)
        d_l, d_r = line_of(lambda n: masked(slice(n, n + 1)), third)
        g_l, g_r = line_of(lambda n: diag[n : n + 1, :], third)
        bo_l, bo_r = line_of(lambda n: part[n : n + 1, :], fourth)
        do_l, do_r = line_of(lambda n: masked(slice(n, n + 1)), fourth)
        out_l = beside(b_l, d_l, g_l, bo_l, do_l)
        out_r = beside(b_r, d_r, g_r, bo_r, do_r)
        for at, value in ((112, turn(g_l, 112)), (113, turn(do_l, 113)), (114, turn(g_r, 3)), (115, turn(do_r, 4))):
            out_r = jnp.where(one == at, value, out_r)
        last_row = jnp.where(one == LANES - 1, top, rows_r)

        @pl.when(sides[c] >= 0)
        def _(c=c, blocks=blocks, diag_rows=diag_rows, singles=(out_l, out_r, rows_l, last_row)):
            at = sides[c] * slot
            slots[pl.ds(at, 6), :] = blocks[0]
            slots[pl.ds(at + 6, 6), :] = blocks[1]
            slots[pl.ds(at + 12, 4), :] = diag_rows
            for n, value in enumerate(singles):
                slots[pl.ds(at + 16 + n, 1), :] = value

    corner = jnp.logical_and(row_of((GROUPS, LANES)) == RIM_ROWS - 1, lane == LANES - 1)
    for c, pack in ((0, pack_w), (1, pack_e)):
        slots[pl.ds(sides[c] * slot, GROUPS), :] = jnp.where(corner, top, pack)
    for c, at in ((4, 0), (5, SLABS), (6, GROUPS - 1), (7, SLABS + GROUPS - 1)):
        @pl.when(sides[c] >= 0)
        def _(c=c, at=at):
            slots[pl.ds(sides[c] * slot, 1), :] = own[at : at + 1]
    send(slots, slots_out.reshape(count * slot, LANES))
    for copy in results:
        copy.wait()


SMEM = pl.BlockSpec(memory_space=pltpu.SMEM)


def solve_kernel(
    levels, tiles_y,
    around_in, rims, fields,
    vectors, hands,
    around, sem, north_in, south_in, fb, fd, fg, pw, pe, ow, oe, ed, eg, ex, we, wn, rows,
):
    copies = fetching([(around_in, around)], sem)
    count = rims.shape[0]
    number_pieces, _, share, first = pieces_of(levels, count)
    slot = RIM_ROWS + number_pieces
    came = rims.reshape(count * slot, LANES)
    hand = hands.reshape(count * share, LANES)
    own = fields.at[pl.ds(PACKS, 56)]
    lane = lane_of((SLABS, LANES))
    slab = row_of((SLABS, LANES))
    one = lane_of((1, LANES))

    none = jnp.zeros((WIDE - ROWS + 4, LANES), jnp.float32)
    for ref in (fb, fd, fg):
        ref[ROWS - 4 : WIDE] = none
    for n, ref in enumerate((fb, fd, fg)):
        ref[0:ROWS] = fields[n * HELD : n * HELD + ROWS]
    copies[0].wait()
    src = [around[4 * count + c] for c in range(8)]

    def fetch(c, low, high):
        value = came[pl.ds(jnp.maximum(src[c], 0) * slot + low, high - low), :]
        return jnp.where(src[c] >= 0, value, 0.0)

    me = lax.axis_index("gx") * tiles_y + lax.axis_index("gy")
    for n in range(number_pieces):
        side = jnp.minimum((n * count + me) // (2 * levels), 3)
        base = (side + 1 - 2 * (side % 2)) * count

        def relay(d, carry, n=n, base=base):
            row = around[base + d] + n
            hand[pl.ds(d * share + first + n, 1), :] = came[pl.ds(row, 1), :]
            return carry

        for d in range(count):
            relay(d, 0)

    north_in[0:RIM_ROWS] = fetch(3, 0, RIM_ROWS)
    south_in[0:RIM_ROWS] = fetch(2, 0, RIM_ROWS)
    strips = {2: south_in, 3: north_in}
    for ref, low, high, n_lane, s_lane in ((fb, 0, 6, 80, 48), (fd, 6, 12, 80, 48), (fg, 12, 16, 96, 32)):
        size = high - low
        row, column = row_of((size, LANES)), lane_of((size, LANES))
        beyond = jnp.logical_and(row == size - 1, column >= n_lane)
        ref[ROWS : ROWS + size] = jnp.where(beyond, 0.0, strips[3][low:high])
        beyond = jnp.logical_and(row == 0, column < s_lane)
        ref[WIDE - size : WIDE] = jnp.where(beyond, 0.0, strips[2][low:high])
    empty = jnp.zeros((SLABS, LANES), jnp.float32)
    for ref, side, north, south in ((pw, 0, 6, 4), (pe, 1, 7, 5)):
        ref[...] = empty
        ref[0:GROUPS] = fetch(side, 0, GROUPS)
        ref[GROUPS : GROUPS + 1] = fetch(north, 0, 1)
        ref[SLABS - 1 : SLABS] = fetch(south, 0, 1)
    for ref, at, north, south in ((ow, 0, 5, 0), (oe, SLABS, 11, 6)):
        ref[...] = empty
        ref[0:GROUPS] = own[at : at + GROUPS]
        ref[GROUPS : GROUPS + 1] = turn(strips[3][north:north + 1], 16)
        ref[SLABS - 1 : SLABS] = turn(strips[2][south:south + 1], 16)

    def spread(ref, j):
        a = START[j]
        first, second = ref[comb(a, SLABS), :], ref[comb(a + 1, SLABS), :]
        third = ref[comb(a + 2, SLABS), :] if a + 2 < PLANES else second
        left = turn(jnp.where(lane >= OFF[j], first, second), -OFF[j])
        right = turn(jnp.where(lane >= OFF[j], second, third), -OFF[j])
        return left, right

    def seam_row(left, right, slab_at, lanes_at):
        east = turn(pe[slab_at : slab_at + 1], 112 - lanes_at)
        west = turn(pw[slab_at : slab_at + 1], 124 - lanes_at)
        right = jnp.where(one < 112, right, jnp.where(one < 116, east, jnp.where(one >= 124, west, 0.0)))
        return jnp.broadcast_to(left, (SLABS, LANES)), jnp.broadcast_to(right, (SLABS, LANES))

    seams = {
        0: ((0, seam_row(strips[2][18:19], strips[2][19:20], SLABS - 1, 28)),
            (GROUPS, seam_row(own[50:51], own[51:52], GROUPS - 1, 28))),
        GROUP - 1: ((GROUPS - 1, seam_row(strips[3][18:19], strips[3][19:20], GROUPS, 12)),
                    (SLABS - 1, seam_row(own[48:49], own[49:50], 0, 12))),
    }
    weight = STERIC / levels

    def missing(target, term, term_out, d, d_out, g):
        term, term_out, d, d_out, g = (
            turn(value[0], target - value[1]) for value in (term, term_out, d, d_out, g)
        )
        term = jnp.where(d > 0, weight * term, 0.0)
        term_out = jnp.where(d_out > 0, weight * term_out, 0.0)
        return jnp.where(one == target, g * term + d * d_out * (term - term_out), 0.0)

    def ring(ref, at):
        return ref[at : at + 1]

    outer = {j: [] for j in range(GROUP)}
    for j, at, beyond, o, lanes in ((0, 0, SLABS - 1, 0, 28), (GROUP - 1, GROUPS - 1, GROUPS, 16, 12)):
        own_row, corner = ring(pe, at), ring(pe, beyond)
        outer[j].append((1, at, missing(
            114, (corner, lanes + 2), (corner, lanes + 3), (own_row, o + 5), (own_row, o + 11), (own_row, o + 10),
        )))
        own_row, corner = ring(pw, at), ring(pw, beyond)
        outer[j].append((1, at, missing(
            125, (corner, lanes + 1), (corner, lanes), (own_row, o + 3), (own_row, o + 11), (own_row, o + 10),
        )))
    for j, at, c, j_out, d_l, d_r in ((2, GROUPS, 3, 3, (9, 96), (11, 79)), (5, SLABS - 1, 2, 4, (6, 48), (8, 31))):
        line_l, line_r = strips[c][16:17], strips[c][17:18]
        corner = ring(pw, at)
        outer[j].append((0, at, line_l + missing(
            0, (corner, OFF[j] + 9), (corner, OFF[j_out] + 9), (strips[c][d_l[0]:d_l[0] + 1], d_l[1]),
            (line_r, 113), (line_r, 112),
        )))
        corner = ring(pe, at)
        outer[j].append((1, at, jnp.where(one < 112, line_r, 0.0) + missing(
            111, (corner, OFF[j] + 9), (corner, OFF[j_out] + 9), (strips[c][d_r[0]:d_r[0] + 1], d_r[1]),
            (line_r, 115), (line_r, 114),
        )))
    for j in range(GROUP):
        o = OFF[j]
        inside = slab < GROUPS
        halves = [
            jnp.zeros((SLABS, LANES), jnp.float32),
            jnp.where(
                jnp.logical_and(inside, lane == 114), turn(pe[...], 114 - o - 8),
                jnp.where(jnp.logical_and(inside, lane == 125), turn(pw[...], 125 - o - 8), 0.0),
            ),
        ]
        for half, at, line in outer[j]:
            halves[half] = halves[half] + jnp.where(slab == at, line, 0.0)
        ex[j, :, 0:LANES] = halves[0]
        ex[j, :, LANES:] = halves[1]

        def rim(right, q, width):
            east = turn(pe[...], 112 - o - q)
            west = turn(pw[...], 128 - width - o - q)
            value = jnp.where(lane < 112 + width, east, jnp.where(lane >= 128 - width, west, 0.0))
            return jnp.where(lane < 112, right, value)

        left, right = spread(fd, j)
        right = rim(right, 3, 3)
        wet_l = jnp.where(left > 0, weight, 0.0)
        wet_r = jnp.where(right > 0, weight, 0.0)
        ed[j, :, 0:LANES] = left
        ed[j, :, LANES:] = right
        left, right = spread(fg, j)
        eg[j, :, 0:LANES] = left
        eg[j, :, LANES:] = rim(right, 6, 2)
        left, right = spread(fb, j)
        right = rim(right, 0, 3)
        seam_l = jnp.where(lane == 0, turn(pw[...], -o - 9), 0.0)
        seam_r = jnp.where(lane == 127, turn(ow[...], 127 - o - 9), 0.0)
        seam_r = jnp.where(lane == 111, turn(pe[...], 111 - o - 9), seam_r)
        seam_r = jnp.where(lane == 112, turn(oe[...], 112 - o - 9), seam_r)
        for at, (row_l, row_r) in seams.get(j, ()):
            seam_l = seam_l + jnp.where(slab == at, row_l, 0.0)
            seam_r = seam_r + jnp.where(slab == at, row_r, 0.0)
        vectors[0, j, :, 0:LANES] = left + wet_l * seam_l
        vectors[0, j, :, LANES:] = right + wet_r * seam_r

    for j in range(GROUP):
        d = ed[j]
        we[j] = d * turn(d, -1)
        above = ed[j + 1] if j < GROUP - 1 else turn(ed[0], -1, 0)
        wn[j] = d * above

    top = jnp.max(came[pl.ds(RIM_ROWS - 1, count, stride=slot), :], axis=0, keepdims=True)
    top = jnp.max(jnp.where(one == LANES - 1, top, 0.0), axis=1, keepdims=True)
    scale = STRETCH / top

    big = (SLABS, 2 * LANES)
    mine = jnp.logical_and(row_of(big) < GROUPS, lane_of(big) < SPAN_X)
    pair = 0
    for k in range(5):
        count_sums = min(k + 1, 4)
        sums = [None] * count_sums
        new = None if k == 4 else vectors.at[k]
        if k:
            v = vectors.at[k - 1]
            flow_below = wn[GROUP - 1] * (v[GROUP - 1] - turn(v[0], -1, 0))
            flow_below = turn(flow_below, 1, 0)
        for j in range(GROUP):
            if k:
                here = v[j]
                above = v[j + 1] if j < GROUP - 1 else turn(v[0], -1, 0)
                flow_x = we[j] * (here - turn(here, -1))
                flow_y = wn[j] * (here - above)
                image = eg[j] * here + (flow_x - turn(flow_x, 1)) + (flow_y - flow_below)
                if k == 1:
                    image = image + ex[j]
                fresh = scale * image - (STRETCH * ROOTS[k - 1]) * here
                flow_below = flow_y
                if k < 4:
                    new[j] = fresh
            else:
                fresh = new[j]
            held = jnp.where(mine, fresh, 0.0)
            for i in range(count_sums):
                other = vectors[i, j] if i < k else held
                value = held * other
                sums[i] = value if sums[i] is None else sums[i] + value
        for i in range(count_sums):
            rows[pair : pair + 1] = jnp.sum(sums[i][:, 0:LANES] + sums[i][:, LANES:], axis=0, keepdims=True)
            pair += 1
    rows[pair : pair + 1] = jnp.where(one == 0, top, 0.0)
    rows[pair + 1 : 16] = jnp.zeros((15 - pair, LANES), jnp.float32)
    total = jnp.sum(rows[...], axis=1, keepdims=True)
    spot = lane_of((16, LANES)) == gram_lane(row_of((16, LANES)))
    line = jnp.sum(jnp.where(spot, total, 0.0), axis=0, keepdims=True)
    line = jnp.broadcast_to(line, (count, LANES))
    if first == 0:
        line = jnp.where(lane_of((count, LANES)) % 16 < 12, hand[pl.ds(0, count, stride=share), :], line)
    hand[pl.ds(0, count, stride=share), :] = line


def finish_kernel(
    levels, per, hands, vectors, edges, inner, tracer_out, surface_out,
    cells, flat, left, right, message, out_sems,
):
    count = hands.shape[0]
    _, runs, share, first = pieces_of(levels, count)
    came = hands.reshape(count * share, LANES)
    steps = levels // per
    chunks = [pl.ds(step * per * ROWS, per * ROWS) for step in range(steps)]
    row = jnp.sum(came[pl.ds(0, count, stride=share), :], axis=0, keepdims=True)
    one = lane_of((1, LANES))
    entry = {}
    pair = 0
    for k in range(5):
        for i in range(min(k + 1, 4)):
            value = jnp.sum(jnp.where(one == gram_lane(pair), row, 0.0), axis=1, keepdims=True)
            entry[i, k] = entry[k, i] = value
            pair += 1
    top = jnp.sum(jnp.where(one == gram_lane(pair), row, 0.0), axis=1, keepdims=True) * (1.0 / count)

    def image(c):
        out = [None] * 5
        for k in range(4):
            if c[k] is None:
                continue
            low = ROOTS[k] * c[k]
            out[k] = low if out[k] is None else out[k] + low
            out[k + 1] = (1.0 / STRETCH) * c[k]
        return out

    def dot(a, b):
        total = None
        for i in range(5):
            if a[i] is None:
                continue
            inner = None
            for j in range(5):
                if b[j] is not None:
                    value = entry[i, j] * b[j]
                    inner = value if inner is None else inner + value
            total = a[i] * inner if total is None else total + a[i] * inner
        return total

    def axpy(a, s, b):
        return [
            x if y is None else (s * y if x is None else x + s * y) for x, y in zip(a, b)
        ]

    r = [jnp.ones((1, 1), jnp.float32)] + [None] * 4
    p = list(r)
    x = [None] * 5
    rr = entry[0, 0]
    for n in range(ITERS):
        q = image(p)
        step = rr / jnp.maximum(dot(p, q), TINY)
        step = jnp.clip(step, top * (1.0 / HIGH_RATE), top * (1.0 / LOW_RATE))
        x = axpy(x, step, p)
        if n < ITERS - 1:
            r = axpy(r, -step, q)
            fresh = jnp.maximum(dot(r, r), 0.0)
            p = axpy(r, fresh / jnp.maximum(rr, TINY), p)
            rr = fresh
    factors = [c / top for c in x[:4]]
    for j in range(GROUP):
        value = None
        for k in range(4):
            term = factors[k] * vectors[k, j]
            value = term if value is None else value + term
        left[j] = turn(value[:, 0:LANES], OFF[j])
        right[j] = turn(value[:, LANES:], OFF[j])
    lane = lane_of((SLABS, LANES))
    for a in range(PLANES):
        value = None
        for j in range(GROUP):
            for half, ref in ((0, left), (1, right)):
                low = max(SPAN_X * j + LANES * half - LANES * a, 0)
                high = min(SPAN_X * j + (LANES if half == 0 else SPAN_X) - LANES * a, LANES)
                if low >= high:
                    continue
                value = ref[j] if value is None else jnp.where(lane >= low, ref[j], value)
        flat[comb(a), :] = value[0:GROUPS]
    results = [pltpu.make_async_copy(flat, surface_out.reshape(ROWS, LANES), out_sems.at[0])]
    results[0].start()

    for c in range(4):
        for j, device, low, size in runs[c ^ 1]:
            value = came[pl.ds(device * share + first + j, size, stride=share), :]
            message[c, low : low + size] = value
    second = lane_of((SLABS, LANES)) % 16 == 1
    sums = []
    for k in range(levels):
        value = edges[2 * levels - 1] * jnp.concatenate([
            jnp.where(second, turn(message[1], 1 - k), turn(message[0], -k)),
            message[2, k : k + 1], message[2, k + levels : k + levels + 1],
            message[3, k : k + 1], message[3, k + levels : k + levels + 1],
            jnp.zeros((EDGE - SLABS - 4, LANES), jnp.float32),
        ], axis=0)
        if k:
            value = value + edges[2 * levels + k - 1] * sums[-1]
        sums.append(value * edges[levels - 1 + k])
    for k in range(levels - 2, -1, -1):
        sums[k] = sums[k] + edges[k] * sums[k + 1]
    lane = lane_of((GROUPS, LANES))
    slab = row_of((GROUPS, LANES))
    for k in range(levels):
        west = sums[k][0:GROUPS]
        east = turn(west, -18)
        south_l, south_r = sums[k][SLABS : SLABS + 1], sums[k][SLABS + 1 : SLABS + 2]
        north_l = turn(sums[k][SLABS + 2 : SLABS + 3], 16)
        north_r = turn(sums[k][SLABS + 3 : SLABS + 4], 16)
        for a in range(PLANES):
            rim = None
            for at, source in [(at, west) for at in FIRST_OF[a]] + [(at, east) for at in LAST_OF[a]]:
                rim = jnp.where(lane == at, source, 0.0 if rim is None else rim)
            rows = comb(k * ROWS + a)
            if rim is None:
                cells[rows, :] = inner[rows, :]
                continue
            if a == 0:
                rim = rim + jnp.where(slab == 0, south_l, 0.0)
            if a == 1:
                rim = rim + jnp.where(jnp.logical_and(slab == 0, lane < 112), south_r, 0.0)
            if a == PLANES - 2:
                rim = rim + jnp.where(jnp.logical_and(slab == GROUPS - 1, lane >= 16), north_l, 0.0)
            if a == PLANES - 1:
                rim = rim + jnp.where(slab == GROUPS - 1, jnp.where(lane < 16, north_l, north_r), 0.0)
            cells[rows, :] = inner[rows, :] + rim
        if k % per == per - 1:
            step = k // per
            copy = pltpu.make_async_copy(
                cells.at[chunks[step]], tracer_out.at[chunks[step]], out_sems.at[1 + step]
            )
            copy.start()
            results.append(copy)
    for copy in results:
        copy.wait()


def tracer_kernel(
    levels, per, sides, around, temp_in, zonal_in, merid_in, rates_in, fields,
    out, edges,
    temp, zonal, merid, rates, ocean,
    te, tw, tn, ts, stepped, border, sems,
):
    steps = levels // per
    pairs = []
    for step in range(steps):
        chunk = pl.ds(step * per * ROWS, per * ROWS)
        pairs += [
            (a.at[chunk], b.at[chunk]) for a, b in ((temp_in, temp), (zonal_in, zonal), (merid_in, merid))
        ]
    copies = fetching(pairs + [(rates_in.reshape((levels - 1) * ROWS, LANES), rates)], sems)
    lane = lane_of((GROUPS, LANES))
    one = lane_of((1, LANES))
    clear_terms(tn, ts)

    ocean[...] = jnp.where(fields[HELD : HELD + ROWS] > 0, 1.0, 0.0)
    for step in range(steps):
        for copy in copies[3 * step : 3 * step + 3]:
            copy.wait()

        def level(k, carry):
            t, u, v = (Level(ref, k * ROWS) for ref in (temp, zonal, merid))
            for a in range(PLANES):
                own = t.plane(a)
                quarter = ADVECT * own
                store_terms(a, own, u.plane(a) * quarter, v.plane(a) * quarter, te, tw, tn, ts)
            for a in range(PLANES):
                own = t.plane(a)
                change = inner_sum(a, te, tw, tn, ts) - 4.0 * DIFFUSE * own
                stepped[k, a] = own + ocean[comb(a), :] * change
            return carry

        lax.fori_loop(step * per, step * per + per, level, 0)
    copies[-1].wait()

    def block(a, carry):
        for low in range(0, GROUPS, 8):
            size = min(8, GROUPS - low)

            def rows(k):
                return pl.ds(k * ROWS + low * PLANES + a, size, stride=PLANES)

            gains = []
            sums = []
            for k in range(levels):
                value = stepped[k, a, low : low + size]
                pivot = 1.0
                if k > 0:
                    pivot = pivot + upper - upper * gains[-1]
                    value = value + upper * sums[-1]
                if k < levels - 1:
                    lower = rates[rows(k), :]
                    inverse = 1.0 / (pivot + lower)
                    gains.append(lower * inverse)
                    upper = lower
                else:
                    inverse = 1.0 / pivot
                sums.append(value * inverse)
            result = sums[-1]
            out[rows(levels - 1), :] = result
            for k in range(levels - 2, -1, -1):
                result = sums[k] + gains[k] * result
                out[rows(k), :] = result
        return carry

    lax.fori_loop(0, PLANES, block, 0)

    def edge(ref, base, at):
        def get(a):
            return ref[comb(base + a), :].astype(jnp.float32)

        border[0:GROUPS] = jnp.where(
            lane % 16 == 1, turn(choose(LAST, lane, get), 18), choose(START, lane, get)
        )
        border[SLABS : SLABS + 2] = ref[base : base + 2, :].astype(jnp.float32)
        rows = ref[base + ROWS - 2 : base + ROWS, :].astype(jnp.float32)
        border[SLABS + 2 : SLABS + 3] = turn(jnp.where(one >= 16, rows[0:1], rows[1:2]), -16)
        border[SLABS + 3 : SLABS + 4] = turn(rows[1:2], -16)
        edges[at] = border[...]

    border[...] = jnp.zeros_like(border)
    edge(ocean, 0, 2 * levels - 1)
    for c in (2, 3):
        rows = pl.ds(SLABS + 2 * (c - 2), 2)
        value = edges[2 * levels - 1, rows]
        edges[2 * levels - 1, rows] = jnp.where(around[sides + c] >= 0, value, 0.0)
    gain = None
    for k in range(levels):
        pivot = 1.0
        if k > 0:
            upper = edges[2 * levels + k - 1]
            pivot = pivot + upper - upper * gain
        if k < levels - 1:
            edge(rates, k * ROWS, 2 * levels + k)
            lower = edges[2 * levels + k]
            inverse = 1.0 / (pivot + lower)
            gain = lower * inverse
            edges[k] = gain
        else:
            inverse = 1.0 / pivot
        edges[levels - 1 + k] = inverse


def on_device(
    thermal_anomaly,
    zonal_flow_ratio,
    meridional_flow_ratio,
    diffusion_rates,
    ocean_bottom_scaled,
    ocean_indicator,
    operator_diagonal,
    elevation_source,
    block_positions,
):
    levels, cells = thermal_anomaly.shape[1:]
    nx = lax.axis_size("gx")
    ny = lax.axis_size("gy")
    count = block_positions.shape[0]
    planes = (ocean_bottom_scaled, ocean_indicator, operator_diagonal, elevation_source)
    depth, ocean, diag, source = planes
    f32 = jnp.float32
    per = next(n for n in (4, 2, 6, levels) if levels % n == 0 and n * ROWS % 8 == 0)
    steps = levels // per
    few = next(n for n in (4, 2, 6, levels) if levels % n == 0 and n * ROWS % 8 == 0)
    params = pltpu.CompilerParams(vmem_limit_bytes=BUDGET)
    temp, zonal, merid = (
        array.reshape(levels * ROWS, LANES)
        for array in (thermal_anomaly, zonal_flow_ratio, meridional_flow_ratio)
    )
    rates = diffusion_rates.reshape(levels - 1, 1, cells)
    temp, zonal, merid, rates, depth, ocean, diag, source, positions = (
        pltpu.with_memory_space_constraint(array, pltpu.HBM)
        for array in (temp, zonal, merid, rates, depth, ocean, diag, source, block_positions)
    )
    hbm = pl.BlockSpec(memory_space=pltpu.HBM)
    here = pl.BlockSpec(memory_space=pltpu.VMEM)

    def vmem(*shape, kind=f32):
        return pltpu.VMEM(shape, kind)

    def out(*shape, kind=f32):
        return jax.ShapeDtypeStruct(shape, kind)

    def sems(number):
        return pltpu.SemaphoreType.DMA((number,))

    deep = vmem(levels * ROWS, LANES)
    flat = vmem(ROWS, LANES)
    flat_int = vmem(ROWS, LANES, kind=jnp.int32)
    plane = vmem(PLANES, GROUPS, LANES)
    tall = vmem(PLANES, 40, LANES)
    numbers = pltpu.SMEM((count,), jnp.int32)
    number_pieces, _, share, _ = pieces_of(levels, count)
    slot = RIM_ROWS + number_pieces
    fields, slots, around = pl.pallas_call(
        functools.partial(forcing_kernel, levels, few, nx, ny),
        in_specs=[hbm] * 8,
        out_specs=[here, hbm, hbm],
        out_shape=[
            out(FIELDS, LANES), pltpu.HBM((count, 1, slot * LANES), f32), out(4 * count + 8, kind=jnp.int32),
        ],
        scratch_shapes=[deep] * 3 + [flat, flat_int, flat]
        + [vmem(count * slot, LANES)]
        + [flat] * 3 + [plane] * 3 + [tall] * 2
        + [vmem(4, 2 * levels, LANES), numbers, numbers]
        + [pltpu.SMEM((4 * count + 8,), jnp.int32), sems(3 * (levels // few) + 5), sems(2)],
        compiler_params=params,
        name="forcing",
    )(positions, temp, zonal, merid, depth, ocean, diag, source)
    rims = lax.all_to_all(slots, BOTH, 0, 0, tiled=True)

    inner, edges = pl.pallas_call(
        functools.partial(tracer_kernel, levels, per, 4 * count),
        in_specs=[SMEM] + [hbm] * 4 + [here],
        out_specs=[here] * 2,
        out_shape=[out(levels * ROWS, LANES), out(3 * levels - 1, EDGE, LANES)],
        scratch_shapes=[deep] * 3 + [vmem((levels - 1) * ROWS, LANES), flat]
        + [plane] * 2 + [tall] * 2
        + [vmem(levels, PLANES, GROUPS, LANES), vmem(EDGE, LANES), sems(3 * steps + 1)],
        compiler_params=params,
        name="tracer",
    )(around, temp, zonal, merid, rates, fields)

    rims, edges = lax.optimization_barrier((rims, edges))
    extended = vmem(GROUP, SLABS, 2 * LANES)
    vectors, hand = pl.pallas_call(
        functools.partial(solve_kernel, levels, ny),
        in_specs=[pl.BlockSpec(memory_space=pl.ANY)] + [here] * 2,
        out_specs=[here] * 2,
        out_shape=[out(4, GROUP, SLABS, 2 * LANES), out(count, 1, share * LANES)],
        scratch_shapes=[pltpu.SMEM((4 * count + 8,), jnp.int32), sems(1)]
        + [vmem(SLABS, LANES)] * 2 + [vmem(WIDE, LANES)] * 3 + [vmem(SLABS, LANES)] * 4 + [extended] * 5 + [vmem(16, LANES)],
        compiler_params=params,
        name="vectors",
    )(around, rims, fields)
    hands = lax.all_to_all(hand, BOTH, 0, 0, tiled=True)

    new_temp, surface = pl.pallas_call(
        functools.partial(finish_kernel, levels, per),
        in_specs=[here] * 4,
        out_specs=[hbm] * 2,
        out_shape=[out(levels * ROWS, LANES), out(1, cells)],
        scratch_shapes=[
            deep, flat, vmem(GROUP, SLABS, LANES), vmem(GROUP, SLABS, LANES), vmem(4, 2 * levels, LANES),
            sems(1 + steps),
        ],
        compiler_params=params,
        name="finish",
    )(hands, vectors, edges, inner)
    return new_temp.reshape(1, levels, cells), surface


def solution(mesh):
    deep = P(BOTH, None, None)
    flat = P(BOTH, None)
    return jax.shard_map(
        on_device,
        mesh=mesh,
        in_specs=(deep, deep, deep, deep, flat, flat, flat, flat, P()),
        out_specs=(deep, flat),
        check_vma=False,
    )
```

```python
import functools

import jax
import jax.numpy as jnp
from jax import lax
from jax.experimental import pallas as pl
from jax.experimental.pallas import tpu as pltpu
from jax.sharding import PartitionSpec as P

ITERS = 4
SPAN_X = 240
SPAN_Y = 160
RIM = 4
ADVECT = 0.25
DIFFUSE = 0.12
STERIC = 0.5
LOW_RATE = 0.05
HIGH_RATE = 32.5
ROOTS = (0.02, 0.35, 0.1, 0.2)
STRETCH = 4.0
TINY = 1e-30
BOTH = ("gx", "gy")
SIDES = ((-1, 0), (1, 0), (0, -1), (0, 1), (-1, -1), (1, -1), (-1, 1), (1, 1))

LANES = 128
GROUP = 8
GROUPS = SPAN_Y // GROUP
PLANES = GROUP * SPAN_X // LANES
ROWS = GROUPS * PLANES
SLABS = GROUPS + 4
WIDE = SLABS * PLANES
START = [SPAN_X * j // LANES for j in range(GROUP)]
OFF = [SPAN_X * j % LANES for j in range(GROUP)]
LAST = [(SPAN_X * j + SPAN_X - 1) // LANES for j in range(GROUP)]
END = [(SPAN_X * j + SPAN_X - 1) % LANES for j in range(GROUP)]
FIRST_OF = [[OFF[j] for j in range(GROUP) if START[j] == a] for a in range(PLANES)]
LAST_OF = [[END[j] for j in range(GROUP) if LAST[j] == a] for a in range(PLANES)]
RIM_ROWS = 20
HELD = -(-ROWS // 8) * 8
PACKS = 3 * HELD
FIELDS = PACKS + 56
EDGE = 32
BUDGET = 32 * 1024 * 1024


def turn(value, shift, axis=1):
    shift = shift % value.shape[axis]
    return value if shift == 0 else pltpu.roll(value, shift, axis)


def fetching(pairs, sems):
    copies = [pltpu.make_async_copy(a, b, sems.at[n]) for n, (a, b) in enumerate(pairs)]
    for copy in copies:
        copy.start()
    return copies


def pieces_of(levels, count):
    rows = 2 * levels
    number = -(-4 * rows // count)
    runs = [[] for _ in range(4)]
    for c in range(4):
        for j in range(number):
            low, high = max(c * rows, j * count), min((c + 1) * rows, (j + 1) * count)
            if low < high:
                runs[c].append((j, low - j * count, low - c * rows, high - low))
    merged = count <= 2 * rows and levels <= 12
    return number, runs, number + (0 if merged else 1), 0 if merged else 1


def gram_lane(n):
    return 16 * (n // 4) + 12 + n % 4


class Level:
    def __init__(self, ref, base):
        self.ref, self.base = ref, base

    def plane(self, a):
        return self.ref[comb(self.base + a), :]

    def rows(self, low, size):
        return self.ref[pl.ds(self.base + low, size), :]


def lane_of(shape):
    return lax.broadcasted_iota(jnp.int32, shape, len(shape) - 1)


def row_of(shape):
    return lax.broadcasted_iota(jnp.int32, shape, 0)


def comb(a, count=GROUPS):
    return pl.ds(a, count, stride=PLANES)


def line_of(get, y):
    lane = lane_of((1, LANES))
    j = y % GROUP
    row = y // GROUP * PLANES + START[j]
    first, second = get(row), get(row + 1)
    third = get(row + 2) if START[j] + 2 < PLANES else second
    left = turn(jnp.where(lane >= OFF[j], first, second), -OFF[j])
    right = turn(jnp.where(lane >= OFF[j], second, third), -OFF[j])
    return left, right


def drop(value, lanes, lane):
    for at in lanes:
        value = jnp.where(lane == at, 0.0, value)
    return value


def store_terms(a, temp, flow_x, flow_y, te, tw, tn, ts):
    spread = DIFFUSE * temp
    te[a] = spread - flow_x
    tw[a] = spread + flow_x
    tn[a, 8 : 8 + GROUPS] = spread - flow_y
    ts[a, 8 : 8 + GROUPS] = spread + flow_y


def clear_terms(tn, ts):
    none = jnp.zeros((PLANES, 1, LANES), jnp.float32)
    for ref in (tn, ts):
        ref[:, 7:8] = none
        ref[:, 8 + GROUPS : 9 + GROUPS] = none


def inner_sum(a, te, tw, tn, ts):
    lane = lane_of((GROUPS, LANES))
    here = te[a]
    east = here if a == PLANES - 1 else jnp.where(lane == 0, te[a + 1], here)
    east = drop(turn(east, -1), LAST_OF[a], lane)
    here = tw[a]
    west = here if a == 0 else jnp.where(lane == LANES - 1, tw[a - 1], here)
    west = drop(turn(west, 1), FIRST_OF[a], lane)

    def plane(ref, at):
        down = 8 + (at >= PLANES) - (at < 0)
        return ref[at % PLANES, down : down + GROUPS]

    north = turn(jnp.where(lane >= LANES - 16, plane(tn, a + 1), plane(tn, a + 2)), 16)
    south = turn(jnp.where(lane < 16, plane(ts, a - 1), plane(ts, a - 2)), -16)
    return east + west + north + south


def choose(planes, lane, get):
    shift = 32 if planes is LAST else 0
    lows = sorted(((OFF[j] - shift) % LANES, planes[j]) for j in range(GROUP))
    value = get(lows[-1][1])
    for low, a in reversed(lows[:-1]):
        value = jnp.where(lane < low + 16, get(a), value)
    return value


def forcing_kernel(
    levels, per, tiles_x, tiles_y,
    pos_in, temp_in, zonal_in, merid_in, depth_in, ocean_in, diag_in, source_in,
    fields, slots_out, around_out,
    temp, zonal, merid, depth, ocean, source, slots,
    st, sx, sy, pt, te, tw, tn, ts, edges, pos, holder, around, sems, out_sems,
):
    count = pos.shape[0]
    steps = levels // per
    number_pieces, runs, _, _ = pieces_of(levels, count)
    slot = RIM_ROWS + number_pieces
    pairs = []
    for step in range(steps):
        chunk = pl.ds(step * per * ROWS, per * ROWS)
        pairs += [
            (a.at[chunk], b.at[chunk]) for a, b in ((temp_in, temp), (zonal_in, zonal), (merid_in, merid))
        ]
    pairs += [
        (a.reshape(ROWS, LANES), b)
        for a, b in (
            (source_in, source), (ocean_in, ocean), (depth_in, depth),
            (diag_in, fields.at[pl.ds(2 * HELD, ROWS)]),
        )
    ]
    copies = fetching([(pos_in, pos)] + pairs, sems)
    copies.pop(0).wait()
    results = []

    def send(value, target):
        copy = pltpu.make_async_copy(value, target, out_sems.at[len(results)])
        copy.start()
        results.append(copy)

    lane = lane_of((GROUPS, LANES))
    one = lane_of((1, LANES))
    q = lane % 16
    edges[...] = jnp.zeros_like(edges)

    def number(d, carry):
        holder[pos[d]] = d
        return carry

    lax.fori_loop(0, count, number, 0)
    me = lax.axis_index("gx") * tiles_y + lax.axis_index("gy")
    here = pos[me]
    row = here // tiles_x
    column = here % tiles_x
    sides = []
    for c, (dx, dy) in enumerate(SIDES):
        there = row + dy
        inside = jnp.logical_and(there >= 0, there < tiles_y)
        target = jnp.where(inside, there, 0) * tiles_x + (column + dx + tiles_x) % tiles_x
        device = jnp.where(inside, holder[target], -1)
        around[4 * count + c] = device
        sides.append(device)

    def look(y, carry):
        line = [holder[y * tiles_x + x] for x in range(tiles_x)]
        below = [holder[jnp.maximum(y - 1, 0) * tiles_x + x] for x in range(tiles_x)]
        above = [holder[jnp.minimum(y + 1, tiles_y - 1) * tiles_x + x] for x in range(tiles_x)]
        for x, device in enumerate(line):
            for c, other in enumerate((line[x - 1], line[(x + 1) % tiles_x], below[x], above[x])):
                around[c * count + device] = other * slot + RIM_ROWS
        return carry

    lax.fori_loop(0, tiles_y, look, 0)
    send(around, around_out)
    clear_terms(tn, ts)

    def add(flats, low, size, fresh):
        rows = pl.ds(low, size)
        total = [None] * 3
        for t, u, v in zip(*flats):
            t = t.rows(low, size)
            new = (t, t * u.rows(low, size), t * v.rows(low, size))
            total = [b if a is None else a + b for a, b in zip(total, new)]
        for ref, value in zip((st, sx, sy), total):
            ref[rows, :] = value if fresh else ref[rows, :] + value

    for step in range(steps):
        for copy in copies[3 * step : 3 * step + 3]:
            copy.wait()
        flats = [
            [Level(ref, (step * per + n) * ROWS) for n in range(per)] for ref in (temp, zonal, merid)
        ]

        def some(m, carry):
            add(flats, pl.multiple_of(m * 8, 8), 8, step == 0)
            return carry

        lax.fori_loop(0, ROWS // 8, some, 0, unroll=4)
        if ROWS % 8:
            add(flats, ROWS - ROWS % 8, ROWS % 8, step == 0)

        for n in range(per):
            k = step * per + n
            t, u, v = (flat[n] for flat in flats)

            def term(planes, sign):
                own = choose(planes, lane, t.plane)
                flow = choose(planes, lane, u.plane)
                return DIFFUSE * own + sign * ADVECT * (flow * own)

            edges[0, 0:GROUPS] = jnp.where(q == k, turn(term(START, -1.0), k), edges[0, 0:GROUPS])
            edges[1, 0:GROUPS] = jnp.where(q == k, turn(term(LAST, 1.0), k + 17), edges[1, 0:GROUPS])
            rows = t.rows(0, 2)
            rows = DIFFUSE * rows - ADVECT * (v.rows(0, 2) * rows)
            edges[2, k : k + 1] = rows[0:1]
            edges[2, k + levels : k + levels + 1] = rows[1:2]
            rows = t.rows(ROWS - 2, 2)
            rows = DIFFUSE * rows + ADVECT * (v.rows(ROWS - 2, 2) * rows)
            edges[3, k : k + 1] = turn(jnp.where(one >= 16, rows[0:1], rows[1:2]), -16)
            edges[3, k + levels : k + levels + 1] = turn(rows[1:2], -16)

    for c in range(4):
        for j, device, low, size in runs[c]:
            slots[pl.ds(device * slot + RIM_ROWS + j, size, stride=slot), :] = edges[c, low : low + size]

    for copy in copies[3 * steps :]:
        copy.wait()

    part = fields.at[pl.ds(0, HELD)]
    mask = fields.at[pl.ds(HELD, HELD)]
    diag = fields.at[pl.ds(2 * HELD, HELD)]
    own = fields.at[pl.ds(PACKS, 56)]
    mask[0:ROWS] = depth[...] * ocean[...].astype(jnp.float32)

    def wet_of(rows):
        return ocean[rows, :].astype(jnp.float32)

    def masked(rows):
        return mask[rows, :]

    for a in range(PLANES):
        total = st[comb(a), :]
        pt[a] = total
        store_terms(a, total, ADVECT * sx[comb(a), :], ADVECT * sy[comb(a), :], te, tw, tn, ts)
    for a in range(PLANES):
        total = pt[a]
        wet = wet_of(comb(a))
        change = inner_sum(a, te, tw, tn, ts) - 4.0 * DIFFUSE * total
        part[comb(a), :] = source[comb(a), :] + (STERIC / levels) * wet * (total + wet * change)

    def mix(*values):
        value = values[-1]
        for at, low in ((6, 12), (5, 11), (4, 10), (3, 9), (2, 8), (1, 6), (0, 3)):
            value = jnp.where(q < low, values[at], value)
        return value

    def ends(planes, low):
        value = tn[planes[0], 8 : 8 + GROUPS]
        last = jnp.logical_and(lane >= low, lane < low + 16)
        return jnp.where(last, ts[planes[7], 8 : 8 + GROUPS], value)

    def beside(b, d, g, b_out, d_out):
        return g * b + d * d_out * (b - b_out)

    bp = choose(START, lane, lambda a: part[comb(a), :])
    dp = choose(START, lane, lambda a: masked(comb(a)))
    gp = choose(START, lane, lambda a: diag[comb(a), :])
    pp = beside(bp, dp, gp, turn(bp, -1), turn(dp, -1))
    pack_w = mix(
        bp, turn(dp, 3), turn(gp, 6), turn(pp, 6), turn(choose(START, lane, lambda a: te[a]), 9),
        turn(gp, 8), turn(dp, 8), turn(ends(START, OFF[7]), 12),
    )
    bp = choose(LAST, lane, lambda a: part[comb(a), :])
    dp = choose(LAST, lane, lambda a: masked(comb(a)))
    gp = choose(LAST, lane, lambda a: diag[comb(a), :])
    pp = beside(bp, dp, gp, turn(bp, 1), turn(dp, 1))
    pack_e = mix(
        turn(bp, 19), turn(dp, 22), turn(gp, 24), turn(pp, 27),
        turn(choose(LAST, lane, lambda a: tw[a]), 26),
        turn(gp, 29), turn(dp, 31), turn(ends(LAST, LANES - 16), 32),
    )
    own[0:GROUPS] = pack_w
    own[SLABS : SLABS + GROUPS] = pack_e
    north_l = tn[0, 8:9]
    north_r = tn[1, 8:9]
    south_13 = ts[PLANES - 2, 7 + GROUPS : 8 + GROUPS]
    south_14 = ts[PLANES - 1, 7 + GROUPS : 8 + GROUPS]
    south_l = turn(jnp.where(one >= 16, south_13, south_14), -16)
    south_r = turn(south_14, -16)
    own[48:49] = north_l
    own[49:50] = north_r
    own[50:51] = south_l
    own[51:52] = south_r
    deep = jnp.max(masked(slice(0, ROWS)), axis=(0, 1), keepdims=True)
    top = jnp.max(diag[0:ROWS], axis=(0, 1), keepdims=True) + 8.0 * deep * deep
    top = jnp.broadcast_to(top, (1, LANES))

    slots[pl.ds(RIM_ROWS - 1, count, stride=slot), :] = jnp.broadcast_to(top, (count, LANES))
    block_lane = lane_of((6, LANES))
    block_row = row_of((6, LANES))
    for c, first, rows_l, rows_r in ((2, True, north_l, north_r), (3, False, south_l, south_r)):
        base = 0 if first else ROWS - 6
        if first:
            spare = jnp.logical_and(block_row == 5, block_lane >= 80)
        else:
            spare = jnp.logical_and(block_row == 0, block_lane < 48)
        g = 0 if first else GROUPS - 1
        blocks = []
        block = slice(base, base + 6)
        for value, at in ((part[block, :], g), (masked(block), SLABS + g)):
            extra = jnp.broadcast_to(turn(own[at : at + 1], -16), (6, LANES))
            blocks.append(jnp.where(spare, extra, value))
        low = 0 if first else ROWS - 4
        diag_rows = diag[low : low + 4, :]
        third, fourth = (2, 3) if first else (SPAN_Y - 3, SPAN_Y - 4)
        b_l, b_r = line_of(lambda n: part[n : n + 1, :], third)
        d_l, d_r = line_of(lambda n: masked(slice(n, n + 1)), third)
        g_l, g_r = line_of(lambda n: diag[n : n + 1, :], third)
        bo_l, bo_r = line_of(lambda n: part[n : n + 1, :], fourth)
        do_l, do_r = line_of(lambda n: masked(slice(n, n + 1)), fourth)
        out_l = beside(b_l, d_l, g_l, bo_l, do_l)
        out_r = beside(b_r, d_r, g_r, bo_r, do_r)
        for at, value in ((112, turn(g_l, 112)), (113, turn(do_l, 113)), (114, turn(g_r, 3)), (115, turn(do_r, 4))):
            out_r = jnp.where(one == at, value, out_r)
        last_row = jnp.where(one == LANES - 1, top, rows_r)

        @pl.when(sides[c] >= 0)
        def _(c=c, blocks=blocks, diag_rows=diag_rows, singles=(out_l, out_r, rows_l, last_row)):
            at = sides[c] * slot
            slots[pl.ds(at, 6), :] = blocks[0]
            slots[pl.ds(at + 6, 6), :] = blocks[1]
            slots[pl.ds(at + 12, 4), :] = diag_rows
            for n, value in enumerate(singles):
                slots[pl.ds(at + 16 + n, 1), :] = value

    corner = jnp.logical_and(row_of((GROUPS, LANES)) == RIM_ROWS - 1, lane == LANES - 1)
    for c, pack in ((0, pack_w), (1, pack_e)):
        slots[pl.ds(sides[c] * slot, GROUPS), :] = jnp.where(corner, top, pack)
    for c, at in ((4, 0), (5, SLABS), (6, GROUPS - 1), (7, SLABS + GROUPS - 1)):
        @pl.when(sides[c] >= 0)
        def _(c=c, at=at):
            slots[pl.ds(sides[c] * slot, 1), :] = own[at : at + 1]
    send(slots, slots_out.reshape(count * slot, LANES))
    for copy in results:
        copy.wait()


SMEM = pl.BlockSpec(memory_space=pltpu.SMEM)


def solve_kernel(
    levels, tiles_y,
    around_in, rims, fields,
    vectors, hands,
    around, sem, north_in, south_in, fb, fd, fg, pw, pe, ow, oe, ed, eg, ex, we, wn, rows,
):
    copies = fetching([(around_in, around)], sem)
    count = rims.shape[0]
    number_pieces, _, share, first = pieces_of(levels, count)
    slot = RIM_ROWS + number_pieces
    came = rims.reshape(count * slot, LANES)
    hand = hands.reshape(count * share, LANES)
    own = fields.at[pl.ds(PACKS, 56)]
    lane = lane_of((SLABS, LANES))
    slab = row_of((SLABS, LANES))
    one = lane_of((1, LANES))

    none = jnp.zeros((WIDE - ROWS + 4, LANES), jnp.float32)
    for ref in (fb, fd, fg):
        ref[ROWS - 4 : WIDE] = none
    for n, ref in enumerate((fb, fd, fg)):
        ref[0:ROWS] = fields[n * HELD : n * HELD + ROWS]
    copies[0].wait()
    src = [around[4 * count + c] for c in range(8)]

    def fetch(c, low, high):
        value = came[pl.ds(jnp.maximum(src[c], 0) * slot + low, high - low), :]
        return jnp.where(src[c] >= 0, value, 0.0)

    me = lax.axis_index("gx") * tiles_y + lax.axis_index("gy")
    for n in range(number_pieces):
        side = jnp.minimum((n * count + me) // (2 * levels), 3)
        base = (side + 1 - 2 * (side % 2)) * count

        def relay(d, carry, n=n, base=base):
            row = around[base + d] + n
            hand[pl.ds(d * share + first + n, 1), :] = came[pl.ds(row, 1), :]
            return carry

        for d in range(count):
            relay(d, 0)

    north_in[0:RIM_ROWS] = fetch(3, 0, RIM_ROWS)
    south_in[0:RIM_ROWS] = fetch(2, 0, RIM_ROWS)
    strips = {2: south_in, 3: north_in}
    for ref, low, high, n_lane, s_lane in ((fb, 0, 6, 80, 48), (fd, 6, 12, 80, 48), (fg, 12, 16, 96, 32)):
        size = high - low
        row, column = row_of((size, LANES)), lane_of((size, LANES))
        beyond = jnp.logical_and(row == size - 1, column >= n_lane)
        ref[ROWS : ROWS + size] = jnp.where(beyond, 0.0, strips[3][low:high])
        beyond = jnp.logical_and(row == 0, column < s_lane)
        ref[WIDE - size : WIDE] = jnp.where(beyond, 0.0, strips[2][low:high])
    empty = jnp.zeros((SLABS, LANES), jnp.float32)
    for ref, side, north, south in ((pw, 0, 6, 4), (pe, 1, 7, 5)):
        ref[...] = empty
        ref[0:GROUPS] = fetch(side, 0, GROUPS)
        ref[GROUPS : GROUPS + 1] = fetch(north, 0, 1)
        ref[SLABS - 1 : SLABS] = fetch(south, 0, 1)
    for ref, at, north, south in ((ow, 0, 5, 0), (oe, SLABS, 11, 6)):
        ref[...] = empty
        ref[0:GROUPS] = own[at : at + GROUPS]
        ref[GROUPS : GROUPS + 1] = turn(strips[3][north:north + 1], 16)
        ref[SLABS - 1 : SLABS] = turn(strips[2][south:south + 1], 16)

    def spread(ref, j):
        a = START[j]
        first, second = ref[comb(a, SLABS), :], ref[comb(a + 1, SLABS), :]
        third = ref[comb(a + 2, SLABS), :] if a + 2 < PLANES else second
        left = turn(jnp.where(lane >= OFF[j], first, second), -OFF[j])
        right = turn(jnp.where(lane >= OFF[j], second, third), -OFF[j])
        return left, right

    def seam_row(left, right, slab_at, lanes_at):
        east = turn(pe[slab_at : slab_at + 1], 112 - lanes_at)
        west = turn(pw[slab_at : slab_at + 1], 124 - lanes_at)
        right = jnp.where(one < 112, right, jnp.where(one < 116, east, jnp.where(one >= 124, west, 0.0)))
        return jnp.broadcast_to(left, (SLABS, LANES)), jnp.broadcast_to(right, (SLABS, LANES))

    seams = {
        0: ((0, seam_row(strips[2][18:19], strips[2][19:20], SLABS - 1, 28)),
            (GROUPS, seam_row(own[50:51], own[51:52], GROUPS - 1, 28))),
        GROUP - 1: ((GROUPS - 1, seam_row(strips[3][18:19], strips[3][19:20], GROUPS, 12)),
                    (SLABS - 1, seam_row(own[48:49], own[49:50], 0, 12))),
    }
    weight = STERIC / levels

    def missing(target, term, term_out, d, d_out, g):
        term, term_out, d, d_out, g = (
            turn(value[0], target - value[1]) for value in (term, term_out, d, d_out, g)
        )
        term = jnp.where(d > 0, weight * term, 0.0)
        term_out = jnp.where(d_out > 0, weight * term_out, 0.0)
        return jnp.where(one == target, g * term + d * d_out * (term - term_out), 0.0)

    def ring(ref, at):
        return ref[at : at + 1]

    outer = {j: [] for j in range(GROUP)}
    for j, at, beyond, o, lanes in ((0, 0, SLABS - 1, 0, 28), (GROUP - 1, GROUPS - 1, GROUPS, 16, 12)):
        own_row, corner = ring(pe, at), ring(pe, beyond)
        outer[j].append((1, at, missing(
            114, (corner, lanes + 2), (corner, lanes + 3), (own_row, o + 5), (own_row, o + 11), (own_row, o + 10),
        )))
        own_row, corner = ring(pw, at), ring(pw, beyond)
        outer[j].append((1, at, missing(
            125, (corner, lanes + 1), (corner, lanes), (own_row, o + 3), (own_row, o + 11), (own_row, o + 10),
        )))
    for j, at, c, j_out, d_l, d_r in ((2, GROUPS, 3, 3, (9, 96), (11, 79)), (5, SLABS - 1, 2, 4, (6, 48), (8, 31))):
        line_l, line_r = strips[c][16:17], strips[c][17:18]
        corner = ring(pw, at)
        outer[j].append((0, at, line_l + missing(
            0, (corner, OFF[j] + 9), (corner, OFF[j_out] + 9), (strips[c][d_l[0]:d_l[0] + 1], d_l[1]),
            (line_r, 113), (line_r, 112),
        )))
        corner = ring(pe, at)
        outer[j].append((1, at, jnp.where(one < 112, line_r, 0.0) + missing(
            111, (corner, OFF[j] + 9), (corner, OFF[j_out] + 9), (strips[c][d_r[0]:d_r[0] + 1], d_r[1]),
            (line_r, 115), (line_r, 114),
        )))
    for j in range(GROUP):
        o = OFF[j]
        inside = slab < GROUPS
        halves = [
            jnp.zeros((SLABS, LANES), jnp.float32),
            jnp.where(
                jnp.logical_and(inside, lane == 114), turn(pe[...], 114 - o - 8),
                jnp.where(jnp.logical_and(inside, lane == 125), turn(pw[...], 125 - o - 8), 0.0),
            ),
        ]
        for half, at, line in outer[j]:
            halves[half] = halves[half] + jnp.where(slab == at, line, 0.0)
        ex[j, :, 0:LANES] = halves[0]
        ex[j, :, LANES:] = halves[1]

        def rim(right, q, width):
            east = turn(pe[...], 112 - o - q)
            west = turn(pw[...], 128 - width - o - q)
            value = jnp.where(lane < 112 + width, east, jnp.where(lane >= 128 - width, west, 0.0))
            return jnp.where(lane < 112, right, value)

        left, right = spread(fd, j)
        right = rim(right, 3, 3)
        wet_l = jnp.where(left > 0, weight, 0.0)
        wet_r = jnp.where(right > 0, weight, 0.0)
        ed[j, :, 0:LANES] = left
        ed[j, :, LANES:] = right
        left, right = spread(fg, j)
        eg[j, :, 0:LANES] = left
        eg[j, :, LANES:] = rim(right, 6, 2)
        left, right = spread(fb, j)
        right = rim(right, 0, 3)
        seam_l = jnp.where(lane == 0, turn(pw[...], -o - 9), 0.0)
        seam_r = jnp.where(lane == 127, turn(ow[...], 127 - o - 9), 0.0)
        seam_r = jnp.where(lane == 111, turn(pe[...], 111 - o - 9), seam_r)
        seam_r = jnp.where(lane == 112, turn(oe[...], 112 - o - 9), seam_r)
        for at, (row_l, row_r) in seams.get(j, ()):
            seam_l = seam_l + jnp.where(slab == at, row_l, 0.0)
            seam_r = seam_r + jnp.where(slab == at, row_r, 0.0)
        vectors[0, j, :, 0:LANES] = left + wet_l * seam_l
        vectors[0, j, :, LANES:] = right + wet_r * seam_r

    for j in range(GROUP):
        d = ed[j]
        we[j] = d * turn(d, -1)
        above = ed[j + 1] if j < GROUP - 1 else turn(ed[0], -1, 0)
        wn[j] = d * above

    top = jnp.max(came[pl.ds(RIM_ROWS - 1, count, stride=slot), :], axis=0, keepdims=True)
    top = jnp.max(jnp.where(one == LANES - 1, top, 0.0), axis=1, keepdims=True)
    scale = STRETCH / top

    big = (SLABS, 2 * LANES)
    mine = jnp.logical_and(row_of(big) < GROUPS, lane_of(big) < SPAN_X)
    pair = 0
    for k in range(5):
        count_sums = min(k + 1, 4)
        sums = [None] * count_sums
        new = None if k == 4 else vectors.at[k]
        if k:
            v = vectors.at[k - 1]
            flow_below = wn[GROUP - 1] * (v[GROUP - 1] - turn(v[0], -1, 0))
            flow_below = turn(flow_below, 1, 0)
        for j in range(GROUP):
            if k:
                here = v[j]
                above = v[j + 1] if j < GROUP - 1 else turn(v[0], -1, 0)
                flow_x = we[j] * (here - turn(here, -1))
                flow_y = wn[j] * (here - above)
                image = eg[j] * here + (flow_x - turn(flow_x, 1)) + (flow_y - flow_below)
                if k == 1:
                    image = image + ex[j]
                fresh = scale * image - (STRETCH * ROOTS[k - 1]) * here
                flow_below = flow_y
                if k < 4:
                    new[j] = fresh
            else:
                fresh = new[j]
            held = jnp.where(mine, fresh, 0.0)
            for i in range(count_sums):
                other = vectors[i, j] if i < k else held
                value = held * other
                sums[i] = value if sums[i] is None else sums[i] + value
        for i in range(count_sums):
            rows[pair : pair + 1] = jnp.sum(sums[i][:, 0:LANES] + sums[i][:, LANES:], axis=0, keepdims=True)
            pair += 1
    rows[pair : pair + 1] = jnp.where(one == 0, top, 0.0)
    rows[pair + 1 : 16] = jnp.zeros((15 - pair, LANES), jnp.float32)
    total = jnp.sum(rows[...], axis=1, keepdims=True)
    spot = lane_of((16, LANES)) == gram_lane(row_of((16, LANES)))
    line = jnp.sum(jnp.where(spot, total, 0.0), axis=0, keepdims=True)
    line = jnp.broadcast_to(line, (count, LANES))
    if first == 0:
        line = jnp.where(lane_of((count, LANES)) % 16 < 12, hand[pl.ds(0, count, stride=share), :], line)
    hand[pl.ds(0, count, stride=share), :] = line


def finish_kernel(
    levels, per, hands, vectors, edges, inner, tracer_out, surface_out,
    cells, flat, left, right, message, out_sems,
):
    count = hands.shape[0]
    _, runs, share, first = pieces_of(levels, count)
    came = hands.reshape(count * share, LANES)
    steps = levels // per
    chunks = [pl.ds(step * per * ROWS, per * ROWS) for step in range(steps)]
    results = []

    for c in range(4):
        for j, device, low, size in runs[c ^ 1]:
            value = came[pl.ds(device * share + first + j, size, stride=share), :]
            message[c, low : low + size] = value
    second = lane_of((SLABS, LANES)) % 16 == 1
    sums = []
    for k in range(levels):
        value = edges[2 * levels - 1] * jnp.concatenate([
            jnp.where(second, turn(message[1], 1 - k), turn(message[0], -k)),
            message[2, k : k + 1], message[2, k + levels : k + levels + 1],
            message[3, k : k + 1], message[3, k + levels : k + levels + 1],
            jnp.zeros((EDGE - SLABS - 4, LANES), jnp.float32),
        ], axis=0)
        if k:
            value = value + edges[2 * levels + k - 1] * sums[-1]
        sums.append(value * edges[levels - 1 + k])
    for k in range(levels - 2, -1, -1):
        sums[k] = sums[k] + edges[k] * sums[k + 1]
    lane = lane_of((GROUPS, LANES))
    slab = row_of((GROUPS, LANES))
    for k in range(levels):
        west = sums[k][0:GROUPS]
        east = turn(west, -18)
        south_l, south_r = sums[k][SLABS : SLABS + 1], sums[k][SLABS + 1 : SLABS + 2]
        north_l = turn(sums[k][SLABS + 2 : SLABS + 3], 16)
        north_r = turn(sums[k][SLABS + 3 : SLABS + 4], 16)
        for a in range(PLANES):
            rim = None
            for at, source in [(at, west) for at in FIRST_OF[a]] + [(at, east) for at in LAST_OF[a]]:
                rim = jnp.where(lane == at, source, 0.0 if rim is None else rim)
            rows = comb(k * ROWS + a)
            if rim is None:
                cells[rows, :] = inner[rows, :]
                continue
            if a == 0:
                rim = rim + jnp.where(slab == 0, south_l, 0.0)
            if a == 1:
                rim = rim + jnp.where(jnp.logical_and(slab == 0, lane < 112), south_r, 0.0)
            if a == PLANES - 2:
                rim = rim + jnp.where(jnp.logical_and(slab == GROUPS - 1, lane >= 16), north_l, 0.0)
            if a == PLANES - 1:
                rim = rim + jnp.where(slab == GROUPS - 1, jnp.where(lane < 16, north_l, north_r), 0.0)
            cells[rows, :] = inner[rows, :] + rim
        if k % per == per - 1:
            step = k // per
            copy = pltpu.make_async_copy(
                cells.at[chunks[step]], tracer_out.at[chunks[step]], out_sems.at[1 + step]
            )
            copy.start()
            results.append(copy)

    row = jnp.sum(came[pl.ds(0, count, stride=share), :], axis=0, keepdims=True)
    one = lane_of((1, LANES))
    entry = {}
    pair = 0
    for k in range(5):
        for i in range(min(k + 1, 4)):
            value = jnp.sum(jnp.where(one == gram_lane(pair), row, 0.0), axis=1, keepdims=True)
            entry[i, k] = entry[k, i] = value
            pair += 1
    top = jnp.sum(jnp.where(one == gram_lane(pair), row, 0.0), axis=1, keepdims=True) * (1.0 / count)

    def image(c):
        out = [None] * 5
        for k in range(4):
            if c[k] is None:
                continue
            low = ROOTS[k] * c[k]
            out[k] = low if out[k] is None else out[k] + low
            out[k + 1] = (1.0 / STRETCH) * c[k]
        return out

    def dot(a, b):
        total = None
        for i in range(5):
            if a[i] is None:
                continue
            inner = None
            for j in range(5):
                if b[j] is not None:
                    value = entry[i, j] * b[j]
                    inner = value if inner is None else inner + value
            total = a[i] * inner if total is None else total + a[i] * inner
        return total

    def axpy(a, s, b):
        return [
            x if y is None else (s * y if x is None else x + s * y) for x, y in zip(a, b)
        ]

    r = [jnp.ones((1, 1), jnp.float32)] + [None] * 4
    p = list(r)
    x = [None] * 5
    rr = entry[0, 0]
    for n in range(ITERS):
        q = image(p)
        step = rr / jnp.maximum(dot(p, q), TINY)
        step = jnp.clip(step, top * (1.0 / HIGH_RATE), top * (1.0 / LOW_RATE))
        x = axpy(x, step, p)
        if n < ITERS - 1:
            r = axpy(r, -step, q)
            fresh = jnp.maximum(dot(r, r), 0.0)
            p = axpy(r, fresh / jnp.maximum(rr, TINY), p)
            rr = fresh
    factors = [c / top for c in x[:4]]
    for j in range(GROUP):
        value = None
        for k in range(4):
            term = factors[k] * vectors[k, j]
            value = term if value is None else value + term
        left[j] = turn(value[:, 0:LANES], OFF[j])
        right[j] = turn(value[:, LANES:], OFF[j])
    lane = lane_of((SLABS, LANES))
    for a in range(PLANES):
        value = None
        for j in range(GROUP):
            for half, ref in ((0, left), (1, right)):
                low = max(SPAN_X * j + LANES * half - LANES * a, 0)
                high = min(SPAN_X * j + (LANES if half == 0 else SPAN_X) - LANES * a, LANES)
                if low >= high:
                    continue
                value = ref[j] if value is None else jnp.where(lane >= low, ref[j], value)
        flat[comb(a), :] = value[0:GROUPS]
    results.append(pltpu.make_async_copy(flat, surface_out.reshape(ROWS, LANES), out_sems.at[0]))
    results[-1].start()
    for copy in results:
        copy.wait()


def tracer_kernel(
    levels, per, sides, around, temp_in, zonal_in, merid_in, rates_in, fields,
    out, edges,
    temp, zonal, merid, rates, ocean,
    te, tw, tn, ts, stepped, border, sems,
):
    steps = levels // per
    pairs = []
    for step in range(steps):
        chunk = pl.ds(step * per * ROWS, per * ROWS)
        pairs += [
            (a.at[chunk], b.at[chunk]) for a, b in ((temp_in, temp), (zonal_in, zonal), (merid_in, merid))
        ]
    copies = fetching(pairs + [(rates_in.reshape((levels - 1) * ROWS, LANES), rates)], sems)
    lane = lane_of((GROUPS, LANES))
    one = lane_of((1, LANES))
    clear_terms(tn, ts)

    ocean[...] = jnp.where(fields[HELD : HELD + ROWS] > 0, 1.0, 0.0)
    for step in range(steps):
        for copy in copies[3 * step : 3 * step + 3]:
            copy.wait()

        def level(k, carry):
            t, u, v = (Level(ref, k * ROWS) for ref in (temp, zonal, merid))
            for a in range(PLANES):
                own = t.plane(a)
                quarter = ADVECT * own
                store_terms(a, own, u.plane(a) * quarter, v.plane(a) * quarter, te, tw, tn, ts)
            for a in range(PLANES):
                own = t.plane(a)
                change = inner_sum(a, te, tw, tn, ts) - 4.0 * DIFFUSE * own
                stepped[k, a] = own + ocean[comb(a), :] * change
            return carry

        lax.fori_loop(step * per, step * per + per, level, 0)
    copies[-1].wait()

    def block(a, carry):
        for low in range(0, GROUPS, 8):
            size = min(8, GROUPS - low)

            def rows(k):
                return pl.ds(k * ROWS + low * PLANES + a, size, stride=PLANES)

            gains = []
            sums = []
            for k in range(levels):
                value = stepped[k, a, low : low + size]
                pivot = 1.0
                if k > 0:
                    pivot = pivot + upper - upper * gains[-1]
                    value = value + upper * sums[-1]
                if k < levels - 1:
                    lower = rates[rows(k), :]
                    inverse = 1.0 / (pivot + lower)
                    gains.append(lower * inverse)
                    upper = lower
                else:
                    inverse = 1.0 / pivot
                sums.append(value * inverse)
            result = sums[-1]
            out[rows(levels - 1), :] = result
            for k in range(levels - 2, -1, -1):
                result = sums[k] + gains[k] * result
                out[rows(k), :] = result
        return carry

    lax.fori_loop(0, PLANES, block, 0)

    def edge(ref, base, at):
        def get(a):
            return ref[comb(base + a), :].astype(jnp.float32)

        border[0:GROUPS] = jnp.where(
            lane % 16 == 1, turn(choose(LAST, lane, get), 18), choose(START, lane, get)
        )
        border[SLABS : SLABS + 2] = ref[base : base + 2, :].astype(jnp.float32)
        rows = ref[base + ROWS - 2 : base + ROWS, :].astype(jnp.float32)
        border[SLABS + 2 : SLABS + 3] = turn(jnp.where(one >= 16, rows[0:1], rows[1:2]), -16)
        border[SLABS + 3 : SLABS + 4] = turn(rows[1:2], -16)
        edges[at] = border[...]

    border[...] = jnp.zeros_like(border)
    edge(ocean, 0, 2 * levels - 1)
    for c in (2, 3):
        rows = pl.ds(SLABS + 2 * (c - 2), 2)
        value = edges[2 * levels - 1, rows]
        edges[2 * levels - 1, rows] = jnp.where(around[sides + c] >= 0, value, 0.0)
    gain = None
    for k in range(levels):
        pivot = 1.0
        if k > 0:
            upper = edges[2 * levels + k - 1]
            pivot = pivot + upper - upper * gain
        if k < levels - 1:
            edge(rates, k * ROWS, 2 * levels + k)
            lower = edges[2 * levels + k]
            inverse = 1.0 / (pivot + lower)
            gain = lower * inverse
            edges[k] = gain
        else:
            inverse = 1.0 / pivot
        edges[levels - 1 + k] = inverse


def on_device(
    thermal_anomaly,
    zonal_flow_ratio,
    meridional_flow_ratio,
    diffusion_rates,
    ocean_bottom_scaled,
    ocean_indicator,
    operator_diagonal,
    elevation_source,
    block_positions,
):
    levels, cells = thermal_anomaly.shape[1:]
    nx = lax.axis_size("gx")
    ny = lax.axis_size("gy")
    count = block_positions.shape[0]
    planes = (ocean_bottom_scaled, ocean_indicator, operator_diagonal, elevation_source)
    depth, ocean, diag, source = planes
    f32 = jnp.float32
    per = next(n for n in (4, 2, 6, levels) if levels % n == 0 and n * ROWS % 8 == 0)
    steps = levels // per
    few = next(n for n in (4, 2, 6, levels) if levels % n == 0 and n * ROWS % 8 == 0)
    params = pltpu.CompilerParams(vmem_limit_bytes=BUDGET)
    temp, zonal, merid = (
        array.reshape(levels * ROWS, LANES)
        for array in (thermal_anomaly, zonal_flow_ratio, meridional_flow_ratio)
    )
    rates = diffusion_rates.reshape(levels - 1, 1, cells)
    temp, zonal, merid, rates, depth, ocean, diag, source, positions = (
        pltpu.with_memory_space_constraint(array, pltpu.HBM)
        for array in (temp, zonal, merid, rates, depth, ocean, diag, source, block_positions)
    )
    hbm = pl.BlockSpec(memory_space=pltpu.HBM)
    here = pl.BlockSpec(memory_space=pltpu.VMEM)

    def vmem(*shape, kind=f32):
        return pltpu.VMEM(shape, kind)

    def out(*shape, kind=f32):
        return jax.ShapeDtypeStruct(shape, kind)

    def sems(number):
        return pltpu.SemaphoreType.DMA((number,))

    deep = vmem(levels * ROWS, LANES)
    flat = vmem(ROWS, LANES)
    flat_int = vmem(ROWS, LANES, kind=jnp.int32)
    plane = vmem(PLANES, GROUPS, LANES)
    tall = vmem(PLANES, 40, LANES)
    numbers = pltpu.SMEM((count,), jnp.int32)
    number_pieces, _, share, _ = pieces_of(levels, count)
    slot = RIM_ROWS + number_pieces
    fields, slots, around = pl.pallas_call(
        functools.partial(forcing_kernel, levels, few, nx, ny),
        in_specs=[hbm] * 8,
        out_specs=[here, hbm, hbm],
        out_shape=[
            out(FIELDS, LANES), pltpu.HBM((count, 1, slot * LANES), f32), out(4 * count + 8, kind=jnp.int32),
        ],
        scratch_shapes=[deep] * 3 + [flat, flat_int, flat]
        + [vmem(count * slot, LANES)]
        + [flat] * 3 + [plane] * 3 + [tall] * 2
        + [vmem(4, 2 * levels, LANES), numbers, numbers]
        + [pltpu.SMEM((4 * count + 8,), jnp.int32), sems(3 * (levels // few) + 5), sems(2)],
        compiler_params=params,
        name="forcing",
    )(positions, temp, zonal, merid, depth, ocean, diag, source)
    rims = lax.all_to_all(slots, BOTH, 0, 0, tiled=True)

    inner, edges = pl.pallas_call(
        functools.partial(tracer_kernel, levels, per, 4 * count),
        in_specs=[SMEM] + [hbm] * 4 + [here],
        out_specs=[here] * 2,
        out_shape=[out(levels * ROWS, LANES), out(3 * levels - 1, EDGE, LANES)],
        scratch_shapes=[deep] * 3 + [vmem((levels - 1) * ROWS, LANES), flat]
        + [plane] * 2 + [tall] * 2
        + [vmem(levels, PLANES, GROUPS, LANES), vmem(EDGE, LANES), sems(3 * steps + 1)],
        compiler_params=params,
        name="tracer",
    )(around, temp, zonal, merid, rates, fields)

    rims, edges = lax.optimization_barrier((rims, edges))
    extended = vmem(GROUP, SLABS, 2 * LANES)
    vectors, hand = pl.pallas_call(
        functools.partial(solve_kernel, levels, ny),
        in_specs=[pl.BlockSpec(memory_space=pl.ANY)] + [here] * 2,
        out_specs=[here] * 2,
        out_shape=[out(4, GROUP, SLABS, 2 * LANES), out(count, 1, share * LANES)],
        scratch_shapes=[pltpu.SMEM((4 * count + 8,), jnp.int32), sems(1)]
        + [vmem(SLABS, LANES)] * 2 + [vmem(WIDE, LANES)] * 3 + [vmem(SLABS, LANES)] * 4 + [extended] * 5 + [vmem(16, LANES)],
        compiler_params=params,
        name="vectors",
    )(around, rims, fields)
    hands = lax.all_to_all(hand, BOTH, 0, 0, tiled=True)

    new_temp, surface = pl.pallas_call(
        functools.partial(finish_kernel, levels, per),
        in_specs=[here] * 4,
        out_specs=[hbm] * 2,
        out_shape=[out(levels * ROWS, LANES), out(1, cells)],
        scratch_shapes=[
            deep, flat, vmem(GROUP, SLABS, LANES), vmem(GROUP, SLABS, LANES), vmem(4, 2 * levels, LANES),
            sems(1 + steps),
        ],
        compiler_params=params,
        name="finish",
    )(hands, vectors, edges, inner)
    return new_temp.reshape(1, levels, cells), surface


def solution(mesh):
    deep = P(BOTH, None, None)
    flat = P(BOTH, None)
    return jax.shard_map(
        on_device,
        mesh=mesh,
        in_specs=(deep, deep, deep, deep, flat, flat, flat, flat, P()),
        out_specs=(deep, flat),
        check_vma=False,
    )
```

```python
import functools

import jax
import jax.numpy as jnp
from jax import lax
from jax.experimental import pallas as pl
from jax.experimental.pallas import tpu as pltpu
from jax.sharding import PartitionSpec as P

ITERS = 4
SPAN_X = 240
SPAN_Y = 160
RIM = 4
ADVECT = 0.25
DIFFUSE = 0.12
STERIC = 0.5
LOW_RATE = 0.05
HIGH_RATE = 32.5
ROOTS = (0.02, 0.35, 0.1, 0.2)
STRETCH = 4.0
TINY = 1e-30
BOTH = ("gx", "gy")
SIDES = ((-1, 0), (1, 0), (0, -1), (0, 1), (-1, -1), (1, -1), (-1, 1), (1, 1))

LANES = 128
GROUP = 8
GROUPS = SPAN_Y // GROUP
PLANES = GROUP * SPAN_X // LANES
ROWS = GROUPS * PLANES
SLABS = GROUPS + 4
WIDE = SLABS * PLANES
START = [SPAN_X * j // LANES for j in range(GROUP)]
OFF = [SPAN_X * j % LANES for j in range(GROUP)]
LAST = [(SPAN_X * j + SPAN_X - 1) // LANES for j in range(GROUP)]
END = [(SPAN_X * j + SPAN_X - 1) % LANES for j in range(GROUP)]
FIRST_OF = [[OFF[j] for j in range(GROUP) if START[j] == a] for a in range(PLANES)]
LAST_OF = [[END[j] for j in range(GROUP) if LAST[j] == a] for a in range(PLANES)]
RIM_ROWS = 20
HELD = -(-ROWS // 8) * 8
PACKS = 3 * HELD
FIELDS = PACKS + 56
EDGE = 32
BUDGET = 32 * 1024 * 1024


def turn(value, shift, axis=1):
    shift = shift % value.shape[axis]
    return value if shift == 0 else pltpu.roll(value, shift, axis)


def fetching(pairs, sems):
    copies = [pltpu.make_async_copy(a, b, sems.at[n]) for n, (a, b) in enumerate(pairs)]
    for copy in copies:
        copy.start()
    return copies


def pieces_of(levels, count):
    rows = 2 * levels
    number = -(-4 * rows // count)
    runs = [[] for _ in range(4)]
    for c in range(4):
        for j in range(number):
            low, high = max(c * rows, j * count), min((c + 1) * rows, (j + 1) * count)
            if low < high:
                runs[c].append((j, low - j * count, low - c * rows, high - low))
    merged = count <= 2 * rows and levels <= 12
    return number, runs, number + (0 if merged else 1), 0 if merged else 1


def gram_lane(n):
    return 16 * (n // 4) + 12 + n % 4


class Level:
    def __init__(self, ref, base):
        self.ref, self.base = ref, base

    def plane(self, a):
        return self.ref[comb(self.base + a), :]

    def rows(self, low, size):
        return self.ref[pl.ds(self.base + low, size), :]


def lane_of(shape):
    return lax.broadcasted_iota(jnp.int32, shape, len(shape) - 1)


def row_of(shape):
    return lax.broadcasted_iota(jnp.int32, shape, 0)


def comb(a, count=GROUPS):
    return pl.ds(a, count, stride=PLANES)


def line_of(get, y):
    lane = lane_of((1, LANES))
    j = y % GROUP
    row = y // GROUP * PLANES + START[j]
    first, second = get(row), get(row + 1)
    third = get(row + 2) if START[j] + 2 < PLANES else second
    left = turn(jnp.where(lane >= OFF[j], first, second), -OFF[j])
    right = turn(jnp.where(lane >= OFF[j], second, third), -OFF[j])
    return left, right


def drop(value, lanes, lane):
    for at in lanes:
        value = jnp.where(lane == at, 0.0, value)
    return value


def store_terms(a, temp, flow_x, flow_y, te, tw, tn, ts):
    spread = DIFFUSE * temp
    te[a] = spread - flow_x
    tw[a] = spread + flow_x
    tn[a, 8 : 8 + GROUPS] = spread - flow_y
    ts[a, 8 : 8 + GROUPS] = spread + flow_y


def clear_terms(tn, ts):
    none = jnp.zeros((PLANES, 1, LANES), jnp.float32)
    for ref in (tn, ts):
        ref[:, 7:8] = none
        ref[:, 8 + GROUPS : 9 + GROUPS] = none


def inner_sum(a, te, tw, tn, ts):
    lane = lane_of((GROUPS, LANES))
    here = te[a]
    east = here if a == PLANES - 1 else jnp.where(lane == 0, te[a + 1], here)
    east = drop(turn(east, -1), LAST_OF[a], lane)
    here = tw[a]
    west = here if a == 0 else jnp.where(lane == LANES - 1, tw[a - 1], here)
    west = drop(turn(west, 1), FIRST_OF[a], lane)

    def plane(ref, at):
        down = 8 + (at >= PLANES) - (at < 0)
        return ref[at % PLANES, down : down + GROUPS]

    north = turn(jnp.where(lane >= LANES - 16, plane(tn, a + 1), plane(tn, a + 2)), 16)
    south = turn(jnp.where(lane < 16, plane(ts, a - 1), plane(ts, a - 2)), -16)
    return east + west + north + south


def choose(planes, lane, get):
    shift = 32 if planes is LAST else 0
    lows = sorted(((OFF[j] - shift) % LANES, planes[j]) for j in range(GROUP))
    value = get(lows[-1][1])
    for low, a in reversed(lows[:-1]):
        value = jnp.where(lane < low + 16, get(a), value)
    return value


def forcing_kernel(
    levels, per, tiles_x, tiles_y,
    pos_in, temp_in, zonal_in, merid_in, depth_in, ocean_in, diag_in, source_in,
    fields, slots_out, around_out,
    temp, zonal, merid, depth, ocean, source, slots,
    st, sx, sy, pt, te, tw, tn, ts, edges, pos, holder, around, sems, out_sems,
):
    count = pos.shape[0]
    steps = levels // per
    number_pieces, runs, _, _ = pieces_of(levels, count)
    slot = RIM_ROWS + number_pieces
    pairs = []
    for step in range(steps):
        chunk = pl.ds(step * per * ROWS, per * ROWS)
        pairs += [
            (a.at[chunk], b.at[chunk]) for a, b in ((temp_in, temp), (zonal_in, zonal), (merid_in, merid))
        ]
    pairs += [
        (a.reshape(ROWS, LANES), b)
        for a, b in (
            (source_in, source), (ocean_in, ocean), (depth_in, depth),
            (diag_in, fields.at[pl.ds(2 * HELD, ROWS)]),
        )
    ]
    copies = fetching([(pos_in, pos)] + pairs, sems)
    copies.pop(0).wait()
    results = []

    def send(value, target):
        copy = pltpu.make_async_copy(value, target, out_sems.at[len(results)])
        copy.start()
        results.append(copy)

    lane = lane_of((GROUPS, LANES))
    one = lane_of((1, LANES))
    q = lane % 16
    edges[...] = jnp.zeros_like(edges)

    def number(d, carry):
        holder[pos[d]] = d
        return carry

    lax.fori_loop(0, count, number, 0)
    me = lax.axis_index("gx") * tiles_y + lax.axis_index("gy")
    here = pos[me]
    row = here // tiles_x
    column = here % tiles_x
    sides = []
    for c, (dx, dy) in enumerate(SIDES):
        there = row + dy
        inside = jnp.logical_and(there >= 0, there < tiles_y)
        target = jnp.where(inside, there, 0) * tiles_x + (column + dx + tiles_x) % tiles_x
        device = jnp.where(inside, holder[target], -1)
        around[4 * count + c] = device
        sides.append(device)

    def look(y, carry):
        line = [holder[y * tiles_x + x] for x in range(tiles_x)]
        below = [holder[jnp.maximum(y - 1, 0) * tiles_x + x] for x in range(tiles_x)]
        above = [holder[jnp.minimum(y + 1, tiles_y - 1) * tiles_x + x] for x in range(tiles_x)]
        for x, device in enumerate(line):
            for c, other in enumerate((line[x - 1], line[(x + 1) % tiles_x], below[x], above[x])):
                around[c * count + device] = other * slot + RIM_ROWS
        return carry

    lax.fori_loop(0, tiles_y, look, 0)
    send(around, around_out)
    clear_terms(tn, ts)

    def add(flats, low, size, fresh):
        rows = pl.ds(low, size)
        total = [None] * 3
        for t, u, v in zip(*flats):
            t = t.rows(low, size)
            new = (t, t * u.rows(low, size), t * v.rows(low, size))
            total = [b if a is None else a + b for a, b in zip(total, new)]
        for ref, value in zip((st, sx, sy), total):
            ref[rows, :] = value if fresh else ref[rows, :] + value

    for step in range(steps):
        for copy in copies[3 * step : 3 * step + 3]:
            copy.wait()
        flats = [
            [Level(ref, (step * per + n) * ROWS) for n in range(per)] for ref in (temp, zonal, merid)
        ]

        for m in range(ROWS // 8):
            add(flats, m * 8, 8, step == 0)
        if ROWS % 8:
            add(flats, ROWS - ROWS % 8, ROWS % 8, step == 0)

        for n in range(per):
            k = step * per + n
            t, u, v = (flat[n] for flat in flats)

            def term(planes, sign):
                own = choose(planes, lane, t.plane)
                flow = choose(planes, lane, u.plane)
                return DIFFUSE * own + sign * ADVECT * (flow * own)

            edges[0, 0:GROUPS] = jnp.where(q == k, turn(term(START, -1.0), k), edges[0, 0:GROUPS])
            edges[1, 0:GROUPS] = jnp.where(q == k, turn(term(LAST, 1.0), k + 17), edges[1, 0:GROUPS])
            rows = t.rows(0, 2)
            rows = DIFFUSE * rows - ADVECT * (v.rows(0, 2) * rows)
            edges[2, k : k + 1] = rows[0:1]
            edges[2, k + levels : k + levels + 1] = rows[1:2]
            rows = t.rows(ROWS - 2, 2)
            rows = DIFFUSE * rows + ADVECT * (v.rows(ROWS - 2, 2) * rows)
            edges[3, k : k + 1] = turn(jnp.where(one >= 16, rows[0:1], rows[1:2]), -16)
            edges[3, k + levels : k + levels + 1] = turn(rows[1:2], -16)

    for c in range(4):
        for j, device, low, size in runs[c]:
            slots[pl.ds(device * slot + RIM_ROWS + j, size, stride=slot), :] = edges[c, low : low + size]

    for copy in copies[3 * steps :]:
        copy.wait()

    part = fields.at[pl.ds(0, HELD)]
    mask = fields.at[pl.ds(HELD, HELD)]
    diag = fields.at[pl.ds(2 * HELD, HELD)]
    own = fields.at[pl.ds(PACKS, 56)]
    mask[0:ROWS] = depth[...] * ocean[...].astype(jnp.float32)

    def wet_of(rows):
        return ocean[rows, :].astype(jnp.float32)

    def masked(rows):
        return mask[rows, :]

    for a in range(PLANES):
        total = st[comb(a), :]
        pt[a] = total
        store_terms(a, total, ADVECT * sx[comb(a), :], ADVECT * sy[comb(a), :], te, tw, tn, ts)
    for a in range(PLANES):
        total = pt[a]
        wet = wet_of(comb(a))
        change = inner_sum(a, te, tw, tn, ts) - 4.0 * DIFFUSE * total
        part[comb(a), :] = source[comb(a), :] + (STERIC / levels) * wet * (total + wet * change)

    def mix(*values):
        value = values[-1]
        for at, low in ((6, 12), (5, 11), (4, 10), (3, 9), (2, 8), (1, 6), (0, 3)):
            value = jnp.where(q < low, values[at], value)
        return value

    def ends(planes, low):
        value = tn[planes[0], 8 : 8 + GROUPS]
        last = jnp.logical_and(lane >= low, lane < low + 16)
        return jnp.where(last, ts[planes[7], 8 : 8 + GROUPS], value)

    def beside(b, d, g, b_out, d_out):
        return g * b + d * d_out * (b - b_out)

    bp = choose(START, lane, lambda a: part[comb(a), :])
    dp = choose(START, lane, lambda a: masked(comb(a)))
    gp = choose(START, lane, lambda a: diag[comb(a), :])
    pp = beside(bp, dp, gp, turn(bp, -1), turn(dp, -1))
    pack_w = mix(
        bp, turn(dp, 3), turn(gp, 6), turn(pp, 6), turn(choose(START, lane, lambda a: te[a]), 9),
        turn(gp, 8), turn(dp, 8), turn(ends(START, OFF[7]), 12),
    )
    bp = choose(LAST, lane, lambda a: part[comb(a), :])
    dp = choose(LAST, lane, lambda a: masked(comb(a)))
    gp = choose(LAST, lane, lambda a: diag[comb(a), :])
    pp = beside(bp, dp, gp, turn(bp, 1), turn(dp, 1))
    pack_e = mix(
        turn(bp, 19), turn(dp, 22), turn(gp, 24), turn(pp, 27),
        turn(choose(LAST, lane, lambda a: tw[a]), 26),
        turn(gp, 29), turn(dp, 31), turn(ends(LAST, LANES - 16), 32),
    )
    own[0:GROUPS] = pack_w
    own[SLABS : SLABS + GROUPS] = pack_e
    north_l = tn[0, 8:9]
    north_r = tn[1, 8:9]
    south_13 = ts[PLANES - 2, 7 + GROUPS : 8 + GROUPS]
    south_14 = ts[PLANES - 1, 7 + GROUPS : 8 + GROUPS]
    south_l = turn(jnp.where(one >= 16, south_13, south_14), -16)
    south_r = turn(south_14, -16)
    own[48:49] = north_l
    own[49:50] = north_r
    own[50:51] = south_l
    own[51:52] = south_r
    deep = jnp.max(masked(slice(0, ROWS)), axis=(0, 1), keepdims=True)
    top = jnp.max(diag[0:ROWS], axis=(0, 1), keepdims=True) + 8.0 * deep * deep
    top = jnp.broadcast_to(top, (1, LANES))

    slots[pl.ds(RIM_ROWS - 1, count, stride=slot), :] = jnp.broadcast_to(top, (count, LANES))
    block_lane = lane_of((6, LANES))
    block_row = row_of((6, LANES))
    for c, first, rows_l, rows_r in ((2, True, north_l, north_r), (3, False, south_l, south_r)):
        base = 0 if first else ROWS - 6
        if first:
            spare = jnp.logical_and(block_row == 5, block_lane >= 80)
        else:
            spare = jnp.logical_and(block_row == 0, block_lane < 48)
        g = 0 if first else GROUPS - 1
        blocks = []
        block = slice(base, base + 6)
        for value, at in ((part[block, :], g), (masked(block), SLABS + g)):
            extra = jnp.broadcast_to(turn(own[at : at + 1], -16), (6, LANES))
            blocks.append(jnp.where(spare, extra, value))
        low = 0 if first else ROWS - 4
        diag_rows = diag[low : low + 4, :]
        third, fourth = (2, 3) if first else (SPAN_Y - 3, SPAN_Y - 4)
        b_l, b_r = line_of(lambda n: part[n : n + 1, :], third)
        d_l, d_r = line_of(lambda n: masked(slice(n, n + 1)), third)
        g_l, g_r = line_of(lambda n: diag[n : n + 1, :], third)
        bo_l, bo_r = line_of(lambda n: part[n : n + 1, :], fourth)
        do_l, do_r = line_of(lambda n: masked(slice(n, n + 1)), fourth)
        out_l = beside(b_l, d_l, g_l, bo_l, do_l)
        out_r = beside(b_r, d_r, g_r, bo_r, do_r)
        for at, value in ((112, turn(g_l, 112)), (113, turn(do_l, 113)), (114, turn(g_r, 3)), (115, turn(do_r, 4))):
            out_r = jnp.where(one == at, value, out_r)
        last_row = jnp.where(one == LANES - 1, top, rows_r)

        @pl.when(sides[c] >= 0)
        def _(c=c, blocks=blocks, diag_rows=diag_rows, singles=(out_l, out_r, rows_l, last_row)):
            at = sides[c] * slot
            slots[pl.ds(at, 6), :] = blocks[0]
            slots[pl.ds(at + 6, 6), :] = blocks[1]
            slots[pl.ds(at + 12, 4), :] = diag_rows
            for n, value in enumerate(singles):
                slots[pl.ds(at + 16 + n, 1), :] = value

    corner = jnp.logical_and(row_of((GROUPS, LANES)) == RIM_ROWS - 1, lane == LANES - 1)
    for c, pack in ((0, pack_w), (1, pack_e)):
        slots[pl.ds(sides[c] * slot, GROUPS), :] = jnp.where(corner, top, pack)
    for c, at in ((4, 0), (5, SLABS), (6, GROUPS - 1), (7, SLABS + GROUPS - 1)):
        @pl.when(sides[c] >= 0)
        def _(c=c, at=at):
            slots[pl.ds(sides[c] * slot, 1), :] = own[at : at + 1]
    send(slots, slots_out.reshape(count * slot, LANES))
    for copy in results:
        copy.wait()


SMEM = pl.BlockSpec(memory_space=pltpu.SMEM)


def solve_kernel(
    levels, tiles_y,
    around_in, rims, fields,
    vectors, hands,
    around, sem, north_in, south_in, fb, fd, fg, pw, pe, ow, oe, ed, eg, ex, we, wn, rows,
):
    copies = fetching([(around_in, around)], sem)
    count = rims.shape[0]
    number_pieces, _, share, first = pieces_of(levels, count)
    slot = RIM_ROWS + number_pieces
    came = rims.reshape(count * slot, LANES)
    hand = hands.reshape(count * share, LANES)
    own = fields.at[pl.ds(PACKS, 56)]
    lane = lane_of((SLABS, LANES))
    slab = row_of((SLABS, LANES))
    one = lane_of((1, LANES))

    none = jnp.zeros((WIDE - ROWS + 4, LANES), jnp.float32)
    for ref in (fb, fd, fg):
        ref[ROWS - 4 : WIDE] = none
    for n, ref in enumerate((fb, fd, fg)):
        ref[0:ROWS] = fields[n * HELD : n * HELD + ROWS]
    copies[0].wait()
    src = [around[4 * count + c] for c in range(8)]

    def fetch(c, low, high):
        value = came[pl.ds(jnp.maximum(src[c], 0) * slot + low, high - low), :]
        return jnp.where(src[c] >= 0, value, 0.0)

    me = lax.axis_index("gx") * tiles_y + lax.axis_index("gy")
    for n in range(number_pieces):
        side = jnp.minimum((n * count + me) // (2 * levels), 3)
        base = (side + 1 - 2 * (side % 2)) * count

        def relay(d, carry, n=n, base=base):
            row = around[base + d] + n
            hand[pl.ds(d * share + first + n, 1), :] = came[pl.ds(row, 1), :]
            return carry

        for d in range(count):
            relay(d, 0)

    north_in[0:RIM_ROWS] = fetch(3, 0, RIM_ROWS)
    south_in[0:RIM_ROWS] = fetch(2, 0, RIM_ROWS)
    strips = {2: south_in, 3: north_in}
    for ref, low, high, n_lane, s_lane in ((fb, 0, 6, 80, 48), (fd, 6, 12, 80, 48), (fg, 12, 16, 96, 32)):
        size = high - low
        row, column = row_of((size, LANES)), lane_of((size, LANES))
        beyond = jnp.logical_and(row == size - 1, column >= n_lane)
        ref[ROWS : ROWS + size] = jnp.where(beyond, 0.0, strips[3][low:high])
        beyond = jnp.logical_and(row == 0, column < s_lane)
        ref[WIDE - size : WIDE] = jnp.where(beyond, 0.0, strips[2][low:high])
    empty = jnp.zeros((SLABS, LANES), jnp.float32)
    for ref, side, north, south in ((pw, 0, 6, 4), (pe, 1, 7, 5)):
        ref[...] = empty
        ref[0:GROUPS] = fetch(side, 0, GROUPS)
        ref[GROUPS : GROUPS + 1] = fetch(north, 0, 1)
        ref[SLABS - 1 : SLABS] = fetch(south, 0, 1)
    for ref, at, north, south in ((ow, 0, 5, 0), (oe, SLABS, 11, 6)):
        ref[...] = empty
        ref[0:GROUPS] = own[at : at + GROUPS]
        ref[GROUPS : GROUPS + 1] = turn(strips[3][north:north + 1], 16)
        ref[SLABS - 1 : SLABS] = turn(strips[2][south:south + 1], 16)

    def spread(ref, j):
        a = START[j]
        first, second = ref[comb(a, SLABS), :], ref[comb(a + 1, SLABS), :]
        third = ref[comb(a + 2, SLABS), :] if a + 2 < PLANES else second
        left = turn(jnp.where(lane >= OFF[j], first, second), -OFF[j])
        right = turn(jnp.where(lane >= OFF[j], second, third), -OFF[j])
        return left, right

    def seam_row(left, right, slab_at, lanes_at):
        east = turn(pe[slab_at : slab_at + 1], 112 - lanes_at)
        west = turn(pw[slab_at : slab_at + 1], 124 - lanes_at)
        right = jnp.where(one < 112, right, jnp.where(one < 116, east, jnp.where(one >= 124, west, 0.0)))
        return jnp.broadcast_to(left, (SLABS, LANES)), jnp.broadcast_to(right, (SLABS, LANES))

    seams = {
        0: ((0, seam_row(strips[2][18:19], strips[2][19:20], SLABS - 1, 28)),
            (GROUPS, seam_row(own[50:51], own[51:52], GROUPS - 1, 28))),
        GROUP - 1: ((GROUPS - 1, seam_row(strips[3][18:19], strips[3][19:20], GROUPS, 12)),
                    (SLABS - 1, seam_row(own[48:49], own[49:50], 0, 12))),
    }
    weight = STERIC / levels

    def missing(target, term, term_out, d, d_out, g):
        term, term_out, d, d_out, g = (
            turn(value[0], target - value[1]) for value in (term, term_out, d, d_out, g)
        )
        term = jnp.where(d > 0, weight * term, 0.0)
        term_out = jnp.where(d_out > 0, weight * term_out, 0.0)
        return jnp.where(one == target, g * term + d * d_out * (term - term_out), 0.0)

    def ring(ref, at):
        return ref[at : at + 1]

    outer = {j: [] for j in range(GROUP)}
    for j, at, beyond, o, lanes in ((0, 0, SLABS - 1, 0, 28), (GROUP - 1, GROUPS - 1, GROUPS, 16, 12)):
        own_row, corner = ring(pe, at), ring(pe, beyond)
        outer[j].append((1, at, missing(
            114, (corner, lanes + 2), (corner, lanes + 3), (own_row, o + 5), (own_row, o + 11), (own_row, o + 10),
        )))
        own_row, corner = ring(pw, at), ring(pw, beyond)
        outer[j].append((1, at, missing(
            125, (corner, lanes + 1), (corner, lanes), (own_row, o + 3), (own_row, o + 11), (own_row, o + 10),
        )))
    for j, at, c, j_out, d_l, d_r in ((2, GROUPS, 3, 3, (9, 96), (11, 79)), (5, SLABS - 1, 2, 4, (6, 48), (8, 31))):
        line_l, line_r = strips[c][16:17], strips[c][17:18]
        corner = ring(pw, at)
        outer[j].append((0, at, line_l + missing(
            0, (corner, OFF[j] + 9), (corner, OFF[j_out] + 9), (strips[c][d_l[0]:d_l[0] + 1], d_l[1]),
            (line_r, 113), (line_r, 112),
        )))
        corner = ring(pe, at)
        outer[j].append((1, at, jnp.where(one < 112, line_r, 0.0) + missing(
            111, (corner, OFF[j] + 9), (corner, OFF[j_out] + 9), (strips[c][d_r[0]:d_r[0] + 1], d_r[1]),
            (line_r, 115), (line_r, 114),
        )))
    for j in range(GROUP):
        o = OFF[j]
        inside = slab < GROUPS
        halves = [
            jnp.zeros((SLABS, LANES), jnp.float32),
            jnp.where(
                jnp.logical_and(inside, lane == 114), turn(pe[...], 114 - o - 8),
                jnp.where(jnp.logical_and(inside, lane == 125), turn(pw[...], 125 - o - 8), 0.0),
            ),
        ]
        for half, at, line in outer[j]:
            halves[half] = halves[half] + jnp.where(slab == at, line, 0.0)
        ex[j, :, 0:LANES] = halves[0]
        ex[j, :, LANES:] = halves[1]

        def rim(right, q, width):
            east = turn(pe[...], 112 - o - q)
            west = turn(pw[...], 128 - width - o - q)
            value = jnp.where(lane < 112 + width, east, jnp.where(lane >= 128 - width, west, 0.0))
            return jnp.where(lane < 112, right, value)

        left, right = spread(fd, j)
        right = rim(right, 3, 3)
        wet_l = jnp.where(left > 0, weight, 0.0)
        wet_r = jnp.where(right > 0, weight, 0.0)
        ed[j, :, 0:LANES] = left
        ed[j, :, LANES:] = right
        left, right = spread(fg, j)
        eg[j, :, 0:LANES] = left
        eg[j, :, LANES:] = rim(right, 6, 2)
        left, right = spread(fb, j)
        right = rim(right, 0, 3)
        seam_l = jnp.where(lane == 0, turn(pw[...], -o - 9), 0.0)
        seam_r = jnp.where(lane == 127, turn(ow[...], 127 - o - 9), 0.0)
        seam_r = jnp.where(lane == 111, turn(pe[...], 111 - o - 9), seam_r)
        seam_r = jnp.where(lane == 112, turn(oe[...], 112 - o - 9), seam_r)
        for at, (row_l, row_r) in seams.get(j, ()):
            seam_l = seam_l + jnp.where(slab == at, row_l, 0.0)
            seam_r = seam_r + jnp.where(slab == at, row_r, 0.0)
        vectors[0, j, :, 0:LANES] = left + wet_l * seam_l
        vectors[0, j, :, LANES:] = right + wet_r * seam_r

    for j in range(GROUP):
        d = ed[j]
        we[j] = d * turn(d, -1)
        above = ed[j + 1] if j < GROUP - 1 else turn(ed[0], -1, 0)
        wn[j] = d * above

    top = jnp.max(came[pl.ds(RIM_ROWS - 1, count, stride=slot), :], axis=0, keepdims=True)
    top = jnp.max(jnp.where(one == LANES - 1, top, 0.0), axis=1, keepdims=True)
    scale = STRETCH / top

    big = (SLABS, 2 * LANES)
    mine = jnp.logical_and(row_of(big) < GROUPS, lane_of(big) < SPAN_X)
    pair = 0
    for k in range(5):
        count_sums = min(k + 1, 4)
        sums = [None] * count_sums
        new = None if k == 4 else vectors.at[k]
        if k:
            v = vectors.at[k - 1]
            flow_below = wn[GROUP - 1] * (v[GROUP - 1] - turn(v[0], -1, 0))
            flow_below = turn(flow_below, 1, 0)
        for j in range(GROUP):
            if k:
                here = v[j]
                above = v[j + 1] if j < GROUP - 1 else turn(v[0], -1, 0)
                flow_x = we[j] * (here - turn(here, -1))
                flow_y = wn[j] * (here - above)
                image = eg[j] * here + (flow_x - turn(flow_x, 1)) + (flow_y - flow_below)
                if k == 1:
                    image = image + ex[j]
                fresh = scale * image - (STRETCH * ROOTS[k - 1]) * here
                flow_below = flow_y
                if k < 4:
                    new[j] = fresh
            else:
                fresh = new[j]
            held = jnp.where(mine, fresh, 0.0)
            for i in range(count_sums):
                other = vectors[i, j] if i < k else held
                value = held * other
                sums[i] = value if sums[i] is None else sums[i] + value
        for i in range(count_sums):
            rows[pair : pair + 1] = jnp.sum(sums[i][:, 0:LANES] + sums[i][:, LANES:], axis=0, keepdims=True)
            pair += 1
    rows[pair : pair + 1] = jnp.where(one == 0, top, 0.0)
    rows[pair + 1 : 16] = jnp.zeros((15 - pair, LANES), jnp.float32)
    total = jnp.sum(rows[...], axis=1, keepdims=True)
    spot = lane_of((16, LANES)) == gram_lane(row_of((16, LANES)))
    line = jnp.sum(jnp.where(spot, total, 0.0), axis=0, keepdims=True)
    line = jnp.broadcast_to(line, (count, LANES))
    if first == 0:
        line = jnp.where(lane_of((count, LANES)) % 16 < 12, hand[pl.ds(0, count, stride=share), :], line)
    hand[pl.ds(0, count, stride=share), :] = line


def finish_kernel(
    levels, per, hands, vectors, edges, inner, tracer_out, surface_out,
    cells, flat, left, right, message, out_sems,
):
    count = hands.shape[0]
    _, runs, share, first = pieces_of(levels, count)
    came = hands.reshape(count * share, LANES)
    steps = levels // per
    chunks = [pl.ds(step * per * ROWS, per * ROWS) for step in range(steps)]
    results = []

    for c in range(4):
        for j, device, low, size in runs[c ^ 1]:
            value = came[pl.ds(device * share + first + j, size, stride=share), :]
            message[c, low : low + size] = value
    second = lane_of((SLABS, LANES)) % 16 == 1
    sums = []
    for k in range(levels):
        value = edges[2 * levels - 1] * jnp.concatenate([
            jnp.where(second, turn(message[1], 1 - k), turn(message[0], -k)),
            message[2, k : k + 1], message[2, k + levels : k + levels + 1],
            message[3, k : k + 1], message[3, k + levels : k + levels + 1],
            jnp.zeros((EDGE - SLABS - 4, LANES), jnp.float32),
        ], axis=0)
        if k:
            value = value + edges[2 * levels + k - 1] * sums[-1]
        sums.append(value * edges[levels - 1 + k])
    for k in range(levels - 2, -1, -1):
        sums[k] = sums[k] + edges[k] * sums[k + 1]
    lane = lane_of((GROUPS, LANES))
    slab = row_of((GROUPS, LANES))
    for k in range(levels):
        west = sums[k][0:GROUPS]
        east = turn(west, -18)
        south_l, south_r = sums[k][SLABS : SLABS + 1], sums[k][SLABS + 1 : SLABS + 2]
        north_l = turn(sums[k][SLABS + 2 : SLABS + 3], 16)
        north_r = turn(sums[k][SLABS + 3 : SLABS + 4], 16)
        for a in range(PLANES):
            rim = None
            for at, source in [(at, west) for at in FIRST_OF[a]] + [(at, east) for at in LAST_OF[a]]:
                rim = jnp.where(lane == at, source, 0.0 if rim is None else rim)
            rows = comb(k * ROWS + a)
            if rim is None:
                cells[rows, :] = inner[rows, :]
                continue
            if a == 0:
                rim = rim + jnp.where(slab == 0, south_l, 0.0)
            if a == 1:
                rim = rim + jnp.where(jnp.logical_and(slab == 0, lane < 112), south_r, 0.0)
            if a == PLANES - 2:
                rim = rim + jnp.where(jnp.logical_and(slab == GROUPS - 1, lane >= 16), north_l, 0.0)
            if a == PLANES - 1:
                rim = rim + jnp.where(slab == GROUPS - 1, jnp.where(lane < 16, north_l, north_r), 0.0)
            cells[rows, :] = inner[rows, :] + rim
        if k % per == per - 1:
            step = k // per
            copy = pltpu.make_async_copy(
                cells.at[chunks[step]], tracer_out.at[chunks[step]], out_sems.at[1 + step]
            )
            copy.start()
            results.append(copy)

    row = jnp.sum(came[pl.ds(0, count, stride=share), :], axis=0, keepdims=True)
    one = lane_of((1, LANES))
    entry = {}
    pair = 0
    for k in range(5):
        for i in range(min(k + 1, 4)):
            value = jnp.sum(jnp.where(one == gram_lane(pair), row, 0.0), axis=1, keepdims=True)
            entry[i, k] = entry[k, i] = value
            pair += 1
    top = jnp.sum(jnp.where(one == gram_lane(pair), row, 0.0), axis=1, keepdims=True) * (1.0 / count)

    def image(c):
        out = [None] * 5
        for k in range(4):
            if c[k] is None:
                continue
            low = ROOTS[k] * c[k]
            out[k] = low if out[k] is None else out[k] + low
            out[k + 1] = (1.0 / STRETCH) * c[k]
        return out

    def dot(a, b):
        total = None
        for i in range(5):
            if a[i] is None:
                continue
            inner = None
            for j in range(5):
                if b[j] is not None:
                    value = entry[i, j] * b[j]
                    inner = value if inner is None else inner + value
            total = a[i] * inner if total is None else total + a[i] * inner
        return total

    def axpy(a, s, b):
        return [
            x if y is None else (s * y if x is None else x + s * y) for x, y in zip(a, b)
        ]

    r = [jnp.ones((1, 1), jnp.float32)] + [None] * 4
    p = list(r)
    x = [None] * 5
    rr = entry[0, 0]
    for n in range(ITERS):
        q = image(p)
        step = rr / jnp.maximum(dot(p, q), TINY)
        step = jnp.clip(step, top * (1.0 / HIGH_RATE), top * (1.0 / LOW_RATE))
        x = axpy(x, step, p)
        if n < ITERS - 1:
            r = axpy(r, -step, q)
            fresh = jnp.maximum(dot(r, r), 0.0)
            p = axpy(r, fresh / jnp.maximum(rr, TINY), p)
            rr = fresh
    factors = [c / top for c in x[:4]]
    for j in range(GROUP):
        value = None
        for k in range(4):
            term = factors[k] * vectors[k, j]
            value = term if value is None else value + term
        left[j] = turn(value[:, 0:LANES], OFF[j])
        right[j] = turn(value[:, LANES:], OFF[j])
    lane = lane_of((SLABS, LANES))
    for a in range(PLANES):
        value = None
        for j in range(GROUP):
            for half, ref in ((0, left), (1, right)):
                low = max(SPAN_X * j + LANES * half - LANES * a, 0)
                high = min(SPAN_X * j + (LANES if half == 0 else SPAN_X) - LANES * a, LANES)
                if low >= high:
                    continue
                value = ref[j] if value is None else jnp.where(lane >= low, ref[j], value)
        flat[comb(a), :] = value[0:GROUPS]
    results.append(pltpu.make_async_copy(flat, surface_out.reshape(ROWS, LANES), out_sems.at[0]))
    results[-1].start()
    for copy in results:
        copy.wait()


def tracer_kernel(
    levels, per, sides, around, temp_in, zonal_in, merid_in, rates_in, fields,
    out, edges,
    temp, zonal, merid, rates, ocean,
    te, tw, tn, ts, stepped, border, sems,
):
    steps = levels // per
    pairs = []
    for step in range(steps):
        chunk = pl.ds(step * per * ROWS, per * ROWS)
        pairs += [
            (a.at[chunk], b.at[chunk]) for a, b in ((temp_in, temp), (zonal_in, zonal), (merid_in, merid))
        ]
    copies = fetching(pairs + [(rates_in.reshape((levels - 1) * ROWS, LANES), rates)], sems)
    lane = lane_of((GROUPS, LANES))
    one = lane_of((1, LANES))
    clear_terms(tn, ts)

    ocean[...] = jnp.where(fields[HELD : HELD + ROWS] > 0, 1.0, 0.0)
    for step in range(steps):
        for copy in copies[3 * step : 3 * step + 3]:
            copy.wait()

        def level(k, carry):
            t, u, v = (Level(ref, k * ROWS) for ref in (temp, zonal, merid))
            for a in range(PLANES):
                own = t.plane(a)
                quarter = ADVECT * own
                store_terms(a, own, u.plane(a) * quarter, v.plane(a) * quarter, te, tw, tn, ts)
            for a in range(PLANES):
                own = t.plane(a)
                change = inner_sum(a, te, tw, tn, ts) - 4.0 * DIFFUSE * own
                stepped[k, a] = own + ocean[comb(a), :] * change
            return carry

        lax.fori_loop(step * per, step * per + per, level, 0)
    copies[-1].wait()

    def block(a, carry):
        for low in range(0, GROUPS, 8):
            size = min(8, GROUPS - low)

            def rows(k):
                return pl.ds(k * ROWS + low * PLANES + a, size, stride=PLANES)

            gains = []
            sums = []
            for k in range(levels):
                value = stepped[k, a, low : low + size]
                pivot = 1.0
                if k > 0:
                    pivot = pivot + upper - upper * gains[-1]
                    value = value + upper * sums[-1]
                if k < levels - 1:
                    lower = rates[rows(k), :]
                    inverse = 1.0 / (pivot + lower)
                    gains.append(lower * inverse)
                    upper = lower
                else:
                    inverse = 1.0 / pivot
                sums.append(value * inverse)
            result = sums[-1]
            out[rows(levels - 1), :] = result
            for k in range(levels - 2, -1, -1):
                result = sums[k] + gains[k] * result
                out[rows(k), :] = result
        return carry

    lax.fori_loop(0, PLANES, block, 0)

    def edge(ref, base, at):
        def get(a):
            return ref[comb(base + a), :].astype(jnp.float32)

        border[0:GROUPS] = jnp.where(
            lane % 16 == 1, turn(choose(LAST, lane, get), 18), choose(START, lane, get)
        )
        border[SLABS : SLABS + 2] = ref[base : base + 2, :].astype(jnp.float32)
        rows = ref[base + ROWS - 2 : base + ROWS, :].astype(jnp.float32)
        border[SLABS + 2 : SLABS + 3] = turn(jnp.where(one >= 16, rows[0:1], rows[1:2]), -16)
        border[SLABS + 3 : SLABS + 4] = turn(rows[1:2], -16)
        edges[at] = border[...]

    border[...] = jnp.zeros_like(border)
    edge(ocean, 0, 2 * levels - 1)
    for c in (2, 3):
        rows = pl.ds(SLABS + 2 * (c - 2), 2)
        value = edges[2 * levels - 1, rows]
        edges[2 * levels - 1, rows] = jnp.where(around[sides + c] >= 0, value, 0.0)
    gain = None
    for k in range(levels):
        pivot = 1.0
        if k > 0:
            upper = edges[2 * levels + k - 1]
            pivot = pivot + upper - upper * gain
        if k < levels - 1:
            edge(rates, k * ROWS, 2 * levels + k)
            lower = edges[2 * levels + k]
            inverse = 1.0 / (pivot + lower)
            gain = lower * inverse
            edges[k] = gain
        else:
            inverse = 1.0 / pivot
        edges[levels - 1 + k] = inverse


def on_device(
    thermal_anomaly,
    zonal_flow_ratio,
    meridional_flow_ratio,
    diffusion_rates,
    ocean_bottom_scaled,
    ocean_indicator,
    operator_diagonal,
    elevation_source,
    block_positions,
):
    levels, cells = thermal_anomaly.shape[1:]
    nx = lax.axis_size("gx")
    ny = lax.axis_size("gy")
    count = block_positions.shape[0]
    planes = (ocean_bottom_scaled, ocean_indicator, operator_diagonal, elevation_source)
    depth, ocean, diag, source = planes
    f32 = jnp.float32
    per = next(n for n in (4, 2, 6, levels) if levels % n == 0 and n * ROWS % 8 == 0)
    steps = levels // per
    few = next(n for n in (4, 2, 6, levels) if levels % n == 0 and n * ROWS % 8 == 0)
    params = pltpu.CompilerParams(vmem_limit_bytes=BUDGET)
    temp, zonal, merid = (
        array.reshape(levels * ROWS, LANES)
        for array in (thermal_anomaly, zonal_flow_ratio, meridional_flow_ratio)
    )
    rates = diffusion_rates.reshape(levels - 1, 1, cells)
    temp, zonal, merid, rates, depth, ocean, diag, source, positions = (
        pltpu.with_memory_space_constraint(array, pltpu.HBM)
        for array in (temp, zonal, merid, rates, depth, ocean, diag, source, block_positions)
    )
    hbm = pl.BlockSpec(memory_space=pltpu.HBM)
    here = pl.BlockSpec(memory_space=pltpu.VMEM)

    def vmem(*shape, kind=f32):
        return pltpu.VMEM(shape, kind)

    def out(*shape, kind=f32):
        return jax.ShapeDtypeStruct(shape, kind)

    def sems(number):
        return pltpu.SemaphoreType.DMA((number,))

    deep = vmem(levels * ROWS, LANES)
    flat = vmem(ROWS, LANES)
    flat_int = vmem(ROWS, LANES, kind=jnp.int32)
    plane = vmem(PLANES, GROUPS, LANES)
    tall = vmem(PLANES, 40, LANES)
    numbers = pltpu.SMEM((count,), jnp.int32)
    number_pieces, _, share, _ = pieces_of(levels, count)
    slot = RIM_ROWS + number_pieces
    fields, slots, around = pl.pallas_call(
        functools.partial(forcing_kernel, levels, few, nx, ny),
        in_specs=[hbm] * 8,
        out_specs=[here, hbm, hbm],
        out_shape=[
            out(FIELDS, LANES), pltpu.HBM((count, 1, slot * LANES), f32), out(4 * count + 8, kind=jnp.int32),
        ],
        scratch_shapes=[deep] * 3 + [flat, flat_int, flat]
        + [vmem(count * slot, LANES)]
        + [flat] * 3 + [plane] * 3 + [tall] * 2
        + [vmem(4, 2 * levels, LANES), numbers, numbers]
        + [pltpu.SMEM((4 * count + 8,), jnp.int32), sems(3 * (levels // few) + 5), sems(2)],
        compiler_params=params,
        name="forcing",
    )(positions, temp, zonal, merid, depth, ocean, diag, source)
    rims = lax.all_to_all(slots, BOTH, 0, 0, tiled=True)

    inner, edges = pl.pallas_call(
        functools.partial(tracer_kernel, levels, per, 4 * count),
        in_specs=[SMEM] + [hbm] * 4 + [here],
        out_specs=[here] * 2,
        out_shape=[out(levels * ROWS, LANES), out(3 * levels - 1, EDGE, LANES)],
        scratch_shapes=[deep] * 3 + [vmem((levels - 1) * ROWS, LANES), flat]
        + [plane] * 2 + [tall] * 2
        + [vmem(levels, PLANES, GROUPS, LANES), vmem(EDGE, LANES), sems(3 * steps + 1)],
        compiler_params=params,
        name="tracer",
    )(around, temp, zonal, merid, rates, fields)

    rims, edges = lax.optimization_barrier((rims, edges))
    extended = vmem(GROUP, SLABS, 2 * LANES)
    vectors, hand = pl.pallas_call(
        functools.partial(solve_kernel, levels, ny),
        in_specs=[pl.BlockSpec(memory_space=pl.ANY)] + [here] * 2,
        out_specs=[here] * 2,
        out_shape=[out(4, GROUP, SLABS, 2 * LANES), out(count, 1, share * LANES)],
        scratch_shapes=[pltpu.SMEM((4 * count + 8,), jnp.int32), sems(1)]
        + [vmem(SLABS, LANES)] * 2 + [vmem(WIDE, LANES)] * 3 + [vmem(SLABS, LANES)] * 4 + [extended] * 5 + [vmem(16, LANES)],
        compiler_params=params,
        name="vectors",
    )(around, rims, fields)
    hands = lax.all_to_all(hand, BOTH, 0, 0, tiled=True)

    new_temp, surface = pl.pallas_call(
        functools.partial(finish_kernel, levels, per),
        in_specs=[here] * 4,
        out_specs=[hbm] * 2,
        out_shape=[out(levels * ROWS, LANES), out(1, cells)],
        scratch_shapes=[
            deep, flat, vmem(GROUP, SLABS, LANES), vmem(GROUP, SLABS, LANES), vmem(4, 2 * levels, LANES),
            sems(1 + steps),
        ],
        compiler_params=params,
        name="finish",
    )(hands, vectors, edges, inner)
    return new_temp.reshape(1, levels, cells), surface


def solution(mesh):
    deep = P(BOTH, None, None)
    flat = P(BOTH, None)
    return jax.shard_map(
        on_device,
        mesh=mesh,
        in_specs=(deep, deep, deep, deep, flat, flat, flat, flat, P()),
        out_specs=(deep, flat),
        check_vma=False,
    )
```

```python
import functools

import jax
import jax.numpy as jnp
from jax import lax
from jax.experimental import pallas as pl
from jax.experimental.pallas import tpu as pltpu
from jax.sharding import PartitionSpec as P

ITERS = 4
SPAN_X = 240
SPAN_Y = 160
RIM = 4
ADVECT = 0.25
DIFFUSE = 0.12
STERIC = 0.5
LOW_RATE = 0.05
HIGH_RATE = 32.5
ROOTS = (0.02, 0.35, 0.1, 0.2)
STRETCH = 4.0
TINY = 1e-30
BOTH = ("gx", "gy")
SIDES = ((-1, 0), (1, 0), (0, -1), (0, 1), (-1, -1), (1, -1), (-1, 1), (1, 1))

LANES = 128
GROUP = 8
GROUPS = SPAN_Y // GROUP
PLANES = GROUP * SPAN_X // LANES
ROWS = GROUPS * PLANES
SLABS = GROUPS + 4
WIDE = SLABS * PLANES
START = [SPAN_X * j // LANES for j in range(GROUP)]
OFF = [SPAN_X * j % LANES for j in range(GROUP)]
LAST = [(SPAN_X * j + SPAN_X - 1) // LANES for j in range(GROUP)]
END = [(SPAN_X * j + SPAN_X - 1) % LANES for j in range(GROUP)]
FIRST_OF = [[OFF[j] for j in range(GROUP) if START[j] == a] for a in range(PLANES)]
LAST_OF = [[END[j] for j in range(GROUP) if LAST[j] == a] for a in range(PLANES)]
RIM_ROWS = 20
HELD = -(-ROWS // 8) * 8
PACKS = 3 * HELD
FIELDS = PACKS + 56
EDGE = 32
BUDGET = 32 * 1024 * 1024


def turn(value, shift, axis=1):
    shift = shift % value.shape[axis]
    return value if shift == 0 else pltpu.roll(value, shift, axis)


def fetching(pairs, sems):
    copies = [pltpu.make_async_copy(a, b, sems.at[n]) for n, (a, b) in enumerate(pairs)]
    for copy in copies:
        copy.start()
    return copies


def pieces_of(levels, count):
    rows = 2 * levels
    number = -(-4 * rows // count)
    runs = [[] for _ in range(4)]
    for c in range(4):
        for j in range(number):
            low, high = max(c * rows, j * count), min((c + 1) * rows, (j + 1) * count)
            if low < high:
                runs[c].append((j, low - j * count, low - c * rows, high - low))
    merged = count <= 2 * rows and levels <= 12
    return number, runs, number + (0 if merged else 1), 0 if merged else 1


def gram_lane(n):
    return 16 * (n // 4) + 12 + n % 4


class Level:
    def __init__(self, ref, base):
        self.ref, self.base = ref, base

    def plane(self, a):
        return self.ref[comb(self.base + a), :]

    def rows(self, low, size):
        return self.ref[pl.ds(self.base + low, size), :]


def lane_of(shape):
    return lax.broadcasted_iota(jnp.int32, shape, len(shape) - 1)


def row_of(shape):
    return lax.broadcasted_iota(jnp.int32, shape, 0)


def comb(a, count=GROUPS):
    return pl.ds(a, count, stride=PLANES)


def line_of(get, y):
    lane = lane_of((1, LANES))
    j = y % GROUP
    row = y // GROUP * PLANES + START[j]
    first, second = get(row), get(row + 1)
    third = get(row + 2) if START[j] + 2 < PLANES else second
    left = turn(jnp.where(lane >= OFF[j], first, second), -OFF[j])
    right = turn(jnp.where(lane >= OFF[j], second, third), -OFF[j])
    return left, right


def drop(value, lanes, lane):
    for at in lanes:
        value = jnp.where(lane == at, 0.0, value)
    return value


def store_terms(a, temp, flow_x, flow_y, te, tw, tn, ts):
    spread = DIFFUSE * temp
    te[a] = spread - flow_x
    tw[a] = spread + flow_x
    tn[a, 8 : 8 + GROUPS] = spread - flow_y
    ts[a, 8 : 8 + GROUPS] = spread + flow_y


def clear_terms(tn, ts):
    none = jnp.zeros((PLANES, 1, LANES), jnp.float32)
    for ref in (tn, ts):
        ref[:, 7:8] = none
        ref[:, 8 + GROUPS : 9 + GROUPS] = none


def inner_sum(a, te, tw, tn, ts):
    lane = lane_of((GROUPS, LANES))
    here = te[a]
    east = here if a == PLANES - 1 else jnp.where(lane == 0, te[a + 1], here)
    east = drop(turn(east, -1), LAST_OF[a], lane)
    here = tw[a]
    west = here if a == 0 else jnp.where(lane == LANES - 1, tw[a - 1], here)
    west = drop(turn(west, 1), FIRST_OF[a], lane)

    def plane(ref, at):
        down = 8 + (at >= PLANES) - (at < 0)
        return ref[at % PLANES, down : down + GROUPS]

    north = turn(jnp.where(lane >= LANES - 16, plane(tn, a + 1), plane(tn, a + 2)), 16)
    south = turn(jnp.where(lane < 16, plane(ts, a - 1), plane(ts, a - 2)), -16)
    return east + west + north + south


def choose(planes, lane, get):
    shift = 32 if planes is LAST else 0
    lows = sorted(((OFF[j] - shift) % LANES, planes[j]) for j in range(GROUP))
    value = get(lows[-1][1])
    for low, a in reversed(lows[:-1]):
        value = jnp.where(lane < low + 16, get(a), value)
    return value


def forcing_kernel(
    levels, per, tiles_x, tiles_y,
    pos_in, temp_in, zonal_in, merid_in, depth_in, ocean_in, diag_in, source_in,
    fields, slots_out, around_out,
    temp, zonal, merid, depth, ocean, source, slots,
    st, sx, sy, pt, te, tw, tn, ts, edges, pos, holder, around, sems, out_sems,
):
    count = pos.shape[0]
    steps = levels // per
    number_pieces, runs, _, _ = pieces_of(levels, count)
    slot = RIM_ROWS + number_pieces
    pairs = []
    for step in range(steps):
        chunk = pl.ds(step * per * ROWS, per * ROWS)
        pairs += [
            (a.at[chunk], b.at[chunk]) for a, b in ((temp_in, temp), (zonal_in, zonal), (merid_in, merid))
        ]
    pairs += [
        (a.reshape(ROWS, LANES), b)
        for a, b in (
            (source_in, source), (ocean_in, ocean), (depth_in, depth),
            (diag_in, fields.at[pl.ds(2 * HELD, ROWS)]),
        )
    ]
    copies = fetching([(pos_in, pos)] + pairs, sems)
    copies.pop(0).wait()
    results = []

    def send(value, target):
        copy = pltpu.make_async_copy(value, target, out_sems.at[len(results)])
        copy.start()
        results.append(copy)

    lane = lane_of((GROUPS, LANES))
    one = lane_of((1, LANES))
    q = lane % 16
    edges[...] = jnp.zeros_like(edges)

    def number(d, carry):
        holder[pos[d]] = d
        return carry

    lax.fori_loop(0, count, number, 0)
    me = lax.axis_index("gx") * tiles_y + lax.axis_index("gy")
    here = pos[me]
    row = here // tiles_x
    column = here % tiles_x
    sides = []
    for c, (dx, dy) in enumerate(SIDES):
        there = row + dy
        inside = jnp.logical_and(there >= 0, there < tiles_y)
        target = jnp.where(inside, there, 0) * tiles_x + (column + dx + tiles_x) % tiles_x
        device = jnp.where(inside, holder[target], -1)
        around[4 * count + c] = device
        sides.append(device)

    def look(y, carry):
        line = [holder[y * tiles_x + x] for x in range(tiles_x)]
        below = [holder[jnp.maximum(y - 1, 0) * tiles_x + x] for x in range(tiles_x)]
        above = [holder[jnp.minimum(y + 1, tiles_y - 1) * tiles_x + x] for x in range(tiles_x)]
        for x, device in enumerate(line):
            for c, other in enumerate((line[x - 1], line[(x + 1) % tiles_x], below[x], above[x])):
                around[c * count + device] = other * slot + RIM_ROWS
        return carry

    lax.fori_loop(0, tiles_y, look, 0)
    send(around, around_out)
    clear_terms(tn, ts)

    def add(flats, low, size, fresh):
        rows = pl.ds(low, size)
        total = [None] * 3
        for t, u, v in zip(*flats):
            t = t.rows(low, size)
            new = (t, t * u.rows(low, size), t * v.rows(low, size))
            total = [b if a is None else a + b for a, b in zip(total, new)]
        for ref, value in zip((st, sx, sy), total):
            ref[rows, :] = value if fresh else ref[rows, :] + value

    for step in range(steps):
        for copy in copies[3 * step : 3 * step + 3]:
            copy.wait()
        flats = [
            [Level(ref, (step * per + n) * ROWS) for n in range(per)] for ref in (temp, zonal, merid)
        ]

        for m in range(ROWS // 8):
            add(flats, m * 8, 8, step == 0)
        if ROWS % 8:
            add(flats, ROWS - ROWS % 8, ROWS % 8, step == 0)

        for n in range(per):
            k = step * per + n
            t, u, v = (flat[n] for flat in flats)

            def term(planes, sign):
                own = choose(planes, lane, t.plane)
                flow = choose(planes, lane, u.plane)
                return DIFFUSE * own + sign * ADVECT * (flow * own)

            edges[0, 0:GROUPS] = jnp.where(q == k, turn(term(START, -1.0), k), edges[0, 0:GROUPS])
            edges[1, 0:GROUPS] = jnp.where(q == k, turn(term(LAST, 1.0), k + 17), edges[1, 0:GROUPS])
            rows = t.rows(0, 2)
            rows = DIFFUSE * rows - ADVECT * (v.rows(0, 2) * rows)
            edges[2, k : k + 1] = rows[0:1]
            edges[2, k + levels : k + levels + 1] = rows[1:2]
            rows = t.rows(ROWS - 2, 2)
            rows = DIFFUSE * rows + ADVECT * (v.rows(ROWS - 2, 2) * rows)
            edges[3, k : k + 1] = turn(jnp.where(one >= 16, rows[0:1], rows[1:2]), -16)
            edges[3, k + levels : k + levels + 1] = turn(rows[1:2], -16)

    for c in range(4):
        for j, device, low, size in runs[c]:
            slots[pl.ds(device * slot + RIM_ROWS + j, size, stride=slot), :] = edges[c, low : low + size]

    for copy in copies[3 * steps :]:
        copy.wait()

    part = fields.at[pl.ds(0, HELD)]
    mask = fields.at[pl.ds(HELD, HELD)]
    diag = fields.at[pl.ds(2 * HELD, HELD)]
    own = fields.at[pl.ds(PACKS, 56)]
    mask[0:ROWS] = depth[...] * ocean[...].astype(jnp.float32)

    def wet_of(rows):
        return ocean[rows, :].astype(jnp.float32)

    def masked(rows):
        return mask[rows, :]

    for a in range(PLANES):
        total = st[comb(a), :]
        pt[a] = total
        store_terms(a, total, ADVECT * sx[comb(a), :], ADVECT * sy[comb(a), :], te, tw, tn, ts)
    for a in range(PLANES):
        total = pt[a]
        wet = wet_of(comb(a))
        change = inner_sum(a, te, tw, tn, ts) - 4.0 * DIFFUSE * total
        part[comb(a), :] = source[comb(a), :] + (STERIC / levels) * wet * (total + wet * change)

    def mix(*values):
        value = values[-1]
        for at, low in ((6, 12), (5, 11), (4, 10), (3, 9), (2, 8), (1, 6), (0, 3)):
            value = jnp.where(q < low, values[at], value)
        return value

    def ends(planes, low):
        value = tn[planes[0], 8 : 8 + GROUPS]
        last = jnp.logical_and(lane >= low, lane < low + 16)
        return jnp.where(last, ts[planes[7], 8 : 8 + GROUPS], value)

    def beside(b, d, g, b_out, d_out):
        return g * b + d * d_out * (b - b_out)

    bp = choose(START, lane, lambda a: part[comb(a), :])
    dp = choose(START, lane, lambda a: masked(comb(a)))
    gp = choose(START, lane, lambda a: diag[comb(a), :])
    pp = beside(bp, dp, gp, turn(bp, -1), turn(dp, -1))
    pack_w = mix(
        bp, turn(dp, 3), turn(gp, 6), turn(pp, 6), turn(choose(START, lane, lambda a: te[a]), 9),
        turn(gp, 8), turn(dp, 8), turn(ends(START, OFF[7]), 12),
    )
    bp = choose(LAST, lane, lambda a: part[comb(a), :])
    dp = choose(LAST, lane, lambda a: masked(comb(a)))
    gp = choose(LAST, lane, lambda a: diag[comb(a), :])
    pp = beside(bp, dp, gp, turn(bp, 1), turn(dp, 1))
    pack_e = mix(
        turn(bp, 19), turn(dp, 22), turn(gp, 24), turn(pp, 27),
        turn(choose(LAST, lane, lambda a: tw[a]), 26),
        turn(gp, 29), turn(dp, 31), turn(ends(LAST, LANES - 16), 32),
    )
    own[0:GROUPS] = pack_w
    own[SLABS : SLABS + GROUPS] = pack_e
    north_l = tn[0, 8:9]
    north_r = tn[1, 8:9]
    south_13 = ts[PLANES - 2, 7 + GROUPS : 8 + GROUPS]
    south_14 = ts[PLANES - 1, 7 + GROUPS : 8 + GROUPS]
    south_l = turn(jnp.where(one >= 16, south_13, south_14), -16)
    south_r = turn(south_14, -16)
    own[48:49] = north_l
    own[49:50] = north_r
    own[50:51] = south_l
    own[51:52] = south_r
    deep = jnp.max(masked(slice(0, ROWS)), axis=(0, 1), keepdims=True)
    top = jnp.max(diag[0:ROWS], axis=(0, 1), keepdims=True) + 8.0 * deep * deep
    top = jnp.broadcast_to(top, (1, LANES))

    slots[pl.ds(RIM_ROWS - 1, count, stride=slot), :] = jnp.broadcast_to(top, (count, LANES))
    block_lane = lane_of((6, LANES))
    block_row = row_of((6, LANES))
    for c, first, rows_l, rows_r in ((2, True, north_l, north_r), (3, False, south_l, south_r)):
        base = 0 if first else ROWS - 6
        if first:
            spare = jnp.logical_and(block_row == 5, block_lane >= 80)
        else:
            spare = jnp.logical_and(block_row == 0, block_lane < 48)
        g = 0 if first else GROUPS - 1
        blocks = []
        block = slice(base, base + 6)
        for value, at in ((part[block, :], g), (masked(block), SLABS + g)):
            extra = jnp.broadcast_to(turn(own[at : at + 1], -16), (6, LANES))
            blocks.append(jnp.where(spare, extra, value))
        low = 0 if first else ROWS - 4
        diag_rows = diag[low : low + 4, :]
        third, fourth = (2, 3) if first else (SPAN_Y - 3, SPAN_Y - 4)
        b_l, b_r = line_of(lambda n: part[n : n + 1, :], third)
        d_l, d_r = line_of(lambda n: masked(slice(n, n + 1)), third)
        g_l, g_r = line_of(lambda n: diag[n : n + 1, :], third)
        bo_l, bo_r = line_of(lambda n: part[n : n + 1, :], fourth)
        do_l, do_r = line_of(lambda n: masked(slice(n, n + 1)), fourth)
        out_l = beside(b_l, d_l, g_l, bo_l, do_l)
        out_r = beside(b_r, d_r, g_r, bo_r, do_r)
        for at, value in ((112, turn(g_l, 112)), (113, turn(do_l, 113)), (114, turn(g_r, 3)), (115, turn(do_r, 4))):
            out_r = jnp.where(one == at, value, out_r)
        last_row = jnp.where(one == LANES - 1, top, rows_r)

        @pl.when(sides[c] >= 0)
        def _(c=c, blocks=blocks, diag_rows=diag_rows, singles=(out_l, out_r, rows_l, last_row)):
            at = sides[c] * slot
            slots[pl.ds(at, 6), :] = blocks[0]
            slots[pl.ds(at + 6, 6), :] = blocks[1]
            slots[pl.ds(at + 12, 4), :] = diag_rows
            for n, value in enumerate(singles):
                slots[pl.ds(at + 16 + n, 1), :] = value

    corner = jnp.logical_and(row_of((GROUPS, LANES)) == RIM_ROWS - 1, lane == LANES - 1)
    for c, pack in ((0, pack_w), (1, pack_e)):
        slots[pl.ds(sides[c] * slot, GROUPS), :] = jnp.where(corner, top, pack)
    for c, at in ((4, 0), (5, SLABS), (6, GROUPS - 1), (7, SLABS + GROUPS - 1)):
        @pl.when(sides[c] >= 0)
        def _(c=c, at=at):
            slots[pl.ds(sides[c] * slot, 1), :] = own[at : at + 1]
    send(slots, slots_out.reshape(count * slot, LANES))
    for copy in results:
        copy.wait()


SMEM = pl.BlockSpec(memory_space=pltpu.SMEM)


def solve_kernel(
    levels, tiles_y,
    around_in, rims, fields,
    vectors, hands,
    around, sem, north_in, south_in, fb, fd, fg, pw, pe, ow, oe, ed, eg, ex, we, wn, rows,
):
    copies = fetching([(around_in, around)], sem)
    count = rims.shape[0]
    number_pieces, _, share, first = pieces_of(levels, count)
    slot = RIM_ROWS + number_pieces
    came = rims.reshape(count * slot, LANES)
    hand = hands.reshape(count * share, LANES)
    own = fields.at[pl.ds(PACKS, 56)]
    lane = lane_of((SLABS, LANES))
    slab = row_of((SLABS, LANES))
    one = lane_of((1, LANES))

    none = jnp.zeros((WIDE - ROWS + 4, LANES), jnp.float32)
    for ref in (fb, fd, fg):
        ref[ROWS - 4 : WIDE] = none
    for n, ref in enumerate((fb, fd, fg)):
        ref[0:ROWS] = fields[n * HELD : n * HELD + ROWS]
    copies[0].wait()
    src = [around[4 * count + c] for c in range(8)]

    def fetch(c, low, high):
        value = came[pl.ds(jnp.maximum(src[c], 0) * slot + low, high - low), :]
        return jnp.where(src[c] >= 0, value, 0.0)

    me = lax.axis_index("gx") * tiles_y + lax.axis_index("gy")
    for n in range(number_pieces):
        side = jnp.minimum((n * count + me) // (2 * levels), 3)
        base = (side + 1 - 2 * (side % 2)) * count

        def relay(d, carry, n=n, base=base):
            row = around[base + d] + n
            hand[pl.ds(d * share + first + n, 1), :] = came[pl.ds(row, 1), :]
            return carry

        for d in range(count):
            relay(d, 0)

    north_in[0:RIM_ROWS] = fetch(3, 0, RIM_ROWS)
    south_in[0:RIM_ROWS] = fetch(2, 0, RIM_ROWS)
    strips = {2: south_in, 3: north_in}
    for ref, low, high, n_lane, s_lane in ((fb, 0, 6, 80, 48), (fd, 6, 12, 80, 48), (fg, 12, 16, 96, 32)):
        size = high - low
        row, column = row_of((size, LANES)), lane_of((size, LANES))
        beyond = jnp.logical_and(row == size - 1, column >= n_lane)
        ref[ROWS : ROWS + size] = jnp.where(beyond, 0.0, strips[3][low:high])
        beyond = jnp.logical_and(row == 0, column < s_lane)
        ref[WIDE - size : WIDE] = jnp.where(beyond, 0.0, strips[2][low:high])
    empty = jnp.zeros((SLABS, LANES), jnp.float32)
    for ref, side, north, south in ((pw, 0, 6, 4), (pe, 1, 7, 5)):
        ref[...] = empty
        ref[0:GROUPS] = fetch(side, 0, GROUPS)
        ref[GROUPS : GROUPS + 1] = fetch(north, 0, 1)
        ref[SLABS - 1 : SLABS] = fetch(south, 0, 1)
    for ref, at, north, south in ((ow, 0, 5, 0), (oe, SLABS, 11, 6)):
        ref[...] = empty
        ref[0:GROUPS] = own[at : at + GROUPS]
        ref[GROUPS : GROUPS + 1] = turn(strips[3][north:north + 1], 16)
        ref[SLABS - 1 : SLABS] = turn(strips[2][south:south + 1], 16)

    def spread(ref, j):
        a = START[j]
        first, second = ref[comb(a, SLABS), :], ref[comb(a + 1, SLABS), :]
        third = ref[comb(a + 2, SLABS), :] if a + 2 < PLANES else second
        left = turn(jnp.where(lane >= OFF[j], first, second), -OFF[j])
        right = turn(jnp.where(lane >= OFF[j], second, third), -OFF[j])
        return left, right

    def seam_row(left, right, slab_at, lanes_at):
        east = turn(pe[slab_at : slab_at + 1], 112 - lanes_at)
        west = turn(pw[slab_at : slab_at + 1], 124 - lanes_at)
        right = jnp.where(one < 112, right, jnp.where(one < 116, east, jnp.where(one >= 124, west, 0.0)))
        return jnp.broadcast_to(left, (SLABS, LANES)), jnp.broadcast_to(right, (SLABS, LANES))

    seams = {
        0: ((0, seam_row(strips[2][18:19], strips[2][19:20], SLABS - 1, 28)),
            (GROUPS, seam_row(own[50:51], own[51:52], GROUPS - 1, 28))),
        GROUP - 1: ((GROUPS - 1, seam_row(strips[3][18:19], strips[3][19:20], GROUPS, 12)),
                    (SLABS - 1, seam_row(own[48:49], own[49:50], 0, 12))),
    }
    weight = STERIC / levels

    def missing(target, term, term_out, d, d_out, g):
        term, term_out, d, d_out, g = (
            turn(value[0], target - value[1]) for value in (term, term_out, d, d_out, g)
        )
        term = jnp.where(d > 0, weight * term, 0.0)
        term_out = jnp.where(d_out > 0, weight * term_out, 0.0)
        return jnp.where(one == target, g * term + d * d_out * (term - term_out), 0.0)

    def ring(ref, at):
        return ref[at : at + 1]

    outer = {j: [] for j in range(GROUP)}
    for j, at, beyond, o, lanes in ((0, 0, SLABS - 1, 0, 28), (GROUP - 1, GROUPS - 1, GROUPS, 16, 12)):
        own_row, corner = ring(pe, at), ring(pe, beyond)
        outer[j].append((1, at, missing(
            114, (corner, lanes + 2), (corner, lanes + 3), (own_row, o + 5), (own_row, o + 11), (own_row, o + 10),
        )))
        own_row, corner = ring(pw, at), ring(pw, beyond)
        outer[j].append((1, at, missing(
            125, (corner, lanes + 1), (corner, lanes), (own_row, o + 3), (own_row, o + 11), (own_row, o + 10),
        )))
    for j, at, c, j_out, d_l, d_r in ((2, GROUPS, 3, 3, (9, 96), (11, 79)), (5, SLABS - 1, 2, 4, (6, 48), (8, 31))):
        line_l, line_r = strips[c][16:17], strips[c][17:18]
        corner = ring(pw, at)
        outer[j].append((0, at, line_l + missing(
            0, (corner, OFF[j] + 9), (corner, OFF[j_out] + 9), (strips[c][d_l[0]:d_l[0] + 1], d_l[1]),
            (line_r, 113), (line_r, 112),
        )))
        corner = ring(pe, at)
        outer[j].append((1, at, jnp.where(one < 112, line_r, 0.0) + missing(
            111, (corner, OFF[j] + 9), (corner, OFF[j_out] + 9), (strips[c][d_r[0]:d_r[0] + 1], d_r[1]),
            (line_r, 115), (line_r, 114),
        )))
    for j in range(GROUP):
        o = OFF[j]
        inside = slab < GROUPS
        halves = [
            jnp.zeros((SLABS, LANES), jnp.float32),
            jnp.where(
                jnp.logical_and(inside, lane == 114), turn(pe[...], 114 - o - 8),
                jnp.where(jnp.logical_and(inside, lane == 125), turn(pw[...], 125 - o - 8), 0.0),
            ),
        ]
        for half, at, line in outer[j]:
            halves[half] = halves[half] + jnp.where(slab == at, line, 0.0)
        ex[j, :, 0:LANES] = halves[0]
        ex[j, :, LANES:] = halves[1]

        def rim(right, q, width):
            east = turn(pe[...], 112 - o - q)
            west = turn(pw[...], 128 - width - o - q)
            value = jnp.where(lane < 112 + width, east, jnp.where(lane >= 128 - width, west, 0.0))
            return jnp.where(lane < 112, right, value)

        left, right = spread(fd, j)
        right = rim(right, 3, 3)
        wet_l = jnp.where(left > 0, weight, 0.0)
        wet_r = jnp.where(right > 0, weight, 0.0)
        ed[j, :, 0:LANES] = left
        ed[j, :, LANES:] = right
        left, right = spread(fg, j)
        eg[j, :, 0:LANES] = left
        eg[j, :, LANES:] = rim(right, 6, 2)
        left, right = spread(fb, j)
        right = rim(right, 0, 3)
        seam_l = jnp.where(lane == 0, turn(pw[...], -o - 9), 0.0)
        seam_r = jnp.where(lane == 127, turn(ow[...], 127 - o - 9), 0.0)
        seam_r = jnp.where(lane == 111, turn(pe[...], 111 - o - 9), seam_r)
        seam_r = jnp.where(lane == 112, turn(oe[...], 112 - o - 9), seam_r)
        for at, (row_l, row_r) in seams.get(j, ()):
            seam_l = seam_l + jnp.where(slab == at, row_l, 0.0)
            seam_r = seam_r + jnp.where(slab == at, row_r, 0.0)
        vectors[0, j, :, 0:LANES] = left + wet_l * seam_l
        vectors[0, j, :, LANES:] = right + wet_r * seam_r

    for j in range(GROUP):
        d = ed[j]
        we[j] = d * turn(d, -1)
        above = ed[j + 1] if j < GROUP - 1 else turn(ed[0], -1, 0)
        wn[j] = d * above

    top = jnp.max(came[pl.ds(RIM_ROWS - 1, count, stride=slot), :], axis=0, keepdims=True)
    top = jnp.max(jnp.where(one == LANES - 1, top, 0.0), axis=1, keepdims=True)
    scale = STRETCH / top

    big = (SLABS, 2 * LANES)
    mine = jnp.logical_and(row_of(big) < GROUPS, lane_of(big) < SPAN_X)
    pair = 0
    for k in range(5):
        count_sums = min(k + 1, 4)
        sums = [None] * count_sums
        new = None if k == 4 else vectors.at[k]
        if k:
            v = vectors.at[k - 1]
            flow_below = wn[GROUP - 1] * (v[GROUP - 1] - turn(v[0], -1, 0))
            flow_below = turn(flow_below, 1, 0)
        for j in range(GROUP):
            if k:
                here = v[j]
                above = v[j + 1] if j < GROUP - 1 else turn(v[0], -1, 0)
                flow_x = we[j] * (here - turn(here, -1))
                flow_y = wn[j] * (here - above)
                image = eg[j] * here + (flow_x - turn(flow_x, 1)) + (flow_y - flow_below)
                if k == 1:
                    image = image + ex[j]
                fresh = scale * image - (STRETCH * ROOTS[k - 1]) * here
                flow_below = flow_y
                if k < 4:
                    new[j] = fresh
            else:
                fresh = new[j]
            held = jnp.where(mine, fresh, 0.0)
            for i in range(count_sums):
                other = vectors[i, j] if i < k else held
                value = held * other
                sums[i] = value if sums[i] is None else sums[i] + value
        for i in range(count_sums):
            rows[pair : pair + 1] = jnp.sum(sums[i][:, 0:LANES] + sums[i][:, LANES:], axis=0, keepdims=True)
            pair += 1
    rows[pair : pair + 1] = jnp.where(one == 0, top, 0.0)
    rows[pair + 1 : 16] = jnp.zeros((15 - pair, LANES), jnp.float32)
    total = jnp.sum(rows[...], axis=1, keepdims=True)
    spot = lane_of((16, LANES)) == gram_lane(row_of((16, LANES)))
    line = jnp.sum(jnp.where(spot, total, 0.0), axis=0, keepdims=True)
    line = jnp.broadcast_to(line, (count, LANES))
    if first == 0:
        line = jnp.where(lane_of((count, LANES)) % 16 < 12, hand[pl.ds(0, count, stride=share), :], line)
    hand[pl.ds(0, count, stride=share), :] = line


def finish_kernel(
    levels, per, hands, vectors, edges, inner, tracer_out, surface_out,
    cells, flat, left, right, message, out_sems,
):
    count = hands.shape[0]
    _, runs, share, first = pieces_of(levels, count)
    came = hands.reshape(count * share, LANES)
    steps = levels // per
    chunks = [pl.ds(step * per * ROWS, per * ROWS) for step in range(steps)]
    results = []

    for c in range(4):
        for j, device, low, size in runs[c ^ 1]:
            value = came[pl.ds(device * share + first + j, size, stride=share), :]
            message[c, low : low + size] = value
    second = lane_of((SLABS, LANES)) % 16 == 1
    sums = []
    for k in range(levels):
        value = edges[2 * levels - 1] * jnp.concatenate([
            jnp.where(second, turn(message[1], 1 - k), turn(message[0], -k)),
            message[2, k : k + 1], message[2, k + levels : k + levels + 1],
            message[3, k : k + 1], message[3, k + levels : k + levels + 1],
            jnp.zeros((EDGE - SLABS - 4, LANES), jnp.float32),
        ], axis=0)
        if k:
            value = value + edges[2 * levels + k - 1] * sums[-1]
        sums.append(value * edges[levels - 1 + k])
    for k in range(levels - 2, -1, -1):
        sums[k] = sums[k] + edges[k] * sums[k + 1]
    lane = lane_of((GROUPS, LANES))
    slab = row_of((GROUPS, LANES))
    for k in range(levels):
        west = sums[k][0:GROUPS]
        east = turn(west, -18)
        south_l, south_r = sums[k][SLABS : SLABS + 1], sums[k][SLABS + 1 : SLABS + 2]
        north_l = turn(sums[k][SLABS + 2 : SLABS + 3], 16)
        north_r = turn(sums[k][SLABS + 3 : SLABS + 4], 16)
        for a in range(PLANES):
            rim = None
            for at, source in [(at, west) for at in FIRST_OF[a]] + [(at, east) for at in LAST_OF[a]]:
                rim = jnp.where(lane == at, source, 0.0 if rim is None else rim)
            rows = comb(k * ROWS + a)
            if rim is None:
                cells[rows, :] = inner[rows, :]
                continue
            if a == 0:
                rim = rim + jnp.where(slab == 0, south_l, 0.0)
            if a == 1:
                rim = rim + jnp.where(jnp.logical_and(slab == 0, lane < 112), south_r, 0.0)
            if a == PLANES - 2:
                rim = rim + jnp.where(jnp.logical_and(slab == GROUPS - 1, lane >= 16), north_l, 0.0)
            if a == PLANES - 1:
                rim = rim + jnp.where(slab == GROUPS - 1, jnp.where(lane < 16, north_l, north_r), 0.0)
            cells[rows, :] = inner[rows, :] + rim
        if k % per == per - 1:
            step = k // per
            copy = pltpu.make_async_copy(
                cells.at[chunks[step]], tracer_out.at[chunks[step]], out_sems.at[1 + step]
            )
            copy.start()
            results.append(copy)

    row = jnp.sum(came[pl.ds(0, count, stride=share), :], axis=0, keepdims=True)
    one = lane_of((1, LANES))
    entry = {}
    pair = 0
    for k in range(5):
        for i in range(min(k + 1, 4)):
            value = jnp.sum(jnp.where(one == gram_lane(pair), row, 0.0), axis=1, keepdims=True)
            entry[i, k] = entry[k, i] = value
            pair += 1
    top = jnp.sum(jnp.where(one == gram_lane(pair), row, 0.0), axis=1, keepdims=True) * (1.0 / count)

    def image(c):
        out = [None] * 5
        for k in range(4):
            if c[k] is None:
                continue
            low = ROOTS[k] * c[k]
            out[k] = low if out[k] is None else out[k] + low
            out[k + 1] = (1.0 / STRETCH) * c[k]
        return out

    def dot(a, b):
        total = None
        for i in range(5):
            if a[i] is None:
                continue
            inner = None
            for j in range(5):
                if b[j] is not None:
                    value = entry[i, j] * b[j]
                    inner = value if inner is None else inner + value
            total = a[i] * inner if total is None else total + a[i] * inner
        return total

    def axpy(a, s, b):
        return [
            x if y is None else (s * y if x is None else x + s * y) for x, y in zip(a, b)
        ]

    r = [jnp.ones((1, 1), jnp.float32)] + [None] * 4
    p = list(r)
    x = [None] * 5
    rr = entry[0, 0]
    for n in range(ITERS):
        q = image(p)
        step = rr / jnp.maximum(dot(p, q), TINY)
        step = jnp.clip(step, top * (1.0 / HIGH_RATE), top * (1.0 / LOW_RATE))
        x = axpy(x, step, p)
        if n < ITERS - 1:
            r = axpy(r, -step, q)
            fresh = jnp.maximum(dot(r, r), 0.0)
            p = axpy(r, fresh / jnp.maximum(rr, TINY), p)
            rr = fresh
    factors = [c / top for c in x[:4]]
    for j in range(GROUP):
        value = None
        for k in range(4):
            term = factors[k] * vectors[k, j]
            value = term if value is None else value + term
        left[j] = turn(value[:, 0:LANES], OFF[j])
        right[j] = turn(value[:, LANES:], OFF[j])
    lane = lane_of((SLABS, LANES))
    for a in range(PLANES):
        value = None
        for j in range(GROUP):
            for half, ref in ((0, left), (1, right)):
                low = max(SPAN_X * j + LANES * half - LANES * a, 0)
                high = min(SPAN_X * j + (LANES if half == 0 else SPAN_X) - LANES * a, LANES)
                if low >= high:
                    continue
                value = ref[j] if value is None else jnp.where(lane >= low, ref[j], value)
        flat[comb(a), :] = value[0:GROUPS]
    results.append(pltpu.make_async_copy(flat, surface_out.reshape(ROWS, LANES), out_sems.at[0]))
    results[-1].start()
    for copy in results:
        copy.wait()


def tracer_kernel(
    levels, per, sides, around, temp_in, zonal_in, merid_in, rates_in, fields,
    out, edges,
    temp, zonal, merid, rates, ocean,
    te, tw, tn, ts, stepped, border, sems,
):
    steps = levels // per
    pairs = []
    for step in range(steps):
        chunk = pl.ds(step * per * ROWS, per * ROWS)
        pairs += [
            (a.at[chunk], b.at[chunk]) for a, b in ((temp_in, temp), (zonal_in, zonal), (merid_in, merid))
        ]
    copies = fetching(pairs + [(rates_in.reshape((levels - 1) * ROWS, LANES), rates)], sems)
    lane = lane_of((GROUPS, LANES))
    one = lane_of((1, LANES))
    clear_terms(tn, ts)

    ocean[...] = jnp.where(fields[HELD : HELD + ROWS] > 0, 1.0, 0.0)
    for step in range(steps):
        for copy in copies[3 * step : 3 * step + 3]:
            copy.wait()

        def level(k, carry):
            t, u, v = (Level(ref, k * ROWS) for ref in (temp, zonal, merid))
            for a in range(PLANES):
                own = t.plane(a)
                quarter = ADVECT * own
                store_terms(a, own, u.plane(a) * quarter, v.plane(a) * quarter, te, tw, tn, ts)
            for a in range(PLANES):
                own = t.plane(a)
                change = inner_sum(a, te, tw, tn, ts) - 4.0 * DIFFUSE * own
                stepped[k, a] = own + ocean[comb(a), :] * change
            return carry

        lax.fori_loop(step * per, step * per + per, level, 0)
    copies[-1].wait()

    def block(a, carry):
        for low in range(0, GROUPS, 8):
            size = min(8, GROUPS - low)

            def rows(k):
                return pl.ds(k * ROWS + low * PLANES + a, size, stride=PLANES)

            gains = []
            sums = []
            for k in range(levels):
                value = stepped[k, a, low : low + size]
                pivot = 1.0
                if k > 0:
                    pivot = pivot + upper - upper * gains[-1]
                    value = value + upper * sums[-1]
                if k < levels - 1:
                    lower = rates[rows(k), :]
                    inverse = 1.0 / (pivot + lower)
                    gains.append(lower * inverse)
                    upper = lower
                else:
                    inverse = 1.0 / pivot
                sums.append(value * inverse)
            result = sums[-1]
            out[rows(levels - 1), :] = result
            for k in range(levels - 2, -1, -1):
                result = sums[k] + gains[k] * result
                out[rows(k), :] = result
        return carry

    lax.fori_loop(0, PLANES, block, 0)

    def edge(ref, base, at):
        def get(a):
            return ref[comb(base + a), :].astype(jnp.float32)

        border[0:GROUPS] = jnp.where(
            lane % 16 == 1, turn(choose(LAST, lane, get), 18), choose(START, lane, get)
        )
        border[SLABS : SLABS + 2] = ref[base : base + 2, :].astype(jnp.float32)
        rows = ref[base + ROWS - 2 : base + ROWS, :].astype(jnp.float32)
        border[SLABS + 2 : SLABS + 3] = turn(jnp.where(one >= 16, rows[0:1], rows[1:2]), -16)
        border[SLABS + 3 : SLABS + 4] = turn(rows[1:2], -16)
        edges[at] = border[...]

    border[...] = jnp.zeros_like(border)
    edge(ocean, 0, 2 * levels - 1)
    for c in (2, 3):
        rows = pl.ds(SLABS + 2 * (c - 2), 2)
        value = edges[2 * levels - 1, rows]
        edges[2 * levels - 1, rows] = jnp.where(around[sides + c] >= 0, value, 0.0)
    gain = None
    for k in range(levels):
        pivot = 1.0
        if k > 0:
            upper = edges[2 * levels + k - 1]
            pivot = pivot + upper - upper * gain
        if k < levels - 1:
            edge(rates, k * ROWS, 2 * levels + k)
            lower = edges[2 * levels + k]
            inverse = 1.0 / (pivot + lower)
            gain = lower * inverse
            edges[k] = gain
        else:
            inverse = 1.0 / pivot
        edges[levels - 1 + k] = inverse


def on_device(
    thermal_anomaly,
    zonal_flow_ratio,
    meridional_flow_ratio,
    diffusion_rates,
    ocean_bottom_scaled,
    ocean_indicator,
    operator_diagonal,
    elevation_source,
    block_positions,
):
    levels, cells = thermal_anomaly.shape[1:]
    nx = lax.axis_size("gx")
    ny = lax.axis_size("gy")
    count = block_positions.shape[0]
    planes = (ocean_bottom_scaled, ocean_indicator, operator_diagonal, elevation_source)
    depth, ocean, diag, source = planes
    f32 = jnp.float32
    per = next(n for n in (4, 2, 6, levels) if levels % n == 0 and n * ROWS % 8 == 0)
    steps = levels // per
    sent = next(n for n in (2, 4, 6, levels) if levels % n == 0 and n * ROWS % 8 == 0)
    few = next(n for n in (4, 2, 6, levels) if levels % n == 0 and n * ROWS % 8 == 0)
    params = pltpu.CompilerParams(vmem_limit_bytes=BUDGET)
    temp, zonal, merid = (
        array.reshape(levels * ROWS, LANES)
        for array in (thermal_anomaly, zonal_flow_ratio, meridional_flow_ratio)
    )
    rates = diffusion_rates.reshape(levels - 1, 1, cells)
    temp, zonal, merid, rates, depth, ocean, diag, source, positions = (
        pltpu.with_memory_space_constraint(array, pltpu.HBM)
        for array in (temp, zonal, merid, rates, depth, ocean, diag, source, block_positions)
    )
    hbm = pl.BlockSpec(memory_space=pltpu.HBM)
    here = pl.BlockSpec(memory_space=pltpu.VMEM)

    def vmem(*shape, kind=f32):
        return pltpu.VMEM(shape, kind)

    def out(*shape, kind=f32):
        return jax.ShapeDtypeStruct(shape, kind)

    def sems(number):
        return pltpu.SemaphoreType.DMA((number,))

    deep = vmem(levels * ROWS, LANES)
    flat = vmem(ROWS, LANES)
    flat_int = vmem(ROWS, LANES, kind=jnp.int32)
    plane = vmem(PLANES, GROUPS, LANES)
    tall = vmem(PLANES, 40, LANES)
    numbers = pltpu.SMEM((count,), jnp.int32)
    number_pieces, _, share, _ = pieces_of(levels, count)
    slot = RIM_ROWS + number_pieces
    fields, slots, around = pl.pallas_call(
        functools.partial(forcing_kernel, levels, few, nx, ny),
        in_specs=[hbm] * 8,
        out_specs=[here, hbm, hbm],
        out_shape=[
            out(FIELDS, LANES), pltpu.HBM((count, 1, slot * LANES), f32), out(4 * count + 8, kind=jnp.int32),
        ],
        scratch_shapes=[deep] * 3 + [flat, flat_int, flat]
        + [vmem(count * slot, LANES)]
        + [flat] * 3 + [plane] * 3 + [tall] * 2
        + [vmem(4, 2 * levels, LANES), numbers, numbers]
        + [pltpu.SMEM((4 * count + 8,), jnp.int32), sems(3 * (levels // few) + 5), sems(2)],
        compiler_params=params,
        name="forcing",
    )(positions, temp, zonal, merid, depth, ocean, diag, source)
    rims = lax.all_to_all(slots, BOTH, 0, 0, tiled=True)

    inner, edges = pl.pallas_call(
        functools.partial(tracer_kernel, levels, per, 4 * count),
        in_specs=[SMEM] + [hbm] * 4 + [here],
        out_specs=[here] * 2,
        out_shape=[out(levels * ROWS, LANES), out(3 * levels - 1, EDGE, LANES)],
        scratch_shapes=[deep] * 3 + [vmem((levels - 1) * ROWS, LANES), flat]
        + [plane] * 2 + [tall] * 2
        + [vmem(levels, PLANES, GROUPS, LANES), vmem(EDGE, LANES), sems(3 * steps + 1)],
        compiler_params=params,
        name="tracer",
    )(around, temp, zonal, merid, rates, fields)

    rims, edges = lax.optimization_barrier((rims, edges))
    extended = vmem(GROUP, SLABS, 2 * LANES)
    vectors, hand = pl.pallas_call(
        functools.partial(solve_kernel, levels, ny),
        in_specs=[pl.BlockSpec(memory_space=pl.ANY)] + [here] * 2,
        out_specs=[here] * 2,
        out_shape=[out(4, GROUP, SLABS, 2 * LANES), out(count, 1, share * LANES)],
        scratch_shapes=[pltpu.SMEM((4 * count + 8,), jnp.int32), sems(1)]
        + [vmem(SLABS, LANES)] * 2 + [vmem(WIDE, LANES)] * 3 + [vmem(SLABS, LANES)] * 4 + [extended] * 5 + [vmem(16, LANES)],
        compiler_params=params,
        name="vectors",
    )(around, rims, fields)
    hands = lax.all_to_all(hand, BOTH, 0, 0, tiled=True)

    new_temp, surface = pl.pallas_call(
        functools.partial(finish_kernel, levels, sent),
        in_specs=[here] * 4,
        out_specs=[hbm] * 2,
        out_shape=[out(levels * ROWS, LANES), out(1, cells)],
        scratch_shapes=[
            deep, flat, vmem(GROUP, SLABS, LANES), vmem(GROUP, SLABS, LANES), vmem(4, 2 * levels, LANES),
            sems(1 + levels // sent),
        ],
        compiler_params=params,
        name="finish",
    )(hands, vectors, edges, inner)
    return new_temp.reshape(1, levels, cells), surface


def solution(mesh):
    deep = P(BOTH, None, None)
    flat = P(BOTH, None)
    return jax.shard_map(
        on_device,
        mesh=mesh,
        in_specs=(deep, deep, deep, deep, flat, flat, flat, flat, P()),
        out_specs=(deep, flat),
        check_vma=False,
    )
```
